32 devices in a mesh: chan: 4 (over z), freq: 8 (over y, x, core).
Axes of the slice: x: 2, y: 2, z: 4, core: 2. Of those that a mesh axis runs over, the one named last changes fastest.
Arguments:
- spectra: bfloat16 [2, 32, 256, 512], P(None, None, 'freq', 'chan'), may hold values from -6 to 6
- block_position: int32 [4], replicated, may hold values from 0 to 3, each once
Outputs:
- taup: float32 [4, 256, 512], P('chan', 'freq')
The draws below stay inside these ranges and needn't reach their ends.
Inputs may be any that keep to these rules, and one draw needn't show every extreme that they name: block_position is a permutation: every fiber position 0 to 3 holds exactly one stored block; group k of the chan axis stores block k.
All inputs are finite; a program needn't handle non-finite values.
Results may differ from the reference program's by a relative error of at most 0.0003.
Values may be sent and summed in bfloat16 or wider, within the bound.
No kernel may reach another device: no remote copies, remote signals or barrier semaphores. Data moves between devices by JAX's collectives and lax.ppermute only.
A program may use at most 64 MiB of HBM per device.

```python
import math
import jax
import jax.numpy as jnp
from jax import lax

SEGMENTS = 32
FREQS = 256
BLOCK = 128
GROUP_BLOCKS = 1
SLOWNESS = 256
LAG_TIMES = 512
BLOCKS = 4
CHANNELS = 512
N_CHAN = 4


def level_of(own_key, shape, shards, low, largest):
    def one(position, parts):
        steps = jax.random.uniform(jax.random.fold_in(jax.random.fold_in(own_key, 6), position), (parts,), jnp.float32, low / len(shards), largest / len(shards))
        return jnp.repeat(jnp.exp(steps), shape[position] // parts).reshape((-1,) + (1,) * (len(shape) - position - 1))

    factor_of = one(*shards[0])
    for cut in shards[1:]:
        factor_of = factor_of * one(*cut)
    return factor_of


def normal_values(stream_key, shape, scale, reach, cuts=(), kind=jnp.bfloat16):
    factor_of = level_of(stream_key, shape, cuts, -0.22, 0.18) if cuts else 1.0
    entries = jax.random.normal(stream_key, shape, jnp.float32) * scale * factor_of
    return jnp.minimum(jnp.maximum(entries, -reach), reach).astype(kind)


def setup_inputs(seed: int = 0) -> dict:
    key_of = jax.random.split(jax.random.key(seed), 3)
    return {
        "spectra": normal_values(key_of[0], (2, SEGMENTS, FREQS, CHANNELS), 1.0, 6.0, ((2, 8), (3, 4))),
        "block_position": jax.random.permutation(key_of[1], BLOCKS).astype(jnp.int32),
    }


def lag_sums(panel):
    leading = panel.shape[:-2]
    extent = panel.shape[-1]
    flat_panel = panel.reshape(leading + (extent * extent,))
    padded = jnp.pad(flat_panel, [(0, 0)] * len(leading) + [(0, extent)])
    skewed = padded.reshape(leading + (extent, extent + 1))
    row_index = lax.broadcasted_iota(jnp.int32, (extent, extent + 1), 0)
    col_index = lax.broadcasted_iota(jnp.int32, (extent, extent + 1), 1)
    before_wrap = row_index + col_index < extent
    forward_lags = lax.optimization_barrier(jnp.sum(jnp.where(before_wrap, skewed, 0.0), axis=-2))
    backward_lags = lax.optimization_barrier(jnp.sum(jnp.where(before_wrap, 0.0, skewed), axis=-2))
    return jnp.concatenate([backward_lags[..., 1:], forward_lags[..., :extent]], axis=-1)

def angles(numerator):
    modulus = 8 * FREQS * BLOCK
    return jnp.mod(numerator, modulus).astype(jnp.float32) * (2.0 * math.pi / modulus)

def inverse_counts(delta_start, delta_count, nblocks):
    deltas = delta_start + lax.broadcasted_iota(jnp.int32, (delta_count, 2 * BLOCK), 0)
    lag_value = lax.broadcasted_iota(jnp.int32, (delta_count, 2 * BLOCK), 1) - BLOCK
    counts = SEGMENTS * (nblocks - deltas) * (BLOCK - jnp.abs(lag_value))
    usable = (lag_value > -BLOCK) & ((deltas >= 1) | (lag_value >= 1))
    inverse = jnp.where(usable, 1.0 / jnp.maximum(counts, 1).astype(jnp.float32), 0.0)
    return jnp.concatenate([inverse, inverse], axis=-1)

def slant_terms(means_block, freq_ids, delta_start, group_blocks):
    bins, delta_count = (means_block.shape[0], means_block.shape[1])
    slow_index = lax.broadcasted_iota(jnp.int32, (1, 1, SLOWNESS), 2) - SLOWNESS // 2
    lag_value = lax.broadcasted_iota(jnp.int32, (1, 2 * BLOCK, 1), 1) - BLOCK
    freq_column = freq_ids.reshape(bins, 1, 1)
    lag_angle = angles(freq_column * slow_index * lag_value)
    cosine = jnp.cos(lag_angle)
    sine_part = jnp.sin(lag_angle)
    lag_table = jnp.concatenate([jnp.concatenate([cosine, sine_part], -1), jnp.concatenate([-sine_part, cosine], -1)], 1)
    rotated = jnp.einsum('fdk,fkp->fdp', means_block, lag_table, precision=lax.Precision.HIGHEST)
    deltas = delta_start + lax.broadcasted_iota(jnp.int32, (1, delta_count, 1), 1)
    offset_angle = angles(freq_column * slow_index * (BLOCK * deltas))
    offset_cos = jnp.cos(offset_angle)
    offset_sin = jnp.sin(offset_angle)
    real_part = rotated[..., :SLOWNESS]
    imag_part = rotated[..., SLOWNESS:]
    shifted_re = real_part * offset_cos - imag_part * offset_sin
    shifted_im = real_part * offset_sin + imag_part * offset_cos
    apertures = delta_count // group_blocks
    summed_re = shifted_re.reshape(bins, apertures, group_blocks, SLOWNESS).sum(axis=2)
    summed_im = shifted_im.reshape(bins, apertures, group_blocks, SLOWNESS).sum(axis=2)
    lag_time = lax.broadcasted_iota(jnp.int32, (1, LAG_TIMES), 1) - LAG_TIMES // 2
    time_angle = angles(freq_ids.reshape(bins, 1) * (4 * BLOCK * lag_time))
    spectrum = jnp.concatenate([summed_re, summed_im], axis=0)
    kernel = jnp.concatenate([jnp.cos(time_angle), -jnp.sin(time_angle)], axis=0)
    result = jnp.einsum('gas,gt->ast', spectrum, kernel, precision=lax.Precision.HIGHEST)
    return result.reshape(apertures * SLOWNESS, LAG_TIMES)

def slant_all(mean_stacks, freq_start, delta_start, group_blocks):
    freq_count, delta_count = (mean_stacks.shape[0], mean_stacks.shape[1])
    block_bins = 4
    block_total = freq_count // block_bins
    blocks = mean_stacks.reshape(block_total, block_bins, delta_count, 4 * BLOCK)
    freq_table = (freq_start + jnp.arange(freq_count, dtype=jnp.int32)).reshape(block_total, block_bins)

    def add_block(running, block_item):
        return (running + slant_terms(block_item[0], block_item[1], delta_start, group_blocks), None)
    initial = jnp.zeros((delta_count // group_blocks * SLOWNESS, LAG_TIMES), jnp.float32)
    summed, unused = lax.scan(add_block, initial, (blocks, freq_table))
    return summed

def cross_of_bin(spectra, freq_id, selector):
    slice_bin = lax.dynamic_index_in_dim(spectra, freq_id, axis=2, keepdims=False).astype(jnp.float32)
    left_side = jnp.concatenate([slice_bin[0], slice_bin[1]], axis=0)
    right_side = jnp.stack([left_side, jnp.concatenate([slice_bin[1], -slice_bin[0]], axis=0)], axis=1)
    cross_block = jnp.einsum('kc,kpd->cpd', left_side, right_side, precision=lax.Precision.HIGHEST)
    nblocks = selector.shape[0]
    panels = cross_block.reshape(nblocks, BLOCK, 2, nblocks, BLOCK).transpose(0, 3, 2, 1, 4)
    lag_block = lag_sums(panels).reshape(nblocks * nblocks, 4 * BLOCK)
    return jnp.dot(selector, lag_block, precision=lax.Precision.HIGHEST)

def reference(spectra, block_position):
    nblocks = block_position.shape[0]
    block_delta = (block_position[None, :] - block_position[:, None]).reshape(1, nblocks * nblocks)
    targets = jnp.arange(nblocks, dtype=jnp.int32)[:, None]
    selector = ((block_delta == targets) & (block_delta >= 0)).astype(jnp.float32)
    stacks = lax.map(lambda freq_id: cross_of_bin(spectra, freq_id, selector), jnp.arange(FREQS, dtype=jnp.int32))
    mean_stacks = stacks * inverse_counts(0, nblocks, nblocks)[None]
    image_term = slant_all(mean_stacks, 0, 0, GROUP_BLOCKS)
    out_scale = math.sqrt(SEGMENTS / (FREQS * GROUP_BLOCKS))
    return (image_term * out_scale).reshape(N_CHAN, SLOWNESS, LAG_TIMES)
```

```python
import functools
import math

import jax
import jax.numpy as jnp
import numpy as np
from jax import lax
from jax.experimental import pallas as pl
from jax.experimental.pallas import tpu as pltpu
from jax.sharding import PartitionSpec as P

SEGMENTS = 32
FREQS = 256
BLOCK = 128
SLOWNESS = 256
LAG_TIMES = 512
MODULUS = 8 * FREQS * BLOCK


def unit_phase(numerator):
    quarter = MODULUS // 4
    turn = numerator & (MODULUS - 1)
    quadrant = lax.shift_right_logical(turn + quarter // 2, quarter.bit_length() - 1)
    x = (turn - quadrant * quarter).astype(jnp.float32) * (2.0 * math.pi / MODULUS)
    y = x * x
    sine = x * (1.0 + y * (-1.0 / 6 + y * (1.0 / 120 + y * (-1.0 / 5040 + y * (1.0 / 362880)))))
    cosine = 1.0 + y * (-0.5 + y * (1.0 / 24 + y * (-1.0 / 720 + y * (1.0 / 40320))))
    odd = (quadrant & 1) == 1
    first = jnp.where(odd, sine, cosine)
    second = jnp.where(odd, cosine, sine)
    first = jnp.where(((quadrant + 1) & 2) == 2, -first, first)
    second = jnp.where((quadrant & 2) == 2, -second, second)
    return first, second


def halves(value):
    high = value.astype(jnp.bfloat16)
    return high, (value - high.astype(jnp.float32)).astype(jnp.bfloat16)


def stack_kernel(groups, bins, spec_ref, position_ref, start_ref, weight_ref, out_ref, wide_ref):
    rows = spec_ref.shape[1] // bins
    windows = rows // 2
    for place in range(groups):
        block = jnp.int32(0)
        for group in range(groups):
            block = jnp.where(position_ref[group] == place, group, block)
        wide_ref[place] = spec_ref[block].astype(jnp.float32)

    row_index = lax.broadcasted_iota(jnp.int32, (BLOCK, BLOCK), 0)
    lag_index = lax.broadcasted_iota(jnp.int32, (BLOCK, BLOCK), 1)
    mirror = jnp.where(row_index + lag_index == BLOCK - 1, 1.0, 0.0).astype(jnp.bfloat16)
    ahead = lag_index <= row_index
    ahead = jnp.concatenate([ahead, ahead], axis=1)
    low_rows = lax.broadcasted_iota(jnp.int32, (8, SLOWNESS), 0)
    high_rows = lax.broadcasted_iota(jnp.int32, (16, SLOWNESS), 0) * 8
    shift_rows = lax.broadcasted_iota(jnp.int32, (2 * groups, SLOWNESS), 0)
    shift_rows = jnp.where(shift_rows < groups, shift_rows, shift_rows - groups - 1) * BLOCK

    def slow(shape):
        return lax.broadcasted_iota(jnp.int32, shape, 1) - SLOWNESS // 2

    for f in range(bins):
        left, right = [], []
        for place in range(groups):
            value = wide_ref[place, pl.ds(f, rows, stride=bins), :]
            real, imag = value[:windows], value[windows:]
            left.append(value)
            right.append(
                jnp.concatenate(
                    [jnp.concatenate([real, imag], 1), jnp.concatenate([imag, -real], 1)], 0
                )
            )
        left = lax.dot_general(
            mirror,
            jnp.concatenate(left, 0).astype(jnp.bfloat16),
            (((1,), (1,)), ((), ())),
            preferred_element_type=jnp.float32,
        ).astype(jnp.bfloat16)
        right = jnp.concatenate(right, 0).astype(jnp.bfloat16)
        forward, backward = [], []
        for delta in range(groups):
            panel = jnp.dot(
                left[:, : rows * (groups - delta)],
                right[rows * delta :],
                preferred_element_type=jnp.float32,
            )
            skewed = jnp.concatenate(
                [
                    pltpu.roll(panel[:, :BLOCK], 1, 1, stride=1, stride_axis=0),
                    pltpu.roll(panel[:, BLOCK:], 1, 1, stride=1, stride_axis=0),
                ],
                axis=1,
            )
            forward.append(jnp.sum(jnp.where(ahead, skewed, 0.0), 0, keepdims=True))
            backward.append(jnp.sum(jnp.where(ahead, 0.0, skewed), 0, keepdims=True))
        lags = jnp.concatenate(forward + backward, 0)
        weight = weight_ref[...]
        means = jnp.concatenate([lags[:, :BLOCK] * weight, lags[:, BLOCK:] * weight], 0)
        mean_high, mean_low = halves(means)
        spread = jnp.concatenate(
            [
                jnp.concatenate([mean_high, mean_high], 1),
                jnp.concatenate([mean_low, jnp.zeros_like(mean_low)], 1),
            ],
            0,
        )
        freq = start_ref[0] + f
        low_cos, low_sin = unit_phase(freq * slow(low_rows.shape) * low_rows)
        high_cos, high_sin = unit_phase(freq * slow(high_rows.shape) * high_rows)
        low_cos, low_sin = low_cos[None], low_sin[None]
        high_cos, high_sin = high_cos[:, None], high_sin[:, None]
        lag_cos = (high_cos * low_cos - high_sin * low_sin).reshape(BLOCK, SLOWNESS)
        lag_sin = (high_sin * low_cos + high_cos * low_sin).reshape(BLOCK, SLOWNESS)
        cos_high, cos_low = halves(lag_cos)
        sin_high, sin_low = halves(lag_sin)
        by_cos = jnp.dot(
            spread, jnp.concatenate([cos_high, cos_low], 0), preferred_element_type=jnp.float32
        )
        by_sin = jnp.dot(
            spread, jnp.concatenate([sin_high, sin_low], 0), preferred_element_type=jnp.float32
        )
        by_cos = by_cos[: 4 * groups] + by_cos[4 * groups :]
        by_sin = by_sin[: 4 * groups] + by_sin[4 * groups :]
        real = by_cos[: 2 * groups] - by_sin[2 * groups :]
        imag = by_sin[: 2 * groups] + by_cos[2 * groups :]
        shift_cos, shift_sin = unit_phase(freq * slow(shift_rows.shape) * shift_rows)
        turned_re = real * shift_cos - imag * shift_sin
        turned_im = real * shift_sin + imag * shift_cos
        out_ref[f, 0] = turned_re[:groups] + turned_re[groups:]
        out_ref[f, 1] = turned_im[:groups] + turned_im[groups:]


def inverse_counts(nblocks):
    delta = np.arange(nblocks)[:, None]
    lag = np.arange(BLOCK)[None, :]
    rows = []
    for lags in (lag, lag - BLOCK):
        usable = (lags > -BLOCK) & ((delta >= 1) | (lags >= 1))
        count = SEGMENTS * (nblocks - delta) * (BLOCK - np.abs(lags))
        rows.append(np.where(usable, 1.0 / np.maximum(count, 1), 0.0))
    return np.concatenate(rows, 0) * math.sqrt(SEGMENTS / FREQS)


def time_table(groups, parts):
    bins = FREQS // parts // groups
    group, part, f = np.meshgrid(
        np.arange(groups), np.arange(parts), np.arange(bins), indexing="ij"
    )
    freq = (part * groups + group) * bins + f
    lag_time = np.arange(LAG_TIMES) - LAG_TIMES // 2
    angle = 2.0 * math.pi / LAG_TIMES * ((freq[..., None] * lag_time) % LAG_TIMES)
    table = np.stack([np.cos(angle), -np.sin(angle)], axis=3)
    return table.reshape(groups * parts, bins, 2, LAG_TIMES).astype(np.float32)


def shards(spectra, block_position):
    groups = lax.axis_size("chan")
    parts = lax.axis_size("freq")
    rows = spectra.shape[0] * spectra.shape[1]
    freq_dev = spectra.shape[2]
    bins = freq_dev // groups
    first_bin = lax.axis_index("freq") * freq_dev + lax.axis_index("chan") * bins

    chunks = spectra.reshape(rows, groups, bins, BLOCK)
    gathered = lax.all_to_all(chunks, "chan", split_axis=1, concat_axis=0, tiled=False)
    gathered = gathered.reshape(groups, rows * bins, BLOCK)
    terms = pl.pallas_call(
        functools.partial(stack_kernel, groups, bins),
        out_shape=jax.ShapeDtypeStruct((bins, 2, groups, SLOWNESS), jnp.float32),
        in_specs=[
            pl.BlockSpec(memory_space=pltpu.VMEM),
            pl.BlockSpec(memory_space=pltpu.SMEM),
            pl.BlockSpec(memory_space=pltpu.SMEM),
            pl.BlockSpec(memory_space=pltpu.VMEM),
        ],
        out_specs=pl.BlockSpec(memory_space=pltpu.VMEM),
        scratch_shapes=[pltpu.VMEM((groups, rows * bins, BLOCK), jnp.float32)],
        compiler_params=pltpu.CompilerParams(vmem_limit_bytes=32 * 1024 * 1024),
        name="stack_and_slant",
    )(
        gathered,
        block_position,
        first_bin.astype(jnp.int32).reshape(1),
        jnp.asarray(inverse_counts(groups), jnp.float32),
    )
    slow_dev = SLOWNESS // parts
    terms = terms.reshape(bins, 2, groups, parts, slow_dev).transpose(2, 3, 0, 1, 4)
    terms = terms.reshape(groups * parts, bins, 2, slow_dev)
    arrived = lax.all_to_all(terms, ("chan", "freq"), split_axis=0, concat_axis=0, tiled=True)
    image = jnp.einsum(
        "gfcs,gfct->st",
        arrived,
        jnp.asarray(time_table(groups, parts)),
        precision=lax.Precision.HIGHEST,
    )
    return image[None]


def solution(mesh):
    return jax.shard_map(
        shards,
        mesh=mesh,
        in_specs=(P(None, None, "freq", "chan"), P()),
        out_specs=P("chan", "freq", None),
        check_vma=False,
    )
```

```python
import functools
import math

import jax
import jax.numpy as jnp
import numpy as np
from jax import lax
from jax.experimental import pallas as pl
from jax.experimental.pallas import tpu as pltpu
from jax.sharding import PartitionSpec as P

SEGMENTS = 32
FREQS = 256
BLOCK = 128
SLOWNESS = 256
LAG_TIMES = 512
MODULUS = 8 * FREQS * BLOCK


def unit_phase(numerator):
    quarter = MODULUS // 4
    turn = numerator & (MODULUS - 1)
    quadrant = lax.shift_right_logical(turn + quarter // 2, quarter.bit_length() - 1)
    x = (turn - quadrant * quarter).astype(jnp.float32) * (2.0 * math.pi / MODULUS)
    y = x * x
    sine = x * (1.0 + y * (-1.0 / 6 + y * (1.0 / 120 + y * (-1.0 / 5040 + y * (1.0 / 362880)))))
    cosine = 1.0 + y * (-0.5 + y * (1.0 / 24 + y * (-1.0 / 720 + y * (1.0 / 40320))))
    odd = (quadrant & 1) == 1
    first = jnp.where(odd, sine, cosine)
    second = jnp.where(odd, cosine, sine)
    first = jnp.where(((quadrant + 1) & 2) == 2, -first, first)
    second = jnp.where((quadrant & 2) == 2, -second, second)
    return first, second


def halves(value):
    high = value.astype(jnp.bfloat16)
    return high, (value - high.astype(jnp.float32)).astype(jnp.bfloat16)


def table_kernel(groups, bins, freq_dev, lag_ref, shift_ref):
    low_rows = lax.broadcasted_iota(jnp.int32, (8, SLOWNESS), 0)
    high_rows = lax.broadcasted_iota(jnp.int32, (BLOCK // 8, SLOWNESS), 0) * 8
    shift_rows = lax.broadcasted_iota(jnp.int32, (2 * groups, SLOWNESS), 0)
    shift_rows = jnp.where(shift_rows < groups, shift_rows, shift_rows - groups - 1) * BLOCK
    first_bin = lax.axis_index("freq") * freq_dev + lax.axis_index("chan") * bins

    def one_bin(f, carry):
        def phases(rows):
            slow = lax.broadcasted_iota(jnp.int32, rows.shape, 1) - SLOWNESS // 2
            return unit_phase((first_bin + f) * slow * rows)

        low_cos, low_sin = phases(low_rows)
        high_cos, high_sin = phases(high_rows)
        low_cos, low_sin = low_cos[None], low_sin[None]
        high_cos, high_sin = high_cos[:, None], high_sin[:, None]
        lag_cos = (high_cos * low_cos - high_sin * low_sin).reshape(BLOCK, SLOWNESS)
        lag_sin = (high_sin * low_cos + high_cos * low_sin).reshape(BLOCK, SLOWNESS)
        cos_high, cos_low = halves(lag_cos)
        sin_high, sin_low = halves(lag_sin)
        lag_ref[f, :BLOCK, :SLOWNESS] = cos_high
        lag_ref[f, BLOCK:, :SLOWNESS] = cos_low
        lag_ref[f, :BLOCK, SLOWNESS:] = sin_high
        lag_ref[f, BLOCK:, SLOWNESS:] = sin_low
        shift_cos, shift_sin = phases(shift_rows)
        shift_ref[f, 0] = shift_cos
        shift_ref[f, 1] = shift_sin
        return carry

    lax.fori_loop(0, bins, one_bin, 0)


def stack_kernel(
    groups, bins, parts, spec_ref, position_ref, weight_ref, lag_ref, shift_ref, out_ref, wide_ref
):
    rows = spec_ref.shape[1] // bins
    windows = rows // 2
    for place in range(groups):
        block = jnp.int32(0)
        for group in range(groups):
            block = jnp.where(position_ref[group] == place, group, block)
        wide_ref[place] = spec_ref[block].astype(jnp.float32)

    row_index = lax.broadcasted_iota(jnp.int32, (BLOCK, BLOCK), 0)
    lag_index = lax.broadcasted_iota(jnp.int32, (BLOCK, BLOCK), 1)
    mirror = jnp.where(row_index + lag_index == BLOCK - 1, 1.0, 0.0).astype(jnp.bfloat16)
    ahead = lag_index <= row_index
    ahead = jnp.concatenate([ahead, ahead], axis=1)

    terms = []
    for f in range(bins):
        left, right = [], []
        for place in range(groups):
            value = wide_ref[place, pl.ds(f, rows, stride=bins), :]
            real, imag = value[:windows], value[windows:]
            left.append(value)
            right.append(
                jnp.concatenate(
                    [jnp.concatenate([real, imag], 1), jnp.concatenate([imag, -real], 1)], 0
                )
            )
        left = lax.dot_general(
            mirror,
            jnp.concatenate(left, 0).astype(jnp.bfloat16),
            (((1,), (1,)), ((), ())),
            preferred_element_type=jnp.float32,
        ).astype(jnp.bfloat16)
        right = jnp.concatenate(right, 0).astype(jnp.bfloat16)
        forward, backward = [], []
        for delta in range(groups):
            panel = jnp.dot(
                left[:, : rows * (groups - delta)],
                right[rows * delta :],
                preferred_element_type=jnp.float32,
            )
            skewed = jnp.concatenate(
                [
                    pltpu.roll(panel[:, :BLOCK], 1, 1, stride=1, stride_axis=0),
                    pltpu.roll(panel[:, BLOCK:], 1, 1, stride=1, stride_axis=0),
                ],
                axis=1,
            )
            forward.append(jnp.sum(jnp.where(ahead, skewed, 0.0), 0, keepdims=True))
            backward.append(jnp.sum(jnp.where(ahead, 0.0, skewed), 0, keepdims=True))
        lags = jnp.concatenate(forward + backward, 0)
        weight = weight_ref[...]
        means = jnp.concatenate([lags[:, :BLOCK] * weight, lags[:, BLOCK:] * weight], 0)
        mean_high, mean_low = halves(means)
        spread = jnp.concatenate(
            [
                jnp.concatenate([mean_high, mean_high], 1),
                jnp.concatenate([mean_low, jnp.zeros_like(mean_low)], 1),
            ],
            0,
        )
        product = jnp.dot(spread, lag_ref[f], preferred_element_type=jnp.float32)
        product = product[: 4 * groups] + product[4 * groups :]
        by_cos, by_sin = product[:, :SLOWNESS], product[:, SLOWNESS:]
        real = by_cos[: 2 * groups] - by_sin[2 * groups :]
        imag = by_sin[: 2 * groups] + by_cos[2 * groups :]
        shift_cos, shift_sin = shift_ref[f, 0], shift_ref[f, 1]
        turned_re = real * shift_cos - imag * shift_sin
        turned_im = real * shift_sin + imag * shift_cos
        terms.append(turned_re[:groups] + turned_re[groups:])
        terms.append(turned_im[:groups] + turned_im[groups:])

    slow_dev = SLOWNESS // parts
    spans = BLOCK // slow_dev
    span_index = lax.broadcasted_iota(jnp.int32, (groups, BLOCK), 1) // slow_dev
    for part in range(parts):
        source = (part % spans) * slow_dev
        lanes = slice(part // spans * BLOCK, (part // spans + 1) * BLOCK)
        for row in range(out_ref.shape[2]):
            packed = jnp.zeros((groups, BLOCK), jnp.float32)
            for span, term in enumerate(terms[row * spans : (row + 1) * spans]):
                moved = pltpu.roll(term[:, lanes], (span * slow_dev - source) % BLOCK, 1)
                packed = jnp.where(span_index == span, moved, packed)
            out_ref[:, part, row, :] = packed


def image_kernel(slow_dev, spans, term_ref, table_ref, out_ref):
    arrived = term_ref[...]
    turned = arrived.reshape(-1, BLOCK).T
    turned = jnp.concatenate(
        [turned[span * slow_dev : (span + 1) * slow_dev] for span in range(spans)], 1
    )
    high, low = halves(turned)
    by_high = jnp.dot(
        jnp.concatenate([high, low], 0), table_ref[0], preferred_element_type=jnp.float32
    )
    by_low = jnp.dot(high, table_ref[1], preferred_element_type=jnp.float32)
    out_ref[0] = by_high[:slow_dev] + by_high[slow_dev:] + by_low


def inverse_counts(nblocks):
    delta = np.arange(nblocks)[:, None]
    lag = np.arange(BLOCK)[None, :]
    rows = []
    for lags in (lag, lag - BLOCK):
        usable = (lags > -BLOCK) & ((delta >= 1) | (lags >= 1))
        count = SEGMENTS * (nblocks - delta) * (BLOCK - np.abs(lags))
        rows.append(np.where(usable, 1.0 / np.maximum(count, 1), 0.0))
    return np.concatenate(rows, 0) * math.sqrt(SEGMENTS / FREQS)


def time_table(groups, parts, bins, slow_dev, message_rows):
    spans = min(BLOCK // slow_dev, 2 * bins)
    span, group, part, row = np.meshgrid(
        np.arange(spans), np.arange(groups), np.arange(parts), np.arange(message_rows), indexing="ij"
    )
    entry = row * spans + span
    freq = (part * groups + group) * bins + entry // 2
    lag_time = np.arange(LAG_TIMES) - LAG_TIMES // 2
    angle = 2.0 * math.pi / LAG_TIMES * ((freq[..., None] * lag_time) % LAG_TIMES)
    table = np.where((entry % 2 == 0)[..., None], np.cos(angle), -np.sin(angle))
    table = table.reshape(-1, LAG_TIMES).astype(np.float32)
    high = table.astype(jnp.bfloat16)
    low = (table - high.astype(np.float32)).astype(jnp.bfloat16)
    return spans, np.stack([high, low])


def shards(spectra, block_position):
    groups = lax.axis_size("chan")
    parts = lax.axis_size("freq")
    rows = spectra.shape[0] * spectra.shape[1]
    freq_dev = spectra.shape[2]
    bins = freq_dev // groups
    slow_dev = SLOWNESS // parts
    message_rows = -(-2 * bins * slow_dev // BLOCK)
    vmem = pl.BlockSpec(memory_space=pltpu.VMEM)
    smem = pl.BlockSpec(memory_space=pltpu.SMEM)
    params = pltpu.CompilerParams(vmem_limit_bytes=32 * 1024 * 1024)

    chunks = spectra.reshape(rows, groups, bins, BLOCK)
    gathered = lax.all_to_all(chunks, "chan", split_axis=1, concat_axis=0, tiled=False)
    gathered = gathered.reshape(groups, rows * bins, BLOCK)
    lag_table, shift_table = pl.pallas_call(
        functools.partial(table_kernel, groups, bins, freq_dev),
        out_shape=(
            jax.ShapeDtypeStruct((bins, 2 * BLOCK, 2 * SLOWNESS), jnp.bfloat16),
            jax.ShapeDtypeStruct((bins, 2, 2 * groups, SLOWNESS), jnp.float32),
        ),
        out_specs=(vmem, vmem),
        compiler_params=params,
        cost_estimate=pl.CostEstimate(flops=10**7, bytes_accessed=4 * 10**6, transcendentals=0),
        name="slant_tables",
    )()
    terms = pl.pallas_call(
        functools.partial(stack_kernel, groups, bins, parts),
        out_shape=jax.ShapeDtypeStruct((groups, parts, message_rows, BLOCK), jnp.float32),
        in_specs=[vmem, smem, vmem, vmem, vmem],
        out_specs=vmem,
        scratch_shapes=[pltpu.VMEM((groups, rows * bins, BLOCK), jnp.float32)],
        compiler_params=params,
        name="stack_and_slant",
    )(
        gathered,
        block_position,
        jnp.asarray(inverse_counts(groups), jnp.float32),
        lag_table,
        shift_table,
    )
    terms = terms.reshape(groups * parts, message_rows, BLOCK)
    arrived = lax.all_to_all(terms, ("chan", "freq"), split_axis=0, concat_axis=0, tiled=True)
    spans, table = time_table(groups, parts, bins, slow_dev, message_rows)
    return pl.pallas_call(
        functools.partial(image_kernel, slow_dev, spans),
        out_shape=jax.ShapeDtypeStruct((1, slow_dev, LAG_TIMES), jnp.float32),
        in_specs=[vmem, vmem],
        out_specs=vmem,
        compiler_params=params,
        name="sum_of_bins",
    )(arrived, jnp.asarray(table))


def solution(mesh):
    return jax.shard_map(
        shards,
        mesh=mesh,
        in_specs=(P(None, None, "freq", "chan"), P()),
        out_specs=P("chan", "freq", None),
        check_vma=False,
    )
```

```python
import functools
import math

import jax
import jax.numpy as jnp
import numpy as np
from jax import lax
from jax.experimental import pallas as pl
from jax.experimental.pallas import tpu as pltpu
from jax.sharding import PartitionSpec as P

SEGMENTS = 32
FREQS = 256
BLOCK = 128
SLOWNESS = 256
LAG_TIMES = 512
MODULUS = 8 * FREQS * BLOCK


def unit_phase(numerator):
    quarter = MODULUS // 4
    turn = numerator & (MODULUS - 1)
    quadrant = lax.shift_right_logical(turn + quarter // 2, quarter.bit_length() - 1)
    x = (turn - quadrant * quarter).astype(jnp.float32) * (2.0 * math.pi / MODULUS)
    y = x * x
    sine = x * (1.0 + y * (-1.0 / 6 + y * (1.0 / 120 + y * (-1.0 / 5040 + y * (1.0 / 362880)))))
    cosine = 1.0 + y * (-0.5 + y * (1.0 / 24 + y * (-1.0 / 720 + y * (1.0 / 40320))))
    odd = (quadrant & 1) == 1
    first = jnp.where(odd, sine, cosine)
    second = jnp.where(odd, cosine, sine)
    first = jnp.where(((quadrant + 1) & 2) == 2, -first, first)
    second = jnp.where((quadrant & 2) == 2, -second, second)
    return first, second


def halves(value):
    high = value.astype(jnp.bfloat16)
    return high, (value - high.astype(jnp.float32)).astype(jnp.bfloat16)


def table_kernel(groups, bins, freq_dev, lag_ref, shift_ref):
    low_rows = lax.broadcasted_iota(jnp.int32, (8, SLOWNESS), 0)
    high_rows = lax.broadcasted_iota(jnp.int32, (BLOCK // 8, SLOWNESS), 0) * 8
    shift_rows = lax.broadcasted_iota(jnp.int32, (2 * groups, SLOWNESS), 0)
    shift_rows = jnp.where(shift_rows < groups, shift_rows, shift_rows - groups - 1) * BLOCK
    first_bin = lax.axis_index("freq") * freq_dev + lax.axis_index("chan") * bins

    def one_bin(f, carry):
        def phases(rows):
            slow = lax.broadcasted_iota(jnp.int32, rows.shape, 1) - SLOWNESS // 2
            return unit_phase((first_bin + f) * slow * rows)

        low_cos, low_sin = phases(low_rows)
        high_cos, high_sin = phases(high_rows)
        low_cos, low_sin = low_cos[None], low_sin[None]
        high_cos, high_sin = high_cos[:, None], high_sin[:, None]
        lag_cos = (high_cos * low_cos - high_sin * low_sin).reshape(BLOCK, SLOWNESS)
        lag_sin = (high_sin * low_cos + high_cos * low_sin).reshape(BLOCK, SLOWNESS)
        cos_high, cos_low = halves(lag_cos)
        sin_high, sin_low = halves(lag_sin)
        lag_ref[f, :BLOCK, :SLOWNESS] = cos_high
        lag_ref[f, BLOCK:, :SLOWNESS] = cos_low
        lag_ref[f, :BLOCK, SLOWNESS:] = sin_high
        lag_ref[f, BLOCK:, SLOWNESS:] = sin_low
        shift_cos, shift_sin = phases(shift_rows)
        shift_ref[f, 0] = shift_cos
        shift_ref[f, 1] = shift_sin
        return carry

    lax.fori_loop(0, bins, one_bin, 0)


def chunk_kernel(groups, bins, spec_ref, *refs):
    out_refs, wide_ref = refs[:-1], refs[-1]
    wide_ref[...] = spec_ref[...].astype(jnp.float32)
    freq_dev = groups * bins
    rows = spec_ref.shape[0] // freq_dev
    own_group = lax.axis_index("chan")
    for distance, out_ref in enumerate(out_refs):
        first = lax.rem(own_group + distance, groups) * bins
        for f in range(bins):
            value = wide_ref[pl.ds(first + f, rows, stride=freq_dev), :]
            out_ref[f] = value.astype(jnp.bfloat16)


def stack_kernel(groups, bins, parts, *refs):
    chunk_refs = refs[:groups]
    position_ref, weight_ref, lag_ref, shift_ref, out_ref, placed_ref = refs[groups:]
    rows = placed_ref.shape[2]
    windows = rows // 2
    own_group = lax.axis_index("chan")
    for distance, chunk_ref in enumerate(chunk_refs):
        place = position_ref[lax.rem(own_group + (groups - distance), groups)]
        placed_ref[place] = chunk_ref[...]

    row_index = lax.broadcasted_iota(jnp.int32, (BLOCK, BLOCK), 0)
    lag_index = lax.broadcasted_iota(jnp.int32, (BLOCK, BLOCK), 1)
    mirror = jnp.where(row_index + lag_index == BLOCK - 1, 1.0, 0.0).astype(jnp.bfloat16)
    ahead = lag_index <= row_index
    ahead = jnp.concatenate([ahead, ahead], axis=1)

    terms = []
    for f in range(bins):
        left, right = [], []
        for place in range(groups):
            value = placed_ref[place, f]
            real, imag = value[:windows], value[windows:]
            left.append(value)
            right.append(
                jnp.concatenate(
                    [jnp.concatenate([real, imag], 1), jnp.concatenate([imag, -real], 1)], 0
                )
            )
        left = lax.dot_general(
            mirror,
            jnp.concatenate(left, 0),
            (((1,), (1,)), ((), ())),
            preferred_element_type=jnp.float32,
        ).astype(jnp.bfloat16)
        right = jnp.concatenate(right, 0)
        forward, backward = [], []
        for delta in range(groups):
            panel = jnp.dot(
                left[:, : rows * (groups - delta)],
                right[rows * delta :],
                preferred_element_type=jnp.float32,
            )
            skewed = jnp.concatenate(
                [
                    pltpu.roll(panel[:, :BLOCK], 1, 1, stride=1, stride_axis=0),
                    pltpu.roll(panel[:, BLOCK:], 1, 1, stride=1, stride_axis=0),
                ],
                axis=1,
            )
            forward.append(jnp.sum(jnp.where(ahead, skewed, 0.0), 0, keepdims=True))
            backward.append(jnp.sum(jnp.where(ahead, 0.0, skewed), 0, keepdims=True))
        lags = jnp.concatenate(forward + backward, 0)
        weight = weight_ref[...]
        means = jnp.concatenate([lags[:, :BLOCK] * weight, lags[:, BLOCK:] * weight], 0)
        mean_high, mean_low = halves(means)
        spread = jnp.concatenate(
            [
                jnp.concatenate([mean_high, mean_high], 1),
                jnp.concatenate([mean_low, jnp.zeros_like(mean_low)], 1),
            ],
            0,
        )
        product = jnp.dot(spread, lag_ref[f], preferred_element_type=jnp.float32)
        product = product[: 4 * groups] + product[4 * groups :]
        by_cos, by_sin = product[:, :SLOWNESS], product[:, SLOWNESS:]
        real = by_cos[: 2 * groups] - by_sin[2 * groups :]
        imag = by_sin[: 2 * groups] + by_cos[2 * groups :]
        shift_cos, shift_sin = shift_ref[f, 0], shift_ref[f, 1]
        turned_re = real * shift_cos - imag * shift_sin
        turned_im = real * shift_sin + imag * shift_cos
        terms.append(turned_re[:groups] + turned_re[groups:])
        terms.append(turned_im[:groups] + turned_im[groups:])

    slow_dev = SLOWNESS // parts
    spans = BLOCK // slow_dev
    span_index = lax.broadcasted_iota(jnp.int32, (groups, BLOCK), 1) // slow_dev
    for part in range(parts):
        source = (part % spans) * slow_dev
        lanes = slice(part // spans * BLOCK, (part // spans + 1) * BLOCK)
        for row in range(out_ref.shape[2]):
            packed = jnp.zeros((groups, BLOCK), jnp.float32)
            for span, term in enumerate(terms[row * spans : (row + 1) * spans]):
                moved = pltpu.roll(term[:, lanes], (span * slow_dev - source) % BLOCK, 1)
                packed = jnp.where(span_index == span, moved, packed)
            out_ref[:, part, row, :] = packed


def image_kernel(slow_dev, spans, term_ref, table_ref, out_ref):
    arrived = term_ref[...]
    turned = arrived.reshape(-1, BLOCK).T
    turned = jnp.concatenate(
        [turned[span * slow_dev : (span + 1) * slow_dev] for span in range(spans)], 1
    )
    high, low = halves(turned)
    by_high = jnp.dot(
        jnp.concatenate([high, low], 0), table_ref[0], preferred_element_type=jnp.float32
    )
    by_low = jnp.dot(high, table_ref[1], preferred_element_type=jnp.float32)
    out_ref[0] = by_high[:slow_dev] + by_high[slow_dev:] + by_low


def inverse_counts(nblocks):
    delta = np.arange(nblocks)[:, None]
    lag = np.arange(BLOCK)[None, :]
    rows = []
    for lags in (lag, lag - BLOCK):
        usable = (lags > -BLOCK) & ((delta >= 1) | (lags >= 1))
        count = SEGMENTS * (nblocks - delta) * (BLOCK - np.abs(lags))
        rows.append(np.where(usable, 1.0 / np.maximum(count, 1), 0.0))
    return np.concatenate(rows, 0) * math.sqrt(SEGMENTS / FREQS)


def time_table(groups, parts, bins, slow_dev, message_rows):
    spans = min(BLOCK // slow_dev, 2 * bins)
    span, group, part, row = np.meshgrid(
        np.arange(spans), np.arange(groups), np.arange(parts), np.arange(message_rows), indexing="ij"
    )
    entry = row * spans + span
    freq = (part * groups + group) * bins + entry // 2
    lag_time = np.arange(LAG_TIMES) - LAG_TIMES // 2
    angle = 2.0 * math.pi / LAG_TIMES * ((freq[..., None] * lag_time) % LAG_TIMES)
    table = np.where((entry % 2 == 0)[..., None], np.cos(angle), -np.sin(angle))
    table = table.reshape(-1, LAG_TIMES).astype(np.float32)
    high = table.astype(jnp.bfloat16)
    low = (table - high.astype(np.float32)).astype(jnp.bfloat16)
    return spans, np.stack([high, low])


def shards(spectra, block_position):
    groups = lax.axis_size("chan")
    parts = lax.axis_size("freq")
    rows = spectra.shape[0] * spectra.shape[1]
    freq_dev = spectra.shape[2]
    bins = freq_dev // groups
    slow_dev = SLOWNESS // parts
    message_rows = -(-2 * bins * slow_dev // BLOCK)
    vmem = pl.BlockSpec(memory_space=pltpu.VMEM)
    smem = pl.BlockSpec(memory_space=pltpu.SMEM)
    params = pltpu.CompilerParams(vmem_limit_bytes=32 * 1024 * 1024)

    chunk = jax.ShapeDtypeStruct((bins, rows, BLOCK), jnp.bfloat16)
    chunks = pl.pallas_call(
        functools.partial(chunk_kernel, groups, bins),
        out_shape=(chunk,) * groups,
        in_specs=[vmem],
        out_specs=(vmem,) * groups,
        scratch_shapes=[pltpu.VMEM((rows * freq_dev, BLOCK), jnp.float32)],
        compiler_params=params,
        name="chunks_of_bins",
    )(spectra.reshape(rows * freq_dev, BLOCK))
    arrived_chunks = list(chunks)
    for distance in sorted(range(1, groups), key=lambda steps: abs(2 * steps - groups)):
        pairs = [(source, (source + distance) % groups) for source in range(groups)]
        arrived_chunks[distance] = lax.ppermute(chunks[distance], "chan", pairs)
    lag_table, shift_table = pl.pallas_call(
        functools.partial(table_kernel, groups, bins, freq_dev),
        out_shape=(
            jax.ShapeDtypeStruct((bins, 2 * BLOCK, 2 * SLOWNESS), jnp.bfloat16),
            jax.ShapeDtypeStruct((bins, 2, 2 * groups, SLOWNESS), jnp.float32),
        ),
        out_specs=(vmem, vmem),
        compiler_params=params,
        cost_estimate=pl.CostEstimate(flops=10**7, bytes_accessed=4 * 10**6, transcendentals=0),
        name="slant_tables",
    )()
    terms = pl.pallas_call(
        functools.partial(stack_kernel, groups, bins, parts),
        out_shape=jax.ShapeDtypeStruct((groups, parts, message_rows, BLOCK), jnp.float32),
        in_specs=[vmem] * groups + [smem, vmem, vmem, vmem],
        out_specs=vmem,
        scratch_shapes=[pltpu.VMEM((groups, bins, rows, BLOCK), jnp.bfloat16)],
        compiler_params=params,
        name="stack_and_slant",
    )(
        *arrived_chunks,
        block_position,
        jnp.asarray(inverse_counts(groups), jnp.float32),
        lag_table,
        shift_table,
    )
    terms = terms.reshape(groups * parts, message_rows, BLOCK)
    arrived = lax.all_to_all(terms, ("chan", "freq"), split_axis=0, concat_axis=0, tiled=True)
    spans, table = time_table(groups, parts, bins, slow_dev, message_rows)
    return pl.pallas_call(
        functools.partial(image_kernel, slow_dev, spans),
        out_shape=jax.ShapeDtypeStruct((1, slow_dev, LAG_TIMES), jnp.float32),
        in_specs=[vmem, vmem],
        out_specs=vmem,
        compiler_params=params,
        name="sum_of_bins",
    )(arrived, jnp.asarray(table))


def solution(mesh):
    return jax.shard_map(
        shards,
        mesh=mesh,
        in_specs=(P(None, None, "freq", "chan"), P()),
        out_specs=P("chan", "freq", None),
        check_vma=False,
    )
```

```python
import functools
import math

import jax
import jax.numpy as jnp
import numpy as np
from jax import lax
from jax.experimental import pallas as pl
from jax.experimental.pallas import tpu as pltpu
from jax.sharding import PartitionSpec as P

SEGMENTS = 32
FREQS = 256
BLOCK = 128
SLOWNESS = 256
LAG_TIMES = 512
MODULUS = 8 * FREQS * BLOCK


def unit_phase(numerator):
    quarter = MODULUS // 4
    turn = numerator & (MODULUS - 1)
    quadrant = lax.shift_right_logical(turn + quarter // 2, quarter.bit_length() - 1)
    x = (turn - quadrant * quarter).astype(jnp.float32) * (2.0 * math.pi / MODULUS)
    y = x * x
    sine = x * (1.0 + y * (-1.0 / 6 + y * (1.0 / 120 + y * (-1.0 / 5040 + y * (1.0 / 362880)))))
    cosine = 1.0 + y * (-0.5 + y * (1.0 / 24 + y * (-1.0 / 720 + y * (1.0 / 40320))))
    odd = (quadrant & 1) == 1
    first = jnp.where(odd, sine, cosine)
    second = jnp.where(odd, cosine, sine)
    first = jnp.where(((quadrant + 1) & 2) == 2, -first, first)
    second = jnp.where((quadrant & 2) == 2, -second, second)
    return first, second


def halves(value):
    high = value.astype(jnp.bfloat16)
    return high, (value - high.astype(jnp.float32)).astype(jnp.bfloat16)


def table_kernel(groups, bins, freq_dev, position_ref, place_ref, lag_ref, shift_ref):
    low_rows = lax.broadcasted_iota(jnp.int32, (8, SLOWNESS), 0)
    high_rows = lax.broadcasted_iota(jnp.int32, (BLOCK // 8, SLOWNESS), 0) * 8
    shift_rows = lax.broadcasted_iota(jnp.int32, (2 * groups, SLOWNESS), 0)
    shift_rows = jnp.where(shift_rows < groups, shift_rows, shift_rows - groups - 1) * BLOCK
    own_group = lax.axis_index("chan")
    first_bin = lax.axis_index("freq") * freq_dev + own_group * bins
    for distance in range(groups):
        place_ref[distance] = position_ref[lax.rem(own_group + (groups - distance), groups)]

    def one_bin(f, carry):
        def phases(rows):
            slow = lax.broadcasted_iota(jnp.int32, rows.shape, 1) - SLOWNESS // 2
            return unit_phase((first_bin + f) * slow * rows)

        low_cos, low_sin = phases(low_rows)
        high_cos, high_sin = phases(high_rows)
        low_cos, low_sin = low_cos[None], low_sin[None]
        high_cos, high_sin = high_cos[:, None], high_sin[:, None]
        lag_cos = (high_cos * low_cos - high_sin * low_sin).reshape(BLOCK, SLOWNESS)
        lag_sin = (high_sin * low_cos + high_cos * low_sin).reshape(BLOCK, SLOWNESS)
        cos_high, cos_low = halves(lag_cos)
        sin_high, sin_low = halves(lag_sin)
        lag_ref[f, :BLOCK, :SLOWNESS] = cos_high
        lag_ref[f, BLOCK:, :SLOWNESS] = cos_low
        lag_ref[f, :BLOCK, SLOWNESS:] = sin_high
        lag_ref[f, BLOCK:, SLOWNESS:] = sin_low
        shift_cos, shift_sin = phases(shift_rows)
        shift_ref[f, 0] = shift_cos
        shift_ref[f, 1] = shift_sin
        return carry

    lax.fori_loop(0, bins, one_bin, 0)


def chunk_kernel(groups, bins, spec_ref, *refs):
    out_refs, wide_ref = refs[:-1], refs[-1]
    wide_ref[...] = spec_ref[...].astype(jnp.float32)
    freq_dev = groups * bins
    rows = spec_ref.shape[0] // freq_dev
    own_group = lax.axis_index("chan")
    for distance, out_ref in enumerate(out_refs):
        first = lax.rem(own_group + distance, groups) * bins
        for f in range(bins):
            value = wide_ref[pl.ds(first + f, rows, stride=freq_dev), :]
            out_ref[f] = value.astype(jnp.bfloat16)


def stack_weights(groups):
    row = lax.broadcasted_iota(jnp.int32, (2 * groups, BLOCK), 0)
    lag = lax.broadcasted_iota(jnp.int32, (2 * groups, BLOCK), 1)
    delta = jnp.where(row < groups, row, row - groups)
    lag = jnp.where(row < groups, lag, lag - BLOCK)
    usable = (lag > -BLOCK) & ((delta >= 1) | (lag >= 1))
    count = SEGMENTS * (groups - delta) * (BLOCK - jnp.abs(lag))
    scale = math.sqrt(SEGMENTS / FREQS)
    return jnp.where(usable, scale / jnp.maximum(count, 1).astype(jnp.float32), 0.0)


def stack_kernel(groups, bins, parts, *refs):
    chunk_refs = refs[:groups]
    place_ref, lag_ref, shift_ref, out_ref, placed_ref, left_ref, part_ref = refs[groups:]
    rows = placed_ref.shape[2]
    windows = rows // 2
    for distance, chunk_ref in enumerate(chunk_refs):
        placed_ref[place_ref[distance]] = chunk_ref[...]

    row_index = lax.broadcasted_iota(jnp.int32, (BLOCK, BLOCK), 0)
    lag_index = lax.broadcasted_iota(jnp.int32, (BLOCK, BLOCK), 1)
    mirror = jnp.where(row_index + lag_index == BLOCK - 1, 1.0, 0.0).astype(jnp.bfloat16)
    ahead = lag_index <= row_index

    for f in range(bins):
        left_ref[f] = lax.dot_general(
            mirror,
            placed_ref[:, f].reshape(groups * rows, BLOCK),
            (((1,), (1,)), ((), ())),
            preferred_element_type=jnp.float32,
        ).astype(jnp.bfloat16)

    for f in range(bins):
        right = []
        for place in range(groups):
            value = placed_ref[place, f]
            real, imag = value[:windows], value[windows:]
            right.append(
                jnp.concatenate(
                    [jnp.concatenate([real, imag], 1), jnp.concatenate([imag, -real], 1)], 0
                )
            )
        right = jnp.concatenate(right, 0)
        for delta in range(groups):
            panel = jnp.dot(
                left_ref[f, :, : rows * (groups - delta)],
                right[rows * delta :],
                preferred_element_type=jnp.float32,
            )
            for half in range(2):
                lanes = slice(half * BLOCK, (half + 1) * BLOCK)
                skewed = pltpu.roll(panel[:, lanes], 1, 1, stride=1, stride_axis=0)
                forward = jnp.where(ahead, skewed, 0.0).reshape(-1, 8, BLOCK).sum(0)
                backward = jnp.where(ahead, 0.0, skewed).reshape(-1, 8, BLOCK).sum(0)
                first = (f * 2 * groups + delta) * 8
                part_ref[half, first : first + 8] = forward
                part_ref[half, first + groups * 8 : first + groups * 8 + 8] = backward

    lags = []
    for half in range(2):
        summed = part_ref[half, pl.ds(0, bins * 2 * groups, stride=8), :]
        for sublane in range(1, 8):
            summed = summed + part_ref[half, pl.ds(sublane, bins * 2 * groups, stride=8), :]
        lags.append(summed)
    weight = stack_weights(groups)

    terms = []
    for f in range(bins):
        lag_rows = slice(f * 2 * groups, (f + 1) * 2 * groups)
        means = jnp.concatenate([half[lag_rows] * weight for half in lags], 0)
        mean_high, mean_low = halves(means)
        spread = jnp.concatenate(
            [
                jnp.concatenate([mean_high, mean_high], 1),
                jnp.concatenate([mean_low, jnp.zeros_like(mean_low)], 1),
            ],
            0,
        )
        product = jnp.dot(spread, lag_ref[f], preferred_element_type=jnp.float32)
        product = product[: 4 * groups] + product[4 * groups :]
        by_cos, by_sin = product[:, :SLOWNESS], product[:, SLOWNESS:]
        real = by_cos[: 2 * groups] - by_sin[2 * groups :]
        imag = by_sin[: 2 * groups] + by_cos[2 * groups :]
        shift_cos, shift_sin = shift_ref[f, 0], shift_ref[f, 1]
        turned_re = real * shift_cos - imag * shift_sin
        turned_im = real * shift_sin + imag * shift_cos
        terms.append(turned_re[:groups] + turned_re[groups:])
        terms.append(turned_im[:groups] + turned_im[groups:])

    slow_dev = SLOWNESS // parts
    spans = BLOCK // slow_dev
    span_index = lax.broadcasted_iota(jnp.int32, (groups, BLOCK), 1) // slow_dev
    for part in range(parts):
        source = (part % spans) * slow_dev
        lanes = slice(part // spans * BLOCK, (part // spans + 1) * BLOCK)
        for row in range(out_ref.shape[2]):
            packed = jnp.zeros((groups, BLOCK), jnp.float32)
            for span, term in enumerate(terms[row * spans : (row + 1) * spans]):
                moved = pltpu.roll(term[:, lanes], (span * slow_dev - source) % BLOCK, 1)
                packed = jnp.where(span_index == span, moved, packed)
            out_ref[:, part, row, :] = packed


def image_kernel(slow_dev, spans, term_ref, table_ref, out_ref):
    arrived = term_ref[...]
    turned = arrived.reshape(-1, BLOCK).T
    turned = jnp.concatenate(
        [turned[span * slow_dev : (span + 1) * slow_dev] for span in range(spans)], 1
    )
    high, low = halves(turned)
    by_high = jnp.dot(
        jnp.concatenate([high, low], 0), table_ref[0], preferred_element_type=jnp.float32
    )
    by_low = jnp.dot(high, table_ref[1], preferred_element_type=jnp.float32)
    out_ref[0] = by_high[:slow_dev] + by_high[slow_dev:] + by_low


def time_table(groups, parts, bins, slow_dev, message_rows):
    spans = min(BLOCK // slow_dev, 2 * bins)
    span, group, part, row = np.meshgrid(
        np.arange(spans), np.arange(groups), np.arange(parts), np.arange(message_rows), indexing="ij"
    )
    entry = row * spans + span
    freq = (part * groups + group) * bins + entry // 2
    lag_time = np.arange(LAG_TIMES) - LAG_TIMES // 2
    angle = 2.0 * math.pi / LAG_TIMES * ((freq[..., None] * lag_time) % LAG_TIMES)
    table = np.where((entry % 2 == 0)[..., None], np.cos(angle), -np.sin(angle))
    table = table.reshape(-1, LAG_TIMES).astype(np.float32)
    high = table.astype(jnp.bfloat16)
    low = (table - high.astype(np.float32)).astype(jnp.bfloat16)
    return spans, np.stack([high, low])


def shards(spectra, block_position):
    groups = lax.axis_size("chan")
    parts = lax.axis_size("freq")
    rows = spectra.shape[0] * spectra.shape[1]
    freq_dev = spectra.shape[2]
    bins = freq_dev // groups
    slow_dev = SLOWNESS // parts
    message_rows = -(-2 * bins * slow_dev // BLOCK)
    vmem = pl.BlockSpec(memory_space=pltpu.VMEM)
    smem = pl.BlockSpec(memory_space=pltpu.SMEM)
    params = pltpu.CompilerParams(vmem_limit_bytes=32 * 1024 * 1024)

    chunk = jax.ShapeDtypeStruct((bins, rows, BLOCK), jnp.bfloat16)
    chunks = pl.pallas_call(
        functools.partial(chunk_kernel, groups, bins),
        out_shape=(chunk,) * groups,
        in_specs=[vmem],
        out_specs=(vmem,) * groups,
        scratch_shapes=[pltpu.VMEM((rows * freq_dev, BLOCK), jnp.float32)],
        compiler_params=params,
        name="chunks_of_bins",
    )(spectra.reshape(rows * freq_dev, BLOCK))
    arrived_chunks = list(chunks)
    for distance in sorted(range(1, groups), key=lambda steps: abs(2 * steps - groups)):
        pairs = [(source, (source + distance) % groups) for source in range(groups)]
        arrived_chunks[distance] = lax.ppermute(chunks[distance], "chan", pairs)
    places, lag_table, shift_table = pl.pallas_call(
        functools.partial(table_kernel, groups, bins, freq_dev),
        out_shape=(
            jax.ShapeDtypeStruct((groups,), jnp.int32),
            jax.ShapeDtypeStruct((bins, 2 * BLOCK, 2 * SLOWNESS), jnp.bfloat16),
            jax.ShapeDtypeStruct((bins, 2, 2 * groups, SLOWNESS), jnp.float32),
        ),
        in_specs=[smem],
        out_specs=(smem, vmem, vmem),
        compiler_params=params,
        cost_estimate=pl.CostEstimate(flops=10**7, bytes_accessed=4 * 10**6, transcendentals=0),
        name="slant_tables",
    )(block_position)
    terms = pl.pallas_call(
        functools.partial(stack_kernel, groups, bins, parts),
        out_shape=jax.ShapeDtypeStruct((groups, parts, message_rows, BLOCK), jnp.float32),
        in_specs=[vmem] * groups + [smem, vmem, vmem],
        out_specs=vmem,
        scratch_shapes=[
            pltpu.VMEM((groups, bins, rows, BLOCK), jnp.bfloat16),
            pltpu.VMEM((bins, BLOCK, groups * rows), jnp.bfloat16),
            pltpu.VMEM((2, bins * 2 * groups * 8, BLOCK), jnp.float32),
        ],
        compiler_params=params,
        name="stack_and_slant",
    )(
        *arrived_chunks,
        places,
        lag_table,
        shift_table,
    )
    terms = terms.reshape(groups * parts, message_rows, BLOCK)
    arrived = lax.all_to_all(terms, ("chan", "freq"), split_axis=0, concat_axis=0, tiled=True)
    spans, table = time_table(groups, parts, bins, slow_dev, message_rows)
    return pl.pallas_call(
        functools.partial(image_kernel, slow_dev, spans),
        out_shape=jax.ShapeDtypeStruct((1, slow_dev, LAG_TIMES), jnp.float32),
        in_specs=[vmem, vmem],
        out_specs=vmem,
        compiler_params=params,
        name="sum_of_bins",
    )(arrived, jnp.asarray(table))


def solution(mesh):
    return jax.shard_map(
        shards,
        mesh=mesh,
        in_specs=(P(None, None, "freq", "chan"), P()),
        out_specs=P("chan", "freq", None),
        check_vma=False,
    )
```

```python
import functools
import math

import jax
import jax.numpy as jnp
import numpy as np
from jax import lax
from jax.experimental import pallas as pl
from jax.experimental.pallas import tpu as pltpu
from jax.sharding import PartitionSpec as P

SEGMENTS = 32
FREQS = 256
BLOCK = 128
SLOWNESS = 256
LAG_TIMES = 512
MODULUS = 8 * FREQS * BLOCK


def unit_phase(numerator):
    quarter = MODULUS // 4
    turn = numerator & (MODULUS - 1)
    quadrant = lax.shift_right_logical(turn + quarter // 2, quarter.bit_length() - 1)
    x = (turn - quadrant * quarter).astype(jnp.float32) * (2.0 * math.pi / MODULUS)
    y = x * x
    sine = x * (1.0 + y * (-1.0 / 6 + y * (1.0 / 120 + y * (-1.0 / 5040 + y * (1.0 / 362880)))))
    cosine = 1.0 + y * (-0.5 + y * (1.0 / 24 + y * (-1.0 / 720 + y * (1.0 / 40320))))
    odd = (quadrant & 1) == 1
    first = jnp.where(odd, sine, cosine)
    second = jnp.where(odd, cosine, sine)
    first = jnp.where(((quadrant + 1) & 2) == 2, -first, first)
    second = jnp.where((quadrant & 2) == 2, -second, second)
    return first, second


def halves(value):
    high = value.astype(jnp.bfloat16)
    return high, (value - high.astype(jnp.float32)).astype(jnp.bfloat16)


def table_kernel(groups, bins, freq_dev, position_ref, place_ref, lag_ref, shift_ref):
    low_rows = lax.broadcasted_iota(jnp.int32, (8, SLOWNESS), 0)
    high_rows = lax.broadcasted_iota(jnp.int32, (BLOCK // 8, SLOWNESS), 0) * 8
    shift_rows = lax.broadcasted_iota(jnp.int32, (2 * groups, SLOWNESS), 0)
    shift_rows = jnp.where(shift_rows < groups, shift_rows, shift_rows - groups - 1) * BLOCK
    own_group = lax.axis_index("chan")
    first_bin = lax.axis_index("freq") * freq_dev + own_group * bins
    for distance in range(groups):
        place_ref[distance] = position_ref[lax.rem(own_group + (groups - distance), groups)]

    def one_bin(f, carry):
        def phases(rows):
            slow = lax.broadcasted_iota(jnp.int32, rows.shape, 1) - SLOWNESS // 2
            return unit_phase((first_bin + f) * slow * rows)

        low_cos, low_sin = phases(low_rows)
        high_cos, high_sin = phases(high_rows)
        low_cos, low_sin = low_cos[None], low_sin[None]
        high_cos, high_sin = high_cos[:, None], high_sin[:, None]
        lag_cos = (high_cos * low_cos - high_sin * low_sin).reshape(BLOCK, SLOWNESS)
        lag_sin = (high_sin * low_cos + high_cos * low_sin).reshape(BLOCK, SLOWNESS)
        cos_high, cos_low = halves(lag_cos)
        sin_high, sin_low = halves(lag_sin)
        lag_ref[f, :BLOCK, :SLOWNESS] = cos_high
        lag_ref[f, BLOCK:, :SLOWNESS] = cos_low
        lag_ref[f, :BLOCK, SLOWNESS:] = sin_high
        lag_ref[f, BLOCK:, SLOWNESS:] = sin_low
        shift_cos, shift_sin = phases(shift_rows)
        shift_ref[f, 0] = shift_cos
        shift_ref[f, 1] = shift_sin
        return carry

    lax.fori_loop(0, bins, one_bin, 0)


def chunk_kernel(groups, bins, spec_ref, *refs):
    out_refs, wide_ref = refs[:-1], refs[-1]
    wide_ref[...] = spec_ref[...].astype(jnp.float32)
    freq_dev = groups * bins
    rows = spec_ref.shape[0] // freq_dev
    own_group = lax.axis_index("chan")
    for distance, out_ref in enumerate(out_refs):
        first = lax.rem(own_group + distance, groups) * bins
        for f in range(bins):
            value = wide_ref[pl.ds(first + f, rows, stride=freq_dev), :]
            out_ref[f] = value.astype(jnp.bfloat16)


def stack_weights(groups):
    row = lax.broadcasted_iota(jnp.int32, (2 * groups, BLOCK), 0)
    lag = lax.broadcasted_iota(jnp.int32, (2 * groups, BLOCK), 1)
    delta = jnp.where(row < groups, row, row - groups)
    lag = jnp.where(row < groups, lag, lag - BLOCK)
    usable = (lag > -BLOCK) & ((delta >= 1) | (lag >= 1))
    count = SEGMENTS * (groups - delta) * (BLOCK - jnp.abs(lag))
    scale = math.sqrt(SEGMENTS / FREQS)
    return jnp.where(usable, scale / jnp.maximum(count, 1).astype(jnp.float32), 0.0)


def stack_kernel(groups, bins, parts, *refs):
    chunk_refs = refs[:groups]
    place_ref, lag_ref, shift_ref, out_ref, placed_ref, left_ref, part_ref = refs[groups:]
    rows = placed_ref.shape[2]
    windows = rows // 2
    for distance, chunk_ref in enumerate(chunk_refs):
        placed_ref[place_ref[distance]] = chunk_ref[...]

    row_index = lax.broadcasted_iota(jnp.int32, (BLOCK, BLOCK), 0)
    lag_index = lax.broadcasted_iota(jnp.int32, (BLOCK, BLOCK), 1)
    mirror = jnp.where(row_index + lag_index == BLOCK - 1, 1.0, 0.0).astype(jnp.bfloat16)
    ahead = lag_index <= row_index

    for f in range(bins):
        left_ref[f] = lax.dot_general(
            mirror,
            placed_ref[:, f].reshape(groups * rows, BLOCK),
            (((1,), (1,)), ((), ())),
            preferred_element_type=jnp.float32,
        ).astype(jnp.bfloat16)

    for f in range(bins):
        right = []
        for place in range(groups):
            value = placed_ref[place, f]
            real, imag = value[:windows], value[windows:]
            right.append(
                jnp.concatenate(
                    [jnp.concatenate([real, imag], 1), jnp.concatenate([imag, -real], 1)], 0
                )
            )
        right = jnp.concatenate(right, 0)
        for delta in range(groups):
            panel = jnp.dot(
                left_ref[f, :, : rows * (groups - delta)],
                right[rows * delta :],
                preferred_element_type=jnp.float32,
            )
            for half in range(2):
                lanes = slice(half * BLOCK, (half + 1) * BLOCK)
                skewed = pltpu.roll(panel[:, lanes], 1, 1, stride=1, stride_axis=0)
                forward = jnp.where(ahead, skewed, 0.0).reshape(-1, 8, BLOCK).sum(0)
                backward = jnp.where(ahead, 0.0, skewed).reshape(-1, 8, BLOCK).sum(0)
                first = (f * 2 * groups + delta) * 8
                part_ref[half, first : first + 8] = forward
                part_ref[half, first + groups * 8 : first + groups * 8 + 8] = backward

    lags = []
    for half in range(2):
        summed = part_ref[half, pl.ds(0, bins * 2 * groups, stride=8), :]
        for sublane in range(1, 8):
            summed = summed + part_ref[half, pl.ds(sublane, bins * 2 * groups, stride=8), :]
        lags.append(summed)
    weight = stack_weights(groups)

    terms = []
    for f in range(bins):
        lag_rows = slice(f * 2 * groups, (f + 1) * 2 * groups)
        means = jnp.concatenate([half[lag_rows] * weight for half in lags], 0)
        mean_high, mean_low = halves(means)
        spread = jnp.concatenate(
            [
                jnp.concatenate([mean_high, mean_high], 1),
                jnp.concatenate([mean_low, jnp.zeros_like(mean_low)], 1),
            ],
            0,
        )
        product = jnp.dot(spread, lag_ref[f], preferred_element_type=jnp.float32)
        product = product[: 4 * groups] + product[4 * groups :]
        by_cos, by_sin = product[:, :SLOWNESS], product[:, SLOWNESS:]
        real = by_cos[: 2 * groups] - by_sin[2 * groups :]
        imag = by_sin[: 2 * groups] + by_cos[2 * groups :]
        shift_cos, shift_sin = shift_ref[f, 0], shift_ref[f, 1]
        turned_re = real * shift_cos - imag * shift_sin
        turned_im = real * shift_sin + imag * shift_cos
        terms.append(turned_re[:groups] + turned_re[groups:])
        terms.append(turned_im[:groups] + turned_im[groups:])

    slow_dev = SLOWNESS // parts
    spans = BLOCK // slow_dev
    span_index = lax.broadcasted_iota(jnp.int32, (groups, BLOCK), 1) // slow_dev
    for part in range(parts):
        source = (part % spans) * slow_dev
        lanes = slice(part // spans * BLOCK, (part // spans + 1) * BLOCK)
        for row in range(out_ref.shape[2]):
            packed = jnp.zeros((groups, BLOCK), jnp.float32)
            for span, term in enumerate(terms[row * spans : (row + 1) * spans]):
                moved = pltpu.roll(term[:, lanes], (span * slow_dev - source) % BLOCK, 1)
                packed = jnp.where(span_index == span, moved, packed)
            out_ref[:, part, row, :] = packed


def image_kernel(slow_dev, spans, term_ref, table_ref, out_ref):
    arrived = term_ref[...]
    turned = arrived.reshape(-1, BLOCK).T
    turned = jnp.concatenate(
        [turned[span * slow_dev : (span + 1) * slow_dev] for span in range(spans)], 1
    )
    high, low = halves(turned)
    by_high = jnp.dot(
        jnp.concatenate([high, low], 0), table_ref[0], preferred_element_type=jnp.float32
    )
    by_low = jnp.dot(high, table_ref[1], preferred_element_type=jnp.float32)
    out_ref[0] = by_high[:slow_dev] + by_high[slow_dev:] + by_low


def time_table(groups, parts, bins, slow_dev, message_rows):
    spans = min(BLOCK // slow_dev, 2 * bins)
    span, group, part, row = np.meshgrid(
        np.arange(spans), np.arange(groups), np.arange(parts), np.arange(message_rows), indexing="ij"
    )
    entry = row * spans + span
    freq = (part * groups + group) * bins + entry // 2
    lag_time = np.arange(LAG_TIMES) - LAG_TIMES // 2
    angle = 2.0 * math.pi / LAG_TIMES * ((freq[..., None] * lag_time) % LAG_TIMES)
    table = np.where((entry % 2 == 0)[..., None], np.cos(angle), -np.sin(angle))
    table = table.reshape(-1, LAG_TIMES).astype(np.float32)
    high = table.astype(jnp.bfloat16)
    low = (table - high.astype(np.float32)).astype(jnp.bfloat16)
    return spans, np.stack([high, low])


def shards(spectra, block_position):
    groups = lax.axis_size("chan")
    parts = lax.axis_size("freq")
    rows = spectra.shape[0] * spectra.shape[1]
    freq_dev = spectra.shape[2]
    bins = freq_dev // groups
    slow_dev = SLOWNESS // parts
    message_rows = -(-2 * bins * slow_dev // BLOCK)
    vmem = pl.BlockSpec(memory_space=pltpu.VMEM)
    smem = pl.BlockSpec(memory_space=pltpu.SMEM)
    params = pltpu.CompilerParams(vmem_limit_bytes=32 * 1024 * 1024)

    chunk = jax.ShapeDtypeStruct((bins, rows, BLOCK), jnp.bfloat16)
    chunks = pl.pallas_call(
        functools.partial(chunk_kernel, groups, bins),
        out_shape=(chunk,) * groups,
        in_specs=[vmem],
        out_specs=(vmem,) * groups,
        scratch_shapes=[pltpu.VMEM((rows * freq_dev, BLOCK), jnp.float32)],
        compiler_params=params,
        name="chunks_of_bins",
    )(spectra.reshape(rows * freq_dev, BLOCK))
    arrived_chunks = list(chunks)
    for distance in sorted(range(1, groups), key=lambda steps: abs(2 * steps - groups)):
        pairs = [(source, (source + distance) % groups) for source in range(groups)]
        arrived_chunks[distance] = lax.ppermute(chunks[distance], "chan", pairs)
    places, lag_table, shift_table = pl.pallas_call(
        functools.partial(table_kernel, groups, bins, freq_dev),
        out_shape=(
            jax.ShapeDtypeStruct((groups,), jnp.int32),
            jax.ShapeDtypeStruct((bins, 2 * BLOCK, 2 * SLOWNESS), jnp.bfloat16),
            jax.ShapeDtypeStruct((bins, 2, 2 * groups, SLOWNESS), jnp.float32),
        ),
        in_specs=[smem],
        out_specs=(smem, vmem, vmem),
        compiler_params=params,
        cost_estimate=pl.CostEstimate(flops=10**7, bytes_accessed=4 * 10**6, transcendentals=0),
        name="slant_tables",
    )(block_position)
    terms = pl.pallas_call(
        functools.partial(stack_kernel, groups, bins, parts),
        out_shape=jax.ShapeDtypeStruct((groups, parts, message_rows, BLOCK), jnp.float32),
        in_specs=[vmem] * groups + [smem, vmem, vmem],
        out_specs=vmem,
        scratch_shapes=[
            pltpu.VMEM((groups, bins, rows, BLOCK), jnp.bfloat16),
            pltpu.VMEM((bins, BLOCK, groups * rows), jnp.bfloat16),
            pltpu.VMEM((2, bins * 2 * groups * 8, BLOCK), jnp.float32),
        ],
        compiler_params=params,
        name="stack_and_slant",
    )(
        *arrived_chunks,
        places,
        lag_table,
        shift_table,
    )
    terms = lax.all_to_all(terms, "chan", split_axis=0, concat_axis=0, tiled=True)
    arrived = lax.all_to_all(terms, "freq", split_axis=1, concat_axis=1, tiled=True)
    arrived = arrived.reshape(groups * parts, message_rows, BLOCK)
    spans, table = time_table(groups, parts, bins, slow_dev, message_rows)
    return pl.pallas_call(
        functools.partial(image_kernel, slow_dev, spans),
        out_shape=jax.ShapeDtypeStruct((1, slow_dev, LAG_TIMES), jnp.float32),
        in_specs=[vmem, vmem],
        out_specs=vmem,
        compiler_params=params,
        name="sum_of_bins",
    )(arrived, jnp.asarray(table))


def solution(mesh):
    return jax.shard_map(
        shards,
        mesh=mesh,
        in_specs=(P(None, None, "freq", "chan"), P()),
        out_specs=P("chan", "freq", None),
        check_vma=False,
    )
```

```python
import functools
import math

import jax
import jax.numpy as jnp
import numpy as np
from jax import lax
from jax.experimental import pallas as pl
from jax.experimental.pallas import tpu as pltpu
from jax.sharding import PartitionSpec as P

SEGMENTS = 32
FREQS = 256
BLOCK = 128
SLOWNESS = 256
LAG_TIMES = 512
MODULUS = 8 * FREQS * BLOCK


def unit_phase(numerator):
    quarter = MODULUS // 4
    turn = numerator & (MODULUS - 1)
    quadrant = lax.shift_right_logical(turn + quarter // 2, quarter.bit_length() - 1)
    x = (turn - quadrant * quarter).astype(jnp.float32) * (2.0 * math.pi / MODULUS)
    y = x * x
    sine = x * (1.0 + y * (-1.0 / 6 + y * (1.0 / 120 + y * (-1.0 / 5040 + y * (1.0 / 362880)))))
    cosine = 1.0 + y * (-0.5 + y * (1.0 / 24 + y * (-1.0 / 720 + y * (1.0 / 40320))))
    odd = (quadrant & 1) == 1
    first = jnp.where(odd, sine, cosine)
    second = jnp.where(odd, cosine, sine)
    first = jnp.where(((quadrant + 1) & 2) == 2, -first, first)
    second = jnp.where((quadrant & 2) == 2, -second, second)
    return first, second


def halves(value):
    high = value.astype(jnp.bfloat16)
    return high, (value - high.astype(jnp.float32)).astype(jnp.bfloat16)


def table_kernel(groups, bins, freq_dev, position_ref, place_ref, lag_ref, shift_ref):
    low_rows = lax.broadcasted_iota(jnp.int32, (8, SLOWNESS), 0)
    high_rows = lax.broadcasted_iota(jnp.int32, (BLOCK // 8, SLOWNESS), 0) * 8
    shift_rows = lax.broadcasted_iota(jnp.int32, (2 * groups, SLOWNESS), 0)
    shift_rows = jnp.where(shift_rows < groups, shift_rows, shift_rows - groups - 1) * BLOCK
    own_group = lax.axis_index("chan")
    first_bin = lax.axis_index("freq") * freq_dev + own_group * bins
    for distance in range(groups):
        place_ref[distance] = position_ref[lax.rem(own_group + (groups - distance), groups)]

    def one_bin(f, carry):
        def phases(rows):
            slow = lax.broadcasted_iota(jnp.int32, rows.shape, 1) - SLOWNESS // 2
            return unit_phase((first_bin + f) * slow * rows)

        low_cos, low_sin = phases(low_rows)
        high_cos, high_sin = phases(high_rows)
        low_cos, low_sin = low_cos[None], low_sin[None]
        high_cos, high_sin = high_cos[:, None], high_sin[:, None]
        lag_cos = (high_cos * low_cos - high_sin * low_sin).reshape(BLOCK, SLOWNESS)
        lag_sin = (high_sin * low_cos + high_cos * low_sin).reshape(BLOCK, SLOWNESS)
        cos_high, cos_low = halves(lag_cos)
        sin_high, sin_low = halves(lag_sin)
        lag_ref[f, :BLOCK, :SLOWNESS] = cos_high
        lag_ref[f, BLOCK:, :SLOWNESS] = cos_low
        lag_ref[f, :BLOCK, SLOWNESS:] = sin_high
        lag_ref[f, BLOCK:, SLOWNESS:] = sin_low
        shift_cos, shift_sin = phases(shift_rows)
        shift_ref[f, 0] = shift_cos
        shift_ref[f, 1] = shift_sin
        return carry

    lax.fori_loop(0, bins, one_bin, 0)


def chunk_kernel(groups, pieces, spec_ref, *refs):
    out_refs, wide_ref = refs[:-1], refs[-1]
    wide_ref[...] = spec_ref[...].astype(jnp.float32)
    bins = sum(size for _, size in pieces)
    freq_dev = groups * bins
    rows = spec_ref.shape[0] // freq_dev
    own_group = lax.axis_index("chan")
    for index, out_ref in enumerate(out_refs):
        start, size = pieces[index // groups]
        first = lax.rem(own_group + index % groups, groups) * bins + start
        for f in range(size):
            value = wide_ref[pl.ds(first + f, rows, stride=freq_dev), :]
            out_ref[f] = value.astype(jnp.bfloat16)


def stack_weights(groups):
    row = lax.broadcasted_iota(jnp.int32, (2 * groups, BLOCK), 0)
    lag = lax.broadcasted_iota(jnp.int32, (2 * groups, BLOCK), 1)
    delta = jnp.where(row < groups, row, row - groups)
    lag = jnp.where(row < groups, lag, lag - BLOCK)
    usable = (lag > -BLOCK) & ((delta >= 1) | (lag >= 1))
    count = SEGMENTS * (groups - delta) * (BLOCK - jnp.abs(lag))
    scale = math.sqrt(SEGMENTS / FREQS)
    return jnp.where(usable, scale / jnp.maximum(count, 1).astype(jnp.float32), 0.0)


def stack_kernel(groups, start, bins, parts, *refs):
    chunk_refs = refs[:groups]
    place_ref, lag_ref, shift_ref = refs[groups : groups + 3]
    earlier_refs = refs[groups + 3 : -4]
    out_ref, placed_ref, left_ref, part_ref = refs[-4:]
    rows = placed_ref.shape[2]
    windows = rows // 2
    for distance, chunk_ref in enumerate(chunk_refs):
        placed_ref[place_ref[distance]] = chunk_ref[...]

    row_index = lax.broadcasted_iota(jnp.int32, (BLOCK, BLOCK), 0)
    lag_index = lax.broadcasted_iota(jnp.int32, (BLOCK, BLOCK), 1)
    mirror = jnp.where(row_index + lag_index == BLOCK - 1, 1.0, 0.0).astype(jnp.bfloat16)
    ahead = lag_index <= row_index

    for f in range(bins):
        left_ref[f] = lax.dot_general(
            mirror,
            placed_ref[:, f].reshape(groups * rows, BLOCK),
            (((1,), (1,)), ((), ())),
            preferred_element_type=jnp.float32,
        ).astype(jnp.bfloat16)

    for f in range(bins):
        right = []
        for place in range(groups):
            value = placed_ref[place, f]
            real, imag = value[:windows], value[windows:]
            right.append(
                jnp.concatenate(
                    [jnp.concatenate([real, imag], 1), jnp.concatenate([imag, -real], 1)], 0
                )
            )
        right = jnp.concatenate(right, 0)
        for delta in range(groups):
            panel = jnp.dot(
                left_ref[f, :, : rows * (groups - delta)],
                right[rows * delta :],
                preferred_element_type=jnp.float32,
            )
            for half in range(2):
                lanes = slice(half * BLOCK, (half + 1) * BLOCK)
                skewed = pltpu.roll(panel[:, lanes], 1, 1, stride=1, stride_axis=0)
                forward = jnp.where(ahead, skewed, 0.0).reshape(-1, 8, BLOCK).sum(0)
                backward = jnp.where(ahead, 0.0, skewed).reshape(-1, 8, BLOCK).sum(0)
                first = (f * 2 * groups + delta) * 8
                part_ref[half, first : first + 8] = forward
                part_ref[half, first + groups * 8 : first + groups * 8 + 8] = backward

    lags = []
    for half in range(2):
        summed = part_ref[half, pl.ds(0, bins * 2 * groups, stride=8), :]
        for sublane in range(1, 8):
            summed = summed + part_ref[half, pl.ds(sublane, bins * 2 * groups, stride=8), :]
        lags.append(summed)
    weight = stack_weights(groups)

    terms = []
    for f in range(bins):
        lag_rows = slice(f * 2 * groups, (f + 1) * 2 * groups)
        means = jnp.concatenate([half[lag_rows] * weight for half in lags], 0)
        mean_high, mean_low = halves(means)
        spread = jnp.concatenate(
            [
                jnp.concatenate([mean_high, mean_high], 1),
                jnp.concatenate([mean_low, jnp.zeros_like(mean_low)], 1),
            ],
            0,
        )
        product = jnp.dot(spread, lag_ref[start + f], preferred_element_type=jnp.float32)
        product = product[: 4 * groups] + product[4 * groups :]
        by_cos, by_sin = product[:, :SLOWNESS], product[:, SLOWNESS:]
        real = by_cos[: 2 * groups] - by_sin[2 * groups :]
        imag = by_sin[: 2 * groups] + by_cos[2 * groups :]
        shift_cos, shift_sin = shift_ref[start + f, 0], shift_ref[start + f, 1]
        turned_re = real * shift_cos - imag * shift_sin
        turned_im = real * shift_sin + imag * shift_cos
        terms.append(turned_re[:groups] + turned_re[groups:])
        terms.append(turned_im[:groups] + turned_im[groups:])

    if parts is None:
        for entry, term in enumerate(terms):
            out_ref[entry] = term
        return
    for earlier_ref in reversed(earlier_refs):
        terms = [earlier_ref[entry] for entry in range(earlier_ref.shape[0])] + terms
    slow_dev = SLOWNESS // parts
    spans = BLOCK // slow_dev
    span_index = lax.broadcasted_iota(jnp.int32, (groups, BLOCK), 1) // slow_dev
    for part in range(parts):
        source = (part % spans) * slow_dev
        lanes = slice(part // spans * BLOCK, (part // spans + 1) * BLOCK)
        for row in range(out_ref.shape[2]):
            packed = jnp.zeros((groups, BLOCK), jnp.float32)
            for span, term in enumerate(terms[row * spans : (row + 1) * spans]):
                moved = pltpu.roll(term[:, lanes], (span * slow_dev - source) % BLOCK, 1)
                packed = jnp.where(span_index == span, moved, packed)
            out_ref[:, part, row, :] = packed


def image_kernel(slow_dev, spans, term_ref, table_ref, out_ref):
    arrived = term_ref[...]
    turned = arrived.reshape(-1, BLOCK).T
    turned = jnp.concatenate(
        [turned[span * slow_dev : (span + 1) * slow_dev] for span in range(spans)], 1
    )
    high, low = halves(turned)
    by_high = jnp.dot(
        jnp.concatenate([high, low], 0), table_ref[0], preferred_element_type=jnp.float32
    )
    by_low = jnp.dot(high, table_ref[1], preferred_element_type=jnp.float32)
    out_ref[0] = by_high[:slow_dev] + by_high[slow_dev:] + by_low


def time_table(groups, parts, bins, slow_dev, message_rows):
    spans = min(BLOCK // slow_dev, 2 * bins)
    span, group, part, row = np.meshgrid(
        np.arange(spans), np.arange(groups), np.arange(parts), np.arange(message_rows), indexing="ij"
    )
    entry = row * spans + span
    freq = (part * groups + group) * bins + entry // 2
    lag_time = np.arange(LAG_TIMES) - LAG_TIMES // 2
    angle = 2.0 * math.pi / LAG_TIMES * ((freq[..., None] * lag_time) % LAG_TIMES)
    table = np.where((entry % 2 == 0)[..., None], np.cos(angle), -np.sin(angle))
    table = table.reshape(-1, LAG_TIMES).astype(np.float32)
    high = table.astype(jnp.bfloat16)
    low = (table - high.astype(np.float32)).astype(jnp.bfloat16)
    return spans, np.stack([high, low])


def shards(spectra, block_position):
    groups = lax.axis_size("chan")
    parts = lax.axis_size("freq")
    rows = spectra.shape[0] * spectra.shape[1]
    freq_dev = spectra.shape[2]
    bins = freq_dev // groups
    slow_dev = SLOWNESS // parts
    message_rows = -(-2 * bins * slow_dev // BLOCK)
    vmem = pl.BlockSpec(memory_space=pltpu.VMEM)
    smem = pl.BlockSpec(memory_space=pltpu.SMEM)
    params = pltpu.CompilerParams(vmem_limit_bytes=32 * 1024 * 1024)

    pieces = [(0, bins - bins // 2), (bins - bins // 2, bins // 2)] if bins > 1 else [(0, 1)]
    chunks = pl.pallas_call(
        functools.partial(chunk_kernel, groups, pieces),
        out_shape=tuple(
            jax.ShapeDtypeStruct((size, rows, BLOCK), jnp.bfloat16)
            for _, size in pieces
            for _ in range(groups)
        ),
        in_specs=[vmem],
        out_specs=(vmem,) * (groups * len(pieces)),
        scratch_shapes=[pltpu.VMEM((rows * freq_dev, BLOCK), jnp.float32)],
        compiler_params=params,
        name="chunks_of_bins",
    )(spectra.reshape(rows * freq_dev, BLOCK))
    chunks = [list(chunks[index * groups : (index + 1) * groups]) for index in range(len(pieces))]
    for piece in chunks:
        for distance in sorted(range(1, groups), key=lambda steps: abs(2 * steps - groups)):
            pairs = [(source, (source + distance) % groups) for source in range(groups)]
            piece[distance] = lax.ppermute(piece[distance], "chan", pairs)
    places, lag_table, shift_table = pl.pallas_call(
        functools.partial(table_kernel, groups, bins, freq_dev),
        out_shape=(
            jax.ShapeDtypeStruct((groups,), jnp.int32),
            jax.ShapeDtypeStruct((bins, 2 * BLOCK, 2 * SLOWNESS), jnp.bfloat16),
            jax.ShapeDtypeStruct((bins, 2, 2 * groups, SLOWNESS), jnp.float32),
        ),
        in_specs=[smem],
        out_specs=(smem, vmem, vmem),
        compiler_params=params,
        cost_estimate=pl.CostEstimate(flops=10**7, bytes_accessed=4 * 10**6, transcendentals=0),
        name="slant_tables",
    )(block_position)
    earlier = []
    for index, (start, size) in enumerate(pieces):
        last = index == len(pieces) - 1
        if last:
            shape = (groups, parts, message_rows, BLOCK)
        else:
            shape = (2 * size, groups, SLOWNESS)
        terms = pl.pallas_call(
            functools.partial(stack_kernel, groups, start, size, parts if last else None),
            out_shape=jax.ShapeDtypeStruct(shape, jnp.float32),
            in_specs=[vmem] * groups + [smem, vmem, vmem] + [vmem] * len(earlier),
            out_specs=vmem,
            scratch_shapes=[
                pltpu.VMEM((groups, size, rows, BLOCK), jnp.bfloat16),
                pltpu.VMEM((size, BLOCK, groups * rows), jnp.bfloat16),
                pltpu.VMEM((2, size * 2 * groups * 8, BLOCK), jnp.float32),
            ],
            compiler_params=params,
            cost_estimate=pl.CostEstimate(
                flops=2 * 10**8, bytes_accessed=4 * 10**6, transcendentals=0
            ),
            name="stack_and_slant",
        )(*chunks[index], places, lag_table, shift_table, *earlier)
        earlier.append(terms)
    terms = terms.reshape(groups * parts, message_rows, BLOCK)
    arrived = lax.all_to_all(terms, ("chan", "freq"), split_axis=0, concat_axis=0, tiled=True)
    spans, table = time_table(groups, parts, bins, slow_dev, message_rows)
    return pl.pallas_call(
        functools.partial(image_kernel, slow_dev, spans),
        out_shape=jax.ShapeDtypeStruct((1, slow_dev, LAG_TIMES), jnp.float32),
        in_specs=[vmem, vmem],
        out_specs=vmem,
        compiler_params=params,
        name="sum_of_bins",
    )(arrived, jnp.asarray(table))


def solution(mesh):
    return jax.shard_map(
        shards,
        mesh=mesh,
        in_specs=(P(None, None, "freq", "chan"), P()),
        out_specs=P("chan", "freq", None),
        check_vma=False,
    )
```

```python
import functools
import math

import jax
import jax.numpy as jnp
import numpy as np
from jax import lax
from jax.experimental import pallas as pl
from jax.experimental.pallas import tpu as pltpu
from jax.sharding import PartitionSpec as P

SEGMENTS = 32
FREQS = 256
BLOCK = 128
SLOWNESS = 256
LAG_TIMES = 512
MODULUS = 8 * FREQS * BLOCK


def unit_phase(numerator):
    quarter = MODULUS // 4
    turn = numerator & (MODULUS - 1)
    quadrant = lax.shift_right_logical(turn + quarter // 2, quarter.bit_length() - 1)
    x = (turn - quadrant * quarter).astype(jnp.float32) * (2.0 * math.pi / MODULUS)
    y = x * x
    sine = x * (1.0 + y * (-1.0 / 6 + y * (1.0 / 120 + y * (-1.0 / 5040 + y * (1.0 / 362880)))))
    cosine = 1.0 + y * (-0.5 + y * (1.0 / 24 + y * (-1.0 / 720 + y * (1.0 / 40320))))
    odd = (quadrant & 1) == 1
    first = jnp.where(odd, sine, cosine)
    second = jnp.where(odd, cosine, sine)
    first = jnp.where(((quadrant + 1) & 2) == 2, -first, first)
    second = jnp.where((quadrant & 2) == 2, -second, second)
    return first, second


def halves(value):
    high = value.astype(jnp.bfloat16)
    return high, (value - high.astype(jnp.float32)).astype(jnp.bfloat16)


def table_kernel(groups, bins, freq_dev, position_ref, place_ref, lag_ref, shift_ref):
    low_rows = lax.broadcasted_iota(jnp.int32, (8, SLOWNESS), 0)
    high_rows = lax.broadcasted_iota(jnp.int32, (BLOCK // 8, SLOWNESS), 0) * 8
    shift_rows = lax.broadcasted_iota(jnp.int32, (2 * groups, SLOWNESS), 0)
    shift_rows = jnp.where(shift_rows < groups, shift_rows, shift_rows - groups - 1) * BLOCK
    own_group = lax.axis_index("chan")
    first_bin = lax.axis_index("freq") * freq_dev + own_group * bins
    sender = lax.broadcasted_iota(jnp.int32, (groups, groups), 1)
    distance = lax.broadcasted_iota(jnp.int32, (groups, groups), 0)
    sends = lax.rem(own_group + groups - distance, groups) == sender
    places = jnp.sum(jnp.where(sends, position_ref[...], 0), axis=1, keepdims=True)
    place_ref[...] = jnp.broadcast_to(places, place_ref.shape)

    def one_bin(f, carry):
        def phases(rows):
            slow = lax.broadcasted_iota(jnp.int32, rows.shape, 1) - SLOWNESS // 2
            return unit_phase((first_bin + f) * slow * rows)

        low_cos, low_sin = phases(low_rows)
        high_cos, high_sin = phases(high_rows)
        low_cos, low_sin = low_cos[None], low_sin[None]
        high_cos, high_sin = high_cos[:, None], high_sin[:, None]
        lag_cos = (high_cos * low_cos - high_sin * low_sin).reshape(BLOCK, SLOWNESS)
        lag_sin = (high_sin * low_cos + high_cos * low_sin).reshape(BLOCK, SLOWNESS)
        cos_high, cos_low = halves(lag_cos)
        sin_high, sin_low = halves(lag_sin)
        lag_ref[f, :BLOCK, :SLOWNESS] = cos_high
        lag_ref[f, BLOCK:, :SLOWNESS] = cos_low
        lag_ref[f, :BLOCK, SLOWNESS:] = sin_high
        lag_ref[f, BLOCK:, SLOWNESS:] = sin_low
        shift_cos, shift_sin = phases(shift_rows)
        shift_ref[f, 0] = shift_cos
        shift_ref[f, 1] = shift_sin
        return carry

    lax.fori_loop(0, bins, one_bin, 0)


def chunk_kernel(groups, bins, spec_ref, *refs):
    out_refs, wide_ref = refs[:-1], refs[-1]
    wide_ref[...] = spec_ref[...].astype(jnp.float32)
    freq_dev = groups * bins
    rows = spec_ref.shape[0] // freq_dev
    own_group = lax.axis_index("chan")
    for distance, out_ref in enumerate(out_refs):
        first = lax.rem(own_group + distance, groups) * bins
        for f in range(bins):
            value = wide_ref[pl.ds(first + f, rows, stride=freq_dev), :]
            out_ref[f] = value.astype(jnp.bfloat16)


def stack_weights(groups):
    row = lax.broadcasted_iota(jnp.int32, (2 * groups, BLOCK), 0)
    lag = lax.broadcasted_iota(jnp.int32, (2 * groups, BLOCK), 1)
    delta = jnp.where(row < groups, row, row - groups)
    lag = jnp.where(row < groups, lag, lag - BLOCK)
    usable = (lag > -BLOCK) & ((delta >= 1) | (lag >= 1))
    count = SEGMENTS * (groups - delta) * (BLOCK - jnp.abs(lag))
    scale = math.sqrt(SEGMENTS / FREQS)
    return jnp.where(usable, scale / jnp.maximum(count, 1).astype(jnp.float32), 0.0)


def stack_kernel(groups, bins, parts, *refs):
    chunk_refs = refs[:groups]
    place_ref, lag_ref, shift_ref, out_ref, placed_ref, left_ref, part_ref = refs[groups:]
    rows = placed_ref.shape[2]
    windows = rows // 2
    places = place_ref[...]
    for distance, chunk_ref in enumerate(chunk_refs):
        placed_ref[places[distance, 0]] = chunk_ref[...]

    row_index = lax.broadcasted_iota(jnp.int32, (BLOCK, BLOCK), 0)
    lag_index = lax.broadcasted_iota(jnp.int32, (BLOCK, BLOCK), 1)
    mirror = jnp.where(row_index + lag_index == BLOCK - 1, 1.0, 0.0).astype(jnp.bfloat16)
    ahead = lag_index <= row_index

    for f in range(bins):
        left_ref[f] = lax.dot_general(
            mirror,
            placed_ref[:, f].reshape(groups * rows, BLOCK),
            (((1,), (1,)), ((), ())),
            preferred_element_type=jnp.float32,
        ).astype(jnp.bfloat16)

    for f in range(bins):
        right = []
        for place in range(groups):
            value = placed_ref[place, f]
            real, imag = value[:windows], value[windows:]
            right.append(
                jnp.concatenate(
                    [jnp.concatenate([real, imag], 1), jnp.concatenate([imag, -real], 1)], 0
                )
            )
        right = jnp.concatenate(right, 0)
        for delta in range(groups):
            panel = jnp.dot(
                left_ref[f, :, : rows * (groups - delta)],
                right[rows * delta :],
                preferred_element_type=jnp.float32,
            )
            for half in range(2):
                lanes = slice(half * BLOCK, (half + 1) * BLOCK)
                skewed = pltpu.roll(panel[:, lanes], 1, 1, stride=1, stride_axis=0)
                forward = jnp.where(ahead, skewed, 0.0).reshape(-1, 8, BLOCK).sum(0)
                backward = jnp.where(ahead, 0.0, skewed).reshape(-1, 8, BLOCK).sum(0)
                first = (f * 2 * groups + delta) * 8
                part_ref[half, first : first + 8] = forward
                part_ref[half, first + groups * 8 : first + groups * 8 + 8] = backward

    lags = []
    for half in range(2):
        summed = part_ref[half, pl.ds(0, bins * 2 * groups, stride=8), :]
        for sublane in range(1, 8):
            summed = summed + part_ref[half, pl.ds(sublane, bins * 2 * groups, stride=8), :]
        lags.append(summed)
    weight = stack_weights(groups)

    terms = []
    for f in range(bins):
        lag_rows = slice(f * 2 * groups, (f + 1) * 2 * groups)
        means = jnp.concatenate([half[lag_rows] * weight for half in lags], 0)
        mean_high, mean_low = halves(means)
        spread = jnp.concatenate(
            [
                jnp.concatenate([mean_high, mean_high], 1),
                jnp.concatenate([mean_low, jnp.zeros_like(mean_low)], 1),
            ],
            0,
        )
        product = jnp.dot(spread, lag_ref[f], preferred_element_type=jnp.float32)
        product = product[: 4 * groups] + product[4 * groups :]
        by_cos, by_sin = product[:, :SLOWNESS], product[:, SLOWNESS:]
        real = by_cos[: 2 * groups] - by_sin[2 * groups :]
        imag = by_sin[: 2 * groups] + by_cos[2 * groups :]
        shift_cos, shift_sin = shift_ref[f, 0], shift_ref[f, 1]
        turned_re = real * shift_cos - imag * shift_sin
        turned_im = real * shift_sin + imag * shift_cos
        terms.append(turned_re[:groups] + turned_re[groups:])
        terms.append(turned_im[:groups] + turned_im[groups:])

    slow_dev = SLOWNESS // parts
    spans = BLOCK // slow_dev
    span_index = lax.broadcasted_iota(jnp.int32, (groups, BLOCK), 1) // slow_dev
    for part in range(parts):
        source = (part % spans) * slow_dev
        lanes = slice(part // spans * BLOCK, (part // spans + 1) * BLOCK)
        for row in range(out_ref.shape[2]):
            packed = jnp.zeros((groups, BLOCK), jnp.float32)
            for span, term in enumerate(terms[row * spans : (row + 1) * spans]):
                moved = pltpu.roll(term[:, lanes], (span * slow_dev - source) % BLOCK, 1)
                packed = jnp.where(span_index == span, moved, packed)
            out_ref[:, part, row, :] = packed


def image_kernel(slow_dev, spans, term_ref, table_ref, out_ref):
    arrived = term_ref[...]
    turned = arrived.reshape(-1, BLOCK).T
    turned = jnp.concatenate(
        [turned[span * slow_dev : (span + 1) * slow_dev] for span in range(spans)], 1
    )
    high, low = halves(turned)
    by_high = jnp.dot(
        jnp.concatenate([high, low], 0), table_ref[0], preferred_element_type=jnp.float32
    )
    by_low = jnp.dot(high, table_ref[1], preferred_element_type=jnp.float32)
    out_ref[0] = by_high[:slow_dev] + by_high[slow_dev:] + by_low


def time_table(groups, parts, bins, slow_dev, message_rows):
    spans = min(BLOCK // slow_dev, 2 * bins)
    span, group, part, row = np.meshgrid(
        np.arange(spans), np.arange(groups), np.arange(parts), np.arange(message_rows), indexing="ij"
    )
    entry = row * spans + span
    freq = (part * groups + group) * bins + entry // 2
    lag_time = np.arange(LAG_TIMES) - LAG_TIMES // 2
    angle = 2.0 * math.pi / LAG_TIMES * ((freq[..., None] * lag_time) % LAG_TIMES)
    table = np.where((entry % 2 == 0)[..., None], np.cos(angle), -np.sin(angle))
    table = table.reshape(-1, LAG_TIMES).astype(np.float32)
    high = table.astype(jnp.bfloat16)
    low = (table - high.astype(np.float32)).astype(jnp.bfloat16)
    return spans, np.stack([high, low])


def shards(spectra, block_position):
    groups = lax.axis_size("chan")
    parts = lax.axis_size("freq")
    rows = spectra.shape[0] * spectra.shape[1]
    freq_dev = spectra.shape[2]
    bins = freq_dev // groups
    slow_dev = SLOWNESS // parts
    message_rows = -(-2 * bins * slow_dev // BLOCK)
    vmem = pl.BlockSpec(memory_space=pltpu.VMEM)
    params = pltpu.CompilerParams(vmem_limit_bytes=32 * 1024 * 1024)

    chunk = jax.ShapeDtypeStruct((bins, rows, BLOCK), jnp.bfloat16)
    chunks = pl.pallas_call(
        functools.partial(chunk_kernel, groups, bins),
        out_shape=(chunk,) * groups,
        in_specs=[vmem],
        out_specs=(vmem,) * groups,
        scratch_shapes=[pltpu.VMEM((rows * freq_dev, BLOCK), jnp.float32)],
        compiler_params=params,
        name="chunks_of_bins",
    )(spectra.reshape(rows * freq_dev, BLOCK))
    arrived_chunks = list(chunks)
    for distance in sorted(range(1, groups), key=lambda steps: abs(2 * steps - groups)):
        pairs = [(source, (source + distance) % groups) for source in range(groups)]
        arrived_chunks[distance] = lax.ppermute(chunks[distance], "chan", pairs)
    places, lag_table, shift_table = pl.pallas_call(
        functools.partial(table_kernel, groups, bins, freq_dev),
        out_shape=(
            jax.ShapeDtypeStruct((groups, BLOCK), jnp.int32),
            jax.ShapeDtypeStruct((bins, 2 * BLOCK, 2 * SLOWNESS), jnp.bfloat16),
            jax.ShapeDtypeStruct((bins, 2, 2 * groups, SLOWNESS), jnp.float32),
        ),
        in_specs=[vmem],
        out_specs=(vmem, vmem, vmem),
        compiler_params=params,
        cost_estimate=pl.CostEstimate(flops=10**7, bytes_accessed=4 * 10**6, transcendentals=0),
        name="slant_tables",
    )(block_position.reshape(1, groups))
    terms = pl.pallas_call(
        functools.partial(stack_kernel, groups, bins, parts),
        out_shape=jax.ShapeDtypeStruct((groups, parts, message_rows, BLOCK), jnp.float32),
        in_specs=[vmem] * (groups + 3),
        out_specs=vmem,
        scratch_shapes=[
            pltpu.VMEM((groups, bins, rows, BLOCK), jnp.bfloat16),
            pltpu.VMEM((bins, BLOCK, groups * rows), jnp.bfloat16),
            pltpu.VMEM((2, bins * 2 * groups * 8, BLOCK), jnp.float32),
        ],
        compiler_params=params,
        name="stack_and_slant",
    )(
        *arrived_chunks,
        places,
        lag_table,
        shift_table,
    )
    terms = terms.reshape(groups * parts, message_rows, BLOCK)
    arrived = lax.all_to_all(terms, ("chan", "freq"), split_axis=0, concat_axis=0, tiled=True)
    spans, table = time_table(groups, parts, bins, slow_dev, message_rows)
    return pl.pallas_call(
        functools.partial(image_kernel, slow_dev, spans),
        out_shape=jax.ShapeDtypeStruct((1, slow_dev, LAG_TIMES), jnp.float32),
        in_specs=[vmem, vmem],
        out_specs=vmem,
        compiler_params=params,
        name="sum_of_bins",
    )(arrived, jnp.asarray(table))


def solution(mesh):
    return jax.shard_map(
        shards,
        mesh=mesh,
        in_specs=(P(None, None, "freq", "chan"), P()),
        out_specs=P("chan", "freq", None),
        check_vma=False,
    )
```

```python
import functools
import math

import jax
import jax.numpy as jnp
import numpy as np
from jax import lax
from jax.experimental import pallas as pl
from jax.experimental.pallas import tpu as pltpu
from jax.sharding import PartitionSpec as P

SEGMENTS = 32
FREQS = 256
BLOCK = 128
SLOWNESS = 256
LAG_TIMES = 512
MODULUS = 8 * FREQS * BLOCK


def unit_phase(numerator):
    quarter = MODULUS // 4
    turn = numerator & (MODULUS - 1)
    quadrant = lax.shift_right_logical(turn + quarter // 2, quarter.bit_length() - 1)
    x = (turn - quadrant * quarter).astype(jnp.float32) * (2.0 * math.pi / MODULUS)
    y = x * x
    sine = x * (1.0 + y * (-1.0 / 6 + y * (1.0 / 120 + y * (-1.0 / 5040 + y * (1.0 / 362880)))))
    cosine = 1.0 + y * (-0.5 + y * (1.0 / 24 + y * (-1.0 / 720 + y * (1.0 / 40320))))
    odd = (quadrant & 1) == 1
    first = jnp.where(odd, sine, cosine)
    second = jnp.where(odd, cosine, sine)
    first = jnp.where(((quadrant + 1) & 2) == 2, -first, first)
    second = jnp.where((quadrant & 2) == 2, -second, second)
    return first, second


def halves(value):
    high = value.astype(jnp.bfloat16)
    return high, (value - high.astype(jnp.float32)).astype(jnp.bfloat16)


def table_kernel(groups, bins, freq_dev, position_ref, place_ref, lag_ref, shift_ref):
    low_rows = lax.broadcasted_iota(jnp.int32, (8, SLOWNESS), 0)
    high_rows = lax.broadcasted_iota(jnp.int32, (BLOCK // 8, SLOWNESS), 0) * 8
    shift_rows = lax.broadcasted_iota(jnp.int32, (2 * groups, SLOWNESS), 0)
    shift_rows = jnp.where(shift_rows < groups, shift_rows, shift_rows - groups - 1) * BLOCK
    own_group = lax.axis_index("chan")
    first_bin = lax.axis_index("freq") * freq_dev + own_group * bins
    sender = lax.broadcasted_iota(jnp.int32, (groups, groups), 1)
    mask = lax.broadcasted_iota(jnp.int32, (groups, groups), 0)
    sends = lax.bitwise_xor(own_group, mask) == sender
    places = jnp.sum(jnp.where(sends, position_ref[...], 0), axis=1, keepdims=True)
    place_ref[...] = jnp.broadcast_to(places, place_ref.shape)

    def one_bin(f, carry):
        def phases(rows):
            slow = lax.broadcasted_iota(jnp.int32, rows.shape, 1) - SLOWNESS // 2
            return unit_phase((first_bin + f) * slow * rows)

        low_cos, low_sin = phases(low_rows)
        high_cos, high_sin = phases(high_rows)
        low_cos, low_sin = low_cos[None], low_sin[None]
        high_cos, high_sin = high_cos[:, None], high_sin[:, None]
        lag_cos = (high_cos * low_cos - high_sin * low_sin).reshape(BLOCK, SLOWNESS)
        lag_sin = (high_sin * low_cos + high_cos * low_sin).reshape(BLOCK, SLOWNESS)
        cos_high, cos_low = halves(lag_cos)
        sin_high, sin_low = halves(lag_sin)
        lag_ref[f, :BLOCK, :SLOWNESS] = cos_high
        lag_ref[f, BLOCK:, :SLOWNESS] = cos_low
        lag_ref[f, :BLOCK, SLOWNESS:] = sin_high
        lag_ref[f, BLOCK:, SLOWNESS:] = sin_low
        shift_cos, shift_sin = phases(shift_rows)
        shift_ref[f, 0] = shift_cos
        shift_ref[f, 1] = shift_sin
        return carry

    lax.fori_loop(0, bins, one_bin, 0)


def chunk_kernel(groups, bins, spec_ref, *refs):
    out_refs, wide_ref = refs[:-1], refs[-1]
    wide_ref[...] = spec_ref[...].astype(jnp.float32)
    freq_dev = groups * bins
    rows = spec_ref.shape[0] // freq_dev
    own_group = lax.axis_index("chan")
    for mask, out_ref in enumerate(out_refs):
        first = lax.bitwise_xor(own_group, mask) * bins
        for f in range(bins):
            value = wide_ref[pl.ds(first + f, rows, stride=freq_dev), :]
            out_ref[f] = value.astype(jnp.bfloat16)


def stack_weights(groups):
    row = lax.broadcasted_iota(jnp.int32, (2 * groups, BLOCK), 0)
    lag = lax.broadcasted_iota(jnp.int32, (2 * groups, BLOCK), 1)
    delta = jnp.where(row < groups, row, row - groups)
    lag = jnp.where(row < groups, lag, lag - BLOCK)
    usable = (lag > -BLOCK) & ((delta >= 1) | (lag >= 1))
    count = SEGMENTS * (groups - delta) * (BLOCK - jnp.abs(lag))
    scale = math.sqrt(SEGMENTS / FREQS)
    return jnp.where(usable, scale / jnp.maximum(count, 1).astype(jnp.float32), 0.0)


def stack_kernel(groups, bins, parts, *refs):
    chunk_refs = refs[:groups]
    place_ref, lag_ref, shift_ref, out_ref, placed_ref, left_ref, part_ref = refs[groups:]
    rows = placed_ref.shape[2]
    windows = rows // 2
    places = place_ref[...]
    for mask, chunk_ref in enumerate(chunk_refs):
        placed_ref[places[mask, 0]] = chunk_ref[...]

    row_index = lax.broadcasted_iota(jnp.int32, (BLOCK, BLOCK), 0)
    lag_index = lax.broadcasted_iota(jnp.int32, (BLOCK, BLOCK), 1)
    mirror = jnp.where(row_index + lag_index == BLOCK - 1, 1.0, 0.0).astype(jnp.bfloat16)
    behind = (lag_index - row_index)[:8]

    for f in range(bins):
        left_ref[f] = lax.dot_general(
            mirror,
            placed_ref[:, f].reshape(groups * rows, BLOCK),
            (((1,), (1,)), ((), ())),
            preferred_element_type=jnp.float32,
        ).astype(jnp.bfloat16)

    for f in range(bins):
        right = []
        for place in range(groups):
            value = placed_ref[place, f]
            real, imag = value[:windows], value[windows:]
            right.append(
                jnp.concatenate(
                    [jnp.concatenate([real, imag], 1), jnp.concatenate([imag, -real], 1)], 0
                )
            )
        right = jnp.concatenate(right, 0)
        for delta in range(groups):
            panel = jnp.dot(
                left_ref[f, :, : rows * (groups - delta)],
                right[rows * delta :],
                preferred_element_type=jnp.float32,
            )
            for half in range(2):
                lanes = slice(half * BLOCK, (half + 1) * BLOCK)
                skewed = pltpu.roll(panel[:, lanes], 1, 1, stride=1, stride_axis=0)
                total = skewed[:8]
                backward = jnp.where(behind > 0, total, 0.0)
                for row in range(8, BLOCK, 8):
                    total = total + skewed[row : row + 8]
                    backward = jnp.where(behind > row, total, backward)
                first = (f * 2 * groups + delta) * 8
                part_ref[half, first : first + 8] = total - backward
                part_ref[half, first + groups * 8 : first + groups * 8 + 8] = backward

    lags = []
    for half in range(2):
        summed = part_ref[half, pl.ds(0, bins * 2 * groups, stride=8), :]
        for sublane in range(1, 8):
            summed = summed + part_ref[half, pl.ds(sublane, bins * 2 * groups, stride=8), :]
        lags.append(summed)
    weight = stack_weights(groups)

    terms = []
    for f in range(bins):
        lag_rows = slice(f * 2 * groups, (f + 1) * 2 * groups)
        means = jnp.concatenate([half[lag_rows] * weight for half in lags], 0)
        mean_high, mean_low = halves(means)
        spread = jnp.concatenate(
            [
                jnp.concatenate([mean_high, mean_high], 1),
                jnp.concatenate([mean_low, jnp.zeros_like(mean_low)], 1),
            ],
            0,
        )
        product = jnp.dot(spread, lag_ref[f], preferred_element_type=jnp.float32)
        product = product[: 4 * groups] + product[4 * groups :]
        by_cos, by_sin = product[:, :SLOWNESS], product[:, SLOWNESS:]
        real = by_cos[: 2 * groups] - by_sin[2 * groups :]
        imag = by_sin[: 2 * groups] + by_cos[2 * groups :]
        shift_cos, shift_sin = shift_ref[f, 0], shift_ref[f, 1]
        turned_re = real * shift_cos - imag * shift_sin
        turned_im = real * shift_sin + imag * shift_cos
        terms.append(turned_re[:groups] + turned_re[groups:])
        terms.append(turned_im[:groups] + turned_im[groups:])

    slow_dev = SLOWNESS // parts
    spans = BLOCK // slow_dev
    span_index = lax.broadcasted_iota(jnp.int32, (groups, BLOCK), 1) // slow_dev
    for part in range(parts):
        source = (part % spans) * slow_dev
        lanes = slice(part // spans * BLOCK, (part // spans + 1) * BLOCK)
        for row in range(out_ref.shape[2]):
            packed = jnp.zeros((groups, BLOCK), jnp.float32)
            for span, term in enumerate(terms[row * spans : (row + 1) * spans]):
                moved = pltpu.roll(term[:, lanes], (span * slow_dev - source) % BLOCK, 1)
                packed = jnp.where(span_index == span, moved, packed)
            out_ref[:, part, row, :] = packed


def image_kernel(slow_dev, spans, term_ref, table_ref, out_ref):
    arrived = term_ref[...]
    turned = arrived.reshape(-1, BLOCK).T
    turned = jnp.concatenate(
        [turned[span * slow_dev : (span + 1) * slow_dev] for span in range(spans)], 1
    )
    high, low = halves(turned)
    by_high = jnp.dot(
        jnp.concatenate([high, low], 0), table_ref[0], preferred_element_type=jnp.float32
    )
    by_low = jnp.dot(high, table_ref[1], preferred_element_type=jnp.float32)
    out_ref[0] = by_high[:slow_dev] + by_high[slow_dev:] + by_low


def time_table(groups, parts, bins, slow_dev, message_rows):
    spans = min(BLOCK // slow_dev, 2 * bins)
    span, group, part, row = np.meshgrid(
        np.arange(spans), np.arange(groups), np.arange(parts), np.arange(message_rows), indexing="ij"
    )
    entry = row * spans + span
    freq = (part * groups + group) * bins + entry // 2
    lag_time = np.arange(LAG_TIMES) - LAG_TIMES // 2
    angle = 2.0 * math.pi / LAG_TIMES * ((freq[..., None] * lag_time) % LAG_TIMES)
    table = np.where((entry % 2 == 0)[..., None], np.cos(angle), -np.sin(angle))
    table = table.reshape(-1, LAG_TIMES).astype(np.float32)
    high = table.astype(jnp.bfloat16)
    low = (table - high.astype(np.float32)).astype(jnp.bfloat16)
    return spans, np.stack([high, low])


def shards(spectra, block_position):
    groups = lax.axis_size("chan")
    parts = lax.axis_size("freq")
    rows = spectra.shape[0] * spectra.shape[1]
    freq_dev = spectra.shape[2]
    bins = freq_dev // groups
    slow_dev = SLOWNESS // parts
    message_rows = -(-2 * bins * slow_dev // BLOCK)
    vmem = pl.BlockSpec(memory_space=pltpu.VMEM)
    params = pltpu.CompilerParams(vmem_limit_bytes=32 * 1024 * 1024)

    chunk = jax.ShapeDtypeStruct((bins, rows, BLOCK), jnp.bfloat16)
    chunks = pl.pallas_call(
        functools.partial(chunk_kernel, groups, bins),
        out_shape=(chunk,) * groups,
        in_specs=[vmem],
        out_specs=(vmem,) * groups,
        scratch_shapes=[pltpu.VMEM((rows * freq_dev, BLOCK), jnp.float32)],
        compiler_params=params,
        name="chunks_of_bins",
    )(spectra.reshape(rows * freq_dev, BLOCK))
    arrived_chunks = list(chunks)
    for mask in list(range(groups // 2, groups)) + list(range(groups // 2 - 1, 0, -1)):
        pairs = [(source, source ^ mask) for source in range(groups)]
        arrived_chunks[mask] = lax.ppermute(chunks[mask], "chan", pairs)
    places, lag_table, shift_table = pl.pallas_call(
        functools.partial(table_kernel, groups, bins, freq_dev),
        out_shape=(
            jax.ShapeDtypeStruct((groups, BLOCK), jnp.int32),
            jax.ShapeDtypeStruct((bins, 2 * BLOCK, 2 * SLOWNESS), jnp.bfloat16),
            jax.ShapeDtypeStruct((bins, 2, 2 * groups, SLOWNESS), jnp.float32),
        ),
        in_specs=[vmem],
        out_specs=(vmem, vmem, vmem),
        compiler_params=params,
        cost_estimate=pl.CostEstimate(flops=10**7, bytes_accessed=4 * 10**6, transcendentals=0),
        name="slant_tables",
    )(block_position.reshape(1, groups))
    terms = pl.pallas_call(
        functools.partial(stack_kernel, groups, bins, parts),
        out_shape=jax.ShapeDtypeStruct((groups, parts, message_rows, BLOCK), jnp.float32),
        in_specs=[vmem] * (groups + 3),
        out_specs=vmem,
        scratch_shapes=[
            pltpu.VMEM((groups, bins, rows, BLOCK), jnp.bfloat16),
            pltpu.VMEM((bins, BLOCK, groups * rows), jnp.bfloat16),
            pltpu.VMEM((2, bins * 2 * groups * 8, BLOCK), jnp.float32),
        ],
        compiler_params=params,
        name="stack_and_slant",
    )(
        *arrived_chunks,
        places,
        lag_table,
        shift_table,
    )
    terms = terms.reshape(groups * parts, message_rows, BLOCK)
    arrived = lax.all_to_all(terms, ("chan", "freq"), split_axis=0, concat_axis=0, tiled=True)
    spans, table = time_table(groups, parts, bins, slow_dev, message_rows)
    return pl.pallas_call(
        functools.partial(image_kernel, slow_dev, spans),
        out_shape=jax.ShapeDtypeStruct((1, slow_dev, LAG_TIMES), jnp.float32),
        in_specs=[vmem, vmem],
        out_specs=vmem,
        compiler_params=params,
        name="sum_of_bins",
    )(arrived, jnp.asarray(table))


def solution(mesh):
    return jax.shard_map(
        shards,
        mesh=mesh,
        in_specs=(P(None, None, "freq", "chan"), P()),
        out_specs=P("chan", "freq", None),
        check_vma=False,
    )
```

```python
import functools
import math

import jax
import jax.numpy as jnp
import numpy as np
from jax import lax
from jax.experimental import pallas as pl
from jax.experimental.pallas import tpu as pltpu
from jax.sharding import PartitionSpec as P

SEGMENTS = 32
FREQS = 256
BLOCK = 128
SLOWNESS = 256
LAG_TIMES = 512
MODULUS = 8 * FREQS * BLOCK


def unit_phase(numerator):
    quarter = MODULUS // 4
    turn = numerator & (MODULUS - 1)
    quadrant = lax.shift_right_logical(turn + quarter // 2, quarter.bit_length() - 1)
    x = (turn - quadrant * quarter).astype(jnp.float32) * (2.0 * math.pi / MODULUS)
    y = x * x
    sine = x * (1.0 + y * (-1.0 / 6 + y * (1.0 / 120 + y * (-1.0 / 5040 + y * (1.0 / 362880)))))
    cosine = 1.0 + y * (-0.5 + y * (1.0 / 24 + y * (-1.0 / 720 + y * (1.0 / 40320))))
    odd = (quadrant & 1) == 1
    first = jnp.where(odd, sine, cosine)
    second = jnp.where(odd, cosine, sine)
    first = jnp.where(((quadrant + 1) & 2) == 2, -first, first)
    second = jnp.where((quadrant & 2) == 2, -second, second)
    return first, second


def halves(value):
    high = value.astype(jnp.bfloat16)
    return high, (value - high.astype(jnp.float32)).astype(jnp.bfloat16)


def table_kernel(groups, bins, freq_dev, position_ref, place_ref, lag_ref, shift_ref):
    low_rows = lax.broadcasted_iota(jnp.int32, (8, SLOWNESS), 0)
    high_rows = lax.broadcasted_iota(jnp.int32, (BLOCK // 8, SLOWNESS), 0) * 8
    shift_rows = lax.broadcasted_iota(jnp.int32, (2 * groups, SLOWNESS), 0)
    shift_rows = jnp.where(shift_rows < groups, shift_rows, shift_rows - groups - 1) * BLOCK
    own_group = lax.axis_index("chan")
    first_bin = lax.axis_index("freq") * freq_dev + own_group * bins
    sender = lax.broadcasted_iota(jnp.int32, (groups, groups), 1)
    mask = lax.broadcasted_iota(jnp.int32, (groups, groups), 0)
    sends = lax.bitwise_xor(own_group, mask) == sender
    places = jnp.sum(jnp.where(sends, position_ref[...], 0), axis=1, keepdims=True)
    place_ref[...] = jnp.broadcast_to(places, place_ref.shape)

    def one_bin(f, carry):
        def phases(rows):
            slow = lax.broadcasted_iota(jnp.int32, rows.shape, 1) - SLOWNESS // 2
            return unit_phase((first_bin + f) * slow * rows)

        low_cos, low_sin = phases(low_rows)
        high_cos, high_sin = phases(high_rows)
        low_cos, low_sin = low_cos[None], low_sin[None]
        high_cos, high_sin = high_cos[:, None], high_sin[:, None]
        lag_cos = (high_cos * low_cos - high_sin * low_sin).reshape(BLOCK, SLOWNESS)
        lag_sin = (high_sin * low_cos + high_cos * low_sin).reshape(BLOCK, SLOWNESS)
        cos_high, cos_low = halves(lag_cos)
        sin_high, sin_low = halves(lag_sin)
        lag_ref[f, :BLOCK, :SLOWNESS] = cos_high
        lag_ref[f, BLOCK:, :SLOWNESS] = cos_low
        lag_ref[f, :BLOCK, SLOWNESS:] = sin_high
        lag_ref[f, BLOCK:, SLOWNESS:] = sin_low
        shift_cos, shift_sin = phases(shift_rows)
        shift_ref[f, 0] = shift_cos
        shift_ref[f, 1] = shift_sin
        return carry

    lax.fori_loop(0, bins, one_bin, 0)


def partner_order(groups):
    return list(range(groups // 2, groups)) + list(range(groups // 2 - 1, -1, -1))


def chunk_kernel(groups, bins, spec_ref, *refs):
    out_refs, wide_ref = refs[:-1], refs[-1]
    wide_ref[...] = spec_ref[...].astype(jnp.float32)
    freq_dev = groups * bins
    rows = spec_ref.shape[0] // freq_dev
    own_group = lax.axis_index("chan")
    for mask, out_ref in enumerate(out_refs):
        first = lax.bitwise_xor(own_group, mask) * bins
        for f in range(bins):
            value = wide_ref[pl.ds(first + f, rows, stride=freq_dev), :]
            out_ref[f] = value.astype(jnp.bfloat16)


def stack_weights(groups):
    row = lax.broadcasted_iota(jnp.int32, (2 * groups, BLOCK), 0)
    lag = lax.broadcasted_iota(jnp.int32, (2 * groups, BLOCK), 1)
    delta = jnp.where(row < groups, row, row - groups)
    lag = jnp.where(row < groups, lag, lag - BLOCK)
    usable = (lag > -BLOCK) & ((delta >= 1) | (lag >= 1))
    count = SEGMENTS * (groups - delta) * (BLOCK - jnp.abs(lag))
    scale = math.sqrt(SEGMENTS / FREQS)
    return jnp.where(usable, scale / jnp.maximum(count, 1).astype(jnp.float32), 0.0)


def stack_kernel(groups, bins, parts, *refs):
    chunk_refs = refs[:groups]
    place_ref, lag_ref, shift_ref, out_ref, placed_ref, left_ref, part_ref = refs[groups:]
    rows = placed_ref.shape[2]
    windows = rows // 2
    places = place_ref[...]
    for mask, chunk_ref in zip(partner_order(groups), chunk_refs):
        placed_ref[places[mask, 0]] = chunk_ref[...]

    row_index = lax.broadcasted_iota(jnp.int32, (BLOCK, BLOCK), 0)
    lag_index = lax.broadcasted_iota(jnp.int32, (BLOCK, BLOCK), 1)
    mirror = jnp.where(row_index + lag_index == BLOCK - 1, 1.0, 0.0).astype(jnp.bfloat16)
    behind = (lag_index - row_index)[:8]

    for f in range(bins):
        left_ref[f] = lax.dot_general(
            mirror,
            placed_ref[:, f].reshape(groups * rows, BLOCK),
            (((1,), (1,)), ((), ())),
            preferred_element_type=jnp.float32,
        ).astype(jnp.bfloat16)

    for f in range(bins):
        right = []
        for place in range(groups):
            value = placed_ref[place, f]
            real, imag = value[:windows], value[windows:]
            right.append(
                jnp.concatenate(
                    [jnp.concatenate([real, imag], 1), jnp.concatenate([imag, -real], 1)], 0
                )
            )
        right = jnp.concatenate(right, 0)
        for delta in range(groups):
            panel = jnp.dot(
                left_ref[f, :, : rows * (groups - delta)],
                right[rows * delta :],
                preferred_element_type=jnp.float32,
            )
            for half in range(2):
                lanes = slice(half * BLOCK, (half + 1) * BLOCK)
                skewed = pltpu.roll(panel[:, lanes], 1, 1, stride=1, stride_axis=0)
                total = skewed[:8]
                backward = jnp.where(behind > 0, total, 0.0)
                for row in range(8, BLOCK, 8):
                    total = total + skewed[row : row + 8]
                    backward = jnp.where(behind > row, total, backward)
                first = (f * 2 * groups + delta) * 8
                part_ref[half, first : first + 8] = total - backward
                part_ref[half, first + groups * 8 : first + groups * 8 + 8] = backward

    lags = []
    for half in range(2):
        summed = part_ref[half, pl.ds(0, bins * 2 * groups, stride=8), :]
        for sublane in range(1, 8):
            summed = summed + part_ref[half, pl.ds(sublane, bins * 2 * groups, stride=8), :]
        lags.append(summed)
    weight = stack_weights(groups)

    terms = []
    for f in range(bins):
        lag_rows = slice(f * 2 * groups, (f + 1) * 2 * groups)
        means = jnp.concatenate([half[lag_rows] * weight for half in lags], 0)
        mean_high, mean_low = halves(means)
        spread = jnp.concatenate(
            [
                jnp.concatenate([mean_high, mean_high], 1),
                jnp.concatenate([mean_low, jnp.zeros_like(mean_low)], 1),
            ],
            0,
        )
        product = jnp.dot(spread, lag_ref[f], preferred_element_type=jnp.float32)
        product = product[: 4 * groups] + product[4 * groups :]
        by_cos, by_sin = product[:, :SLOWNESS], product[:, SLOWNESS:]
        real = by_cos[: 2 * groups] - by_sin[2 * groups :]
        imag = by_sin[: 2 * groups] + by_cos[2 * groups :]
        shift_cos, shift_sin = shift_ref[f, 0], shift_ref[f, 1]
        turned_re = real * shift_cos - imag * shift_sin
        turned_im = real * shift_sin + imag * shift_cos
        terms.append(turned_re[:groups] + turned_re[groups:])
        terms.append(turned_im[:groups] + turned_im[groups:])

    slow_dev = SLOWNESS // parts
    spans = BLOCK // slow_dev
    span_index = lax.broadcasted_iota(jnp.int32, (groups, BLOCK), 1) // slow_dev
    for part in range(parts):
        source = (part % spans) * slow_dev
        lanes = slice(part // spans * BLOCK, (part // spans + 1) * BLOCK)
        for row in range(out_ref.shape[2]):
            packed = jnp.zeros((groups, BLOCK), jnp.float32)
            for span, term in enumerate(terms[row * spans : (row + 1) * spans]):
                moved = pltpu.roll(term[:, lanes], (span * slow_dev - source) % BLOCK, 1)
                packed = jnp.where(span_index == span, moved, packed)
            out_ref[:, part, row, :] = packed


def image_kernel(slow_dev, spans, term_ref, table_ref, out_ref):
    arrived = term_ref[...]
    turned = arrived.reshape(-1, BLOCK).T
    turned = jnp.concatenate(
        [turned[span * slow_dev : (span + 1) * slow_dev] for span in range(spans)], 1
    )
    high, low = halves(turned)
    by_high = jnp.dot(
        jnp.concatenate([high, low], 0), table_ref[0], preferred_element_type=jnp.float32
    )
    by_low = jnp.dot(high, table_ref[1], preferred_element_type=jnp.float32)
    out_ref[0] = by_high[:slow_dev] + by_high[slow_dev:] + by_low


def time_table(groups, parts, bins, slow_dev, message_rows):
    spans = min(BLOCK // slow_dev, 2 * bins)
    span, group, part, row = np.meshgrid(
        np.arange(spans), np.arange(groups), np.arange(parts), np.arange(message_rows), indexing="ij"
    )
    entry = row * spans + span
    freq = (part * groups + group) * bins + entry // 2
    lag_time = np.arange(LAG_TIMES) - LAG_TIMES // 2
    angle = 2.0 * math.pi / LAG_TIMES * ((freq[..., None] * lag_time) % LAG_TIMES)
    table = np.where((entry % 2 == 0)[..., None], np.cos(angle), -np.sin(angle))
    table = table.reshape(-1, LAG_TIMES).astype(np.float32)
    high = table.astype(jnp.bfloat16)
    low = (table - high.astype(np.float32)).astype(jnp.bfloat16)
    return spans, np.stack([high, low])


def shards(spectra, block_position):
    groups = lax.axis_size("chan")
    parts = lax.axis_size("freq")
    rows = spectra.shape[0] * spectra.shape[1]
    freq_dev = spectra.shape[2]
    bins = freq_dev // groups
    slow_dev = SLOWNESS // parts
    message_rows = -(-2 * bins * slow_dev // BLOCK)
    vmem = pl.BlockSpec(memory_space=pltpu.VMEM)
    params = pltpu.CompilerParams(vmem_limit_bytes=32 * 1024 * 1024)

    chunk = jax.ShapeDtypeStruct((bins, rows, BLOCK), jnp.bfloat16)
    chunks = pl.pallas_call(
        functools.partial(chunk_kernel, groups, bins),
        out_shape=(chunk,) * groups,
        in_specs=[vmem],
        out_specs=(vmem,) * groups,
        scratch_shapes=[pltpu.VMEM((rows * freq_dev, BLOCK), jnp.float32)],
        compiler_params=params,
        name="chunks_of_bins",
    )(spectra.reshape(rows * freq_dev, BLOCK))
    arrived_chunks = list(chunks)
    order = partner_order(groups)
    for mask in order[:-1]:
        pairs = [(source, source ^ mask) for source in range(groups)]
        arrived_chunks[mask] = lax.ppermute(chunks[mask], "chan", pairs)
    places, lag_table, shift_table = pl.pallas_call(
        functools.partial(table_kernel, groups, bins, freq_dev),
        out_shape=(
            jax.ShapeDtypeStruct((groups, BLOCK), jnp.int32),
            jax.ShapeDtypeStruct((bins, 2 * BLOCK, 2 * SLOWNESS), jnp.bfloat16),
            jax.ShapeDtypeStruct((bins, 2, 2 * groups, SLOWNESS), jnp.float32),
        ),
        in_specs=[vmem],
        out_specs=(vmem, vmem, vmem),
        compiler_params=params,
        cost_estimate=pl.CostEstimate(flops=10**7, bytes_accessed=4 * 10**6, transcendentals=0),
        name="slant_tables",
    )(block_position.reshape(1, groups))
    terms = pl.pallas_call(
        functools.partial(stack_kernel, groups, bins, parts),
        out_shape=jax.ShapeDtypeStruct((groups, parts, message_rows, BLOCK), jnp.float32),
        in_specs=[vmem] * (groups + 3),
        out_specs=vmem,
        scratch_shapes=[
            pltpu.VMEM((groups, bins, rows, BLOCK), jnp.bfloat16),
            pltpu.VMEM((bins, BLOCK, groups * rows), jnp.bfloat16),
            pltpu.VMEM((2, bins * 2 * groups * 8, BLOCK), jnp.float32),
        ],
        compiler_params=params,
        name="stack_and_slant",
    )(
        *[arrived_chunks[mask] for mask in order],
        places,
        lag_table,
        shift_table,
    )
    terms = terms.reshape(groups * parts, message_rows, BLOCK)
    arrived = lax.all_to_all(terms, ("chan", "freq"), split_axis=0, concat_axis=0, tiled=True)
    spans, table = time_table(groups, parts, bins, slow_dev, message_rows)
    return pl.pallas_call(
        functools.partial(image_kernel, slow_dev, spans),
        out_shape=jax.ShapeDtypeStruct((1, slow_dev, LAG_TIMES), jnp.float32),
        in_specs=[vmem, vmem],
        out_specs=vmem,
        compiler_params=params,
        name="sum_of_bins",
    )(arrived, jnp.asarray(table))


def solution(mesh):
    return jax.shard_map(
        shards,
        mesh=mesh,
        in_specs=(P(None, None, "freq", "chan"), P()),
        out_specs=P("chan", "freq", None),
        check_vma=False,
    )
```

```python
import functools
import math

import jax
import jax.numpy as jnp
import numpy as np
from jax import lax
from jax.experimental import pallas as pl
from jax.experimental.pallas import tpu as pltpu
from jax.sharding import PartitionSpec as P

SEGMENTS = 32
FREQS = 256
BLOCK = 128
SLOWNESS = 256
LAG_TIMES = 512
MODULUS = 8 * FREQS * BLOCK


def unit_phase(numerator):
    quarter = MODULUS // 4
    turn = numerator & (MODULUS - 1)
    quadrant = lax.shift_right_logical(turn + quarter // 2, quarter.bit_length() - 1)
    x = (turn - quadrant * quarter).astype(jnp.float32) * (2.0 * math.pi / MODULUS)
    y = x * x
    sine = x * (1.0 + y * (-1.0 / 6 + y * (1.0 / 120 + y * (-1.0 / 5040 + y * (1.0 / 362880)))))
    cosine = 1.0 + y * (-0.5 + y * (1.0 / 24 + y * (-1.0 / 720 + y * (1.0 / 40320))))
    odd = (quadrant & 1) == 1
    first = jnp.where(odd, sine, cosine)
    second = jnp.where(odd, cosine, sine)
    first = jnp.where(((quadrant + 1) & 2) == 2, -first, first)
    second = jnp.where((quadrant & 2) == 2, -second, second)
    return first, second


def halves(value):
    high = value.astype(jnp.bfloat16)
    return high, (value - high.astype(jnp.float32)).astype(jnp.bfloat16)


def table_kernel(
    groups, bins, freq_dev, position_ref, far_ref, place_ref, ordered_ref, lag_ref, shift_ref, wide_ref
):
    rows = far_ref.shape[0] // bins
    wide_ref[...] = far_ref[...].astype(jnp.float32)
    for f in range(bins):
        ordered_ref[f] = wide_ref[pl.ds(f, rows, stride=bins), :].astype(jnp.bfloat16)
    low_rows = lax.broadcasted_iota(jnp.int32, (8, SLOWNESS), 0)
    high_rows = lax.broadcasted_iota(jnp.int32, (BLOCK // 8, SLOWNESS), 0) * 8
    shift_rows = lax.broadcasted_iota(jnp.int32, (2 * groups, SLOWNESS), 0)
    shift_rows = jnp.where(shift_rows < groups, shift_rows, shift_rows - groups - 1) * BLOCK
    own_group = lax.axis_index("chan")
    first_bin = lax.axis_index("freq") * freq_dev + own_group * bins
    sender = lax.broadcasted_iota(jnp.int32, (groups, groups), 1)
    mask = lax.broadcasted_iota(jnp.int32, (groups, groups), 0)
    sends = lax.bitwise_xor(own_group, mask) == sender
    places = jnp.sum(jnp.where(sends, position_ref[...], 0), axis=1, keepdims=True)
    place_ref[...] = jnp.broadcast_to(places, place_ref.shape)

    def one_bin(f, carry):
        def phases(rows):
            slow = lax.broadcasted_iota(jnp.int32, rows.shape, 1) - SLOWNESS // 2
            return unit_phase((first_bin + f) * slow * rows)

        low_cos, low_sin = phases(low_rows)
        high_cos, high_sin = phases(high_rows)
        low_cos, low_sin = low_cos[None], low_sin[None]
        high_cos, high_sin = high_cos[:, None], high_sin[:, None]
        lag_cos = (high_cos * low_cos - high_sin * low_sin).reshape(BLOCK, SLOWNESS)
        lag_sin = (high_sin * low_cos + high_cos * low_sin).reshape(BLOCK, SLOWNESS)
        cos_high, cos_low = halves(lag_cos)
        sin_high, sin_low = halves(lag_sin)
        lag_ref[f, :BLOCK, :SLOWNESS] = cos_high
        lag_ref[f, BLOCK:, :SLOWNESS] = cos_low
        lag_ref[f, :BLOCK, SLOWNESS:] = sin_high
        lag_ref[f, BLOCK:, SLOWNESS:] = sin_low
        shift_cos, shift_sin = phases(shift_rows)
        shift_ref[f, 0] = shift_cos
        shift_ref[f, 1] = shift_sin
        return carry

    lax.fori_loop(0, bins, one_bin, 0)


def partner_order(groups):
    return list(range(groups // 2, groups)) + list(range(groups // 2 - 1, -1, -1))


def chunk_kernel(groups, bins, masks, spec_ref, far_ref, *refs):
    out_refs, wide_ref = refs[:-1], refs[-1]
    wide_ref[...] = spec_ref[...].astype(jnp.float32)
    freq_dev = groups * bins
    rows = spec_ref.shape[0] // freq_dev
    own_group = lax.axis_index("chan")
    for mask, out_ref in zip(masks, out_refs):
        first = lax.bitwise_xor(own_group, mask) * bins
        for f in range(bins):
            value = wide_ref[pl.ds(first + f, rows, stride=freq_dev), :]
            out_ref[f] = value.astype(jnp.bfloat16)


def stack_weights(groups):
    row = lax.broadcasted_iota(jnp.int32, (2 * groups, BLOCK), 0)
    lag = lax.broadcasted_iota(jnp.int32, (2 * groups, BLOCK), 1)
    delta = jnp.where(row < groups, row, row - groups)
    lag = jnp.where(row < groups, lag, lag - BLOCK)
    usable = (lag > -BLOCK) & ((delta >= 1) | (lag >= 1))
    count = SEGMENTS * (groups - delta) * (BLOCK - jnp.abs(lag))
    scale = math.sqrt(SEGMENTS / FREQS)
    return jnp.where(usable, scale / jnp.maximum(count, 1).astype(jnp.float32), 0.0)


def stack_kernel(groups, bins, parts, *refs):
    chunk_refs = refs[:groups]
    place_ref, lag_ref, shift_ref, out_ref, placed_ref, left_ref, part_ref = refs[groups:]
    rows = placed_ref.shape[2]
    windows = rows // 2
    places = place_ref[...]
    for mask, chunk_ref in zip(partner_order(groups), chunk_refs):
        placed_ref[places[mask, 0]] = chunk_ref[...]

    row_index = lax.broadcasted_iota(jnp.int32, (BLOCK, BLOCK), 0)
    lag_index = lax.broadcasted_iota(jnp.int32, (BLOCK, BLOCK), 1)
    mirror = jnp.where(row_index + lag_index == BLOCK - 1, 1.0, 0.0).astype(jnp.bfloat16)
    behind = (lag_index - row_index)[:8]

    for f in range(bins):
        left_ref[f] = lax.dot_general(
            mirror,
            placed_ref[:, f].reshape(groups * rows, BLOCK),
            (((1,), (1,)), ((), ())),
            preferred_element_type=jnp.float32,
        ).astype(jnp.bfloat16)

    for f in range(bins):
        right = []
        for place in range(groups):
            value = placed_ref[place, f]
            real, imag = value[:windows], value[windows:]
            right.append(
                jnp.concatenate(
                    [jnp.concatenate([real, imag], 1), jnp.concatenate([imag, -real], 1)], 0
                )
            )
        right = jnp.concatenate(right, 0)
        for delta in range(groups):
            panel = jnp.dot(
                left_ref[f, :, : rows * (groups - delta)],
                right[rows * delta :],
                preferred_element_type=jnp.float32,
            )
            for half in range(2):
                lanes = slice(half * BLOCK, (half + 1) * BLOCK)
                skewed = pltpu.roll(panel[:, lanes], 1, 1, stride=1, stride_axis=0)
                total = skewed[:8]
                backward = jnp.where(behind > 0, total, 0.0)
                for row in range(8, BLOCK, 8):
                    total = total + skewed[row : row + 8]
                    backward = jnp.where(behind > row, total, backward)
                first = (f * 2 * groups + delta) * 8
                part_ref[half, first : first + 8] = total - backward
                part_ref[half, first + groups * 8 : first + groups * 8 + 8] = backward

    lags = []
    for half in range(2):
        summed = part_ref[half, pl.ds(0, bins * 2 * groups, stride=8), :]
        for sublane in range(1, 8):
            summed = summed + part_ref[half, pl.ds(sublane, bins * 2 * groups, stride=8), :]
        lags.append(summed)
    weight = stack_weights(groups)

    terms = []
    for f in range(bins):
        lag_rows = slice(f * 2 * groups, (f + 1) * 2 * groups)
        means = jnp.concatenate([half[lag_rows] * weight for half in lags], 0)
        mean_high, mean_low = halves(means)
        spread = jnp.concatenate(
            [
                jnp.concatenate([mean_high, mean_high], 1),
                jnp.concatenate([mean_low, jnp.zeros_like(mean_low)], 1),
            ],
            0,
        )
        product = jnp.dot(spread, lag_ref[f], preferred_element_type=jnp.float32)
        product = product[: 4 * groups] + product[4 * groups :]
        by_cos, by_sin = product[:, :SLOWNESS], product[:, SLOWNESS:]
        real = by_cos[: 2 * groups] - by_sin[2 * groups :]
        imag = by_sin[: 2 * groups] + by_cos[2 * groups :]
        shift_cos, shift_sin = shift_ref[f, 0], shift_ref[f, 1]
        turned_re = real * shift_cos - imag * shift_sin
        turned_im = real * shift_sin + imag * shift_cos
        terms.append(turned_re[:groups] + turned_re[groups:])
        terms.append(turned_im[:groups] + turned_im[groups:])

    slow_dev = SLOWNESS // parts
    spans = BLOCK // slow_dev
    span_index = lax.broadcasted_iota(jnp.int32, (groups, BLOCK), 1) // slow_dev
    for part in range(parts):
        source = (part % spans) * slow_dev
        lanes = slice(part // spans * BLOCK, (part // spans + 1) * BLOCK)
        for row in range(out_ref.shape[2]):
            packed = jnp.zeros((groups, BLOCK), jnp.float32)
            for span, term in enumerate(terms[row * spans : (row + 1) * spans]):
                moved = pltpu.roll(term[:, lanes], (span * slow_dev - source) % BLOCK, 1)
                packed = jnp.where(span_index == span, moved, packed)
            out_ref[:, part, row, :] = packed


def image_kernel(slow_dev, spans, term_ref, table_ref, out_ref):
    arrived = term_ref[...]
    turned = arrived.reshape(-1, BLOCK).T
    turned = jnp.concatenate(
        [turned[span * slow_dev : (span + 1) * slow_dev] for span in range(spans)], 1
    )
    high, low = halves(turned)
    by_high = jnp.dot(
        jnp.concatenate([high, low], 0), table_ref[0], preferred_element_type=jnp.float32
    )
    by_low = jnp.dot(high, table_ref[1], preferred_element_type=jnp.float32)
    out_ref[0] = by_high[:slow_dev] + by_high[slow_dev:] + by_low


def time_table(groups, parts, bins, slow_dev, message_rows):
    spans = min(BLOCK // slow_dev, 2 * bins)
    span, group, part, row = np.meshgrid(
        np.arange(spans), np.arange(groups), np.arange(parts), np.arange(message_rows), indexing="ij"
    )
    entry = row * spans + span
    freq = (part * groups + group) * bins + entry // 2
    lag_time = np.arange(LAG_TIMES) - LAG_TIMES // 2
    angle = 2.0 * math.pi / LAG_TIMES * ((freq[..., None] * lag_time) % LAG_TIMES)
    table = np.where((entry % 2 == 0)[..., None], np.cos(angle), -np.sin(angle))
    table = table.reshape(-1, LAG_TIMES).astype(np.float32)
    high = table.astype(jnp.bfloat16)
    low = (table - high.astype(np.float32)).astype(jnp.bfloat16)
    return spans, np.stack([high, low])


def shards(spectra, block_position):
    groups = lax.axis_size("chan")
    parts = lax.axis_size("freq")
    rows = spectra.shape[0] * spectra.shape[1]
    freq_dev = spectra.shape[2]
    bins = freq_dev // groups
    slow_dev = SLOWNESS // parts
    message_rows = -(-2 * bins * slow_dev // BLOCK)
    vmem = pl.BlockSpec(memory_space=pltpu.VMEM)
    params = pltpu.CompilerParams(vmem_limit_bytes=32 * 1024 * 1024)

    order = partner_order(groups)
    far, others = order[0], order[1:]
    group = lax.bitwise_xor(lax.axis_index("chan"), far)
    by_group = spectra.reshape(rows, groups, bins, BLOCK)
    far_chunk = lax.dynamic_index_in_dim(by_group, group, 1, False).reshape(rows * bins, BLOCK)
    other_chunks = pl.pallas_call(
        functools.partial(chunk_kernel, groups, bins, others),
        out_shape=(jax.ShapeDtypeStruct((bins, rows, BLOCK), jnp.bfloat16),) * len(others),
        in_specs=[vmem, pl.BlockSpec(memory_space=pl.ANY)],
        out_specs=(vmem,) * len(others),
        scratch_shapes=[pltpu.VMEM((rows * freq_dev, BLOCK), jnp.float32)],
        compiler_params=params,
        cost_estimate=pl.CostEstimate(flops=10**7, bytes_accessed=4 * 10**6, transcendentals=0),
        name="chunks_of_bins",
    )(spectra.reshape(rows * freq_dev, BLOCK), far_chunk)
    chunks = dict(zip(order, (far_chunk, *other_chunks)))
    for mask in order[:-1]:
        pairs = [(source, source ^ mask) for source in range(groups)]
        chunks[mask] = lax.ppermute(chunks[mask], "chan", pairs)
    places, chunks[far], lag_table, shift_table = pl.pallas_call(
        functools.partial(table_kernel, groups, bins, freq_dev),
        out_shape=(
            jax.ShapeDtypeStruct((groups, BLOCK), jnp.int32),
            jax.ShapeDtypeStruct((bins, rows, BLOCK), jnp.bfloat16),
            jax.ShapeDtypeStruct((bins, 2 * BLOCK, 2 * SLOWNESS), jnp.bfloat16),
            jax.ShapeDtypeStruct((bins, 2, 2 * groups, SLOWNESS), jnp.float32),
        ),
        in_specs=[vmem, vmem],
        out_specs=(vmem,) * 4,
        scratch_shapes=[pltpu.VMEM((rows * bins, BLOCK), jnp.float32)],
        compiler_params=params,
        cost_estimate=pl.CostEstimate(flops=10**7, bytes_accessed=4 * 10**6, transcendentals=0),
        name="slant_tables",
    )(block_position.reshape(1, groups), chunks[far])
    terms = pl.pallas_call(
        functools.partial(stack_kernel, groups, bins, parts),
        out_shape=jax.ShapeDtypeStruct((groups, parts, message_rows, BLOCK), jnp.float32),
        in_specs=[vmem] * (groups + 3),
        out_specs=vmem,
        scratch_shapes=[
            pltpu.VMEM((groups, bins, rows, BLOCK), jnp.bfloat16),
            pltpu.VMEM((bins, BLOCK, groups * rows), jnp.bfloat16),
            pltpu.VMEM((2, bins * 2 * groups * 8, BLOCK), jnp.float32),
        ],
        compiler_params=params,
        name="stack_and_slant",
    )(
        *[chunks[mask] for mask in order],
        places,
        lag_table,
        shift_table,
    )
    terms = terms.reshape(groups * parts, message_rows, BLOCK)
    arrived = lax.all_to_all(terms, ("chan", "freq"), split_axis=0, concat_axis=0, tiled=True)
    spans, table = time_table(groups, parts, bins, slow_dev, message_rows)
    return pl.pallas_call(
        functools.partial(image_kernel, slow_dev, spans),
        out_shape=jax.ShapeDtypeStruct((1, slow_dev, LAG_TIMES), jnp.float32),
        in_specs=[vmem, vmem],
        out_specs=vmem,
        compiler_params=params,
        name="sum_of_bins",
    )(arrived, jnp.asarray(table))


def solution(mesh):
    return jax.shard_map(
        shards,
        mesh=mesh,
        in_specs=(P(None, None, "freq", "chan"), P()),
        out_specs=P("chan", "freq", None),
        check_vma=False,
    )
```

```python
import functools
import math

import jax
import jax.numpy as jnp
import numpy as np
from jax import lax
from jax.experimental import pallas as pl
from jax.experimental.pallas import tpu as pltpu
from jax.sharding import PartitionSpec as P

SEGMENTS = 32
FREQS = 256
BLOCK = 128
SLOWNESS = 256
LAG_TIMES = 512
MODULUS = 8 * FREQS * BLOCK


def unit_phase(numerator):
    quarter = MODULUS // 4
    turn = numerator & (MODULUS - 1)
    quadrant = lax.shift_right_logical(turn + quarter // 2, quarter.bit_length() - 1)
    x = (turn - quadrant * quarter).astype(jnp.float32) * (2.0 * math.pi / MODULUS)
    y = x * x
    sine = x * (1.0 + y * (-1.0 / 6 + y * (1.0 / 120 + y * (-1.0 / 5040 + y * (1.0 / 362880)))))
    cosine = 1.0 + y * (-0.5 + y * (1.0 / 24 + y * (-1.0 / 720 + y * (1.0 / 40320))))
    odd = (quadrant & 1) == 1
    first = jnp.where(odd, sine, cosine)
    second = jnp.where(odd, cosine, sine)
    first = jnp.where(((quadrant + 1) & 2) == 2, -first, first)
    second = jnp.where((quadrant & 2) == 2, -second, second)
    return first, second


def halves(value):
    high = value.astype(jnp.bfloat16)
    return high, (value - high.astype(jnp.float32)).astype(jnp.bfloat16)


def table_kernel(groups, bins, freq_dev, position_ref, place_ref, lag_ref, shift_ref):
    low_rows = lax.broadcasted_iota(jnp.int32, (8, SLOWNESS), 0)
    high_rows = lax.broadcasted_iota(jnp.int32, (BLOCK // 8, SLOWNESS), 0) * 8
    shift_rows = lax.broadcasted_iota(jnp.int32, (2 * groups, SLOWNESS), 0)
    shift_rows = jnp.where(shift_rows < groups, shift_rows, shift_rows - groups - 1) * BLOCK
    own_group = lax.axis_index("chan")
    first_bin = lax.axis_index("freq") * freq_dev + own_group * bins
    sender = lax.broadcasted_iota(jnp.int32, (groups, groups), 1)
    distance = lax.broadcasted_iota(jnp.int32, (groups, groups), 0)
    sends = lax.rem(own_group + groups - distance, groups) == sender
    places = jnp.sum(jnp.where(sends, position_ref[...], 0), axis=1, keepdims=True)
    place_ref[...] = jnp.broadcast_to(places, place_ref.shape)

    def one_bin(f, carry):
        def phases(rows):
            slow = lax.broadcasted_iota(jnp.int32, rows.shape, 1) - SLOWNESS // 2
            return unit_phase((first_bin + f) * slow * rows)

        low_cos, low_sin = phases(low_rows)
        high_cos, high_sin = phases(high_rows)
        low_cos, low_sin = low_cos[None], low_sin[None]
        high_cos, high_sin = high_cos[:, None], high_sin[:, None]
        lag_cos = (high_cos * low_cos - high_sin * low_sin).reshape(BLOCK, SLOWNESS)
        lag_sin = (high_sin * low_cos + high_cos * low_sin).reshape(BLOCK, SLOWNESS)
        cos_high, cos_low = halves(lag_cos)
        sin_high, sin_low = halves(lag_sin)
        lag_ref[f, :BLOCK, :SLOWNESS] = cos_high
        lag_ref[f, BLOCK:, :SLOWNESS] = cos_low
        lag_ref[f, :BLOCK, SLOWNESS:] = sin_high
        lag_ref[f, BLOCK:, SLOWNESS:] = sin_low
        shift_cos, shift_sin = phases(shift_rows)
        shift_ref[f, 0] = shift_cos
        shift_ref[f, 1] = shift_sin
        return carry

    lax.fori_loop(0, bins, one_bin, 0)


def chunk_kernel(groups, bins, spec_ref, *refs):
    out_refs, wide_ref = refs[:-1], refs[-1]
    wide_ref[...] = spec_ref[...].astype(jnp.float32)
    freq_dev = groups * bins
    rows = spec_ref.shape[0] // freq_dev
    own_group = lax.axis_index("chan")
    for distance, out_ref in enumerate(out_refs):
        first = lax.rem(own_group + distance, groups) * bins
        for f in range(bins):
            value = wide_ref[pl.ds(first + f, rows, stride=freq_dev), :]
            out_ref[f] = value.astype(jnp.bfloat16)


def stack_weights(groups):
    row = lax.broadcasted_iota(jnp.int32, (2 * groups, BLOCK), 0)
    lag = lax.broadcasted_iota(jnp.int32, (2 * groups, BLOCK), 1)
    delta = jnp.where(row < groups, row, row - groups)
    lag = jnp.where(row < groups, lag, lag - BLOCK)
    usable = (lag > -BLOCK) & ((delta >= 1) | (lag >= 1))
    count = SEGMENTS * (groups - delta) * (BLOCK - jnp.abs(lag))
    scale = math.sqrt(SEGMENTS / FREQS)
    return jnp.where(usable, scale / jnp.maximum(count, 1).astype(jnp.float32), 0.0)


def stack_kernel(groups, bins, parts, *refs):
    chunk_refs = refs[:groups]
    place_ref, lag_ref, shift_ref, out_ref, placed_ref, left_ref, part_ref = refs[groups:]
    rows = placed_ref.shape[2]
    windows = rows // 2
    places = place_ref[...]
    for distance, chunk_ref in enumerate(chunk_refs):
        placed_ref[places[distance, 0]] = chunk_ref[...]

    row_index = lax.broadcasted_iota(jnp.int32, (BLOCK, BLOCK), 0)
    lag_index = lax.broadcasted_iota(jnp.int32, (BLOCK, BLOCK), 1)
    mirror = jnp.where(row_index + lag_index == BLOCK - 1, 1.0, 0.0).astype(jnp.bfloat16)
    behind = (lag_index - row_index)[:8]

    for f in range(bins):
        left = lax.dot_general(
            mirror,
            placed_ref[:, f].reshape(groups * rows, BLOCK),
            (((1,), (1,)), ((), ())),
            preferred_element_type=jnp.float32,
        )
        for delta in range(groups):
            shifted = left
            if delta:
                ahead = jnp.zeros((BLOCK, rows * delta), jnp.float32)
                shifted = jnp.concatenate([ahead, left[:, : rows * (groups - delta)]], 1)
            left_ref[f, delta * BLOCK : (delta + 1) * BLOCK] = shifted.astype(jnp.bfloat16)

    for f in range(bins):
        right = []
        for place in range(groups):
            value = placed_ref[place, f]
            real, imag = value[:windows], value[windows:]
            right.append(
                jnp.concatenate(
                    [jnp.concatenate([real, imag], 1), jnp.concatenate([imag, -real], 1)], 0
                )
            )
        right = jnp.concatenate(right, 0)
        panels = jnp.dot(left_ref[f], right, preferred_element_type=jnp.float32)
        for delta in range(groups):
            panel = panels[delta * BLOCK : (delta + 1) * BLOCK]
            for half in range(2):
                lanes = slice(half * BLOCK, (half + 1) * BLOCK)
                skewed = pltpu.roll(panel[:, lanes], 1, 1, stride=1, stride_axis=0)
                total = skewed[:8]
                backward = jnp.where(behind > 0, total, 0.0)
                for row in range(8, BLOCK, 8):
                    total = total + skewed[row : row + 8]
                    backward = jnp.where(behind > row, total, backward)
                first = (f * 2 * groups + delta) * 8
                part_ref[half, first : first + 8] = total - backward
                part_ref[half, first + groups * 8 : first + groups * 8 + 8] = backward

    lags = []
    for half in range(2):
        summed = part_ref[half, pl.ds(0, bins * 2 * groups, stride=8), :]
        for sublane in range(1, 8):
            summed = summed + part_ref[half, pl.ds(sublane, bins * 2 * groups, stride=8), :]
        lags.append(summed)
    weight = stack_weights(groups)

    terms = []
    for f in range(bins):
        lag_rows = slice(f * 2 * groups, (f + 1) * 2 * groups)
        means = jnp.concatenate([half[lag_rows] * weight for half in lags], 0)
        mean_high, mean_low = halves(means)
        spread = jnp.concatenate(
            [
                jnp.concatenate([mean_high, mean_high], 1),
                jnp.concatenate([mean_low, jnp.zeros_like(mean_low)], 1),
            ],
            0,
        )
        product = jnp.dot(spread, lag_ref[f], preferred_element_type=jnp.float32)
        product = product[: 4 * groups] + product[4 * groups :]
        by_cos, by_sin = product[:, :SLOWNESS], product[:, SLOWNESS:]
        real = by_cos[: 2 * groups] - by_sin[2 * groups :]
        imag = by_sin[: 2 * groups] + by_cos[2 * groups :]
        shift_cos, shift_sin = shift_ref[f, 0], shift_ref[f, 1]
        turned_re = real * shift_cos - imag * shift_sin
        turned_im = real * shift_sin + imag * shift_cos
        terms.append(turned_re[:groups] + turned_re[groups:])
        terms.append(turned_im[:groups] + turned_im[groups:])

    slow_dev = SLOWNESS // parts
    spans = BLOCK // slow_dev
    span_index = lax.broadcasted_iota(jnp.int32, (groups, BLOCK), 1) // slow_dev
    for part in range(parts):
        source = (part % spans) * slow_dev
        lanes = slice(part // spans * BLOCK, (part // spans + 1) * BLOCK)
        for row in range(out_ref.shape[2]):
            packed = jnp.zeros((groups, BLOCK), jnp.float32)
            for span, term in enumerate(terms[row * spans : (row + 1) * spans]):
                moved = pltpu.roll(term[:, lanes], (span * slow_dev - source) % BLOCK, 1)
                packed = jnp.where(span_index == span, moved, packed)
            out_ref[:, part, row, :] = packed


def image_kernel(slow_dev, spans, term_ref, table_ref, out_ref):
    arrived = term_ref[...]
    turned = arrived.reshape(-1, BLOCK).T
    turned = jnp.concatenate(
        [turned[span * slow_dev : (span + 1) * slow_dev] for span in range(spans)], 1
    )
    high, low = halves(turned)
    by_high = jnp.dot(
        jnp.concatenate([high, low], 0), table_ref[0], preferred_element_type=jnp.float32
    )
    by_low = jnp.dot(high, table_ref[1], preferred_element_type=jnp.float32)
    out_ref[0] = by_high[:slow_dev] + by_high[slow_dev:] + by_low


def time_table(groups, parts, bins, slow_dev, message_rows):
    spans = min(BLOCK // slow_dev, 2 * bins)
    span, group, part, row = np.meshgrid(
        np.arange(spans), np.arange(groups), np.arange(parts), np.arange(message_rows), indexing="ij"
    )
    entry = row * spans + span
    freq = (part * groups + group) * bins + entry // 2
    lag_time = np.arange(LAG_TIMES) - LAG_TIMES // 2
    angle = 2.0 * math.pi / LAG_TIMES * ((freq[..., None] * lag_time) % LAG_TIMES)
    table = np.where((entry % 2 == 0)[..., None], np.cos(angle), -np.sin(angle))
    table = table.reshape(-1, LAG_TIMES).astype(np.float32)
    high = table.astype(jnp.bfloat16)
    low = (table - high.astype(np.float32)).astype(jnp.bfloat16)
    return spans, np.stack([high, low])


def shards(spectra, block_position):
    groups = lax.axis_size("chan")
    parts = lax.axis_size("freq")
    rows = spectra.shape[0] * spectra.shape[1]
    freq_dev = spectra.shape[2]
    bins = freq_dev // groups
    slow_dev = SLOWNESS // parts
    message_rows = -(-2 * bins * slow_dev // BLOCK)
    vmem = pl.BlockSpec(memory_space=pltpu.VMEM)
    params = pltpu.CompilerParams(vmem_limit_bytes=32 * 1024 * 1024)

    chunk = jax.ShapeDtypeStruct((bins, rows, BLOCK), jnp.bfloat16)
    chunks = pl.pallas_call(
        functools.partial(chunk_kernel, groups, bins),
        out_shape=(chunk,) * groups,
        in_specs=[vmem],
        out_specs=(vmem,) * groups,
        scratch_shapes=[pltpu.VMEM((rows * freq_dev, BLOCK), jnp.float32)],
        compiler_params=params,
        name="chunks_of_bins",
    )(spectra.reshape(rows * freq_dev, BLOCK))
    arrived_chunks = list(chunks)
    for distance in sorted(range(1, groups), key=lambda steps: abs(2 * steps - groups)):
        pairs = [(source, (source + distance) % groups) for source in range(groups)]
        arrived_chunks[distance] = lax.ppermute(chunks[distance], "chan", pairs)
    places, lag_table, shift_table = pl.pallas_call(
        functools.partial(table_kernel, groups, bins, freq_dev),
        out_shape=(
            jax.ShapeDtypeStruct((groups, BLOCK), jnp.int32),
            jax.ShapeDtypeStruct((bins, 2 * BLOCK, 2 * SLOWNESS), jnp.bfloat16),
            jax.ShapeDtypeStruct((bins, 2, 2 * groups, SLOWNESS), jnp.float32),
        ),
        in_specs=[vmem],
        out_specs=(vmem, vmem, vmem),
        compiler_params=params,
        cost_estimate=pl.CostEstimate(flops=10**7, bytes_accessed=4 * 10**6, transcendentals=0),
        name="slant_tables",
    )(block_position.reshape(1, groups))
    terms = pl.pallas_call(
        functools.partial(stack_kernel, groups, bins, parts),
        out_shape=jax.ShapeDtypeStruct((groups, parts, message_rows, BLOCK), jnp.float32),
        in_specs=[vmem] * (groups + 3),
        out_specs=vmem,
        scratch_shapes=[
            pltpu.VMEM((groups, bins, rows, BLOCK), jnp.bfloat16),
            pltpu.VMEM((bins, groups * BLOCK, groups * rows), jnp.bfloat16),
            pltpu.VMEM((2, bins * 2 * groups * 8, BLOCK), jnp.float32),
        ],
        compiler_params=params,
        name="stack_and_slant",
    )(
        *arrived_chunks,
        places,
        lag_table,
        shift_table,
    )
    terms = terms.reshape(groups * parts, message_rows, BLOCK)
    arrived = lax.all_to_all(terms, ("chan", "freq"), split_axis=0, concat_axis=0, tiled=True)
    spans, table = time_table(groups, parts, bins, slow_dev, message_rows)
    return pl.pallas_call(
        functools.partial(image_kernel, slow_dev, spans),
        out_shape=jax.ShapeDtypeStruct((1, slow_dev, LAG_TIMES), jnp.float32),
        in_specs=[vmem, vmem],
        out_specs=vmem,
        compiler_params=params,
        name="sum_of_bins",
    )(arrived, jnp.asarray(table))


def solution(mesh):
    return jax.shard_map(
        shards,
        mesh=mesh,
        in_specs=(P(None, None, "freq", "chan"), P()),
        out_specs=P("chan", "freq", None),
        check_vma=False,
    )
```

```python
import functools
import math

import jax
import jax.numpy as jnp
import numpy as np
from jax import lax
from jax.experimental import pallas as pl
from jax.experimental.pallas import tpu as pltpu
from jax.sharding import PartitionSpec as P

SEGMENTS = 32
FREQS = 256
BLOCK = 128
SLOWNESS = 256
LAG_TIMES = 512
MODULUS = 8 * FREQS * BLOCK


def unit_phase(numerator):
    quarter = MODULUS // 4
    turn = numerator & (MODULUS - 1)
    quadrant = lax.shift_right_logical(turn + quarter // 2, quarter.bit_length() - 1)
    x = (turn - quadrant * quarter).astype(jnp.float32) * (2.0 * math.pi / MODULUS)
    y = x * x
    sine = x * (1.0 + y * (-1.0 / 6 + y * (1.0 / 120 + y * (-1.0 / 5040 + y * (1.0 / 362880)))))
    cosine = 1.0 + y * (-0.5 + y * (1.0 / 24 + y * (-1.0 / 720 + y * (1.0 / 40320))))
    odd = (quadrant & 1) == 1
    first = jnp.where(odd, sine, cosine)
    second = jnp.where(odd, cosine, sine)
    first = jnp.where(((quadrant + 1) & 2) == 2, -first, first)
    second = jnp.where((quadrant & 2) == 2, -second, second)
    return first, second


def halves(value):
    high = value.astype(jnp.bfloat16)
    return high, (value - high.astype(jnp.float32)).astype(jnp.bfloat16)


def table_kernel(groups, bins, freq_dev, position_ref, place_ref, lag_ref, shift_ref):
    low_rows = lax.broadcasted_iota(jnp.int32, (8, SLOWNESS), 0)
    high_rows = lax.broadcasted_iota(jnp.int32, (BLOCK // 8, SLOWNESS), 0) * 8
    shift_rows = lax.broadcasted_iota(jnp.int32, (2 * groups, SLOWNESS), 0)
    shift_rows = jnp.where(shift_rows < groups, shift_rows, shift_rows - groups - 1) * BLOCK
    own_group = lax.axis_index("chan")
    first_bin = lax.axis_index("freq") * freq_dev + own_group * bins
    sender = lax.broadcasted_iota(jnp.int32, (groups, groups), 1)
    distance = lax.broadcasted_iota(jnp.int32, (groups, groups), 0)
    sends = lax.rem(own_group + groups - distance, groups) == sender
    places = jnp.sum(jnp.where(sends, position_ref[...], 0), axis=1, keepdims=True)
    place_ref[...] = jnp.broadcast_to(places, place_ref.shape)

    def one_bin(f, carry):
        def phases(rows):
            slow = lax.broadcasted_iota(jnp.int32, rows.shape, 1) - SLOWNESS // 2
            return unit_phase((first_bin + f) * slow * rows)

        low_cos, low_sin = phases(low_rows)
        high_cos, high_sin = phases(high_rows)
        low_cos, low_sin = low_cos[None], low_sin[None]
        high_cos, high_sin = high_cos[:, None], high_sin[:, None]
        lag_cos = (high_cos * low_cos - high_sin * low_sin).reshape(BLOCK, SLOWNESS)
        lag_sin = (high_sin * low_cos + high_cos * low_sin).reshape(BLOCK, SLOWNESS)
        cos_high, cos_low = halves(lag_cos)
        sin_high, sin_low = halves(lag_sin)
        lag_ref[f, :BLOCK, :SLOWNESS] = cos_high
        lag_ref[f, BLOCK:, :SLOWNESS] = cos_low
        lag_ref[f, :BLOCK, SLOWNESS:] = sin_high
        lag_ref[f, BLOCK:, SLOWNESS:] = sin_low
        shift_cos, shift_sin = phases(shift_rows)
        shift_ref[f, 0] = shift_cos
        shift_ref[f, 1] = shift_sin
        return carry

    lax.fori_loop(0, bins, one_bin, 0)


def chunk_kernel(groups, bins, spec_ref, *refs):
    out_refs, wide_ref = refs[:-1], refs[-1]
    wide_ref[...] = spec_ref[...].astype(jnp.float32)
    freq_dev = groups * bins
    rows = spec_ref.shape[0] // freq_dev
    own_group = lax.axis_index("chan")
    for distance, out_ref in enumerate(out_refs):
        first = lax.rem(own_group + distance, groups) * bins

        def one_bin(f, carry, first=first, out_ref=out_ref):
            value = wide_ref[pl.ds(first + f, rows, stride=freq_dev), :]
            out_ref[f] = value.astype(jnp.bfloat16)
            return carry

        lax.fori_loop(0, bins, one_bin, 0, unroll=min(bins, 2))


def stack_weights(groups):
    row = lax.broadcasted_iota(jnp.int32, (2 * groups, BLOCK), 0)
    lag = lax.broadcasted_iota(jnp.int32, (2 * groups, BLOCK), 1)
    delta = jnp.where(row < groups, row, row - groups)
    lag = jnp.where(row < groups, lag, lag - BLOCK)
    usable = (lag > -BLOCK) & ((delta >= 1) | (lag >= 1))
    count = SEGMENTS * (groups - delta) * (BLOCK - jnp.abs(lag))
    scale = math.sqrt(SEGMENTS / FREQS)
    return jnp.where(usable, scale / jnp.maximum(count, 1).astype(jnp.float32), 0.0)


def stack_kernel(groups, bins, parts, *refs):
    chunk_refs = refs[:groups]
    place_ref, lag_ref, shift_ref, out_ref, placed_ref, part_ref = refs[groups:]
    rows = placed_ref.shape[2]
    windows = rows // 2
    places = place_ref[...]
    for distance, chunk_ref in enumerate(chunk_refs):
        placed_ref[places[distance, 0]] = chunk_ref[...]

    row_index = lax.broadcasted_iota(jnp.int32, (BLOCK, BLOCK), 0)
    lag_index = lax.broadcasted_iota(jnp.int32, (BLOCK, BLOCK), 1)
    mirror = jnp.where(row_index + lag_index == BLOCK - 1, 1.0, 0.0).astype(jnp.bfloat16)
    behind = (lag_index - row_index)[:8]

    def one_bin(f, carry):
        left = lax.dot_general(
            mirror,
            placed_ref[:, f].reshape(groups * rows, BLOCK),
            (((1,), (1,)), ((), ())),
            preferred_element_type=jnp.float32,
        ).astype(jnp.bfloat16)
        right = []
        for place in range(groups):
            value = placed_ref[place, f]
            real, imag = value[:windows], value[windows:]
            right.append(
                jnp.concatenate(
                    [jnp.concatenate([real, imag], 1), jnp.concatenate([imag, -real], 1)], 0
                )
            )
        right = jnp.concatenate(right, 0)
        for delta in range(groups):
            panel = jnp.dot(
                left[:, : rows * (groups - delta)],
                right[rows * delta :],
                preferred_element_type=jnp.float32,
            )
            for half in range(2):
                lanes = slice(half * BLOCK, (half + 1) * BLOCK)
                skewed = pltpu.roll(panel[:, lanes], 1, 1, stride=1, stride_axis=0)
                total = skewed[:8]
                backward = jnp.where(behind > 0, total, 0.0)
                for row in range(8, BLOCK, 8):
                    total = total + skewed[row : row + 8]
                    backward = jnp.where(behind > row, total, backward)
                first = (f * 2 * groups + delta) * 8
                part_ref[half, pl.ds(pl.multiple_of(first, 8), 8)] = total - backward
                first = first + groups * 8
                part_ref[half, pl.ds(pl.multiple_of(first, 8), 8)] = backward
        return carry

    lax.fori_loop(0, bins, one_bin, 0, unroll=min(bins, 2))

    lags = []
    for half in range(2):
        summed = part_ref[half, pl.ds(0, bins * 2 * groups, stride=8), :]
        for sublane in range(1, 8):
            summed = summed + part_ref[half, pl.ds(sublane, bins * 2 * groups, stride=8), :]
        lags.append(summed)
    weight = stack_weights(groups)

    terms = []
    for f in range(bins):
        lag_rows = slice(f * 2 * groups, (f + 1) * 2 * groups)
        means = jnp.concatenate([half[lag_rows] * weight for half in lags], 0)
        mean_high, mean_low = halves(means)
        spread = jnp.concatenate(
            [
                jnp.concatenate([mean_high, mean_high], 1),
                jnp.concatenate([mean_low, jnp.zeros_like(mean_low)], 1),
            ],
            0,
        )
        product = jnp.dot(spread, lag_ref[f], preferred_element_type=jnp.float32)
        product = product[: 4 * groups] + product[4 * groups :]
        by_cos, by_sin = product[:, :SLOWNESS], product[:, SLOWNESS:]
        real = by_cos[: 2 * groups] - by_sin[2 * groups :]
        imag = by_sin[: 2 * groups] + by_cos[2 * groups :]
        shift_cos, shift_sin = shift_ref[f, 0], shift_ref[f, 1]
        turned_re = real * shift_cos - imag * shift_sin
        turned_im = real * shift_sin + imag * shift_cos
        terms.append(turned_re[:groups] + turned_re[groups:])
        terms.append(turned_im[:groups] + turned_im[groups:])

    slow_dev = SLOWNESS // parts
    spans = BLOCK // slow_dev
    span_index = lax.broadcasted_iota(jnp.int32, (groups, BLOCK), 1) // slow_dev
    for part in range(parts):
        source = (part % spans) * slow_dev
        lanes = slice(part // spans * BLOCK, (part // spans + 1) * BLOCK)
        for row in range(out_ref.shape[2]):
            packed = jnp.zeros((groups, BLOCK), jnp.float32)
            for span, term in enumerate(terms[row * spans : (row + 1) * spans]):
                moved = pltpu.roll(term[:, lanes], (span * slow_dev - source) % BLOCK, 1)
                packed = jnp.where(span_index == span, moved, packed)
            out_ref[:, part, row, :] = packed


def image_kernel(slow_dev, spans, term_ref, table_ref, out_ref):
    arrived = term_ref[...]
    turned = arrived.reshape(-1, BLOCK).T
    turned = jnp.concatenate(
        [turned[span * slow_dev : (span + 1) * slow_dev] for span in range(spans)], 1
    )
    high, low = halves(turned)
    by_high = jnp.dot(
        jnp.concatenate([high, low], 0), table_ref[0], preferred_element_type=jnp.float32
    )
    by_low = jnp.dot(high, table_ref[1], preferred_element_type=jnp.float32)
    out_ref[0] = by_high[:slow_dev] + by_high[slow_dev:] + by_low


def time_table(groups, parts, bins, slow_dev, message_rows):
    spans = min(BLOCK // slow_dev, 2 * bins)
    span, group, part, row = np.meshgrid(
        np.arange(spans), np.arange(groups), np.arange(parts), np.arange(message_rows), indexing="ij"
    )
    entry = row * spans + span
    freq = (part * groups + group) * bins + entry // 2
    lag_time = np.arange(LAG_TIMES) - LAG_TIMES // 2
    angle = 2.0 * math.pi / LAG_TIMES * ((freq[..., None] * lag_time) % LAG_TIMES)
    table = np.where((entry % 2 == 0)[..., None], np.cos(angle), -np.sin(angle))
    table = table.reshape(-1, LAG_TIMES).astype(np.float32)
    high = table.astype(jnp.bfloat16)
    low = (table - high.astype(np.float32)).astype(jnp.bfloat16)
    return spans, np.stack([high, low])


def shards(spectra, block_position):
    groups = lax.axis_size("chan")
    parts = lax.axis_size("freq")
    rows = spectra.shape[0] * spectra.shape[1]
    freq_dev = spectra.shape[2]
    bins = freq_dev // groups
    slow_dev = SLOWNESS // parts
    message_rows = -(-2 * bins * slow_dev // BLOCK)
    vmem = pl.BlockSpec(memory_space=pltpu.VMEM)
    params = pltpu.CompilerParams(vmem_limit_bytes=32 * 1024 * 1024)

    chunk = jax.ShapeDtypeStruct((bins, rows, BLOCK), jnp.bfloat16)
    chunks = pl.pallas_call(
        functools.partial(chunk_kernel, groups, bins),
        out_shape=(chunk,) * groups,
        in_specs=[vmem],
        out_specs=(vmem,) * groups,
        scratch_shapes=[pltpu.VMEM((rows * freq_dev, BLOCK), jnp.float32)],
        compiler_params=params,
        name="chunks_of_bins",
    )(spectra.reshape(rows * freq_dev, BLOCK))
    arrived_chunks = list(chunks)
    for distance in sorted(range(1, groups), key=lambda steps: abs(2 * steps - groups)):
        pairs = [(source, (source + distance) % groups) for source in range(groups)]
        arrived_chunks[distance] = lax.ppermute(chunks[distance], "chan", pairs)
    places, lag_table, shift_table = pl.pallas_call(
        functools.partial(table_kernel, groups, bins, freq_dev),
        out_shape=(
            jax.ShapeDtypeStruct((groups, BLOCK), jnp.int32),
            jax.ShapeDtypeStruct((bins, 2 * BLOCK, 2 * SLOWNESS), jnp.bfloat16),
            jax.ShapeDtypeStruct((bins, 2, 2 * groups, SLOWNESS), jnp.float32),
        ),
        in_specs=[vmem],
        out_specs=(vmem, vmem, vmem),
        compiler_params=params,
        cost_estimate=pl.CostEstimate(flops=10**7, bytes_accessed=4 * 10**6, transcendentals=0),
        name="slant_tables",
    )(block_position.reshape(1, groups))
    terms = pl.pallas_call(
        functools.partial(stack_kernel, groups, bins, parts),
        out_shape=jax.ShapeDtypeStruct((groups, parts, message_rows, BLOCK), jnp.float32),
        in_specs=[vmem] * (groups + 3),
        out_specs=vmem,
        scratch_shapes=[
            pltpu.VMEM((groups, bins, rows, BLOCK), jnp.bfloat16),
            pltpu.VMEM((2, bins * 2 * groups * 8, BLOCK), jnp.float32),
        ],
        compiler_params=params,
        name="stack_and_slant",
    )(
        *arrived_chunks,
        places,
        lag_table,
        shift_table,
    )
    terms = terms.reshape(groups * parts, message_rows, BLOCK)
    arrived = lax.all_to_all(terms, ("chan", "freq"), split_axis=0, concat_axis=0, tiled=True)
    spans, table = time_table(groups, parts, bins, slow_dev, message_rows)
    return pl.pallas_call(
        functools.partial(image_kernel, slow_dev, spans),
        out_shape=jax.ShapeDtypeStruct((1, slow_dev, LAG_TIMES), jnp.float32),
        in_specs=[vmem, vmem],
        out_specs=vmem,
        compiler_params=params,
        name="sum_of_bins",
    )(arrived, jnp.asarray(table))


def solution(mesh):
    return jax.shard_map(
        shards,
        mesh=mesh,
        in_specs=(P(None, None, "freq", "chan"), P()),
        out_specs=P("chan", "freq", None),
        check_vma=False,
    )
```

```python
import functools
import math

import jax
import jax.numpy as jnp
import numpy as np
from jax import lax
from jax.experimental import pallas as pl
from jax.experimental.pallas import tpu as pltpu
from jax.sharding import PartitionSpec as P

SEGMENTS = 32
FREQS = 256
BLOCK = 128
SLOWNESS = 256
LAG_TIMES = 512
MODULUS = 8 * FREQS * BLOCK


def unit_phase(numerator):
    quarter = MODULUS // 4
    turn = numerator & (MODULUS - 1)
    quadrant = lax.shift_right_logical(turn + quarter // 2, quarter.bit_length() - 1)
    x = (turn - quadrant * quarter).astype(jnp.float32) * (2.0 * math.pi / MODULUS)
    y = x * x
    sine = x * (1.0 + y * (-1.0 / 6 + y * (1.0 / 120 + y * (-1.0 / 5040 + y * (1.0 / 362880)))))
    cosine = 1.0 + y * (-0.5 + y * (1.0 / 24 + y * (-1.0 / 720 + y * (1.0 / 40320))))
    odd = (quadrant & 1) == 1
    first = jnp.where(odd, sine, cosine)
    second = jnp.where(odd, cosine, sine)
    first = jnp.where(((quadrant + 1) & 2) == 2, -first, first)
    second = jnp.where((quadrant & 2) == 2, -second, second)
    return first, second


def halves(value):
    high = value.astype(jnp.bfloat16)
    return high, (value - high.astype(jnp.float32)).astype(jnp.bfloat16)


def table_kernel(groups, bins, freq_dev, position_ref, place_ref, lag_ref, shift_ref):
    low_rows = lax.broadcasted_iota(jnp.int32, (8, SLOWNESS), 0)
    high_rows = lax.broadcasted_iota(jnp.int32, (BLOCK // 8, SLOWNESS), 0) * 8
    shift_rows = lax.broadcasted_iota(jnp.int32, (2 * groups, SLOWNESS), 0)
    shift_rows = jnp.where(shift_rows < groups, shift_rows, shift_rows - groups - 1) * BLOCK
    own_group = lax.axis_index("chan")
    first_bin = lax.axis_index("freq") * freq_dev + own_group * bins
    sender = lax.broadcasted_iota(jnp.int32, (groups, groups), 1)
    distance = lax.broadcasted_iota(jnp.int32, (groups, groups), 0)
    sends = lax.rem(own_group + groups - distance, groups) == sender
    places = jnp.sum(jnp.where(sends, position_ref[...], 0), axis=1, keepdims=True)
    place_ref[...] = jnp.broadcast_to(places, place_ref.shape)

    def one_bin(f, carry):
        def phases(rows):
            slow = lax.broadcasted_iota(jnp.int32, rows.shape, 1) - SLOWNESS // 2
            return unit_phase((first_bin + f) * slow * rows)

        low_cos, low_sin = phases(low_rows)
        high_cos, high_sin = phases(high_rows)
        low_cos, low_sin = low_cos[None], low_sin[None]
        high_cos, high_sin = high_cos[:, None], high_sin[:, None]
        lag_cos = (high_cos * low_cos - high_sin * low_sin).reshape(BLOCK, SLOWNESS)
        lag_sin = (high_sin * low_cos + high_cos * low_sin).reshape(BLOCK, SLOWNESS)
        cos_high, cos_low = halves(lag_cos)
        sin_high, sin_low = halves(lag_sin)
        lag_ref[f, :BLOCK, :SLOWNESS] = cos_high
        lag_ref[f, BLOCK:, :SLOWNESS] = cos_low
        lag_ref[f, :BLOCK, SLOWNESS:] = sin_high
        lag_ref[f, BLOCK:, SLOWNESS:] = sin_low
        shift_cos, shift_sin = phases(shift_rows)
        shift_ref[f, 0] = shift_cos
        shift_ref[f, 1] = shift_sin
        return carry

    lax.fori_loop(0, bins, one_bin, 0)


def chunk_kernel(groups, bins, spec_ref, *refs):
    out_refs, wide_ref = refs[:-1], refs[-1]
    wide_ref[...] = spec_ref[...].astype(jnp.float32)
    freq_dev = groups * bins
    rows = spec_ref.shape[0] // freq_dev
    own_group = lax.axis_index("chan")
    for distance, out_ref in enumerate(out_refs):
        first = lax.rem(own_group + distance, groups) * bins
        for f in range(bins):
            value = wide_ref[pl.ds(first + f, rows, stride=freq_dev), :]
            out_ref[f] = value.astype(jnp.bfloat16)


def stack_weights(groups):
    row = lax.broadcasted_iota(jnp.int32, (2 * groups, BLOCK), 0)
    lag = lax.broadcasted_iota(jnp.int32, (2 * groups, BLOCK), 1)
    delta = jnp.where(row < groups, row, row - groups)
    lag = jnp.where(row < groups, lag, lag - BLOCK)
    usable = (lag > -BLOCK) & ((delta >= 1) | (lag >= 1))
    count = SEGMENTS * (groups - delta) * (BLOCK - jnp.abs(lag))
    scale = math.sqrt(SEGMENTS / FREQS)
    return jnp.where(usable, scale / jnp.maximum(count, 1).astype(jnp.float32), 0.0)


def stack_kernel(groups, bins, parts, *refs):
    chunk_refs = refs[:groups]
    place_ref, lag_ref, shift_ref, out_ref, placed_ref, left_ref, part_ref = refs[groups:]
    rows = placed_ref.shape[2]
    windows = rows // 2
    places = place_ref[...]
    for distance, chunk_ref in enumerate(chunk_refs):
        placed_ref[places[distance, 0]] = chunk_ref[...]

    row_index = lax.broadcasted_iota(jnp.int32, (BLOCK, BLOCK), 0)
    lag_index = lax.broadcasted_iota(jnp.int32, (BLOCK, BLOCK), 1)
    mirror = jnp.where(row_index + lag_index == BLOCK - 1, 1.0, 0.0).astype(jnp.bfloat16)
    ahead = lag_index <= row_index

    for f in range(bins):
        left_ref[f] = lax.dot_general(
            mirror,
            placed_ref[:, f].reshape(groups * rows, BLOCK),
            (((1,), (1,)), ((), ())),
            preferred_element_type=jnp.float32,
        ).astype(jnp.bfloat16)

    for f in range(bins):
        right = []
        for place in range(groups):
            value = placed_ref[place, f]
            real, imag = value[:windows], value[windows:]
            right.append(
                jnp.concatenate(
                    [jnp.concatenate([real, imag], 1), jnp.concatenate([imag, -real], 1)], 0
                )
            )
        right = jnp.concatenate(right, 0)
        for delta in range(groups):
            panel = jnp.dot(
                left_ref[f, :, : rows * (groups - delta)],
                right[rows * delta :],
                preferred_element_type=jnp.float32,
            )
            for half in range(2):
                lanes = slice(half * BLOCK, (half + 1) * BLOCK)
                skewed = pltpu.roll(panel[:, lanes], 1, 1, stride=1, stride_axis=0)
                forward = jnp.where(ahead, skewed, 0.0).reshape(-1, 8, BLOCK).sum(0)
                backward = jnp.where(ahead, 0.0, skewed).reshape(-1, 8, BLOCK).sum(0)
                first = (f * 2 * groups + delta) * 8
                part_ref[half, first : first + 8] = forward
                part_ref[half, first + groups * 8 : first + groups * 8 + 8] = backward

    lags = []
    for half in range(2):
        summed = part_ref[half, pl.ds(0, bins * 2 * groups, stride=8), :]
        for sublane in range(1, 8):
            summed = summed + part_ref[half, pl.ds(sublane, bins * 2 * groups, stride=8), :]
        lags.append(summed)
    weight = stack_weights(groups)

    terms = []
    for f in range(bins):
        lag_rows = slice(f * 2 * groups, (f + 1) * 2 * groups)
        means = jnp.concatenate([half[lag_rows] * weight for half in lags], 0)
        mean_high, mean_low = halves(means)
        spread = jnp.concatenate(
            [
                jnp.concatenate([mean_high, mean_high], 1),
                jnp.concatenate([mean_low, jnp.zeros_like(mean_low)], 1),
            ],
            0,
        )
        product = jnp.dot(spread, lag_ref[f], preferred_element_type=jnp.float32)
        product = product[: 4 * groups] + product[4 * groups :]
        by_cos, by_sin = product[:, :SLOWNESS], product[:, SLOWNESS:]
        real = by_cos[: 2 * groups] - by_sin[2 * groups :]
        imag = by_sin[: 2 * groups] + by_cos[2 * groups :]
        shift_cos, shift_sin = shift_ref[f, 0], shift_ref[f, 1]
        turned_re = real * shift_cos - imag * shift_sin
        turned_im = real * shift_sin + imag * shift_cos
        terms.append(turned_re[:groups] + turned_re[groups:])
        terms.append(turned_im[:groups] + turned_im[groups:])

    slow_dev = SLOWNESS // parts
    spans = BLOCK // slow_dev
    span_index = lax.broadcasted_iota(jnp.int32, (groups, BLOCK), 1) // slow_dev
    for part in range(parts):
        source = (part % spans) * slow_dev
        lanes = slice(part // spans * BLOCK, (part // spans + 1) * BLOCK)
        for row in range(out_ref.shape[2]):
            packed = jnp.zeros((groups, BLOCK), jnp.float32)
            for span, term in enumerate(terms[row * spans : (row + 1) * spans]):
                moved = pltpu.roll(term[:, lanes], (span * slow_dev - source) % BLOCK, 1)
                packed = jnp.where(span_index == span, moved, packed)
            out_ref[:, part, row, :] = packed


def split_kernel(table_ref, term_ref, out_ref):
    out_ref[0], out_ref[1] = halves(table_ref[...])


def image_kernel(slow_dev, spans, term_ref, table_ref, out_ref):
    arrived = term_ref[...]
    turned = arrived.reshape(-1, BLOCK).T
    turned = jnp.concatenate(
        [turned[span * slow_dev : (span + 1) * slow_dev] for span in range(spans)], 1
    )
    high, low = halves(turned)
    by_high = jnp.dot(
        jnp.concatenate([high, low], 0), table_ref[0], preferred_element_type=jnp.float32
    )
    by_low = jnp.dot(high, table_ref[1], preferred_element_type=jnp.float32)
    out_ref[0] = by_high[:slow_dev] + by_high[slow_dev:] + by_low


def time_table(groups, parts, bins, slow_dev, message_rows):
    spans = min(BLOCK // slow_dev, 2 * bins)
    span, group, part, row = np.meshgrid(
        np.arange(spans), np.arange(groups), np.arange(parts), np.arange(message_rows), indexing="ij"
    )
    entry = row * spans + span
    freq = (part * groups + group) * bins + entry // 2
    lag_time = np.arange(LAG_TIMES) - LAG_TIMES // 2
    angle = 2.0 * math.pi / LAG_TIMES * ((freq[..., None] * lag_time) % LAG_TIMES)
    table = np.where((entry % 2 == 0)[..., None], np.cos(angle), -np.sin(angle))
    return spans, table.reshape(-1, LAG_TIMES).astype(np.float32)


def shards(spectra, block_position):
    groups = lax.axis_size("chan")
    parts = lax.axis_size("freq")
    rows = spectra.shape[0] * spectra.shape[1]
    freq_dev = spectra.shape[2]
    bins = freq_dev // groups
    slow_dev = SLOWNESS // parts
    message_rows = -(-2 * bins * slow_dev // BLOCK)
    vmem = pl.BlockSpec(memory_space=pltpu.VMEM)
    params = pltpu.CompilerParams(vmem_limit_bytes=32 * 1024 * 1024)

    chunk = jax.ShapeDtypeStruct((bins, rows, BLOCK), jnp.bfloat16)
    chunks = pl.pallas_call(
        functools.partial(chunk_kernel, groups, bins),
        out_shape=(chunk,) * groups,
        in_specs=[vmem],
        out_specs=(vmem,) * groups,
        scratch_shapes=[pltpu.VMEM((rows * freq_dev, BLOCK), jnp.float32)],
        compiler_params=params,
        name="chunks_of_bins",
    )(spectra.reshape(rows * freq_dev, BLOCK))
    arrived_chunks = list(chunks)
    for distance in sorted(range(1, groups), key=lambda steps: abs(2 * steps - groups)):
        pairs = [(source, (source + distance) % groups) for source in range(groups)]
        arrived_chunks[distance] = lax.ppermute(chunks[distance], "chan", pairs)
    places, lag_table, shift_table = pl.pallas_call(
        functools.partial(table_kernel, groups, bins, freq_dev),
        out_shape=(
            jax.ShapeDtypeStruct((groups, BLOCK), jnp.int32),
            jax.ShapeDtypeStruct((bins, 2 * BLOCK, 2 * SLOWNESS), jnp.bfloat16),
            jax.ShapeDtypeStruct((bins, 2, 2 * groups, SLOWNESS), jnp.float32),
        ),
        in_specs=[vmem],
        out_specs=(vmem, vmem, vmem),
        compiler_params=params,
        cost_estimate=pl.CostEstimate(flops=10**7, bytes_accessed=4 * 10**6, transcendentals=0),
        name="slant_tables",
    )(block_position.reshape(1, groups))
    terms = pl.pallas_call(
        functools.partial(stack_kernel, groups, bins, parts),
        out_shape=jax.ShapeDtypeStruct((groups, parts, message_rows, BLOCK), jnp.float32),
        in_specs=[vmem] * (groups + 3),
        out_specs=vmem,
        scratch_shapes=[
            pltpu.VMEM((groups, bins, rows, BLOCK), jnp.bfloat16),
            pltpu.VMEM((bins, BLOCK, groups * rows), jnp.bfloat16),
            pltpu.VMEM((2, bins * 2 * groups * 8, BLOCK), jnp.float32),
        ],
        compiler_params=params,
        name="stack_and_slant",
    )(
        *arrived_chunks,
        places,
        lag_table,
        shift_table,
    )
    terms = terms.reshape(groups * parts, message_rows, BLOCK)
    arrived = lax.all_to_all(terms, ("chan", "freq"), split_axis=0, concat_axis=0, tiled=True)
    spans, table = time_table(groups, parts, bins, slow_dev, message_rows)
    table = pl.pallas_call(
        split_kernel,
        out_shape=jax.ShapeDtypeStruct((2,) + table.shape, jnp.bfloat16),
        in_specs=[vmem, pl.BlockSpec(memory_space=pl.ANY)],
        out_specs=vmem,
        compiler_params=params,
        cost_estimate=pl.CostEstimate(flops=10**7, bytes_accessed=4 * 10**6, transcendentals=0),
        name="table_halves",
    )(jnp.asarray(table), terms)
    return pl.pallas_call(
        functools.partial(image_kernel, slow_dev, spans),
        out_shape=jax.ShapeDtypeStruct((1, slow_dev, LAG_TIMES), jnp.float32),
        in_specs=[vmem, vmem],
        out_specs=vmem,
        compiler_params=params,
        name="sum_of_bins",
    )(arrived, table)


def solution(mesh):
    return jax.shard_map(
        shards,
        mesh=mesh,
        in_specs=(P(None, None, "freq", "chan"), P()),
        out_specs=P("chan", "freq", None),
        check_vma=False,
    )
```

```python
import functools
import math

import jax
import jax.numpy as jnp
import numpy as np
from jax import lax
from jax.experimental import pallas as pl
from jax.experimental.pallas import tpu as pltpu
from jax.sharding import PartitionSpec as P

SEGMENTS = 32
FREQS = 256
BLOCK = 128
SLOWNESS = 256
LAG_TIMES = 512
MODULUS = 8 * FREQS * BLOCK


def unit_phase(numerator):
    quarter = MODULUS // 4
    turn = numerator & (MODULUS - 1)
    quadrant = lax.shift_right_logical(turn + quarter // 2, quarter.bit_length() - 1)
    x = (turn - quadrant * quarter).astype(jnp.float32) * (2.0 * math.pi / MODULUS)
    y = x * x
    sine = x * (1.0 + y * (-1.0 / 6 + y * (1.0 / 120 + y * (-1.0 / 5040 + y * (1.0 / 362880)))))
    cosine = 1.0 + y * (-0.5 + y * (1.0 / 24 + y * (-1.0 / 720 + y * (1.0 / 40320))))
    odd = (quadrant & 1) == 1
    first = jnp.where(odd, sine, cosine)
    second = jnp.where(odd, cosine, sine)
    first = jnp.where(((quadrant + 1) & 2) == 2, -first, first)
    second = jnp.where((quadrant & 2) == 2, -second, second)
    return first, second


def halves(value):
    high = value.astype(jnp.bfloat16)
    return high, (value - high.astype(jnp.float32)).astype(jnp.bfloat16)


def table_kernel(groups, bins, freq_dev, position_ref, place_ref, lag_ref, shift_ref):
    low_rows = lax.broadcasted_iota(jnp.int32, (8, SLOWNESS), 0)
    high_rows = lax.broadcasted_iota(jnp.int32, (BLOCK // 8, SLOWNESS), 0) * 8
    shift_rows = lax.broadcasted_iota(jnp.int32, (2 * groups, SLOWNESS), 0)
    shift_rows = jnp.where(shift_rows < groups, shift_rows, shift_rows - groups - 1) * BLOCK
    own_group = lax.axis_index("chan")
    first_bin = lax.axis_index("freq") * freq_dev + own_group * bins
    sender = lax.broadcasted_iota(jnp.int32, (groups, groups), 1)
    distance = lax.broadcasted_iota(jnp.int32, (groups, groups), 0)
    sends = lax.rem(own_group + groups - distance, groups) == sender
    places = jnp.sum(jnp.where(sends, position_ref[...], 0), axis=1, keepdims=True)
    place_ref[...] = jnp.broadcast_to(places, place_ref.shape)

    def one_bin(f, carry):
        def phases(rows):
            slow = lax.broadcasted_iota(jnp.int32, rows.shape, 1) - SLOWNESS // 2
            return unit_phase((first_bin + f) * slow * rows)

        low_cos, low_sin = phases(low_rows)
        high_cos, high_sin = phases(high_rows)
        low_cos, low_sin = low_cos[None], low_sin[None]
        high_cos, high_sin = high_cos[:, None], high_sin[:, None]
        lag_cos = (high_cos * low_cos - high_sin * low_sin).reshape(BLOCK, SLOWNESS)
        lag_sin = (high_sin * low_cos + high_cos * low_sin).reshape(BLOCK, SLOWNESS)
        cos_high, cos_low = halves(lag_cos)
        sin_high, sin_low = halves(lag_sin)
        lag_ref[f, :BLOCK, :SLOWNESS] = cos_high
        lag_ref[f, BLOCK:, :SLOWNESS] = cos_low
        lag_ref[f, :BLOCK, SLOWNESS:] = sin_high
        lag_ref[f, BLOCK:, SLOWNESS:] = sin_low
        shift_cos, shift_sin = phases(shift_rows)
        shift_ref[f, 0] = shift_cos
        shift_ref[f, 1] = shift_sin
        return carry

    lax.fori_loop(0, bins, one_bin, 0)


def chunk_kernel(groups, pieces, spec_ref, *refs):
    out_refs, wide_ref = refs[:-1], refs[-1]
    wide_ref[...] = spec_ref[...].astype(jnp.float32)
    bins = sum(size for _, size in pieces)
    freq_dev = groups * bins
    rows = spec_ref.shape[0] // freq_dev
    own_group = lax.axis_index("chan")
    for index, out_ref in enumerate(out_refs):
        start, size = pieces[index // groups]
        first = lax.rem(own_group + index % groups, groups) * bins + start
        for f in range(size):
            value = wide_ref[pl.ds(first + f, rows, stride=freq_dev), :]
            out_ref[f] = value.astype(jnp.bfloat16)


def stack_weights(groups):
    row = lax.broadcasted_iota(jnp.int32, (2 * groups, BLOCK), 0)
    lag = lax.broadcasted_iota(jnp.int32, (2 * groups, BLOCK), 1)
    delta = jnp.where(row < groups, row, row - groups)
    lag = jnp.where(row < groups, lag, lag - BLOCK)
    usable = (lag > -BLOCK) & ((delta >= 1) | (lag >= 1))
    count = SEGMENTS * (groups - delta) * (BLOCK - jnp.abs(lag))
    scale = math.sqrt(SEGMENTS / FREQS)
    return jnp.where(usable, scale / jnp.maximum(count, 1).astype(jnp.float32), 0.0)


def stack_kernel(groups, start, bins, parts, *refs):
    chunk_refs = refs[:groups]
    place_ref, lag_ref, shift_ref = refs[groups : groups + 3]
    earlier_refs = refs[groups + 3 : -4]
    out_ref, placed_ref, left_ref, part_ref = refs[-4:]
    rows = placed_ref.shape[2]
    windows = rows // 2
    places = place_ref[...]
    for distance, chunk_ref in enumerate(chunk_refs):
        placed_ref[places[distance, 0]] = chunk_ref[...]

    row_index = lax.broadcasted_iota(jnp.int32, (BLOCK, BLOCK), 0)
    lag_index = lax.broadcasted_iota(jnp.int32, (BLOCK, BLOCK), 1)
    mirror = jnp.where(row_index + lag_index == BLOCK - 1, 1.0, 0.0).astype(jnp.bfloat16)
    ahead = lag_index <= row_index

    for f in range(bins):
        left_ref[f] = lax.dot_general(
            mirror,
            placed_ref[:, f].reshape(groups * rows, BLOCK),
            (((1,), (1,)), ((), ())),
            preferred_element_type=jnp.float32,
        ).astype(jnp.bfloat16)

    for f in range(bins):
        right = []
        for place in range(groups):
            value = placed_ref[place, f]
            real, imag = value[:windows], value[windows:]
            right.append(
                jnp.concatenate(
                    [jnp.concatenate([real, imag], 1), jnp.concatenate([imag, -real], 1)], 0
                )
            )
        right = jnp.concatenate(right, 0)
        for delta in range(groups):
            panel = jnp.dot(
                left_ref[f, :, : rows * (groups - delta)],
                right[rows * delta :],
                preferred_element_type=jnp.float32,
            )
            for half in range(2):
                lanes = slice(half * BLOCK, (half + 1) * BLOCK)
                skewed = pltpu.roll(panel[:, lanes], 1, 1, stride=1, stride_axis=0)
                forward = jnp.where(ahead, skewed, 0.0).reshape(-1, 8, BLOCK).sum(0)
                backward = jnp.where(ahead, 0.0, skewed).reshape(-1, 8, BLOCK).sum(0)
                first = (f * 2 * groups + delta) * 8
                part_ref[half, first : first + 8] = forward
                part_ref[half, first + groups * 8 : first + groups * 8 + 8] = backward

    lags = []
    for half in range(2):
        summed = part_ref[half, pl.ds(0, bins * 2 * groups, stride=8), :]
        for sublane in range(1, 8):
            summed = summed + part_ref[half, pl.ds(sublane, bins * 2 * groups, stride=8), :]
        lags.append(summed)
    weight = stack_weights(groups)

    terms = []
    for f in range(bins):
        lag_rows = slice(f * 2 * groups, (f + 1) * 2 * groups)
        means = jnp.concatenate([half[lag_rows] * weight for half in lags], 0)
        mean_high, mean_low = halves(means)
        spread = jnp.concatenate(
            [
                jnp.concatenate([mean_high, mean_high], 1),
                jnp.concatenate([mean_low, jnp.zeros_like(mean_low)], 1),
            ],
            0,
        )
        product = jnp.dot(spread, lag_ref[start + f], preferred_element_type=jnp.float32)
        product = product[: 4 * groups] + product[4 * groups :]
        by_cos, by_sin = product[:, :SLOWNESS], product[:, SLOWNESS:]
        real = by_cos[: 2 * groups] - by_sin[2 * groups :]
        imag = by_sin[: 2 * groups] + by_cos[2 * groups :]
        shift_cos, shift_sin = shift_ref[start + f, 0], shift_ref[start + f, 1]
        turned_re = real * shift_cos - imag * shift_sin
        turned_im = real * shift_sin + imag * shift_cos
        terms.append(turned_re[:groups] + turned_re[groups:])
        terms.append(turned_im[:groups] + turned_im[groups:])

    if parts is None:
        for entry, term in enumerate(terms):
            out_ref[entry] = term
        return
    for earlier_ref in reversed(earlier_refs):
        terms = [earlier_ref[entry] for entry in range(earlier_ref.shape[0])] + terms
    slow_dev = SLOWNESS // parts
    spans = BLOCK // slow_dev
    span_index = lax.broadcasted_iota(jnp.int32, (groups, BLOCK), 1) // slow_dev
    for part in range(parts):
        source = (part % spans) * slow_dev
        lanes = slice(part // spans * BLOCK, (part // spans + 1) * BLOCK)
        for row in range(out_ref.shape[2]):
            packed = jnp.zeros((groups, BLOCK), jnp.float32)
            for span, term in enumerate(terms[row * spans : (row + 1) * spans]):
                moved = pltpu.roll(term[:, lanes], (span * slow_dev - source) % BLOCK, 1)
                packed = jnp.where(span_index == span, moved, packed)
            out_ref[:, part, row, :] = packed


def image_kernel(slow_dev, spans, term_ref, table_ref, out_ref):
    arrived = term_ref[...]
    turned = arrived.reshape(-1, BLOCK).T
    turned = jnp.concatenate(
        [turned[span * slow_dev : (span + 1) * slow_dev] for span in range(spans)], 1
    )
    high, low = halves(turned)
    by_high = jnp.dot(
        jnp.concatenate([high, low], 0), table_ref[0], preferred_element_type=jnp.float32
    )
    by_low = jnp.dot(high, table_ref[1], preferred_element_type=jnp.float32)
    out_ref[0] = by_high[:slow_dev] + by_high[slow_dev:] + by_low


def time_table(groups, parts, bins, slow_dev, message_rows):
    spans = min(BLOCK // slow_dev, 2 * bins)
    span, group, part, row = np.meshgrid(
        np.arange(spans), np.arange(groups), np.arange(parts), np.arange(message_rows), indexing="ij"
    )
    entry = row * spans + span
    freq = (part * groups + group) * bins + entry // 2
    lag_time = np.arange(LAG_TIMES) - LAG_TIMES // 2
    angle = 2.0 * math.pi / LAG_TIMES * ((freq[..., None] * lag_time) % LAG_TIMES)
    table = np.where((entry % 2 == 0)[..., None], np.cos(angle), -np.sin(angle))
    table = table.reshape(-1, LAG_TIMES).astype(np.float32)
    high = table.astype(jnp.bfloat16)
    low = (table - high.astype(np.float32)).astype(jnp.bfloat16)
    return spans, np.stack([high, low])


def shards(spectra, block_position):
    groups = lax.axis_size("chan")
    parts = lax.axis_size("freq")
    rows = spectra.shape[0] * spectra.shape[1]
    freq_dev = spectra.shape[2]
    bins = freq_dev // groups
    slow_dev = SLOWNESS // parts
    message_rows = -(-2 * bins * slow_dev // BLOCK)
    vmem = pl.BlockSpec(memory_space=pltpu.VMEM)
    params = pltpu.CompilerParams(vmem_limit_bytes=32 * 1024 * 1024)

    late = max(1, bins // 4)
    pieces = [(0, bins - late), (bins - late, late)] if bins > 1 else [(0, 1)]
    chunks = pl.pallas_call(
        functools.partial(chunk_kernel, groups, pieces),
        out_shape=tuple(
            jax.ShapeDtypeStruct((size, rows, BLOCK), jnp.bfloat16)
            for _, size in pieces
            for _ in range(groups)
        ),
        in_specs=[vmem],
        out_specs=(vmem,) * (groups * len(pieces)),
        scratch_shapes=[pltpu.VMEM((rows * freq_dev, BLOCK), jnp.float32)],
        compiler_params=params,
        name="chunks_of_bins",
    )(spectra.reshape(rows * freq_dev, BLOCK))
    chunks = [list(chunks[index * groups : (index + 1) * groups]) for index in range(len(pieces))]
    for piece in chunks:
        for distance in sorted(range(1, groups), key=lambda steps: abs(2 * steps - groups)):
            pairs = [(source, (source + distance) % groups) for source in range(groups)]
            piece[distance] = lax.ppermute(piece[distance], "chan", pairs)
    places, lag_table, shift_table = pl.pallas_call(
        functools.partial(table_kernel, groups, bins, freq_dev),
        out_shape=(
            jax.ShapeDtypeStruct((groups, BLOCK), jnp.int32),
            jax.ShapeDtypeStruct((bins, 2 * BLOCK, 2 * SLOWNESS), jnp.bfloat16),
            jax.ShapeDtypeStruct((bins, 2, 2 * groups, SLOWNESS), jnp.float32),
        ),
        in_specs=[vmem],
        out_specs=(vmem, vmem, vmem),
        compiler_params=params,
        cost_estimate=pl.CostEstimate(flops=10**7, bytes_accessed=4 * 10**6, transcendentals=0),
        name="slant_tables",
    )(block_position.reshape(1, groups))
    earlier = []
    for index, (start, size) in enumerate(pieces):
        last = index == len(pieces) - 1
        if last:
            shape = (groups, parts, message_rows, BLOCK)
        else:
            shape = (2 * size, groups, SLOWNESS)
        terms = pl.pallas_call(
            functools.partial(stack_kernel, groups, start, size, parts if last else None),
            out_shape=jax.ShapeDtypeStruct(shape, jnp.float32),
            in_specs=[vmem] * (groups + 3 + len(earlier)),
            out_specs=vmem,
            scratch_shapes=[
                pltpu.VMEM((groups, size, rows, BLOCK), jnp.bfloat16),
                pltpu.VMEM((size, BLOCK, groups * rows), jnp.bfloat16),
                pltpu.VMEM((2, size * 2 * groups * 8, BLOCK), jnp.float32),
            ],
            compiler_params=params,
            cost_estimate=pl.CostEstimate(
                flops=2 * 10**8, bytes_accessed=4 * 10**6, transcendentals=0
            ),
            name="stack_and_slant",
        )(*chunks[index], places, lag_table, shift_table, *earlier)
        earlier.append(terms)
    terms = terms.reshape(groups * parts, message_rows, BLOCK)
    arrived = lax.all_to_all(terms, ("chan", "freq"), split_axis=0, concat_axis=0, tiled=True)
    spans, table = time_table(groups, parts, bins, slow_dev, message_rows)
    return pl.pallas_call(
        functools.partial(image_kernel, slow_dev, spans),
        out_shape=jax.ShapeDtypeStruct((1, slow_dev, LAG_TIMES), jnp.float32),
        in_specs=[vmem, vmem],
        out_specs=vmem,
        compiler_params=params,
        name="sum_of_bins",
    )(arrived, jnp.asarray(table))


def solution(mesh):
    return jax.shard_map(
        shards,
        mesh=mesh,
        in_specs=(P(None, None, "freq", "chan"), P()),
        out_specs=P("chan", "freq", None),
        check_vma=False,
    )
```

```python
import functools
import math

import jax
import jax.numpy as jnp
import numpy as np
from jax import lax
from jax.experimental import pallas as pl
from jax.experimental.pallas import tpu as pltpu
from jax.sharding import PartitionSpec as P

SEGMENTS = 32
FREQS = 256
BLOCK = 128
SLOWNESS = 256
LAG_TIMES = 512
MODULUS = 8 * FREQS * BLOCK


def unit_phase(numerator):
    quarter = MODULUS // 4
    turn = numerator & (MODULUS - 1)
    quadrant = lax.shift_right_logical(turn + quarter // 2, quarter.bit_length() - 1)
    x = (turn - quadrant * quarter).astype(jnp.float32) * (2.0 * math.pi / MODULUS)
    y = x * x
    sine = x * (1.0 + y * (-1.0 / 6 + y * (1.0 / 120 + y * (-1.0 / 5040 + y * (1.0 / 362880)))))
    cosine = 1.0 + y * (-0.5 + y * (1.0 / 24 + y * (-1.0 / 720 + y * (1.0 / 40320))))
    odd = (quadrant & 1) == 1
    first = jnp.where(odd, sine, cosine)
    second = jnp.where(odd, cosine, sine)
    first = jnp.where(((quadrant + 1) & 2) == 2, -first, first)
    second = jnp.where((quadrant & 2) == 2, -second, second)
    return first, second


def halves(value):
    high = value.astype(jnp.bfloat16)
    return high, (value - high.astype(jnp.float32)).astype(jnp.bfloat16)


def table_kernel(groups, bins, freq_dev, position_ref, far_ref, place_ref, lag_ref, shift_ref):
    low_rows = lax.broadcasted_iota(jnp.int32, (8, SLOWNESS), 0)
    high_rows = lax.broadcasted_iota(jnp.int32, (BLOCK // 8, SLOWNESS), 0) * 8
    shift_rows = lax.broadcasted_iota(jnp.int32, (2 * groups, SLOWNESS), 0)
    shift_rows = jnp.where(shift_rows < groups, shift_rows, shift_rows - groups - 1) * BLOCK
    own_group = lax.axis_index("chan")
    first_bin = lax.axis_index("freq") * freq_dev + own_group * bins
    sender = lax.broadcasted_iota(jnp.int32, (groups, groups), 1)
    distance = lax.broadcasted_iota(jnp.int32, (groups, groups), 0)
    sends = lax.rem(own_group + groups - distance, groups) == sender
    places = jnp.sum(jnp.where(sends, position_ref[...], 0), axis=1, keepdims=True)
    place_ref[...] = jnp.broadcast_to(places, place_ref.shape)

    def one_bin(f, carry):
        def phases(rows):
            slow = lax.broadcasted_iota(jnp.int32, rows.shape, 1) - SLOWNESS // 2
            return unit_phase((first_bin + f) * slow * rows)

        low_cos, low_sin = phases(low_rows)
        high_cos, high_sin = phases(high_rows)
        low_cos, low_sin = low_cos[None], low_sin[None]
        high_cos, high_sin = high_cos[:, None], high_sin[:, None]
        lag_cos = (high_cos * low_cos - high_sin * low_sin).reshape(BLOCK, SLOWNESS)
        lag_sin = (high_sin * low_cos + high_cos * low_sin).reshape(BLOCK, SLOWNESS)
        cos_high, cos_low = halves(lag_cos)
        sin_high, sin_low = halves(lag_sin)
        lag_ref[f, :BLOCK, :SLOWNESS] = cos_high
        lag_ref[f, BLOCK:, :SLOWNESS] = cos_low
        lag_ref[f, :BLOCK, SLOWNESS:] = sin_high
        lag_ref[f, BLOCK:, SLOWNESS:] = sin_low
        shift_cos, shift_sin = phases(shift_rows)
        shift_ref[f, 0] = shift_cos
        shift_ref[f, 1] = shift_sin
        return carry

    lax.fori_loop(0, bins, one_bin, 0)


def chunk_kernel(distances, spec_ref, *refs):
    rows, groups, bins, _ = spec_ref.shape
    out_refs, wide_ref = refs[-1 - len(distances) : -1], refs[-1]
    own_group = lax.axis_index("chan")
    for index, (distance, out_ref) in enumerate(zip(distances, out_refs)):
        group = lax.rem(own_group + distance, groups)
        wide_ref[index] = spec_ref[:, group].astype(jnp.float32).reshape(rows * bins, BLOCK)
        for f in range(bins):
            value = wide_ref[index, pl.ds(f, rows, stride=bins), :]
            out_ref[f] = value.astype(jnp.bfloat16)


def stack_weights(groups):
    row = lax.broadcasted_iota(jnp.int32, (2 * groups, BLOCK), 0)
    lag = lax.broadcasted_iota(jnp.int32, (2 * groups, BLOCK), 1)
    delta = jnp.where(row < groups, row, row - groups)
    lag = jnp.where(row < groups, lag, lag - BLOCK)
    usable = (lag > -BLOCK) & ((delta >= 1) | (lag >= 1))
    count = SEGMENTS * (groups - delta) * (BLOCK - jnp.abs(lag))
    scale = math.sqrt(SEGMENTS / FREQS)
    return jnp.where(usable, scale / jnp.maximum(count, 1).astype(jnp.float32), 0.0)


def stack_kernel(groups, bins, parts, *refs):
    chunk_refs = refs[:groups]
    place_ref, lag_ref, shift_ref, out_ref, placed_ref, left_ref, part_ref = refs[groups:]
    rows = placed_ref.shape[2]
    windows = rows // 2
    places = place_ref[...]
    for distance, chunk_ref in enumerate(chunk_refs):
        placed_ref[places[distance, 0]] = chunk_ref[...]

    row_index = lax.broadcasted_iota(jnp.int32, (BLOCK, BLOCK), 0)
    lag_index = lax.broadcasted_iota(jnp.int32, (BLOCK, BLOCK), 1)
    mirror = jnp.where(row_index + lag_index == BLOCK - 1, 1.0, 0.0).astype(jnp.bfloat16)
    ahead = lag_index <= row_index

    for f in range(bins):
        left_ref[f] = lax.dot_general(
            mirror,
            placed_ref[:, f].reshape(groups * rows, BLOCK),
            (((1,), (1,)), ((), ())),
            preferred_element_type=jnp.float32,
        ).astype(jnp.bfloat16)

    for f in range(bins):
        right = []
        for place in range(groups):
            value = placed_ref[place, f]
            real, imag = value[:windows], value[windows:]
            right.append(
                jnp.concatenate(
                    [jnp.concatenate([real, imag], 1), jnp.concatenate([imag, -real], 1)], 0
                )
            )
        right = jnp.concatenate(right, 0)
        for delta in range(groups):
            panel = jnp.dot(
                left_ref[f, :, : rows * (groups - delta)],
                right[rows * delta :],
                preferred_element_type=jnp.float32,
            )
            for half in range(2):
                lanes = slice(half * BLOCK, (half + 1) * BLOCK)
                skewed = pltpu.roll(panel[:, lanes], 1, 1, stride=1, stride_axis=0)
                forward = jnp.where(ahead, skewed, 0.0).reshape(-1, 8, BLOCK).sum(0)
                backward = jnp.where(ahead, 0.0, skewed).reshape(-1, 8, BLOCK).sum(0)
                first = (f * 2 * groups + delta) * 8
                part_ref[half, first : first + 8] = forward
                part_ref[half, first + groups * 8 : first + groups * 8 + 8] = backward

    lags = []
    for half in range(2):
        summed = part_ref[half, pl.ds(0, bins * 2 * groups, stride=8), :]
        for sublane in range(1, 8):
            summed = summed + part_ref[half, pl.ds(sublane, bins * 2 * groups, stride=8), :]
        lags.append(summed)
    weight = stack_weights(groups)

    terms = []
    for f in range(bins):
        lag_rows = slice(f * 2 * groups, (f + 1) * 2 * groups)
        means = jnp.concatenate([half[lag_rows] * weight for half in lags], 0)
        mean_high, mean_low = halves(means)
        spread = jnp.concatenate(
            [
                jnp.concatenate([mean_high, mean_high], 1),
                jnp.concatenate([mean_low, jnp.zeros_like(mean_low)], 1),
            ],
            0,
        )
        product = jnp.dot(spread, lag_ref[f], preferred_element_type=jnp.float32)
        product = product[: 4 * groups] + product[4 * groups :]
        by_cos, by_sin = product[:, :SLOWNESS], product[:, SLOWNESS:]
        real = by_cos[: 2 * groups] - by_sin[2 * groups :]
        imag = by_sin[: 2 * groups] + by_cos[2 * groups :]
        shift_cos, shift_sin = shift_ref[f, 0], shift_ref[f, 1]
        turned_re = real * shift_cos - imag * shift_sin
        turned_im = real * shift_sin + imag * shift_cos
        terms.append(turned_re[:groups] + turned_re[groups:])
        terms.append(turned_im[:groups] + turned_im[groups:])

    slow_dev = SLOWNESS // parts
    spans = BLOCK // slow_dev
    span_index = lax.broadcasted_iota(jnp.int32, (groups, BLOCK), 1) // slow_dev
    for part in range(parts):
        source = (part % spans) * slow_dev
        lanes = slice(part // spans * BLOCK, (part // spans + 1) * BLOCK)
        for row in range(out_ref.shape[2]):
            packed = jnp.zeros((groups, BLOCK), jnp.float32)
            for span, term in enumerate(terms[row * spans : (row + 1) * spans]):
                moved = pltpu.roll(term[:, lanes], (span * slow_dev - source) % BLOCK, 1)
                packed = jnp.where(span_index == span, moved, packed)
            out_ref[:, part, row, :] = packed


def image_kernel(slow_dev, spans, term_ref, table_ref, out_ref):
    arrived = term_ref[...]
    turned = arrived.reshape(-1, BLOCK).T
    turned = jnp.concatenate(
        [turned[span * slow_dev : (span + 1) * slow_dev] for span in range(spans)], 1
    )
    high, low = halves(turned)
    by_high = jnp.dot(
        jnp.concatenate([high, low], 0), table_ref[0], preferred_element_type=jnp.float32
    )
    by_low = jnp.dot(high, table_ref[1], preferred_element_type=jnp.float32)
    out_ref[0] = by_high[:slow_dev] + by_high[slow_dev:] + by_low


def time_table(groups, parts, bins, slow_dev, message_rows):
    spans = min(BLOCK // slow_dev, 2 * bins)
    span, group, part, row = np.meshgrid(
        np.arange(spans), np.arange(groups), np.arange(parts), np.arange(message_rows), indexing="ij"
    )
    entry = row * spans + span
    freq = (part * groups + group) * bins + entry // 2
    lag_time = np.arange(LAG_TIMES) - LAG_TIMES // 2
    angle = 2.0 * math.pi / LAG_TIMES * ((freq[..., None] * lag_time) % LAG_TIMES)
    table = np.where((entry % 2 == 0)[..., None], np.cos(angle), -np.sin(angle))
    table = table.reshape(-1, LAG_TIMES).astype(np.float32)
    high = table.astype(jnp.bfloat16)
    low = (table - high.astype(np.float32)).astype(jnp.bfloat16)
    return spans, np.stack([high, low])


def shards(spectra, block_position):
    groups = lax.axis_size("chan")
    parts = lax.axis_size("freq")
    rows = spectra.shape[0] * spectra.shape[1]
    freq_dev = spectra.shape[2]
    bins = freq_dev // groups
    slow_dev = SLOWNESS // parts
    message_rows = -(-2 * bins * slow_dev // BLOCK)
    vmem = pl.BlockSpec(memory_space=pltpu.VMEM)
    anywhere = pl.BlockSpec(memory_space=pl.ANY)
    params = pltpu.CompilerParams(vmem_limit_bytes=32 * 1024 * 1024)

    whole = spectra.reshape(rows, groups, bins, BLOCK)

    def cut(distances, *earlier):
        return pl.pallas_call(
            functools.partial(chunk_kernel, distances),
            out_shape=(jax.ShapeDtypeStruct((bins, rows, BLOCK), jnp.bfloat16),) * len(distances),
            in_specs=[vmem] + [anywhere] * len(earlier),
            out_specs=(vmem,) * len(distances),
            scratch_shapes=[pltpu.VMEM((len(distances), rows * bins, BLOCK), jnp.float32)],
            compiler_params=params,
            cost_estimate=pl.CostEstimate(flops=10**7, bytes_accessed=10**6, transcendentals=0),
            name="chunks_of_bins",
        )(whole, *earlier)

    far = groups // 2
    order = [far] + [distance for distance in range(1, groups) if distance != far] + [0]
    (far_chunk,) = cut(order[:1])
    chunks = dict(zip(order, (far_chunk, *cut(order[1:], far_chunk))))
    for distance in order[:-1]:
        pairs = [(source, (source + distance) % groups) for source in range(groups)]
        chunks[distance] = lax.ppermute(chunks[distance], "chan", pairs)
    places, lag_table, shift_table = pl.pallas_call(
        functools.partial(table_kernel, groups, bins, freq_dev),
        out_shape=(
            jax.ShapeDtypeStruct((groups, BLOCK), jnp.int32),
            jax.ShapeDtypeStruct((bins, 2 * BLOCK, 2 * SLOWNESS), jnp.bfloat16),
            jax.ShapeDtypeStruct((bins, 2, 2 * groups, SLOWNESS), jnp.float32),
        ),
        in_specs=[vmem, anywhere],
        out_specs=(vmem, vmem, vmem),
        compiler_params=params,
        cost_estimate=pl.CostEstimate(flops=10**7, bytes_accessed=4 * 10**6, transcendentals=0),
        name="slant_tables",
    )(block_position.reshape(1, groups), chunks[far])
    terms = pl.pallas_call(
        functools.partial(stack_kernel, groups, bins, parts),
        out_shape=jax.ShapeDtypeStruct((groups, parts, message_rows, BLOCK), jnp.float32),
        in_specs=[vmem] * (groups + 3),
        out_specs=vmem,
        scratch_shapes=[
            pltpu.VMEM((groups, bins, rows, BLOCK), jnp.bfloat16),
            pltpu.VMEM((bins, BLOCK, groups * rows), jnp.bfloat16),
            pltpu.VMEM((2, bins * 2 * groups * 8, BLOCK), jnp.float32),
        ],
        compiler_params=params,
        name="stack_and_slant",
    )(
        *[chunks[distance] for distance in range(groups)],
        places,
        lag_table,
        shift_table,
    )
    terms = terms.reshape(groups * parts, message_rows, BLOCK)
    arrived = lax.all_to_all(terms, ("chan", "freq"), split_axis=0, concat_axis=0, tiled=True)
    spans, table = time_table(groups, parts, bins, slow_dev, message_rows)
    return pl.pallas_call(
        functools.partial(image_kernel, slow_dev, spans),
        out_shape=jax.ShapeDtypeStruct((1, slow_dev, LAG_TIMES), jnp.float32),
        in_specs=[vmem, vmem],
        out_specs=vmem,
        compiler_params=params,
        name="sum_of_bins",
    )(arrived, jnp.asarray(table))


def solution(mesh):
    return jax.shard_map(
        shards,
        mesh=mesh,
        in_specs=(P(None, None, "freq", "chan"), P()),
        out_specs=P("chan", "freq", None),
        check_vma=False,
    )
```

```python
import functools
import math

import jax
import jax.numpy as jnp
import numpy as np
from jax import lax
from jax.experimental import pallas as pl
from jax.experimental.pallas import tpu as pltpu
from jax.sharding import PartitionSpec as P

SEGMENTS = 32
FREQS = 256
BLOCK = 128
SLOWNESS = 256
LAG_TIMES = 512
MODULUS = 8 * FREQS * BLOCK


def unit_phase(numerator):
    quarter = MODULUS // 4
    turn = numerator & (MODULUS - 1)
    quadrant = lax.shift_right_logical(turn + quarter // 2, quarter.bit_length() - 1)
    x = (turn - quadrant * quarter).astype(jnp.float32) * (2.0 * math.pi / MODULUS)
    y = x * x
    sine = x * (1.0 + y * (-1.0 / 6 + y * (1.0 / 120 + y * (-1.0 / 5040 + y * (1.0 / 362880)))))
    cosine = 1.0 + y * (-0.5 + y * (1.0 / 24 + y * (-1.0 / 720 + y * (1.0 / 40320))))
    odd = (quadrant & 1) == 1
    first = jnp.where(odd, sine, cosine)
    second = jnp.where(odd, cosine, sine)
    first = jnp.where(((quadrant + 1) & 2) == 2, -first, first)
    second = jnp.where((quadrant & 2) == 2, -second, second)
    return first, second


def halves(value):
    high = value.astype(jnp.bfloat16)
    return high, (value - high.astype(jnp.float32)).astype(jnp.bfloat16)


def table_kernel(groups, bins, freq_dev, position_ref, far_ref, place_ref, lag_ref, shift_ref):
    low_rows = lax.broadcasted_iota(jnp.int32, (8, SLOWNESS), 0)
    high_rows = lax.broadcasted_iota(jnp.int32, (BLOCK // 8, SLOWNESS), 0) * 8
    shift_rows = lax.broadcasted_iota(jnp.int32, (2 * groups, SLOWNESS), 0)
    shift_rows = jnp.where(shift_rows < groups, shift_rows, shift_rows - groups - 1) * BLOCK
    own_group = lax.axis_index("chan")
    first_bin = lax.axis_index("freq") * freq_dev + own_group * bins
    sender = lax.broadcasted_iota(jnp.int32, (groups, groups), 1)
    distance = lax.broadcasted_iota(jnp.int32, (groups, groups), 0)
    sends = lax.rem(own_group + groups - distance, groups) == sender
    places = jnp.sum(jnp.where(sends, position_ref[...], 0), axis=1, keepdims=True)
    place_ref[...] = jnp.broadcast_to(places, place_ref.shape)

    def one_bin(f, carry):
        def phases(rows):
            slow = lax.broadcasted_iota(jnp.int32, rows.shape, 1) - SLOWNESS // 2
            return unit_phase((first_bin + f) * slow * rows)

        low_cos, low_sin = phases(low_rows)
        high_cos, high_sin = phases(high_rows)
        low_cos, low_sin = low_cos[None], low_sin[None]
        high_cos, high_sin = high_cos[:, None], high_sin[:, None]
        lag_cos = (high_cos * low_cos - high_sin * low_sin).reshape(BLOCK, SLOWNESS)
        lag_sin = (high_sin * low_cos + high_cos * low_sin).reshape(BLOCK, SLOWNESS)
        cos_high, cos_low = halves(lag_cos)
        sin_high, sin_low = halves(lag_sin)
        lag_ref[f, :BLOCK, :SLOWNESS] = cos_high
        lag_ref[f, BLOCK:, :SLOWNESS] = cos_low
        lag_ref[f, :BLOCK, SLOWNESS:] = sin_high
        lag_ref[f, BLOCK:, SLOWNESS:] = sin_low
        shift_cos, shift_sin = phases(shift_rows)
        shift_ref[f, 0] = shift_cos
        shift_ref[f, 1] = shift_sin
        return carry

    lax.fori_loop(0, bins, one_bin, 0)


def chunk_kernel(distances, spec_ref, *refs):
    rows, groups, bins, _ = spec_ref.shape
    out_refs, wide_ref = refs[-1 - len(distances) : -1], refs[-1]
    own_group = lax.axis_index("chan")
    for index, (distance, out_ref) in enumerate(zip(distances, out_refs)):
        group = lax.rem(own_group + distance, groups)
        wide_ref[index] = spec_ref[:, group].astype(jnp.float32).reshape(rows * bins, BLOCK)
        for f in range(bins):
            value = wide_ref[index, pl.ds(f, rows, stride=bins), :]
            out_ref[f] = value.astype(jnp.bfloat16)


def stack_weights(groups):
    row = lax.broadcasted_iota(jnp.int32, (2 * groups, BLOCK), 0)
    lag = lax.broadcasted_iota(jnp.int32, (2 * groups, BLOCK), 1)
    delta = jnp.where(row < groups, row, row - groups)
    lag = jnp.where(row < groups, lag, lag - BLOCK)
    usable = (lag > -BLOCK) & ((delta >= 1) | (lag >= 1))
    count = SEGMENTS * (groups - delta) * (BLOCK - jnp.abs(lag))
    scale = math.sqrt(SEGMENTS / FREQS)
    return jnp.where(usable, scale / jnp.maximum(count, 1).astype(jnp.float32), 0.0)


def stack_kernel(groups, bins, parts, *refs):
    chunk_refs = refs[:groups]
    place_ref, lag_ref, shift_ref, out_ref, placed_ref, left_ref, part_ref = refs[groups:]
    rows = placed_ref.shape[2]
    windows = rows // 2
    places = place_ref[...]
    for distance, chunk_ref in enumerate(chunk_refs):
        placed_ref[places[distance, 0]] = chunk_ref[...]

    row_index = lax.broadcasted_iota(jnp.int32, (BLOCK, BLOCK), 0)
    lag_index = lax.broadcasted_iota(jnp.int32, (BLOCK, BLOCK), 1)
    mirror = jnp.where(row_index + lag_index == BLOCK - 1, 1.0, 0.0).astype(jnp.bfloat16)
    ahead = lag_index <= row_index

    for f in range(bins):
        left_ref[f] = lax.dot_general(
            mirror,
            placed_ref[:, f].reshape(groups * rows, BLOCK),
            (((1,), (1,)), ((), ())),
            preferred_element_type=jnp.float32,
        ).astype(jnp.bfloat16)

    for f in range(bins):
        right = []
        for place in range(groups):
            value = placed_ref[place, f]
            real, imag = value[:windows], value[windows:]
            right.append(
                jnp.concatenate(
                    [jnp.concatenate([real, imag], 1), jnp.concatenate([imag, -real], 1)], 0
                )
            )
        right = jnp.concatenate(right, 0)
        for delta in range(groups):
            panel = jnp.dot(
                left_ref[f, :, : rows * (groups - delta)],
                right[rows * delta :],
                preferred_element_type=jnp.float32,
            )
            for half in range(2):
                lanes = slice(half * BLOCK, (half + 1) * BLOCK)
                skewed = pltpu.roll(panel[:, lanes], 1, 1, stride=1, stride_axis=0)
                forward = jnp.where(ahead, skewed, 0.0).reshape(-1, 8, BLOCK).sum(0)
                backward = jnp.where(ahead, 0.0, skewed).reshape(-1, 8, BLOCK).sum(0)
                first = (f * 2 * groups + delta) * 8
                part_ref[half, first : first + 8] = forward
                part_ref[half, first + groups * 8 : first + groups * 8 + 8] = backward

    lags = []
    for half in range(2):
        summed = part_ref[half, pl.ds(0, bins * 2 * groups, stride=8), :]
        for sublane in range(1, 8):
            summed = summed + part_ref[half, pl.ds(sublane, bins * 2 * groups, stride=8), :]
        lags.append(summed)
    weight = stack_weights(groups)

    terms = []
    for f in range(bins):
        lag_rows = slice(f * 2 * groups, (f + 1) * 2 * groups)
        means = jnp.concatenate([half[lag_rows] * weight for half in lags], 0)
        mean_high, mean_low = halves(means)
        spread = jnp.concatenate(
            [
                jnp.concatenate([mean_high, mean_high], 1),
                jnp.concatenate([mean_low, jnp.zeros_like(mean_low)], 1),
            ],
            0,
        )
        product = jnp.dot(spread, lag_ref[f], preferred_element_type=jnp.float32)
        product = product[: 4 * groups] + product[4 * groups :]
        by_cos, by_sin = product[:, :SLOWNESS], product[:, SLOWNESS:]
        real = by_cos[: 2 * groups] - by_sin[2 * groups :]
        imag = by_sin[: 2 * groups] + by_cos[2 * groups :]
        shift_cos, shift_sin = shift_ref[f, 0], shift_ref[f, 1]
        turned_re = real * shift_cos - imag * shift_sin
        turned_im = real * shift_sin + imag * shift_cos
        terms.append(turned_re[:groups] + turned_re[groups:])
        terms.append(turned_im[:groups] + turned_im[groups:])

    slow_dev = SLOWNESS // parts
    spans = BLOCK // slow_dev
    span_index = lax.broadcasted_iota(jnp.int32, (groups, BLOCK), 1) // slow_dev
    for part in range(parts):
        source = (part % spans) * slow_dev
        lanes = slice(part // spans * BLOCK, (part // spans + 1) * BLOCK)
        for row in range(out_ref.shape[2]):
            packed = jnp.zeros((groups, BLOCK), jnp.float32)
            for span, term in enumerate(terms[row * spans : (row + 1) * spans]):
                moved = pltpu.roll(term[:, lanes], (span * slow_dev - source) % BLOCK, 1)
                packed = jnp.where(span_index == span, moved, packed)
            out_ref[:, part, row, :] = packed


def image_kernel(slow_dev, spans, term_ref, table_ref, out_ref):
    arrived = term_ref[...]
    turned = arrived.reshape(-1, BLOCK).T
    sums = []
    for odd, chosen in enumerate(spans):
        terms = jnp.concatenate(
            [turned[span * slow_dev : (span + 1) * slow_dev] for span in chosen], 1
        )
        high, low = halves(terms)
        by_high = jnp.dot(
            jnp.concatenate([high, low], 0), table_ref[odd, 0], preferred_element_type=jnp.float32
        )
        by_low = jnp.dot(high, table_ref[odd, 1], preferred_element_type=jnp.float32)
        sums.append(by_high[:slow_dev] + by_high[slow_dev:] + by_low)
    even, odd = sums
    out_ref[0, :, : LAG_TIMES // 2] = even - odd
    out_ref[0, :, LAG_TIMES // 2 :] = even + odd


def time_table(groups, parts, bins, slow_dev, message_rows):
    count = min(BLOCK // slow_dev, 2 * bins)
    spans = [[span for span in range(count) if span // 2 % 2 == odd] for odd in range(2)]
    tables = []
    for chosen in spans:
        span, group, part, row = np.meshgrid(
            chosen, np.arange(groups), np.arange(parts), np.arange(message_rows), indexing="ij"
        )
        entry = row * count + span
        freq = (part * groups + group) * bins + entry // 2
        lag_time = np.arange(LAG_TIMES // 2)
        angle = 2.0 * math.pi / LAG_TIMES * ((freq[..., None] * lag_time) % LAG_TIMES)
        table = np.where((entry % 2 == 0)[..., None], np.cos(angle), -np.sin(angle))
        table = table.reshape(-1, LAG_TIMES // 2).astype(np.float32)
        high = table.astype(jnp.bfloat16)
        low = (table - high.astype(np.float32)).astype(jnp.bfloat16)
        tables.append(np.stack([high, low]))
    return spans, np.stack(tables)


def shards(spectra, block_position):
    groups = lax.axis_size("chan")
    parts = lax.axis_size("freq")
    rows = spectra.shape[0] * spectra.shape[1]
    freq_dev = spectra.shape[2]
    bins = freq_dev // groups
    slow_dev = SLOWNESS // parts
    message_rows = -(-2 * bins * slow_dev // BLOCK)
    vmem = pl.BlockSpec(memory_space=pltpu.VMEM)
    anywhere = pl.BlockSpec(memory_space=pl.ANY)
    params = pltpu.CompilerParams(vmem_limit_bytes=32 * 1024 * 1024)

    whole = spectra.reshape(rows, groups, bins, BLOCK)

    def cut(distances, *earlier):
        return pl.pallas_call(
            functools.partial(chunk_kernel, distances),
            out_shape=(jax.ShapeDtypeStruct((bins, rows, BLOCK), jnp.bfloat16),) * len(distances),
            in_specs=[vmem] + [anywhere] * len(earlier),
            out_specs=(vmem,) * len(distances),
            scratch_shapes=[pltpu.VMEM((len(distances), rows * bins, BLOCK), jnp.float32)],
            compiler_params=params,
            cost_estimate=pl.CostEstimate(flops=10**7, bytes_accessed=10**6, transcendentals=0),
            name="chunks_of_bins",
        )(whole, *earlier)

    far = groups // 2
    order = [far] + [distance for distance in range(1, groups) if distance != far] + [0]
    (far_chunk,) = cut(order[:1])
    chunks = dict(zip(order, (far_chunk, *cut(order[1:], far_chunk))))
    for distance in order[:-1]:
        pairs = [(source, (source + distance) % groups) for source in range(groups)]
        chunks[distance] = lax.ppermute(chunks[distance], "chan", pairs)
    places, lag_table, shift_table = pl.pallas_call(
        functools.partial(table_kernel, groups, bins, freq_dev),
        out_shape=(
            jax.ShapeDtypeStruct((groups, BLOCK), jnp.int32),
            jax.ShapeDtypeStruct((bins, 2 * BLOCK, 2 * SLOWNESS), jnp.bfloat16),
            jax.ShapeDtypeStruct((bins, 2, 2 * groups, SLOWNESS), jnp.float32),
        ),
        in_specs=[vmem, anywhere],
        out_specs=(vmem, vmem, vmem),
        compiler_params=params,
        cost_estimate=pl.CostEstimate(flops=10**7, bytes_accessed=4 * 10**6, transcendentals=0),
        name="slant_tables",
    )(block_position.reshape(1, groups), chunks[far])
    terms = pl.pallas_call(
        functools.partial(stack_kernel, groups, bins, parts),
        out_shape=jax.ShapeDtypeStruct((groups, parts, message_rows, BLOCK), jnp.float32),
        in_specs=[vmem] * (groups + 3),
        out_specs=vmem,
        scratch_shapes=[
            pltpu.VMEM((groups, bins, rows, BLOCK), jnp.bfloat16),
            pltpu.VMEM((bins, BLOCK, groups * rows), jnp.bfloat16),
            pltpu.VMEM((2, bins * 2 * groups * 8, BLOCK), jnp.float32),
        ],
        compiler_params=params,
        name="stack_and_slant",
    )(
        *[chunks[distance] for distance in range(groups)],
        places,
        lag_table,
        shift_table,
    )
    terms = terms.reshape(groups * parts, message_rows, BLOCK)
    arrived = lax.all_to_all(terms, ("chan", "freq"), split_axis=0, concat_axis=0, tiled=True)
    spans, table = time_table(groups, parts, bins, slow_dev, message_rows)
    return pl.pallas_call(
        functools.partial(image_kernel, slow_dev, spans),
        out_shape=jax.ShapeDtypeStruct((1, slow_dev, LAG_TIMES), jnp.float32),
        in_specs=[vmem, vmem],
        out_specs=vmem,
        compiler_params=params,
        name="sum_of_bins",
    )(arrived, jnp.asarray(table))


def solution(mesh):
    return jax.shard_map(
        shards,
        mesh=mesh,
        in_specs=(P(None, None, "freq", "chan"), P()),
        out_specs=P("chan", "freq", None),
        check_vma=False,
    )
```

```python
import functools
import math

import jax
import jax.numpy as jnp
import numpy as np
from jax import lax
from jax.experimental import pallas as pl
from jax.experimental.pallas import tpu as pltpu
from jax.sharding import PartitionSpec as P

SEGMENTS = 32
FREQS = 256
BLOCK = 128
SLOWNESS = 256
LAG_TIMES = 512
MODULUS = 8 * FREQS * BLOCK


def unit_phase(numerator):
    quarter = MODULUS // 4
    turn = numerator & (MODULUS - 1)
    quadrant = lax.shift_right_logical(turn + quarter // 2, quarter.bit_length() - 1)
    x = (turn - quadrant * quarter).astype(jnp.float32) * (2.0 * math.pi / MODULUS)
    y = x * x
    sine = x * (1.0 + y * (-1.0 / 6 + y * (1.0 / 120 + y * (-1.0 / 5040 + y * (1.0 / 362880)))))
    cosine = 1.0 + y * (-0.5 + y * (1.0 / 24 + y * (-1.0 / 720 + y * (1.0 / 40320))))
    odd = (quadrant & 1) == 1
    first = jnp.where(odd, sine, cosine)
    second = jnp.where(odd, cosine, sine)
    first = jnp.where(((quadrant + 1) & 2) == 2, -first, first)
    second = jnp.where((quadrant & 2) == 2, -second, second)
    return first, second


def halves(value):
    high = value.astype(jnp.bfloat16)
    return high, (value - high.astype(jnp.float32)).astype(jnp.bfloat16)


def copy_kernel(in_ref, out_ref):
    out_ref[...] = in_ref[...]


def table_kernel(groups, bins, freq_dev, position_ref, place_ref, lag_ref, shift_ref):
    low_rows = lax.broadcasted_iota(jnp.int32, (8, SLOWNESS), 0)
    high_rows = lax.broadcasted_iota(jnp.int32, (BLOCK // 8, SLOWNESS), 0) * 8
    shift_rows = lax.broadcasted_iota(jnp.int32, (2 * groups, SLOWNESS), 0)
    shift_rows = jnp.where(shift_rows < groups, shift_rows, shift_rows - groups - 1) * BLOCK
    own_group = lax.axis_index("chan")
    first_bin = lax.axis_index("freq") * freq_dev + own_group * bins
    sender = lax.broadcasted_iota(jnp.int32, (groups, groups), 1)
    distance = lax.broadcasted_iota(jnp.int32, (groups, groups), 0)
    sends = lax.rem(own_group + groups - distance, groups) == sender
    places = jnp.sum(jnp.where(sends, position_ref[...], 0), axis=1, keepdims=True)
    place_ref[...] = jnp.broadcast_to(places, place_ref.shape)

    def one_bin(f, carry):
        def phases(rows):
            slow = lax.broadcasted_iota(jnp.int32, rows.shape, 1) - SLOWNESS // 2
            return unit_phase((first_bin + f) * slow * rows)

        low_cos, low_sin = phases(low_rows)
        high_cos, high_sin = phases(high_rows)
        low_cos, low_sin = low_cos[None], low_sin[None]
        high_cos, high_sin = high_cos[:, None], high_sin[:, None]
        lag_cos = (high_cos * low_cos - high_sin * low_sin).reshape(BLOCK, SLOWNESS)
        lag_sin = (high_sin * low_cos + high_cos * low_sin).reshape(BLOCK, SLOWNESS)
        cos_high, cos_low = halves(lag_cos)
        sin_high, sin_low = halves(lag_sin)
        lag_ref[f, :BLOCK, :SLOWNESS] = cos_high
        lag_ref[f, BLOCK:, :SLOWNESS] = cos_low
        lag_ref[f, :BLOCK, SLOWNESS:] = sin_high
        lag_ref[f, BLOCK:, SLOWNESS:] = sin_low
        shift_cos, shift_sin = phases(shift_rows)
        shift_ref[f, 0] = shift_cos
        shift_ref[f, 1] = shift_sin
        return carry

    lax.fori_loop(0, bins, one_bin, 0)


def chunk_kernel(distances, spec_ref, *refs):
    rows, groups, bins, _ = spec_ref.shape
    out_refs, wide_ref = refs[-1 - len(distances) : -1], refs[-1]
    own_group = lax.axis_index("chan")
    for index, (distance, out_ref) in enumerate(zip(distances, out_refs)):
        group = lax.rem(own_group + distance, groups)
        wide_ref[index] = spec_ref[:, group].astype(jnp.float32).reshape(rows * bins, BLOCK)
        for f in range(bins):
            value = wide_ref[index, pl.ds(f, rows, stride=bins), :]
            out_ref[f] = value.astype(jnp.bfloat16)


def stack_weights(groups):
    row = lax.broadcasted_iota(jnp.int32, (2 * groups, BLOCK), 0)
    lag = lax.broadcasted_iota(jnp.int32, (2 * groups, BLOCK), 1)
    delta = jnp.where(row < groups, row, row - groups)
    lag = jnp.where(row < groups, lag, lag - BLOCK)
    usable = (lag > -BLOCK) & ((delta >= 1) | (lag >= 1))
    count = SEGMENTS * (groups - delta) * (BLOCK - jnp.abs(lag))
    scale = math.sqrt(SEGMENTS / FREQS)
    return jnp.where(usable, scale / jnp.maximum(count, 1).astype(jnp.float32), 0.0)


def stack_kernel(groups, bins, parts, *refs):
    chunk_refs = refs[:groups]
    place_ref, lag_ref, shift_ref, out_ref, placed_ref, left_ref, part_ref = refs[groups:]
    rows = placed_ref.shape[2]
    windows = rows // 2
    places = place_ref[...]
    for distance, chunk_ref in enumerate(chunk_refs):
        placed_ref[places[distance, 0]] = chunk_ref[...]

    row_index = lax.broadcasted_iota(jnp.int32, (BLOCK, BLOCK), 0)
    lag_index = lax.broadcasted_iota(jnp.int32, (BLOCK, BLOCK), 1)
    mirror = jnp.where(row_index + lag_index == BLOCK - 1, 1.0, 0.0).astype(jnp.bfloat16)
    ahead = lag_index <= row_index

    for f in range(bins):
        left_ref[f] = lax.dot_general(
            mirror,
            placed_ref[:, f].reshape(groups * rows, BLOCK),
            (((1,), (1,)), ((), ())),
            preferred_element_type=jnp.float32,
        ).astype(jnp.bfloat16)

    for f in range(bins):
        right = []
        for place in range(groups):
            value = placed_ref[place, f]
            real, imag = value[:windows], value[windows:]
            right.append(
                jnp.concatenate(
                    [jnp.concatenate([real, imag], 1), jnp.concatenate([imag, -real], 1)], 0
                )
            )
        right = jnp.concatenate(right, 0)
        for delta in range(groups):
            panel = jnp.dot(
                left_ref[f, :, : rows * (groups - delta)],
                right[rows * delta :],
                preferred_element_type=jnp.float32,
            )
            for half in range(2):
                lanes = slice(half * BLOCK, (half + 1) * BLOCK)
                skewed = pltpu.roll(panel[:, lanes], 1, 1, stride=1, stride_axis=0)
                forward = jnp.where(ahead, skewed, 0.0).reshape(-1, 8, BLOCK).sum(0)
                backward = jnp.where(ahead, 0.0, skewed).reshape(-1, 8, BLOCK).sum(0)
                first = (f * 2 * groups + delta) * 8
                part_ref[half, first : first + 8] = forward
                part_ref[half, first + groups * 8 : first + groups * 8 + 8] = backward

    lags = []
    for half in range(2):
        summed = part_ref[half, pl.ds(0, bins * 2 * groups, stride=8), :]
        for sublane in range(1, 8):
            summed = summed + part_ref[half, pl.ds(sublane, bins * 2 * groups, stride=8), :]
        lags.append(summed)
    weight = stack_weights(groups)

    terms = []
    for f in range(bins):
        lag_rows = slice(f * 2 * groups, (f + 1) * 2 * groups)
        means = jnp.concatenate([half[lag_rows] * weight for half in lags], 0)
        mean_high, mean_low = halves(means)
        spread = jnp.concatenate(
            [
                jnp.concatenate([mean_high, mean_high], 1),
                jnp.concatenate([mean_low, jnp.zeros_like(mean_low)], 1),
            ],
            0,
        )
        product = jnp.dot(spread, lag_ref[f], preferred_element_type=jnp.float32)
        product = product[: 4 * groups] + product[4 * groups :]
        by_cos, by_sin = product[:, :SLOWNESS], product[:, SLOWNESS:]
        real = by_cos[: 2 * groups] - by_sin[2 * groups :]
        imag = by_sin[: 2 * groups] + by_cos[2 * groups :]
        shift_cos, shift_sin = shift_ref[f, 0], shift_ref[f, 1]
        turned_re = real * shift_cos - imag * shift_sin
        turned_im = real * shift_sin + imag * shift_cos
        terms.append(turned_re[:groups] + turned_re[groups:])
        terms.append(turned_im[:groups] + turned_im[groups:])

    slow_dev = SLOWNESS // parts
    spans = BLOCK // slow_dev
    span_index = lax.broadcasted_iota(jnp.int32, (groups, BLOCK), 1) // slow_dev
    for part in range(parts):
        source = (part % spans) * slow_dev
        lanes = slice(part // spans * BLOCK, (part // spans + 1) * BLOCK)
        for row in range(out_ref.shape[2]):
            packed = jnp.zeros((groups, BLOCK), jnp.float32)
            for span, term in enumerate(terms[row * spans : (row + 1) * spans]):
                moved = pltpu.roll(term[:, lanes], (span * slow_dev - source) % BLOCK, 1)
                packed = jnp.where(span_index == span, moved, packed)
            out_ref[:, part, row, :] = packed


def image_kernel(slow_dev, spans, term_ref, table_ref, out_ref):
    arrived = term_ref[...]
    turned = arrived.reshape(-1, BLOCK).T
    sums = []
    for odd, chosen in enumerate(spans):
        terms = jnp.concatenate(
            [turned[span * slow_dev : (span + 1) * slow_dev] for span in chosen], 1
        )
        high, low = halves(terms)
        by_high = jnp.dot(
            jnp.concatenate([high, low], 0), table_ref[odd, 0], preferred_element_type=jnp.float32
        )
        by_low = jnp.dot(high, table_ref[odd, 1], preferred_element_type=jnp.float32)
        sums.append(by_high[:slow_dev] + by_high[slow_dev:] + by_low)
    even, odd = sums
    out_ref[0, :, : LAG_TIMES // 2] = even - odd
    out_ref[0, :, LAG_TIMES // 2 :] = even + odd


def time_table(groups, parts, bins, slow_dev, message_rows):
    count = min(BLOCK // slow_dev, 2 * bins)
    spans = [[span for span in range(count) if span // 2 % 2 == odd] for odd in range(2)]
    tables = []
    for chosen in spans:
        span, group, part, row = np.meshgrid(
            chosen, np.arange(groups), np.arange(parts), np.arange(message_rows), indexing="ij"
        )
        entry = row * count + span
        freq = (part * groups + group) * bins + entry // 2
        lag_time = np.arange(LAG_TIMES // 2)
        angle = 2.0 * math.pi / LAG_TIMES * ((freq[..., None] * lag_time) % LAG_TIMES)
        table = np.where((entry % 2 == 0)[..., None], np.cos(angle), -np.sin(angle))
        table = table.reshape(-1, LAG_TIMES // 2).astype(np.float32)
        high = table.astype(jnp.bfloat16)
        low = (table - high.astype(np.float32)).astype(jnp.bfloat16)
        tables.append(np.stack([high, low]))
    return spans, np.stack(tables)


def shards(spectra, block_position):
    groups = lax.axis_size("chan")
    parts = lax.axis_size("freq")
    rows = spectra.shape[0] * spectra.shape[1]
    freq_dev = spectra.shape[2]
    bins = freq_dev // groups
    slow_dev = SLOWNESS // parts
    message_rows = -(-2 * bins * slow_dev // BLOCK)
    vmem = pl.BlockSpec(memory_space=pltpu.VMEM)
    anywhere = pl.BlockSpec(memory_space=pl.ANY)
    params = pltpu.CompilerParams(vmem_limit_bytes=32 * 1024 * 1024)

    whole = spectra.reshape(rows, groups, bins, BLOCK)

    def cut(distances, *earlier):
        return pl.pallas_call(
            functools.partial(chunk_kernel, distances),
            out_shape=(jax.ShapeDtypeStruct((bins, rows, BLOCK), jnp.bfloat16),) * len(distances),
            in_specs=[vmem] + [anywhere] * len(earlier),
            out_specs=(vmem,) * len(distances),
            scratch_shapes=[pltpu.VMEM((len(distances), rows * bins, BLOCK), jnp.float32)],
            compiler_params=params,
            cost_estimate=pl.CostEstimate(flops=10**7, bytes_accessed=10**6, transcendentals=0),
            name="chunks_of_bins",
        )(whole, *earlier)

    order = list(range(1, groups)) + [0]
    (first_chunk,) = cut(order[:1])
    chunks = dict(zip(order, (first_chunk, *cut(order[1:], first_chunk))))
    for distance in order[:-1]:
        pairs = [(source, (source + distance) % groups) for source in range(groups)]
        chunks[distance] = lax.ppermute(chunks[distance], "chan", pairs)
    first = order[0]
    chunks[first] = pl.pallas_call(
        copy_kernel,
        out_shape=jax.ShapeDtypeStruct((bins, rows, BLOCK), jnp.bfloat16),
        in_specs=[vmem],
        out_specs=vmem,
        compiler_params=params,
        name="first_arrived",
    )(chunks[first])
    places, lag_table, shift_table = pl.pallas_call(
        functools.partial(table_kernel, groups, bins, freq_dev),
        out_shape=(
            jax.ShapeDtypeStruct((groups, BLOCK), jnp.int32),
            jax.ShapeDtypeStruct((bins, 2 * BLOCK, 2 * SLOWNESS), jnp.bfloat16),
            jax.ShapeDtypeStruct((bins, 2, 2 * groups, SLOWNESS), jnp.float32),
        ),
        in_specs=[vmem],
        out_specs=(vmem, vmem, vmem),
        compiler_params=params,
        cost_estimate=pl.CostEstimate(flops=10**7, bytes_accessed=4 * 10**6, transcendentals=0),
        name="slant_tables",
    )(block_position.reshape(1, groups))
    terms = pl.pallas_call(
        functools.partial(stack_kernel, groups, bins, parts),
        out_shape=jax.ShapeDtypeStruct((groups, parts, message_rows, BLOCK), jnp.float32),
        in_specs=[vmem] * (groups + 3),
        out_specs=vmem,
        scratch_shapes=[
            pltpu.VMEM((groups, bins, rows, BLOCK), jnp.bfloat16),
            pltpu.VMEM((bins, BLOCK, groups * rows), jnp.bfloat16),
            pltpu.VMEM((2, bins * 2 * groups * 8, BLOCK), jnp.float32),
        ],
        compiler_params=params,
        name="stack_and_slant",
    )(
        *[chunks[distance] for distance in range(groups)],
        places,
        lag_table,
        shift_table,
    )
    terms = terms.reshape(groups * parts, message_rows, BLOCK)
    arrived = lax.all_to_all(terms, ("chan", "freq"), split_axis=0, concat_axis=0, tiled=True)
    spans, table = time_table(groups, parts, bins, slow_dev, message_rows)
    return pl.pallas_call(
        functools.partial(image_kernel, slow_dev, spans),
        out_shape=jax.ShapeDtypeStruct((1, slow_dev, LAG_TIMES), jnp.float32),
        in_specs=[vmem, vmem],
        out_specs=vmem,
        compiler_params=params,
        name="sum_of_bins",
    )(arrived, jnp.asarray(table))


def solution(mesh):
    return jax.shard_map(
        shards,
        mesh=mesh,
        in_specs=(P(None, None, "freq", "chan"), P()),
        out_specs=P("chan", "freq", None),
        check_vma=False,
    )
```

```python
import functools
import math

import jax
import jax.numpy as jnp
import numpy as np
from jax import lax
from jax.experimental import pallas as pl
from jax.experimental.pallas import tpu as pltpu
from jax.sharding import PartitionSpec as P

SEGMENTS = 32
FREQS = 256
BLOCK = 128
SLOWNESS = 256
LAG_TIMES = 512
MODULUS = 8 * FREQS * BLOCK


def unit_phase(numerator):
    quarter = MODULUS // 4
    turn = numerator & (MODULUS - 1)
    quadrant = lax.shift_right_logical(turn + quarter // 2, quarter.bit_length() - 1)
    x = (turn - quadrant * quarter).astype(jnp.float32) * (2.0 * math.pi / MODULUS)
    y = x * x
    sine = x * (1.0 + y * (-1.0 / 6 + y * (1.0 / 120 + y * (-1.0 / 5040 + y * (1.0 / 362880)))))
    cosine = 1.0 + y * (-0.5 + y * (1.0 / 24 + y * (-1.0 / 720 + y * (1.0 / 40320))))
    odd = (quadrant & 1) == 1
    first = jnp.where(odd, sine, cosine)
    second = jnp.where(odd, cosine, sine)
    first = jnp.where(((quadrant + 1) & 2) == 2, -first, first)
    second = jnp.where((quadrant & 2) == 2, -second, second)
    return first, second


def halves(value):
    high = value.astype(jnp.bfloat16)
    return high, (value - high.astype(jnp.float32)).astype(jnp.bfloat16)


def copy_kernel(in_ref, out_ref):
    out_ref[...] = in_ref[...]


def table_kernel(groups, bins, freq_dev, position_ref, place_ref, lag_ref, shift_ref):
    low_rows = lax.broadcasted_iota(jnp.int32, (8, SLOWNESS), 0)
    high_rows = lax.broadcasted_iota(jnp.int32, (BLOCK // 8, SLOWNESS), 0) * 8
    shift_rows = lax.broadcasted_iota(jnp.int32, (2 * groups, SLOWNESS), 0)
    shift_rows = jnp.where(shift_rows < groups, shift_rows, shift_rows - groups - 1) * BLOCK
    own_group = lax.axis_index("chan")
    first_bin = lax.axis_index("freq") * freq_dev + own_group * bins
    sender = lax.broadcasted_iota(jnp.int32, (groups, groups), 1)
    distance = lax.broadcasted_iota(jnp.int32, (groups, groups), 0)
    sends = lax.rem(own_group + groups - distance, groups) == sender
    places = jnp.sum(jnp.where(sends, position_ref[...], 0), axis=1, keepdims=True)
    place_ref[...] = jnp.broadcast_to(places, place_ref.shape)

    def one_bin(f, carry):
        def phases(rows):
            slow = lax.broadcasted_iota(jnp.int32, rows.shape, 1) - SLOWNESS // 2
            return unit_phase((first_bin + f) * slow * rows)

        low_cos, low_sin = phases(low_rows)
        high_cos, high_sin = phases(high_rows)
        low_cos, low_sin = low_cos[None], low_sin[None]
        high_cos, high_sin = high_cos[:, None], high_sin[:, None]
        lag_cos = (high_cos * low_cos - high_sin * low_sin).reshape(BLOCK, SLOWNESS)
        lag_sin = (high_sin * low_cos + high_cos * low_sin).reshape(BLOCK, SLOWNESS)
        cos_high, cos_low = halves(lag_cos)
        sin_high, sin_low = halves(lag_sin)
        lag_ref[f, :BLOCK, :SLOWNESS] = cos_high
        lag_ref[f, BLOCK:, :SLOWNESS] = cos_low
        lag_ref[f, :BLOCK, SLOWNESS:] = sin_high
        lag_ref[f, BLOCK:, SLOWNESS:] = sin_low
        shift_cos, shift_sin = phases(shift_rows)
        shift_ref[f, 0] = shift_cos
        shift_ref[f, 1] = shift_sin
        return carry

    lax.fori_loop(0, bins, one_bin, 0)


def chunk_kernel(distances, spec_ref, *refs):
    rows, groups, bins, _ = spec_ref.shape
    out_refs, wide_ref = refs[-1 - len(distances) : -1], refs[-1]
    own_group = lax.axis_index("chan")
    for index, (distance, out_ref) in enumerate(zip(distances, out_refs)):
        group = lax.rem(own_group + distance, groups)
        wide_ref[index] = spec_ref[:, group].astype(jnp.float32).reshape(rows * bins, BLOCK)
        for f in range(bins):
            value = wide_ref[index, pl.ds(f, rows, stride=bins), :]
            out_ref[f] = value.astype(jnp.bfloat16)


def stack_weights(groups):
    row = lax.broadcasted_iota(jnp.int32, (2 * groups, BLOCK), 0)
    lag = lax.broadcasted_iota(jnp.int32, (2 * groups, BLOCK), 1)
    delta = jnp.where(row < groups, row, row - groups)
    lag = jnp.where(row < groups, lag, lag - BLOCK)
    usable = (lag > -BLOCK) & ((delta >= 1) | (lag >= 1))
    count = SEGMENTS * (groups - delta) * (BLOCK - jnp.abs(lag))
    scale = math.sqrt(SEGMENTS / FREQS)
    return jnp.where(usable, scale / jnp.maximum(count, 1).astype(jnp.float32), 0.0)


def stack_kernel(groups, bins, parts, *refs):
    chunk_refs = refs[:groups]
    place_ref, lag_ref, shift_ref, out_ref, placed_ref, *part_refs = refs[groups:]
    rows = placed_ref.shape[2]
    windows = rows // 2
    places = place_ref[...]
    for distance, chunk_ref in enumerate(chunk_refs):
        placed_ref[places[distance, 0]] = chunk_ref[...]

    row_index = lax.broadcasted_iota(jnp.int32, (BLOCK, BLOCK), 0)
    lag_index = lax.broadcasted_iota(jnp.int32, (BLOCK, BLOCK), 1)
    mirror = jnp.where(row_index + lag_index == BLOCK - 1, 1.0, 0.0).astype(jnp.bfloat16)
    behind = (lag_index - row_index)[:8]

    weight = stack_weights(groups)
    lefts, lags = {}, {}

    def turn(f):
        lefts[f] = lax.dot_general(
            mirror,
            placed_ref[:, f].reshape(groups * rows, BLOCK),
            (((1,), (1,)), ((), ())),
            preferred_element_type=jnp.float32,
        ).astype(jnp.bfloat16)

    def correlate(f):
        right = []
        for place in range(groups):
            value = placed_ref[place, f]
            real, imag = value[:windows], value[windows:]
            right.append(
                jnp.concatenate(
                    [jnp.concatenate([real, imag], 1), jnp.concatenate([imag, -real], 1)], 0
                )
            )
        right = jnp.concatenate(right, 0)
        for delta in range(groups):
            panel = jnp.dot(
                lefts[f][:, : rows * (groups - delta)],
                right[rows * delta :],
                preferred_element_type=jnp.float32,
            )
            for half in range(2):
                lanes = slice(half * BLOCK, (half + 1) * BLOCK)
                skewed = pltpu.roll(panel[:, lanes], 1, 1, stride=1, stride_axis=0)
                total = skewed[:8]
                backward = jnp.where(behind > 0, total, 0.0)
                for row in range(8, BLOCK, 8):
                    total = total + skewed[row : row + 8]
                    backward = jnp.where(behind > row, total, backward)
                part_refs[f][half, delta * 8 : delta * 8 + 8] = total - backward
                first = (groups + delta) * 8
                part_refs[f][half, first : first + 8] = backward
        lags[f] = []
        for half in range(2):
            summed = part_refs[f][half, pl.ds(0, 2 * groups, stride=8), :]
            for sublane in range(1, 8):
                summed = summed + part_refs[f][half, pl.ds(sublane, 2 * groups, stride=8), :]
            lags[f].append(summed)

    terms = []

    def slant(f):
        means = jnp.concatenate([half * weight for half in lags[f]], 0)
        mean_high, mean_low = halves(means)
        spread = jnp.concatenate(
            [
                jnp.concatenate([mean_high, mean_high], 1),
                jnp.concatenate([mean_low, jnp.zeros_like(mean_low)], 1),
            ],
            0,
        )
        product = jnp.dot(spread, lag_ref[f], preferred_element_type=jnp.float32)
        product = product[: 4 * groups] + product[4 * groups :]
        by_cos, by_sin = product[:, :SLOWNESS], product[:, SLOWNESS:]
        real = by_cos[: 2 * groups] - by_sin[2 * groups :]
        imag = by_sin[: 2 * groups] + by_cos[2 * groups :]
        shift_cos, shift_sin = shift_ref[f, 0], shift_ref[f, 1]
        turned_re = real * shift_cos - imag * shift_sin
        turned_im = real * shift_sin + imag * shift_cos
        terms.append(turned_re[:groups] + turned_re[groups:])
        terms.append(turned_im[:groups] + turned_im[groups:])

    turn(0)
    for f in range(bins):
        if f + 1 < bins:
            turn(f + 1)
        correlate(f)
        if f:
            slant(f - 1)
    slant(bins - 1)

    slow_dev = SLOWNESS // parts
    spans = BLOCK // slow_dev
    count = min(spans, len(terms))
    span_index = lax.broadcasted_iota(jnp.int32, (groups, BLOCK), 1) // slow_dev
    for row in range(out_ref.shape[2]):
        for half in range(SLOWNESS // BLOCK):
            lanes = slice(half * BLOCK, (half + 1) * BLOCK)
            moved = [
                pltpu.roll(term[:, lanes], span * slow_dev, 1) if span else term[:, lanes]
                for span, term in enumerate(terms[row * count : (row + 1) * count])
            ]
            for part in range(spans):
                packed = jnp.zeros((groups, BLOCK), jnp.float32)
                for span, value in enumerate(moved):
                    packed = jnp.where(span_index == (span + part) % spans, value, packed)
                out_ref[:, half * spans + part, row, :] = packed


def image_kernel(slow_dev, spans, term_ref, table_ref, out_ref):
    count = BLOCK // slow_dev
    back = count - lax.rem(lax.axis_index("freq"), count)
    arrived = pltpu.roll(term_ref[...].reshape(-1, BLOCK), back * slow_dev, 1)
    turned = arrived.T
    sums = []
    for odd, chosen in enumerate(spans):
        terms = jnp.concatenate(
            [turned[span * slow_dev : (span + 1) * slow_dev] for span in chosen], 1
        )
        high, low = halves(terms)
        by_high = jnp.dot(
            jnp.concatenate([high, low], 0), table_ref[odd, 0], preferred_element_type=jnp.float32
        )
        by_low = jnp.dot(high, table_ref[odd, 1], preferred_element_type=jnp.float32)
        sums.append(by_high[:slow_dev] + by_high[slow_dev:] + by_low)
    even, odd = sums
    out_ref[0, :, : LAG_TIMES // 2] = even - odd
    out_ref[0, :, LAG_TIMES // 2 :] = even + odd


def time_table(groups, parts, bins, slow_dev, message_rows):
    count = min(BLOCK // slow_dev, 2 * bins)
    spans = [[span for span in range(count) if span // 2 % 2 == odd] for odd in range(2)]
    tables = []
    for chosen in spans:
        span, group, part, row = np.meshgrid(
            chosen, np.arange(groups), np.arange(parts), np.arange(message_rows), indexing="ij"
        )
        entry = row * count + span
        freq = (part * groups + group) * bins + entry // 2
        lag_time = np.arange(LAG_TIMES // 2)
        angle = 2.0 * math.pi / LAG_TIMES * ((freq[..., None] * lag_time) % LAG_TIMES)
        table = np.where((entry % 2 == 0)[..., None], np.cos(angle), -np.sin(angle))
        table = table.reshape(-1, LAG_TIMES // 2).astype(np.float32)
        high = table.astype(jnp.bfloat16)
        low = (table - high.astype(np.float32)).astype(jnp.bfloat16)
        tables.append(np.stack([high, low]))
    return spans, np.stack(tables)


def shards(spectra, block_position):
    groups = lax.axis_size("chan")
    parts = lax.axis_size("freq")
    rows = spectra.shape[0] * spectra.shape[1]
    freq_dev = spectra.shape[2]
    bins = freq_dev // groups
    slow_dev = SLOWNESS // parts
    message_rows = -(-2 * bins * slow_dev // BLOCK)
    vmem = pl.BlockSpec(memory_space=pltpu.VMEM)
    anywhere = pl.BlockSpec(memory_space=pl.ANY)
    params = pltpu.CompilerParams(vmem_limit_bytes=32 * 1024 * 1024)

    whole = spectra.reshape(rows, groups, bins, BLOCK)

    def cut(distances, *earlier):
        return pl.pallas_call(
            functools.partial(chunk_kernel, distances),
            out_shape=(jax.ShapeDtypeStruct((bins, rows, BLOCK), jnp.bfloat16),) * len(distances),
            in_specs=[vmem] + [anywhere] * len(earlier),
            out_specs=(vmem,) * len(distances),
            scratch_shapes=[pltpu.VMEM((len(distances), rows * bins, BLOCK), jnp.float32)],
            compiler_params=params,
            cost_estimate=pl.CostEstimate(flops=10**7, bytes_accessed=10**6, transcendentals=0),
            name="chunks_of_bins",
        )(whole, *earlier)

    order = list(range(1, groups)) + [0]
    (first_chunk,) = cut(order[:1])
    chunks = dict(zip(order, (first_chunk, *cut(order[1:], first_chunk))))
    for distance in order[:-1]:
        pairs = [(source, (source + distance) % groups) for source in range(groups)]
        chunks[distance] = lax.ppermute(chunks[distance], "chan", pairs)
    first = order[0]
    chunks[first] = pl.pallas_call(
        copy_kernel,
        out_shape=jax.ShapeDtypeStruct((bins, rows, BLOCK), jnp.bfloat16),
        in_specs=[vmem],
        out_specs=vmem,
        compiler_params=params,
        name="first_arrived",
    )(chunks[first])
    places, lag_table, shift_table = pl.pallas_call(
        functools.partial(table_kernel, groups, bins, freq_dev),
        out_shape=(
            jax.ShapeDtypeStruct((groups, BLOCK), jnp.int32),
            jax.ShapeDtypeStruct((bins, 2 * BLOCK, 2 * SLOWNESS), jnp.bfloat16),
            jax.ShapeDtypeStruct((bins, 2, 2 * groups, SLOWNESS), jnp.float32),
        ),
        in_specs=[vmem],
        out_specs=(vmem, vmem, vmem),
        compiler_params=params,
        cost_estimate=pl.CostEstimate(flops=10**7, bytes_accessed=4 * 10**6, transcendentals=0),
        name="slant_tables",
    )(block_position.reshape(1, groups))
    terms = pl.pallas_call(
        functools.partial(stack_kernel, groups, bins, parts),
        out_shape=jax.ShapeDtypeStruct((groups, parts, message_rows, BLOCK), jnp.float32),
        in_specs=[vmem] * (groups + 3),
        out_specs=vmem,
        scratch_shapes=[
            pltpu.VMEM((groups, bins, rows, BLOCK), jnp.bfloat16),
        ]
        + [pltpu.VMEM((2, 2 * groups * 8, BLOCK), jnp.float32)] * bins,
        compiler_params=params,
        name="stack_and_slant",
    )(
        *[chunks[distance] for distance in range(groups)],
        places,
        lag_table,
        shift_table,
    )
    terms = terms.reshape(groups * parts, message_rows, BLOCK)
    arrived = lax.all_to_all(terms, ("chan", "freq"), split_axis=0, concat_axis=0, tiled=True)
    spans, table = time_table(groups, parts, bins, slow_dev, message_rows)
    return pl.pallas_call(
        functools.partial(image_kernel, slow_dev, spans),
        out_shape=jax.ShapeDtypeStruct((1, slow_dev, LAG_TIMES), jnp.float32),
        in_specs=[vmem, vmem],
        out_specs=vmem,
        compiler_params=params,
        name="sum_of_bins",
    )(arrived, jnp.asarray(table))


def solution(mesh):
    return jax.shard_map(
        shards,
        mesh=mesh,
        in_specs=(P(None, None, "freq", "chan"), P()),
        out_specs=P("chan", "freq", None),
        check_vma=False,
    )
```

```python
import functools
import math

import jax
import jax.numpy as jnp
import numpy as np
from jax import lax
from jax.experimental import pallas as pl
from jax.experimental.pallas import tpu as pltpu
from jax.sharding import PartitionSpec as P

SEGMENTS = 32
FREQS = 256
BLOCK = 128
SLOWNESS = 256
LAG_TIMES = 512
MODULUS = 8 * FREQS * BLOCK


def unit_phase(numerator):
    quarter = MODULUS // 4
    turn = numerator & (MODULUS - 1)
    quadrant = lax.shift_right_logical(turn + quarter // 2, quarter.bit_length() - 1)
    x = (turn - quadrant * quarter).astype(jnp.float32) * (2.0 * math.pi / MODULUS)
    y = x * x
    sine = x * (1.0 + y * (-1.0 / 6 + y * (1.0 / 120 + y * (-1.0 / 5040 + y * (1.0 / 362880)))))
    cosine = 1.0 + y * (-0.5 + y * (1.0 / 24 + y * (-1.0 / 720 + y * (1.0 / 40320))))
    odd = (quadrant & 1) == 1
    first = jnp.where(odd, sine, cosine)
    second = jnp.where(odd, cosine, sine)
    first = jnp.where(((quadrant + 1) & 2) == 2, -first, first)
    second = jnp.where((quadrant & 2) == 2, -second, second)
    return first, second


def halves(value):
    high = value.astype(jnp.bfloat16)
    return high, (value - high.astype(jnp.float32)).astype(jnp.bfloat16)


def copy_kernel(in_ref, out_ref):
    out_ref[...] = in_ref[...]


def table_kernel(groups, bins, freq_dev, position_ref, place_ref, lag_ref, shift_ref):
    low_rows = lax.broadcasted_iota(jnp.int32, (8, SLOWNESS), 0)
    high_rows = lax.broadcasted_iota(jnp.int32, (BLOCK // 8, SLOWNESS), 0) * 8
    shift_rows = lax.broadcasted_iota(jnp.int32, (2 * groups, SLOWNESS), 0)
    shift_rows = jnp.where(shift_rows < groups, shift_rows, shift_rows - groups - 1) * BLOCK
    own_group = lax.axis_index("chan")
    first_bin = lax.axis_index("freq") * freq_dev + own_group * bins
    sender = lax.broadcasted_iota(jnp.int32, (groups, groups), 1)
    distance = lax.broadcasted_iota(jnp.int32, (groups, groups), 0)
    sends = lax.rem(own_group + groups - distance, groups) == sender
    places = jnp.sum(jnp.where(sends, position_ref[...], 0), axis=1, keepdims=True)
    place_ref[...] = jnp.broadcast_to(places, place_ref.shape)

    def one_bin(f, carry):
        def phases(rows):
            slow = lax.broadcasted_iota(jnp.int32, rows.shape, 1) - SLOWNESS // 2
            return unit_phase((first_bin + f) * slow * rows)

        low_cos, low_sin = phases(low_rows)
        high_cos, high_sin = phases(high_rows)
        low_cos, low_sin = low_cos[None], low_sin[None]
        high_cos, high_sin = high_cos[:, None], high_sin[:, None]
        lag_cos = (high_cos * low_cos - high_sin * low_sin).reshape(BLOCK, SLOWNESS)
        lag_sin = (high_sin * low_cos + high_cos * low_sin).reshape(BLOCK, SLOWNESS)
        cos_high, cos_low = halves(lag_cos)
        sin_high, sin_low = halves(lag_sin)
        lag_ref[f, :BLOCK, :SLOWNESS] = cos_high
        lag_ref[f, BLOCK:, :SLOWNESS] = cos_low
        lag_ref[f, :BLOCK, SLOWNESS:] = sin_high
        lag_ref[f, BLOCK:, SLOWNESS:] = sin_low
        shift_cos, shift_sin = phases(shift_rows)
        shift_ref[f, 0] = shift_cos
        shift_ref[f, 1] = shift_sin
        return carry

    lax.fori_loop(0, bins, one_bin, 0)


def chunk_kernel(distances, spec_ref, *refs):
    rows, groups, bins, _ = spec_ref.shape
    out_refs, wide_ref = refs[-1 - len(distances) : -1], refs[-1]
    own_group = lax.axis_index("chan")
    for index, (distance, out_ref) in enumerate(zip(distances, out_refs)):
        group = lax.rem(own_group + distance, groups)
        wide_ref[index] = spec_ref[:, group].astype(jnp.float32).reshape(rows * bins, BLOCK)
        for f in range(bins):
            value = wide_ref[index, pl.ds(f, rows, stride=bins), :]
            out_ref[f] = value.astype(jnp.bfloat16)


def stack_weights(groups):
    row = lax.broadcasted_iota(jnp.int32, (2 * groups, BLOCK), 0)
    lag = lax.broadcasted_iota(jnp.int32, (2 * groups, BLOCK), 1)
    delta = jnp.where(row < groups, row, row - groups)
    lag = jnp.where(row < groups, lag, lag - BLOCK)
    usable = (lag > -BLOCK) & ((delta >= 1) | (lag >= 1))
    count = SEGMENTS * (groups - delta) * (BLOCK - jnp.abs(lag))
    scale = math.sqrt(SEGMENTS / FREQS)
    return jnp.where(usable, scale / jnp.maximum(count, 1).astype(jnp.float32), 0.0)


def stack_kernel(groups, bins, parts, *refs):
    chunk_refs = refs[:groups]
    place_ref, lag_ref, shift_ref, out_ref, placed_ref, left_ref, part_ref = refs[groups:]
    rows = placed_ref.shape[2]
    windows = rows // 2
    places = place_ref[...]
    for distance, chunk_ref in enumerate(chunk_refs):
        placed_ref[places[distance, 0]] = chunk_ref[...]

    row_index = lax.broadcasted_iota(jnp.int32, (BLOCK, BLOCK), 0)
    lag_index = lax.broadcasted_iota(jnp.int32, (BLOCK, BLOCK), 1)
    mirror = jnp.where(row_index + lag_index == BLOCK - 1, 1.0, 0.0).astype(jnp.bfloat16)
    ahead = lag_index <= row_index

    for f in range(bins):
        left_ref[f] = lax.dot_general(
            mirror,
            placed_ref[:, f].reshape(groups * rows, BLOCK),
            (((1,), (1,)), ((), ())),
            preferred_element_type=jnp.float32,
        ).astype(jnp.bfloat16)

    for f in range(bins):
        right = []
        for place in range(groups):
            value = placed_ref[place, f]
            real, imag = value[:windows], value[windows:]
            right.append(
                jnp.concatenate(
                    [jnp.concatenate([real, imag], 1), jnp.concatenate([imag, -real], 1)], 0
                )
            )
        right = jnp.concatenate(right, 0)
        for delta in range(groups):
            panel = jnp.dot(
                left_ref[f, :, : rows * (groups - delta)],
                right[rows * delta :],
                preferred_element_type=jnp.float32,
            )
            for half in range(2):
                lanes = slice(half * BLOCK, (half + 1) * BLOCK)
                skewed = pltpu.roll(panel[:, lanes], 1, 1, stride=1, stride_axis=0)
                forward = jnp.where(ahead, skewed, 0.0).reshape(-1, 8, BLOCK).sum(0)
                backward = jnp.where(ahead, 0.0, skewed).reshape(-1, 8, BLOCK).sum(0)
                first = (f * 2 * groups + delta) * 8
                part_ref[half, first : first + 8] = forward
                part_ref[half, first + groups * 8 : first + groups * 8 + 8] = backward

    lags = []
    for half in range(2):
        summed = part_ref[half, pl.ds(0, bins * 2 * groups, stride=8), :]
        for sublane in range(1, 8):
            summed = summed + part_ref[half, pl.ds(sublane, bins * 2 * groups, stride=8), :]
        lags.append(summed)
    weight = stack_weights(groups)

    terms = []
    for f in range(bins):
        lag_rows = slice(f * 2 * groups, (f + 1) * 2 * groups)
        means = jnp.concatenate([half[lag_rows] * weight for half in lags], 0)
        mean_high, mean_low = halves(means)
        spread = jnp.concatenate(
            [
                jnp.concatenate([mean_high, mean_high], 1),
                jnp.concatenate([mean_low, jnp.zeros_like(mean_low)], 1),
            ],
            0,
        )
        product = jnp.dot(spread, lag_ref[f], preferred_element_type=jnp.float32)
        product = product[: 4 * groups] + product[4 * groups :]
        by_cos, by_sin = product[:, :SLOWNESS], product[:, SLOWNESS:]
        real = by_cos[: 2 * groups] - by_sin[2 * groups :]
        imag = by_sin[: 2 * groups] + by_cos[2 * groups :]
        shift_cos, shift_sin = shift_ref[f, 0], shift_ref[f, 1]
        turned_re = real * shift_cos - imag * shift_sin
        turned_im = real * shift_sin + imag * shift_cos
        terms.append(turned_re[:groups] + turned_re[groups:])
        terms.append(turned_im[:groups] + turned_im[groups:])

    slow_dev = SLOWNESS // parts
    spans = BLOCK // slow_dev
    span_index = lax.broadcasted_iota(jnp.int32, (groups, BLOCK), 1) // slow_dev
    for part in range(parts):
        source = (part % spans) * slow_dev
        lanes = slice(part // spans * BLOCK, (part // spans + 1) * BLOCK)
        for row in range(out_ref.shape[2]):
            packed = jnp.zeros((groups, BLOCK), jnp.float32)
            for span, term in enumerate(terms[row * spans : (row + 1) * spans]):
                moved = pltpu.roll(term[:, lanes], (span * slow_dev - source) % BLOCK, 1)
                packed = jnp.where(span_index == span, moved, packed)
            for delta in range(groups):
                out_ref[groups - 1 - delta, parts - 1 - part, row] = packed[delta]


def image_kernel(slow_dev, spans, term_ref, table_ref, out_ref):
    arrived = term_ref[...]
    turned = arrived.reshape(-1, BLOCK).T
    sums = []
    for odd, chosen in enumerate(spans):
        terms = jnp.concatenate(
            [turned[span * slow_dev : (span + 1) * slow_dev] for span in chosen], 1
        )
        high, low = halves(terms)
        by_high = jnp.dot(
            jnp.concatenate([high, low], 0), table_ref[odd, 0], preferred_element_type=jnp.float32
        )
        by_low = jnp.dot(high, table_ref[odd, 1], preferred_element_type=jnp.float32)
        sums.append(by_high[:slow_dev] + by_high[slow_dev:] + by_low)
    even, odd = sums
    out_ref[0, :, : LAG_TIMES // 2] = even - odd
    out_ref[0, :, LAG_TIMES // 2 :] = even + odd


def time_table(groups, parts, bins, slow_dev, message_rows):
    count = min(BLOCK // slow_dev, 2 * bins)
    spans = [[span for span in range(count) if span // 2 % 2 == odd] for odd in range(2)]
    tables = []
    for chosen in spans:
        span, group, part, row = np.meshgrid(
            chosen,
            np.arange(groups)[::-1],
            np.arange(parts)[::-1],
            np.arange(message_rows),
            indexing="ij",
        )
        entry = row * count + span
        freq = (part * groups + group) * bins + entry // 2
        lag_time = np.arange(LAG_TIMES // 2)
        angle = 2.0 * math.pi / LAG_TIMES * ((freq[..., None] * lag_time) % LAG_TIMES)
        table = np.where((entry % 2 == 0)[..., None], np.cos(angle), -np.sin(angle))
        table = table.reshape(-1, LAG_TIMES // 2).astype(np.float32)
        high = table.astype(jnp.bfloat16)
        low = (table - high.astype(np.float32)).astype(jnp.bfloat16)
        tables.append(np.stack([high, low]))
    return spans, np.stack(tables)


def shards(spectra, block_position):
    groups = lax.axis_size("chan")
    parts = lax.axis_size("freq")
    rows = spectra.shape[0] * spectra.shape[1]
    freq_dev = spectra.shape[2]
    bins = freq_dev // groups
    slow_dev = SLOWNESS // parts
    message_rows = -(-2 * bins * slow_dev // BLOCK)
    vmem = pl.BlockSpec(memory_space=pltpu.VMEM)
    anywhere = pl.BlockSpec(memory_space=pl.ANY)
    params = pltpu.CompilerParams(vmem_limit_bytes=32 * 1024 * 1024)

    whole = spectra.reshape(rows, groups, bins, BLOCK)

    def cut(distances, *earlier):
        return pl.pallas_call(
            functools.partial(chunk_kernel, distances),
            out_shape=(jax.ShapeDtypeStruct((bins, rows, BLOCK), jnp.bfloat16),) * len(distances),
            in_specs=[vmem] + [anywhere] * len(earlier),
            out_specs=(vmem,) * len(distances),
            scratch_shapes=[pltpu.VMEM((len(distances), rows * bins, BLOCK), jnp.float32)],
            compiler_params=params,
            cost_estimate=pl.CostEstimate(flops=10**7, bytes_accessed=10**6, transcendentals=0),
            name="chunks_of_bins",
        )(whole, *earlier)

    order = list(range(1, groups)) + [0]
    (first_chunk,) = cut(order[:1])
    chunks = dict(zip(order, (first_chunk, *cut(order[1:], first_chunk))))
    for distance in order[:-1]:
        pairs = [(source, (source + distance) % groups) for source in range(groups)]
        chunks[distance] = lax.ppermute(chunks[distance], "chan", pairs)
    first = order[0]
    chunks[first] = pl.pallas_call(
        copy_kernel,
        out_shape=jax.ShapeDtypeStruct((bins, rows, BLOCK), jnp.bfloat16),
        in_specs=[vmem],
        out_specs=vmem,
        compiler_params=params,
        name="first_arrived",
    )(chunks[first])
    places, lag_table, shift_table = pl.pallas_call(
        functools.partial(table_kernel, groups, bins, freq_dev),
        out_shape=(
            jax.ShapeDtypeStruct((groups, BLOCK), jnp.int32),
            jax.ShapeDtypeStruct((bins, 2 * BLOCK, 2 * SLOWNESS), jnp.bfloat16),
            jax.ShapeDtypeStruct((bins, 2, 2 * groups, SLOWNESS), jnp.float32),
        ),
        in_specs=[vmem],
        out_specs=(vmem, vmem, vmem),
        compiler_params=params,
        cost_estimate=pl.CostEstimate(flops=10**7, bytes_accessed=4 * 10**6, transcendentals=0),
        name="slant_tables",
    )(block_position.reshape(1, groups))
    terms = pl.pallas_call(
        functools.partial(stack_kernel, groups, bins, parts),
        out_shape=jax.ShapeDtypeStruct((groups, parts, message_rows, BLOCK), jnp.float32),
        in_specs=[vmem] * (groups + 3),
        out_specs=vmem,
        scratch_shapes=[
            pltpu.VMEM((groups, bins, rows, BLOCK), jnp.bfloat16),
            pltpu.VMEM((bins, BLOCK, groups * rows), jnp.bfloat16),
            pltpu.VMEM((2, bins * 2 * groups * 8, BLOCK), jnp.float32),
        ],
        compiler_params=params,
        name="stack_and_slant",
    )(
        *[chunks[distance] for distance in range(groups)],
        places,
        lag_table,
        shift_table,
    )
    terms = terms.reshape(groups * parts, message_rows, BLOCK)
    arrived = lax.all_to_all(
        terms,
        ("chan", "freq"),
        split_axis=0,
        concat_axis=0,
        axis_index_groups=[list(range(groups * parts))[::-1]],
        tiled=True,
    )
    spans, table = time_table(groups, parts, bins, slow_dev, message_rows)
    return pl.pallas_call(
        functools.partial(image_kernel, slow_dev, spans),
        out_shape=jax.ShapeDtypeStruct((1, slow_dev, LAG_TIMES), jnp.float32),
        in_specs=[vmem, vmem],
        out_specs=vmem,
        compiler_params=params,
        name="sum_of_bins",
    )(arrived, jnp.asarray(table))


def solution(mesh):
    return jax.shard_map(
        shards,
        mesh=mesh,
        in_specs=(P(None, None, "freq", "chan"), P()),
        out_specs=P("chan", "freq", None),
        check_vma=False,
    )
```

```python
import functools
import math

import jax
import jax.numpy as jnp
import numpy as np
from jax import lax
from jax.experimental import pallas as pl
from jax.experimental.pallas import tpu as pltpu
from jax.sharding import PartitionSpec as P

SEGMENTS = 32
FREQS = 256
BLOCK = 128
SLOWNESS = 256
LAG_TIMES = 512
MODULUS = 8 * FREQS * BLOCK


def unit_phase(numerator):
    quarter = MODULUS // 4
    turn = numerator & (MODULUS - 1)
    quadrant = lax.shift_right_logical(turn + quarter // 2, quarter.bit_length() - 1)
    x = (turn - quadrant * quarter).astype(jnp.float32) * (2.0 * math.pi / MODULUS)
    y = x * x
    sine = x * (1.0 + y * (-1.0 / 6 + y * (1.0 / 120 + y * (-1.0 / 5040 + y * (1.0 / 362880)))))
    cosine = 1.0 + y * (-0.5 + y * (1.0 / 24 + y * (-1.0 / 720 + y * (1.0 / 40320))))
    odd = (quadrant & 1) == 1
    first = jnp.where(odd, sine, cosine)
    second = jnp.where(odd, cosine, sine)
    first = jnp.where(((quadrant + 1) & 2) == 2, -first, first)
    second = jnp.where((quadrant & 2) == 2, -second, second)
    return first, second


def halves(value):
    high = value.astype(jnp.bfloat16)
    return high, (value - high.astype(jnp.float32)).astype(jnp.bfloat16)


def copy_kernel(in_ref, out_ref):
    out_ref[...] = in_ref[...]


def table_kernel(groups, bins, freq_dev, position_ref, place_ref, lag_ref, shift_ref):
    low_rows = lax.broadcasted_iota(jnp.int32, (8, SLOWNESS), 0)
    high_rows = lax.broadcasted_iota(jnp.int32, (BLOCK // 8, SLOWNESS), 0) * 8
    shift_rows = lax.broadcasted_iota(jnp.int32, (2 * groups, SLOWNESS), 0)
    shift_rows = jnp.where(shift_rows < groups, shift_rows, shift_rows - groups - 1) * BLOCK
    own_group = lax.axis_index("chan")
    first_bin = lax.axis_index("freq") * freq_dev + own_group * bins
    sender = lax.broadcasted_iota(jnp.int32, (groups, groups), 1)
    distance = lax.broadcasted_iota(jnp.int32, (groups, groups), 0)
    sends = lax.rem(own_group + groups - distance, groups) == sender
    places = jnp.sum(jnp.where(sends, position_ref[...], 0), axis=1, keepdims=True)
    place_ref[...] = jnp.broadcast_to(places, place_ref.shape)

    def one_bin(f, carry):
        def phases(rows):
            slow = lax.broadcasted_iota(jnp.int32, rows.shape, 1) - SLOWNESS // 2
            return unit_phase((first_bin + f) * slow * rows)

        low_cos, low_sin = phases(low_rows)
        high_cos, high_sin = phases(high_rows)
        low_cos, low_sin = low_cos[None], low_sin[None]
        high_cos, high_sin = high_cos[:, None], high_sin[:, None]
        lag_cos = (high_cos * low_cos - high_sin * low_sin).reshape(BLOCK, SLOWNESS)
        lag_sin = (high_sin * low_cos + high_cos * low_sin).reshape(BLOCK, SLOWNESS)
        cos_high, cos_low = halves(lag_cos)
        sin_high, sin_low = halves(lag_sin)
        lag_ref[f, :BLOCK, :SLOWNESS] = cos_high
        lag_ref[f, BLOCK:, :SLOWNESS] = cos_low
        lag_ref[f, :BLOCK, SLOWNESS:] = sin_high
        lag_ref[f, BLOCK:, SLOWNESS:] = sin_low
        shift_cos, shift_sin = phases(shift_rows)
        shift_ref[f, 0] = shift_cos
        shift_ref[f, 1] = shift_sin
        return carry

    lax.fori_loop(0, bins, one_bin, 0)


def chunk_kernel(distances, spec_ref, *refs):
    rows, groups, bins, _ = spec_ref.shape
    out_refs, wide_ref = refs[-1 - len(distances) : -1], refs[-1]
    own_group = lax.axis_index("chan")
    for index, (distance, out_ref) in enumerate(zip(distances, out_refs)):
        group = lax.rem(own_group + distance, groups)
        wide_ref[index] = spec_ref[:, group].astype(jnp.float32).reshape(rows * bins, BLOCK)
        for f in range(bins):
            value = wide_ref[index, pl.ds(f, rows, stride=bins), :]
            out_ref[f] = value.astype(jnp.bfloat16)


def stack_weights(groups):
    row = lax.broadcasted_iota(jnp.int32, (2 * groups, BLOCK), 0)
    lag = lax.broadcasted_iota(jnp.int32, (2 * groups, BLOCK), 1)
    delta = jnp.where(row < groups, row, row - groups)
    lag = jnp.where(row < groups, lag, lag - BLOCK)
    usable = (lag > -BLOCK) & ((delta >= 1) | (lag >= 1))
    count = SEGMENTS * (groups - delta) * (BLOCK - jnp.abs(lag))
    scale = math.sqrt(SEGMENTS / FREQS)
    return jnp.where(usable, scale / jnp.maximum(count, 1).astype(jnp.float32), 0.0)


def stack_kernel(groups, bins, parts, *refs):
    chunk_refs = refs[:groups]
    place_ref, lag_ref, shift_ref, out_ref, right_ref, left_ref, part_ref = refs[groups:]
    rows = right_ref.shape[1] // groups
    windows = rows // 2
    places = place_ref[...]
    for distance, chunk_ref in enumerate(chunk_refs):
        here = pl.multiple_of(places[distance, 0] * rows, rows)
        for f in range(bins):
            value = chunk_ref[f]
            right_ref[f, pl.ds(here, rows), :BLOCK] = value
            turned = jnp.concatenate([value[windows:], -value[:windows]], 0)
            right_ref[f, pl.ds(here, rows), BLOCK:] = turned

    row_index = lax.broadcasted_iota(jnp.int32, (BLOCK, BLOCK), 0)
    lag_index = lax.broadcasted_iota(jnp.int32, (BLOCK, BLOCK), 1)
    mirror = jnp.where(row_index + lag_index == BLOCK - 1, 1.0, 0.0).astype(jnp.bfloat16)
    behind = (lag_index - row_index)[:8]

    for f in range(bins):
        left_ref[f] = lax.dot_general(
            mirror,
            right_ref[f, :, :BLOCK],
            (((1,), (1,)), ((), ())),
            preferred_element_type=jnp.float32,
        ).astype(jnp.bfloat16)

    for f in range(bins):
        for delta in range(groups):
            panel = jnp.dot(
                left_ref[f, :, : rows * (groups - delta)],
                right_ref[f, rows * delta :],
                preferred_element_type=jnp.float32,
            )
            for half in range(2):
                lanes = slice(half * BLOCK, (half + 1) * BLOCK)
                skewed = pltpu.roll(panel[:, lanes], 1, 1, stride=1, stride_axis=0)
                total = skewed[:8]
                backward = jnp.where(behind > 0, total, 0.0)
                for row in range(8, BLOCK, 8):
                    total = total + skewed[row : row + 8]
                    backward = jnp.where(behind > row, total, backward)
                first = (f * 2 * groups + delta) * 8
                part_ref[half, first : first + 8] = total - backward
                part_ref[half, first + groups * 8 : first + groups * 8 + 8] = backward

    lags = []
    for half in range(2):
        summed = part_ref[half, pl.ds(0, bins * 2 * groups, stride=8), :]
        for sublane in range(1, 8):
            summed = summed + part_ref[half, pl.ds(sublane, bins * 2 * groups, stride=8), :]
        lags.append(summed)
    weight = stack_weights(groups)

    terms = []
    for f in range(bins):
        lag_rows = slice(f * 2 * groups, (f + 1) * 2 * groups)
        means = jnp.concatenate([half[lag_rows] * weight for half in lags], 0)
        mean_high, mean_low = halves(means)
        spread = jnp.concatenate(
            [
                jnp.concatenate([mean_high, mean_high], 1),
                jnp.concatenate([mean_low, jnp.zeros_like(mean_low)], 1),
            ],
            0,
        )
        product = jnp.dot(spread, lag_ref[f], preferred_element_type=jnp.float32)
        product = product[: 4 * groups] + product[4 * groups :]
        by_cos, by_sin = product[:, :SLOWNESS], product[:, SLOWNESS:]
        real = by_cos[: 2 * groups] - by_sin[2 * groups :]
        imag = by_sin[: 2 * groups] + by_cos[2 * groups :]
        shift_cos, shift_sin = shift_ref[f, 0], shift_ref[f, 1]
        turned_re = real * shift_cos - imag * shift_sin
        turned_im = real * shift_sin + imag * shift_cos
        terms.append(turned_re[:groups] + turned_re[groups:])
        terms.append(turned_im[:groups] + turned_im[groups:])

    slow_dev = SLOWNESS // parts
    spans = BLOCK // slow_dev
    span_index = lax.broadcasted_iota(jnp.int32, (groups, BLOCK), 1) // slow_dev
    for part in range(parts):
        source = (part % spans) * slow_dev
        lanes = slice(part // spans * BLOCK, (part // spans + 1) * BLOCK)
        for row in range(out_ref.shape[2]):
            packed = jnp.zeros((groups, BLOCK), jnp.float32)
            for span, term in enumerate(terms[row * spans : (row + 1) * spans]):
                moved = pltpu.roll(term[:, lanes], (span * slow_dev - source) % BLOCK, 1)
                packed = jnp.where(span_index == span, moved, packed)
            for delta in range(groups):
                out_ref[groups - 1 - delta, parts - 1 - part, row] = packed[delta]


def image_kernel(slow_dev, spans, term_ref, table_ref, out_ref):
    arrived = term_ref[...]
    turned = arrived.reshape(-1, BLOCK).T
    sums = []
    for odd, chosen in enumerate(spans):
        terms = jnp.concatenate(
            [turned[span * slow_dev : (span + 1) * slow_dev] for span in chosen], 1
        )
        high, low = halves(terms)
        by_high = jnp.dot(
            jnp.concatenate([high, low], 0), table_ref[odd, 0], preferred_element_type=jnp.float32
        )
        by_low = jnp.dot(high, table_ref[odd, 1], preferred_element_type=jnp.float32)
        sums.append(by_high[:slow_dev] + by_high[slow_dev:] + by_low)
    even, odd = sums
    out_ref[0, :, : LAG_TIMES // 2] = even - odd
    out_ref[0, :, LAG_TIMES // 2 :] = even + odd


def time_table(groups, parts, bins, slow_dev, message_rows):
    count = min(BLOCK // slow_dev, 2 * bins)
    spans = [[span for span in range(count) if span // 2 % 2 == odd] for odd in range(2)]
    tables = []
    for chosen in spans:
        span, group, part, row = np.meshgrid(
            chosen,
            np.arange(groups)[::-1],
            np.arange(parts)[::-1],
            np.arange(message_rows),
            indexing="ij",
        )
        entry = row * count + span
        freq = (part * groups + group) * bins + entry // 2
        lag_time = np.arange(LAG_TIMES // 2)
        angle = 2.0 * math.pi / LAG_TIMES * ((freq[..., None] * lag_time) % LAG_TIMES)
        table = np.where((entry % 2 == 0)[..., None], np.cos(angle), -np.sin(angle))
        table = table.reshape(-1, LAG_TIMES // 2).astype(np.float32)
        high = table.astype(jnp.bfloat16)
        low = (table - high.astype(np.float32)).astype(jnp.bfloat16)
        tables.append(np.stack([high, low]))
    return spans, np.stack(tables)


def shards(spectra, block_position):
    groups = lax.axis_size("chan")
    parts = lax.axis_size("freq")
    rows = spectra.shape[0] * spectra.shape[1]
    freq_dev = spectra.shape[2]
    bins = freq_dev // groups
    slow_dev = SLOWNESS // parts
    message_rows = -(-2 * bins * slow_dev // BLOCK)
    vmem = pl.BlockSpec(memory_space=pltpu.VMEM)
    anywhere = pl.BlockSpec(memory_space=pl.ANY)
    params = pltpu.CompilerParams(vmem_limit_bytes=32 * 1024 * 1024)

    whole = spectra.reshape(rows, groups, bins, BLOCK)

    def cut(distances, *earlier):
        return pl.pallas_call(
            functools.partial(chunk_kernel, distances),
            out_shape=(jax.ShapeDtypeStruct((bins, rows, BLOCK), jnp.bfloat16),) * len(distances),
            in_specs=[vmem] + [anywhere] * len(earlier),
            out_specs=(vmem,) * len(distances),
            scratch_shapes=[pltpu.VMEM((len(distances), rows * bins, BLOCK), jnp.float32)],
            compiler_params=params,
            cost_estimate=pl.CostEstimate(flops=10**7, bytes_accessed=10**6, transcendentals=0),
            name="chunks_of_bins",
        )(whole, *earlier)

    order = list(range(1, groups)) + [0]
    (first_chunk,) = cut(order[:1])
    chunks = dict(zip(order, (first_chunk, *cut(order[1:], first_chunk))))
    for distance in order[:-1]:
        pairs = [(source, (source + distance) % groups) for source in range(groups)]
        chunks[distance] = lax.ppermute(chunks[distance], "chan", pairs)
    first = order[0]
    chunks[first] = pl.pallas_call(
        copy_kernel,
        out_shape=jax.ShapeDtypeStruct((bins, rows, BLOCK), jnp.bfloat16),
        in_specs=[vmem],
        out_specs=vmem,
        compiler_params=params,
        name="first_arrived",
    )(chunks[first])
    places, lag_table, shift_table = pl.pallas_call(
        functools.partial(table_kernel, groups, bins, freq_dev),
        out_shape=(
            jax.ShapeDtypeStruct((groups, BLOCK), jnp.int32),
            jax.ShapeDtypeStruct((bins, 2 * BLOCK, 2 * SLOWNESS), jnp.bfloat16),
            jax.ShapeDtypeStruct((bins, 2, 2 * groups, SLOWNESS), jnp.float32),
        ),
        in_specs=[vmem],
        out_specs=(vmem, vmem, vmem),
        compiler_params=params,
        cost_estimate=pl.CostEstimate(flops=10**7, bytes_accessed=4 * 10**6, transcendentals=0),
        name="slant_tables",
    )(block_position.reshape(1, groups))
    terms = pl.pallas_call(
        functools.partial(stack_kernel, groups, bins, parts),
        out_shape=jax.ShapeDtypeStruct((groups, parts, message_rows, BLOCK), jnp.float32),
        in_specs=[vmem] * (groups + 3),
        out_specs=vmem,
        scratch_shapes=[
            pltpu.VMEM((bins, groups * rows, 2 * BLOCK), jnp.bfloat16),
            pltpu.VMEM((bins, BLOCK, groups * rows), jnp.bfloat16),
            pltpu.VMEM((2, bins * 2 * groups * 8, BLOCK), jnp.float32),
        ],
        compiler_params=params,
        name="stack_and_slant",
    )(
        *[chunks[distance] for distance in range(groups)],
        places,
        lag_table,
        shift_table,
    )
    terms = terms.reshape(groups * parts, message_rows, BLOCK)
    arrived = lax.all_to_all(
        terms,
        ("chan", "freq"),
        split_axis=0,
        concat_axis=0,
        axis_index_groups=[list(range(groups * parts))[::-1]],
        tiled=True,
    )
    spans, table = time_table(groups, parts, bins, slow_dev, message_rows)
    return pl.pallas_call(
        functools.partial(image_kernel, slow_dev, spans),
        out_shape=jax.ShapeDtypeStruct((1, slow_dev, LAG_TIMES), jnp.float32),
        in_specs=[vmem, vmem],
        out_specs=vmem,
        compiler_params=params,
        name="sum_of_bins",
    )(arrived, jnp.asarray(table))


def solution(mesh):
    return jax.shard_map(
        shards,
        mesh=mesh,
        in_specs=(P(None, None, "freq", "chan"), P()),
        out_specs=P("chan", "freq", None),
        check_vma=False,
    )
```

```python
import functools
import math

import jax
import jax.numpy as jnp
import numpy as np
from jax import lax
from jax.experimental import pallas as pl
from jax.experimental.pallas import tpu as pltpu
from jax.sharding import PartitionSpec as P

SEGMENTS = 32
FREQS = 256
BLOCK = 128
SLOWNESS = 256
LAG_TIMES = 512
MODULUS = 8 * FREQS * BLOCK


def unit_phase(numerator):
    quarter = MODULUS // 4
    turn = numerator & (MODULUS - 1)
    quadrant = lax.shift_right_logical(turn + quarter // 2, quarter.bit_length() - 1)
    x = (turn - quadrant * quarter).astype(jnp.float32) * (2.0 * math.pi / MODULUS)
    y = x * x
    sine = x * (1.0 + y * (-1.0 / 6 + y * (1.0 / 120 + y * (-1.0 / 5040 + y * (1.0 / 362880)))))
    cosine = 1.0 + y * (-0.5 + y * (1.0 / 24 + y * (-1.0 / 720 + y * (1.0 / 40320))))
    odd = (quadrant & 1) == 1
    first = jnp.where(odd, sine, cosine)
    second = jnp.where(odd, cosine, sine)
    first = jnp.where(((quadrant + 1) & 2) == 2, -first, first)
    second = jnp.where((quadrant & 2) == 2, -second, second)
    return first, second


def halves(value):
    high = value.astype(jnp.bfloat16)
    return high, (value - high.astype(jnp.float32)).astype(jnp.bfloat16)


def copy_kernel(in_ref, out_ref):
    out_ref[...] = in_ref[...]


def table_kernel(groups, bins, freq_dev, position_ref, place_ref, lag_ref, shift_ref):
    low_rows = lax.broadcasted_iota(jnp.int32, (8, SLOWNESS), 0)
    high_rows = lax.broadcasted_iota(jnp.int32, (BLOCK // 8, SLOWNESS), 0) * 8
    shift_rows = lax.broadcasted_iota(jnp.int32, (2 * groups, SLOWNESS), 0)
    shift_rows = jnp.where(shift_rows < groups, shift_rows, shift_rows - groups - 1) * BLOCK
    own_group = lax.axis_index("chan")
    first_bin = lax.axis_index("freq") * freq_dev + own_group * bins
    sender = lax.broadcasted_iota(jnp.int32, (groups, groups), 1)
    distance = lax.broadcasted_iota(jnp.int32, (groups, groups), 0)
    sends = lax.rem(own_group + groups - distance, groups) == sender
    places = jnp.sum(jnp.where(sends, position_ref[...], 0), axis=1, keepdims=True)
    place_ref[...] = jnp.broadcast_to(places, place_ref.shape)

    def one_bin(f, carry):
        def phases(rows):
            slow = lax.broadcasted_iota(jnp.int32, rows.shape, 1) - SLOWNESS // 2
            return unit_phase((first_bin + f) * slow * rows)

        low_cos, low_sin = phases(low_rows)
        high_cos, high_sin = phases(high_rows)
        low_cos, low_sin = low_cos[None], low_sin[None]
        high_cos, high_sin = high_cos[:, None], high_sin[:, None]
        lag_cos = (high_cos * low_cos - high_sin * low_sin).reshape(BLOCK, SLOWNESS)
        lag_sin = (high_sin * low_cos + high_cos * low_sin).reshape(BLOCK, SLOWNESS)
        cos_high, cos_low = halves(lag_cos)
        sin_high, sin_low = halves(lag_sin)
        lag_ref[f, :BLOCK, :SLOWNESS] = cos_high
        lag_ref[f, BLOCK:, :SLOWNESS] = cos_low
        lag_ref[f, :BLOCK, SLOWNESS:] = sin_high
        lag_ref[f, BLOCK:, SLOWNESS:] = sin_low
        shift_cos, shift_sin = phases(shift_rows)
        shift_ref[f, 0] = shift_cos
        shift_ref[f, 1] = shift_sin
        return carry

    lax.fori_loop(0, bins, one_bin, 0)


def chunk_kernel(cuts, spec_ref, *refs):
    rows, groups, bins, _ = spec_ref.shape
    out_refs, wide_ref = refs[-1 - len(cuts) : -1], refs[-1]
    own_group = lax.axis_index("chan")
    widened = []
    for (distance, start, size), out_ref in zip(cuts, out_refs):
        if distance not in widened:
            group = lax.rem(own_group + distance, groups)
            index = len(widened)
            wide_ref[index] = spec_ref[:, group].astype(jnp.float32).reshape(rows * bins, BLOCK)
            widened.append(distance)
        for f in range(size):
            value = wide_ref[widened.index(distance), pl.ds(start + f, rows, stride=bins), :]
            out_ref[f] = value.astype(jnp.bfloat16)


def stack_weights(groups):
    row = lax.broadcasted_iota(jnp.int32, (2 * groups, BLOCK), 0)
    lag = lax.broadcasted_iota(jnp.int32, (2 * groups, BLOCK), 1)
    delta = jnp.where(row < groups, row, row - groups)
    lag = jnp.where(row < groups, lag, lag - BLOCK)
    usable = (lag > -BLOCK) & ((delta >= 1) | (lag >= 1))
    count = SEGMENTS * (groups - delta) * (BLOCK - jnp.abs(lag))
    scale = math.sqrt(SEGMENTS / FREQS)
    return jnp.where(usable, scale / jnp.maximum(count, 1).astype(jnp.float32), 0.0)


def stack_kernel(groups, start, bins, parts, *refs):
    chunk_refs = refs[:groups]
    place_ref, lag_ref, shift_ref = refs[groups : groups + 3]
    earlier_refs = refs[groups + 3 : -4]
    out_ref, placed_ref, left_ref, part_ref = refs[-4:]
    rows = placed_ref.shape[2]
    windows = rows // 2
    places = place_ref[...]
    for distance, chunk_ref in enumerate(chunk_refs):
        placed_ref[places[distance, 0]] = chunk_ref[...]

    row_index = lax.broadcasted_iota(jnp.int32, (BLOCK, BLOCK), 0)
    lag_index = lax.broadcasted_iota(jnp.int32, (BLOCK, BLOCK), 1)
    mirror = jnp.where(row_index + lag_index == BLOCK - 1, 1.0, 0.0).astype(jnp.bfloat16)
    ahead = lag_index <= row_index

    for f in range(bins):
        left_ref[f] = lax.dot_general(
            mirror,
            placed_ref[:, f].reshape(groups * rows, BLOCK),
            (((1,), (1,)), ((), ())),
            preferred_element_type=jnp.float32,
        ).astype(jnp.bfloat16)

    for f in range(bins):
        right = []
        for place in range(groups):
            value = placed_ref[place, f]
            real, imag = value[:windows], value[windows:]
            right.append(
                jnp.concatenate(
                    [jnp.concatenate([real, imag], 1), jnp.concatenate([imag, -real], 1)], 0
                )
            )
        right = jnp.concatenate(right, 0)
        for delta in range(groups):
            panel = jnp.dot(
                left_ref[f, :, : rows * (groups - delta)],
                right[rows * delta :],
                preferred_element_type=jnp.float32,
            )
            for half in range(2):
                lanes = slice(half * BLOCK, (half + 1) * BLOCK)
                skewed = pltpu.roll(panel[:, lanes], 1, 1, stride=1, stride_axis=0)
                forward = jnp.where(ahead, skewed, 0.0).reshape(-1, 8, BLOCK).sum(0)
                backward = jnp.where(ahead, 0.0, skewed).reshape(-1, 8, BLOCK).sum(0)
                first = (f * 2 * groups + delta) * 8
                part_ref[half, first : first + 8] = forward
                part_ref[half, first + groups * 8 : first + groups * 8 + 8] = backward

    lags = []
    for half in range(2):
        summed = part_ref[half, pl.ds(0, bins * 2 * groups, stride=8), :]
        for sublane in range(1, 8):
            summed = summed + part_ref[half, pl.ds(sublane, bins * 2 * groups, stride=8), :]
        lags.append(summed)
    weight = stack_weights(groups)

    terms = []
    for f in range(bins):
        lag_rows = slice(f * 2 * groups, (f + 1) * 2 * groups)
        means = jnp.concatenate([half[lag_rows] * weight for half in lags], 0)
        mean_high, mean_low = halves(means)
        spread = jnp.concatenate(
            [
                jnp.concatenate([mean_high, mean_high], 1),
                jnp.concatenate([mean_low, jnp.zeros_like(mean_low)], 1),
            ],
            0,
        )
        product = jnp.dot(spread, lag_ref[start + f], preferred_element_type=jnp.float32)
        product = product[: 4 * groups] + product[4 * groups :]
        by_cos, by_sin = product[:, :SLOWNESS], product[:, SLOWNESS:]
        real = by_cos[: 2 * groups] - by_sin[2 * groups :]
        imag = by_sin[: 2 * groups] + by_cos[2 * groups :]
        shift_cos, shift_sin = shift_ref[start + f, 0], shift_ref[start + f, 1]
        turned_re = real * shift_cos - imag * shift_sin
        turned_im = real * shift_sin + imag * shift_cos
        terms.append(turned_re[:groups] + turned_re[groups:])
        terms.append(turned_im[:groups] + turned_im[groups:])

    if parts is None:
        for entry, term in enumerate(terms):
            out_ref[entry] = term
        return
    for earlier_ref in reversed(earlier_refs):
        terms = [earlier_ref[entry] for entry in range(earlier_ref.shape[0])] + terms
    slow_dev = SLOWNESS // parts
    spans = BLOCK // slow_dev
    span_index = lax.broadcasted_iota(jnp.int32, (groups, BLOCK), 1) // slow_dev
    for part in range(parts):
        source = (part % spans) * slow_dev
        lanes = slice(part // spans * BLOCK, (part // spans + 1) * BLOCK)
        for row in range(out_ref.shape[2]):
            packed = jnp.zeros((groups, BLOCK), jnp.float32)
            for span, term in enumerate(terms[row * spans : (row + 1) * spans]):
                moved = pltpu.roll(term[:, lanes], (span * slow_dev - source) % BLOCK, 1)
                packed = jnp.where(span_index == span, moved, packed)
            for delta in range(groups):
                out_ref[groups - 1 - delta, parts - 1 - part, row] = packed[delta]


def image_kernel(slow_dev, spans, term_ref, table_ref, out_ref):
    arrived = term_ref[...]
    turned = arrived.reshape(-1, BLOCK).T
    sums = []
    for odd, chosen in enumerate(spans):
        terms = jnp.concatenate(
            [turned[span * slow_dev : (span + 1) * slow_dev] for span in chosen], 1
        )
        high, low = halves(terms)
        by_high = jnp.dot(
            jnp.concatenate([high, low], 0), table_ref[odd, 0], preferred_element_type=jnp.float32
        )
        by_low = jnp.dot(high, table_ref[odd, 1], preferred_element_type=jnp.float32)
        sums.append(by_high[:slow_dev] + by_high[slow_dev:] + by_low)
    even, odd = sums
    out_ref[0, :, : LAG_TIMES // 2] = even - odd
    out_ref[0, :, LAG_TIMES // 2 :] = even + odd


def time_table(groups, parts, bins, slow_dev, message_rows):
    count = min(BLOCK // slow_dev, 2 * bins)
    spans = [[span for span in range(count) if span // 2 % 2 == odd] for odd in range(2)]
    tables = []
    for chosen in spans:
        span, group, part, row = np.meshgrid(
            chosen,
            np.arange(groups)[::-1],
            np.arange(parts)[::-1],
            np.arange(message_rows),
            indexing="ij",
        )
        entry = row * count + span
        freq = (part * groups + group) * bins + entry // 2
        lag_time = np.arange(LAG_TIMES // 2)
        angle = 2.0 * math.pi / LAG_TIMES * ((freq[..., None] * lag_time) % LAG_TIMES)
        table = np.where((entry % 2 == 0)[..., None], np.cos(angle), -np.sin(angle))
        table = table.reshape(-1, LAG_TIMES // 2).astype(np.float32)
        high = table.astype(jnp.bfloat16)
        low = (table - high.astype(np.float32)).astype(jnp.bfloat16)
        tables.append(np.stack([high, low]))
    return spans, np.stack(tables)


def shards(spectra, block_position):
    groups = lax.axis_size("chan")
    parts = lax.axis_size("freq")
    rows = spectra.shape[0] * spectra.shape[1]
    freq_dev = spectra.shape[2]
    bins = freq_dev // groups
    slow_dev = SLOWNESS // parts
    message_rows = -(-2 * bins * slow_dev // BLOCK)
    vmem = pl.BlockSpec(memory_space=pltpu.VMEM)
    anywhere = pl.BlockSpec(memory_space=pl.ANY)
    params = pltpu.CompilerParams(vmem_limit_bytes=32 * 1024 * 1024)

    whole = spectra.reshape(rows, groups, bins, BLOCK)

    def cut(cuts, *earlier):
        distances = {distance for distance, _, _ in cuts}
        return pl.pallas_call(
            functools.partial(chunk_kernel, cuts),
            out_shape=tuple(
                jax.ShapeDtypeStruct((size, rows, BLOCK), jnp.bfloat16) for _, _, size in cuts
            ),
            in_specs=[vmem] + [anywhere] * len(earlier),
            out_specs=(vmem,) * len(cuts),
            scratch_shapes=[pltpu.VMEM((len(distances), rows * bins, BLOCK), jnp.float32)],
            compiler_params=params,
            cost_estimate=pl.CostEstimate(flops=10**7, bytes_accessed=10**6, transcendentals=0),
            name="chunks_of_bins",
        )(whole, *earlier)

    late = bins // 2
    pieces = [(0, bins - late), (bins - late, late)] if late else [(0, bins)]
    cuts = [(distance, *piece) for piece in pieces for distance in list(range(1, groups)) + [0]]
    (first_chunk,) = cut(cuts[:1])
    chunks = dict(zip(cuts, (first_chunk, *cut(cuts[1:], first_chunk))))
    for key in cuts:
        if key[0]:
            pairs = [(source, (source + key[0]) % groups) for source in range(groups)]
            chunks[key] = lax.ppermute(chunks[key], "chan", pairs)
    chunks[cuts[0]] = pl.pallas_call(
        copy_kernel,
        out_shape=jax.ShapeDtypeStruct(first_chunk.shape, jnp.bfloat16),
        in_specs=[vmem],
        out_specs=vmem,
        compiler_params=params,
        name="first_arrived",
    )(chunks[cuts[0]])
    places, lag_table, shift_table = pl.pallas_call(
        functools.partial(table_kernel, groups, bins, freq_dev),
        out_shape=(
            jax.ShapeDtypeStruct((groups, BLOCK), jnp.int32),
            jax.ShapeDtypeStruct((bins, 2 * BLOCK, 2 * SLOWNESS), jnp.bfloat16),
            jax.ShapeDtypeStruct((bins, 2, 2 * groups, SLOWNESS), jnp.float32),
        ),
        in_specs=[vmem],
        out_specs=(vmem, vmem, vmem),
        compiler_params=params,
        cost_estimate=pl.CostEstimate(flops=10**7, bytes_accessed=4 * 10**6, transcendentals=0),
        name="slant_tables",
    )(block_position.reshape(1, groups))
    earlier = []
    for start, size in pieces:
        last = start + size == bins
        shape = (groups, parts, message_rows, BLOCK) if last else (2 * size, groups, SLOWNESS)
        terms = pl.pallas_call(
            functools.partial(stack_kernel, groups, start, size, parts if last else None),
            out_shape=jax.ShapeDtypeStruct(shape, jnp.float32),
            in_specs=[vmem] * (groups + 3 + len(earlier)),
            out_specs=vmem,
            scratch_shapes=[
                pltpu.VMEM((groups, size, rows, BLOCK), jnp.bfloat16),
                pltpu.VMEM((size, BLOCK, groups * rows), jnp.bfloat16),
                pltpu.VMEM((2, size * 2 * groups * 8, BLOCK), jnp.float32),
            ],
            compiler_params=params,
            cost_estimate=pl.CostEstimate(
                flops=2 * 10**8, bytes_accessed=4 * 10**6, transcendentals=0
            ),
            name="stack_and_slant",
        )(
            *[chunks[distance, start, size] for distance in range(groups)],
            places,
            lag_table,
            shift_table,
            *earlier,
        )
        earlier.append(terms)
    terms = terms.reshape(groups * parts, message_rows, BLOCK)
    arrived = lax.all_to_all(
        terms,
        ("chan", "freq"),
        split_axis=0,
        concat_axis=0,
        axis_index_groups=[list(range(groups * parts))[::-1]],
        tiled=True,
    )
    spans, table = time_table(groups, parts, bins, slow_dev, message_rows)
    return pl.pallas_call(
        functools.partial(image_kernel, slow_dev, spans),
        out_shape=jax.ShapeDtypeStruct((1, slow_dev, LAG_TIMES), jnp.float32),
        in_specs=[vmem, vmem],
        out_specs=vmem,
        compiler_params=params,
        name="sum_of_bins",
    )(arrived, jnp.asarray(table))


def solution(mesh):
    return jax.shard_map(
        shards,
        mesh=mesh,
        in_specs=(P(None, None, "freq", "chan"), P()),
        out_specs=P("chan", "freq", None),
        check_vma=False,
    )
```

```python
import functools
import math

import jax
import jax.numpy as jnp
import numpy as np
from jax import lax
from jax.experimental import pallas as pl
from jax.experimental.pallas import tpu as pltpu
from jax.sharding import PartitionSpec as P

SEGMENTS = 32
FREQS = 256
BLOCK = 128
SLOWNESS = 256
LAG_TIMES = 512
MODULUS = 8 * FREQS * BLOCK


def unit_phase(numerator):
    quarter = MODULUS // 4
    turn = numerator & (MODULUS - 1)
    quadrant = lax.shift_right_logical(turn + quarter // 2, quarter.bit_length() - 1)
    x = (turn - quadrant * quarter).astype(jnp.float32) * (2.0 * math.pi / MODULUS)
    y = x * x
    sine = x * (1.0 + y * (-1.0 / 6 + y * (1.0 / 120 + y * (-1.0 / 5040 + y * (1.0 / 362880)))))
    cosine = 1.0 + y * (-0.5 + y * (1.0 / 24 + y * (-1.0 / 720 + y * (1.0 / 40320))))
    odd = (quadrant & 1) == 1
    first = jnp.where(odd, sine, cosine)
    second = jnp.where(odd, cosine, sine)
    first = jnp.where(((quadrant + 1) & 2) == 2, -first, first)
    second = jnp.where((quadrant & 2) == 2, -second, second)
    return first, second


def halves(value):
    high = value.astype(jnp.bfloat16)
    return high, (value - high.astype(jnp.float32)).astype(jnp.bfloat16)


def copy_kernel(in_ref, out_ref):
    out_ref[...] = in_ref[...]


def table_kernel(groups, bins, freq_dev, position_ref, place_ref, lag_ref, shift_ref):
    low_rows = lax.broadcasted_iota(jnp.int32, (8, SLOWNESS), 0)
    high_rows = lax.broadcasted_iota(jnp.int32, (BLOCK // 8, SLOWNESS), 0) * 8
    shift_rows = lax.broadcasted_iota(jnp.int32, (2 * groups, SLOWNESS), 0)
    shift_rows = jnp.where(shift_rows < groups, shift_rows, shift_rows - groups - 1) * BLOCK
    own_group = lax.axis_index("chan")
    first_bin = lax.axis_index("freq") * freq_dev + own_group * bins
    sender = lax.broadcasted_iota(jnp.int32, (groups, groups), 1)
    distance = lax.broadcasted_iota(jnp.int32, (groups, groups), 0)
    sends = lax.rem(own_group + groups - distance, groups) == sender
    places = jnp.sum(jnp.where(sends, position_ref[...], 0), axis=1, keepdims=True)
    place_ref[...] = jnp.broadcast_to(places, place_ref.shape)

    def one_bin(f, carry):
        def phases(rows):
            slow = lax.broadcasted_iota(jnp.int32, rows.shape, 1) - SLOWNESS // 2
            return unit_phase((first_bin + f) * slow * rows)

        low_cos, low_sin = phases(low_rows)
        high_cos, high_sin = phases(high_rows)
        low_cos, low_sin = low_cos[None], low_sin[None]
        high_cos, high_sin = high_cos[:, None], high_sin[:, None]
        lag_cos = (high_cos * low_cos - high_sin * low_sin).reshape(BLOCK, SLOWNESS)
        lag_sin = (high_sin * low_cos + high_cos * low_sin).reshape(BLOCK, SLOWNESS)
        cos_high, cos_low = halves(lag_cos)
        sin_high, sin_low = halves(lag_sin)
        lag_ref[f, :BLOCK, :SLOWNESS] = cos_high
        lag_ref[f, BLOCK:, :SLOWNESS] = cos_low
        lag_ref[f, :BLOCK, SLOWNESS:] = sin_high
        lag_ref[f, BLOCK:, SLOWNESS:] = sin_low
        shift_cos, shift_sin = phases(shift_rows)
        shift_ref[f, 0] = shift_cos
        shift_ref[f, 1] = shift_sin
        return carry

    lax.fori_loop(0, bins, one_bin, 0)


def chunk_kernel(cuts, spec_ref, *refs):
    rows, groups, bins, _ = spec_ref.shape
    out_refs, wide_ref = refs[-1 - len(cuts) : -1], refs[-1]
    own_group = lax.axis_index("chan")
    widened = []
    for (distance, start, size), out_ref in zip(cuts, out_refs):
        if distance not in widened:
            group = lax.rem(own_group + distance, groups)
            index = len(widened)
            wide_ref[index] = spec_ref[:, group].astype(jnp.float32).reshape(rows * bins, BLOCK)
            widened.append(distance)
        for f in range(size):
            value = wide_ref[widened.index(distance), pl.ds(start + f, rows, stride=bins), :]
            out_ref[f] = value.astype(jnp.bfloat16)


def stack_weights(groups):
    row = lax.broadcasted_iota(jnp.int32, (2 * groups, BLOCK), 0)
    lag = lax.broadcasted_iota(jnp.int32, (2 * groups, BLOCK), 1)
    delta = jnp.where(row < groups, row, row - groups)
    lag = jnp.where(row < groups, lag, lag - BLOCK)
    usable = (lag > -BLOCK) & ((delta >= 1) | (lag >= 1))
    count = SEGMENTS * (groups - delta) * (BLOCK - jnp.abs(lag))
    scale = math.sqrt(SEGMENTS / FREQS)
    return jnp.where(usable, scale / jnp.maximum(count, 1).astype(jnp.float32), 0.0)


def stack_kernel(order, start, bins, parts, *refs):
    groups = len(order)
    chunk_refs = refs[:groups]
    place_ref, lag_ref, shift_ref = refs[groups : groups + 3]
    earlier_refs = refs[groups + 3 : -4]
    out_ref, placed_ref, left_ref, part_ref = refs[-4:]
    rows = placed_ref.shape[2]
    windows = rows // 2
    places = place_ref[...]
    for distance, chunk_ref in zip(order, chunk_refs):
        placed_ref[places[distance, 0]] = chunk_ref[...]

    row_index = lax.broadcasted_iota(jnp.int32, (BLOCK, BLOCK), 0)
    lag_index = lax.broadcasted_iota(jnp.int32, (BLOCK, BLOCK), 1)
    mirror = jnp.where(row_index + lag_index == BLOCK - 1, 1.0, 0.0).astype(jnp.bfloat16)
    ahead = lag_index <= row_index

    for f in range(bins):
        left_ref[f] = lax.dot_general(
            mirror,
            placed_ref[:, f].reshape(groups * rows, BLOCK),
            (((1,), (1,)), ((), ())),
            preferred_element_type=jnp.float32,
        ).astype(jnp.bfloat16)

    for f in range(bins):
        right = []
        for place in range(groups):
            value = placed_ref[place, f]
            real, imag = value[:windows], value[windows:]
            right.append(
                jnp.concatenate(
                    [jnp.concatenate([real, imag], 1), jnp.concatenate([imag, -real], 1)], 0
                )
            )
        right = jnp.concatenate(right, 0)
        for delta in range(groups):
            panel = jnp.dot(
                left_ref[f, :, : rows * (groups - delta)],
                right[rows * delta :],
                preferred_element_type=jnp.float32,
            )
            for half in range(2):
                lanes = slice(half * BLOCK, (half + 1) * BLOCK)
                skewed = pltpu.roll(panel[:, lanes], 1, 1, stride=1, stride_axis=0)
                forward = jnp.where(ahead, skewed, 0.0).reshape(-1, 8, BLOCK).sum(0)
                backward = jnp.where(ahead, 0.0, skewed).reshape(-1, 8, BLOCK).sum(0)
                first = (f * 2 * groups + delta) * 8
                part_ref[half, first : first + 8] = forward
                part_ref[half, first + groups * 8 : first + groups * 8 + 8] = backward

    lags = []
    for half in range(2):
        summed = part_ref[half, pl.ds(0, bins * 2 * groups, stride=8), :]
        for sublane in range(1, 8):
            summed = summed + part_ref[half, pl.ds(sublane, bins * 2 * groups, stride=8), :]
        lags.append(summed)
    weight = stack_weights(groups)

    terms = []
    for f in range(bins):
        lag_rows = slice(f * 2 * groups, (f + 1) * 2 * groups)
        means = jnp.concatenate([half[lag_rows] * weight for half in lags], 0)
        mean_high, mean_low = halves(means)
        spread = jnp.concatenate(
            [
                jnp.concatenate([mean_high, mean_high], 1),
                jnp.concatenate([mean_low, jnp.zeros_like(mean_low)], 1),
            ],
            0,
        )
        product = jnp.dot(spread, lag_ref[start + f], preferred_element_type=jnp.float32)
        product = product[: 4 * groups] + product[4 * groups :]
        by_cos, by_sin = product[:, :SLOWNESS], product[:, SLOWNESS:]
        real = by_cos[: 2 * groups] - by_sin[2 * groups :]
        imag = by_sin[: 2 * groups] + by_cos[2 * groups :]
        shift_cos, shift_sin = shift_ref[start + f, 0], shift_ref[start + f, 1]
        turned_re = real * shift_cos - imag * shift_sin
        turned_im = real * shift_sin + imag * shift_cos
        terms.append(turned_re[:groups] + turned_re[groups:])
        terms.append(turned_im[:groups] + turned_im[groups:])

    if parts is None:
        for entry, term in enumerate(terms):
            out_ref[entry] = term
        return
    for earlier_ref in reversed(earlier_refs):
        terms = [earlier_ref[entry] for entry in range(earlier_ref.shape[0])] + terms
    slow_dev = SLOWNESS // parts
    spans = BLOCK // slow_dev
    span_index = lax.broadcasted_iota(jnp.int32, (groups, BLOCK), 1) // slow_dev
    for part in range(parts):
        source = (part % spans) * slow_dev
        lanes = slice(part // spans * BLOCK, (part // spans + 1) * BLOCK)
        for row in range(out_ref.shape[2]):
            packed = jnp.zeros((groups, BLOCK), jnp.float32)
            for span, term in enumerate(terms[row * spans : (row + 1) * spans]):
                moved = pltpu.roll(term[:, lanes], (span * slow_dev - source) % BLOCK, 1)
                packed = jnp.where(span_index == span, moved, packed)
            for delta in range(groups):
                out_ref[groups - 1 - delta, parts - 1 - part, row] = packed[delta]


def image_kernel(slow_dev, spans, term_ref, table_ref, out_ref):
    arrived = term_ref[...]
    turned = arrived.reshape(-1, BLOCK).T
    sums = []
    for odd, chosen in enumerate(spans):
        terms = jnp.concatenate(
            [turned[span * slow_dev : (span + 1) * slow_dev] for span in chosen], 1
        )
        high, low = halves(terms)
        by_high = jnp.dot(
            jnp.concatenate([high, low], 0), table_ref[odd, 0], preferred_element_type=jnp.float32
        )
        by_low = jnp.dot(high, table_ref[odd, 1], preferred_element_type=jnp.float32)
        sums.append(by_high[:slow_dev] + by_high[slow_dev:] + by_low)
    even, odd = sums
    out_ref[0, :, : LAG_TIMES // 2] = even - odd
    out_ref[0, :, LAG_TIMES // 2 :] = even + odd


def time_table(groups, parts, bins, slow_dev, message_rows):
    count = min(BLOCK // slow_dev, 2 * bins)
    spans = [[span for span in range(count) if span // 2 % 2 == odd] for odd in range(2)]
    tables = []
    for chosen in spans:
        span, group, part, row = np.meshgrid(
            chosen,
            np.arange(groups)[::-1],
            np.arange(parts)[::-1],
            np.arange(message_rows),
            indexing="ij",
        )
        entry = row * count + span
        freq = (part * groups + group) * bins + entry // 2
        lag_time = np.arange(LAG_TIMES // 2)
        angle = 2.0 * math.pi / LAG_TIMES * ((freq[..., None] * lag_time) % LAG_TIMES)
        table = np.where((entry % 2 == 0)[..., None], np.cos(angle), -np.sin(angle))
        table = table.reshape(-1, LAG_TIMES // 2).astype(np.float32)
        high = table.astype(jnp.bfloat16)
        low = (table - high.astype(np.float32)).astype(jnp.bfloat16)
        tables.append(np.stack([high, low]))
    return spans, np.stack(tables)


def shards(spectra, block_position):
    groups = lax.axis_size("chan")
    parts = lax.axis_size("freq")
    rows = spectra.shape[0] * spectra.shape[1]
    freq_dev = spectra.shape[2]
    bins = freq_dev // groups
    slow_dev = SLOWNESS // parts
    message_rows = -(-2 * bins * slow_dev // BLOCK)
    vmem = pl.BlockSpec(memory_space=pltpu.VMEM)
    anywhere = pl.BlockSpec(memory_space=pl.ANY)
    params = pltpu.CompilerParams(vmem_limit_bytes=32 * 1024 * 1024)

    whole = spectra.reshape(rows, groups, bins, BLOCK)

    def cut(cuts, *earlier):
        distances = {distance for distance, _, _ in cuts}
        return pl.pallas_call(
            functools.partial(chunk_kernel, cuts),
            out_shape=tuple(
                jax.ShapeDtypeStruct((size, rows, BLOCK), jnp.bfloat16) for _, _, size in cuts
            ),
            in_specs=[vmem] + [anywhere] * len(earlier),
            out_specs=(vmem,) * len(cuts),
            scratch_shapes=[pltpu.VMEM((len(distances), rows * bins, BLOCK), jnp.float32)],
            compiler_params=params,
            cost_estimate=pl.CostEstimate(flops=10**7, bytes_accessed=10**6, transcendentals=0),
            name="chunks_of_bins",
        )(whole, *earlier)

    late = max(1, 3 * bins // 8) if bins > 1 else 0
    pieces = [(0, bins - late), (bins - late, late)] if late else [(0, bins)]
    near_first = list(range(1, groups)) + [0]
    far_first = sorted(range(1, groups), key=lambda steps: abs(2 * steps - groups)) + [0]
    orders = [near_first, far_first][: len(pieces)]
    cuts = [(distance, *piece) for piece, order in zip(pieces, orders) for distance in order]
    (first_chunk,) = cut(cuts[:1])
    chunks = dict(zip(cuts, (first_chunk, *cut(cuts[1:], first_chunk))))
    for key in cuts:
        if key[0]:
            pairs = [(source, (source + key[0]) % groups) for source in range(groups)]
            chunks[key] = lax.ppermute(chunks[key], "chan", pairs)
    chunks[cuts[0]] = pl.pallas_call(
        copy_kernel,
        out_shape=jax.ShapeDtypeStruct(first_chunk.shape, jnp.bfloat16),
        in_specs=[vmem],
        out_specs=vmem,
        compiler_params=params,
        name="first_arrived",
    )(chunks[cuts[0]])
    places, lag_table, shift_table = pl.pallas_call(
        functools.partial(table_kernel, groups, bins, freq_dev),
        out_shape=(
            jax.ShapeDtypeStruct((groups, BLOCK), jnp.int32),
            jax.ShapeDtypeStruct((bins, 2 * BLOCK, 2 * SLOWNESS), jnp.bfloat16),
            jax.ShapeDtypeStruct((bins, 2, 2 * groups, SLOWNESS), jnp.float32),
        ),
        in_specs=[vmem],
        out_specs=(vmem, vmem, vmem),
        compiler_params=params,
        cost_estimate=pl.CostEstimate(flops=10**7, bytes_accessed=4 * 10**6, transcendentals=0),
        name="slant_tables",
    )(block_position.reshape(1, groups))
    earlier = []
    for (start, size), order in zip(pieces, orders):
        last = start + size == bins
        shape = (groups, parts, message_rows, BLOCK) if last else (2 * size, groups, SLOWNESS)
        terms = pl.pallas_call(
            functools.partial(stack_kernel, order, start, size, parts if last else None),
            out_shape=jax.ShapeDtypeStruct(shape, jnp.float32),
            in_specs=[vmem] * (groups + 3 + len(earlier)),
            out_specs=vmem,
            scratch_shapes=[
                pltpu.VMEM((groups, size, rows, BLOCK), jnp.bfloat16),
                pltpu.VMEM((size, BLOCK, groups * rows), jnp.bfloat16),
                pltpu.VMEM((2, size * 2 * groups * 8, BLOCK), jnp.float32),
            ],
            compiler_params=params,
            cost_estimate=pl.CostEstimate(
                flops=2 * 10**8, bytes_accessed=4 * 10**6, transcendentals=0
            ),
            name="stack_and_slant",
        )(
            *[chunks[distance, start, size] for distance in order],
            places,
            lag_table,
            shift_table,
            *earlier,
        )
        earlier.append(terms)
    terms = terms.reshape(groups * parts, message_rows, BLOCK)
    arrived = lax.all_to_all(
        terms,
        ("chan", "freq"),
        split_axis=0,
        concat_axis=0,
        axis_index_groups=[list(range(groups * parts))[::-1]],
        tiled=True,
    )
    spans, table = time_table(groups, parts, bins, slow_dev, message_rows)
    return pl.pallas_call(
        functools.partial(image_kernel, slow_dev, spans),
        out_shape=jax.ShapeDtypeStruct((1, slow_dev, LAG_TIMES), jnp.float32),
        in_specs=[vmem, vmem],
        out_specs=vmem,
        compiler_params=params,
        name="sum_of_bins",
    )(arrived, jnp.asarray(table))


def solution(mesh):
    return jax.shard_map(
        shards,
        mesh=mesh,
        in_specs=(P(None, None, "freq", "chan"), P()),
        out_specs=P("chan", "freq", None),
        check_vma=False,
    )
```

```python
import functools
import math

import jax
import jax.numpy as jnp
import numpy as np
from jax import lax
from jax.experimental import pallas as pl
from jax.experimental.pallas import tpu as pltpu
from jax.sharding import PartitionSpec as P

SEGMENTS = 32
FREQS = 256
BLOCK = 128
SLOWNESS = 256
LAG_TIMES = 512
MODULUS = 8 * FREQS * BLOCK


def unit_phase(numerator):
    quarter = MODULUS // 4
    turn = numerator & (MODULUS - 1)
    quadrant = lax.shift_right_logical(turn + quarter // 2, quarter.bit_length() - 1)
    x = (turn - quadrant * quarter).astype(jnp.float32) * (2.0 * math.pi / MODULUS)
    y = x * x
    sine = x * (1.0 + y * (-1.0 / 6 + y * (1.0 / 120 + y * (-1.0 / 5040 + y * (1.0 / 362880)))))
    cosine = 1.0 + y * (-0.5 + y * (1.0 / 24 + y * (-1.0 / 720 + y * (1.0 / 40320))))
    odd = (quadrant & 1) == 1
    first = jnp.where(odd, sine, cosine)
    second = jnp.where(odd, cosine, sine)
    first = jnp.where(((quadrant + 1) & 2) == 2, -first, first)
    second = jnp.where((quadrant & 2) == 2, -second, second)
    return first, second


def halves(value):
    high = value.astype(jnp.bfloat16)
    return high, (value - high.astype(jnp.float32)).astype(jnp.bfloat16)


def copy_kernel(in_ref, out_ref):
    out_ref[...] = in_ref[...]


def table_kernel(groups, bins, freq_dev, position_ref, place_ref, lag_ref, shift_ref):
    low_rows = lax.broadcasted_iota(jnp.int32, (8, SLOWNESS), 0)
    high_rows = lax.broadcasted_iota(jnp.int32, (BLOCK // 8, SLOWNESS), 0) * 8
    shift_rows = lax.broadcasted_iota(jnp.int32, (2 * groups, SLOWNESS), 0)
    shift_rows = jnp.where(shift_rows < groups, shift_rows, shift_rows - groups - 1) * BLOCK
    own_group = lax.axis_index("chan")
    first_bin = lax.axis_index("freq") * freq_dev + own_group * bins
    sender = lax.broadcasted_iota(jnp.int32, (groups, groups), 1)
    distance = lax.broadcasted_iota(jnp.int32, (groups, groups), 0)
    sends = lax.rem(own_group + groups - distance, groups) == sender
    places = jnp.sum(jnp.where(sends, position_ref[...], 0), axis=1, keepdims=True)
    place_ref[...] = jnp.broadcast_to(places, place_ref.shape)

    def one_bin(f, carry):
        def phases(rows):
            slow = lax.broadcasted_iota(jnp.int32, rows.shape, 1) - SLOWNESS // 2
            return unit_phase((first_bin + f) * slow * rows)

        low_cos, low_sin = phases(low_rows)
        high_cos, high_sin = phases(high_rows)
        low_cos, low_sin = low_cos[None], low_sin[None]
        high_cos, high_sin = high_cos[:, None], high_sin[:, None]
        lag_cos = (high_cos * low_cos - high_sin * low_sin).reshape(BLOCK, SLOWNESS)
        lag_sin = (high_sin * low_cos + high_cos * low_sin).reshape(BLOCK, SLOWNESS)
        cos_high, cos_low = halves(lag_cos)
        sin_high, sin_low = halves(lag_sin)
        lag_ref[f, :BLOCK, :SLOWNESS] = cos_high
        lag_ref[f, BLOCK:, :SLOWNESS] = cos_low
        lag_ref[f, :BLOCK, SLOWNESS:] = sin_high
        lag_ref[f, BLOCK:, SLOWNESS:] = sin_low
        shift_cos, shift_sin = phases(shift_rows)
        shift_ref[f, 0] = shift_cos
        shift_ref[f, 1] = shift_sin
        return carry

    lax.fori_loop(0, bins, one_bin, 0)


def chunk_kernel(cuts, spec_ref, *refs):
    rows, groups, bins, _ = spec_ref.shape
    out_refs, wide_ref = refs[-1 - len(cuts) : -1], refs[-1]
    own_group = lax.axis_index("chan")
    widened = []
    for (distance, start, size), out_ref in zip(cuts, out_refs):
        if distance not in widened:
            group = lax.rem(own_group + distance, groups)
            index = len(widened)
            wide_ref[index] = spec_ref[:, group].astype(jnp.float32).reshape(rows * bins, BLOCK)
            widened.append(distance)
        for f in range(size):
            value = wide_ref[widened.index(distance), pl.ds(start + f, rows, stride=bins), :]
            out_ref[f] = value.astype(jnp.bfloat16)


def stack_weights(groups):
    row = lax.broadcasted_iota(jnp.int32, (2 * groups, BLOCK), 0)
    lag = lax.broadcasted_iota(jnp.int32, (2 * groups, BLOCK), 1)
    delta = jnp.where(row < groups, row, row - groups)
    lag = jnp.where(row < groups, lag, lag - BLOCK)
    usable = (lag > -BLOCK) & ((delta >= 1) | (lag >= 1))
    count = SEGMENTS * (groups - delta) * (BLOCK - jnp.abs(lag))
    scale = math.sqrt(SEGMENTS / FREQS)
    return jnp.where(usable, scale / jnp.maximum(count, 1).astype(jnp.float32), 0.0)


def stack_kernel(order, start, bins, parts, *refs):
    groups = len(order)
    chunk_refs = refs[:groups]
    place_ref, lag_ref, shift_ref = refs[groups : groups + 3]
    earlier_refs = refs[groups + 3 : -4]
    out_ref, placed_ref, left_ref, part_ref = refs[-4:]
    rows = placed_ref.shape[2]
    windows = rows // 2
    places = place_ref[...]
    for distance, chunk_ref in zip(order, chunk_refs):
        placed_ref[places[distance, 0]] = chunk_ref[...]

    row_index = lax.broadcasted_iota(jnp.int32, (BLOCK, BLOCK), 0)
    lag_index = lax.broadcasted_iota(jnp.int32, (BLOCK, BLOCK), 1)
    mirror = jnp.where(row_index + lag_index == BLOCK - 1, 1.0, 0.0).astype(jnp.bfloat16)
    ahead = lag_index <= row_index

    for f in range(bins):
        left_ref[f] = lax.dot_general(
            mirror,
            placed_ref[:, f].reshape(groups * rows, BLOCK),
            (((1,), (1,)), ((), ())),
            preferred_element_type=jnp.float32,
        ).astype(jnp.bfloat16)

    for f in range(bins):
        right = []
        for place in range(groups):
            value = placed_ref[place, f]
            real, imag = value[:windows], value[windows:]
            right.append(
                jnp.concatenate(
                    [jnp.concatenate([real, imag], 1), jnp.concatenate([imag, -real], 1)], 0
                )
            )
        right = jnp.concatenate(right, 0)
        for delta in range(groups):
            panel = jnp.dot(
                left_ref[f, :, : rows * (groups - delta)],
                right[rows * delta :],
                preferred_element_type=jnp.float32,
            )
            for half in range(2):
                lanes = slice(half * BLOCK, (half + 1) * BLOCK)
                skewed = pltpu.roll(panel[:, lanes], 1, 1, stride=1, stride_axis=0)
                forward = jnp.where(ahead, skewed, 0.0).reshape(-1, 8, BLOCK).sum(0)
                backward = jnp.where(ahead, 0.0, skewed).reshape(-1, 8, BLOCK).sum(0)
                first = (f * 2 * groups + delta) * 8
                part_ref[half, first : first + 8] = forward
                part_ref[half, first + groups * 8 : first + groups * 8 + 8] = backward

    lags = []
    for half in range(2):
        summed = part_ref[half, pl.ds(0, bins * 2 * groups, stride=8), :]
        for sublane in range(1, 8):
            summed = summed + part_ref[half, pl.ds(sublane, bins * 2 * groups, stride=8), :]
        lags.append(summed)
    weight = stack_weights(groups)

    terms = []
    for f in range(bins):
        lag_rows = slice(f * 2 * groups, (f + 1) * 2 * groups)
        means = jnp.concatenate([half[lag_rows] * weight for half in lags], 0)
        mean_high, mean_low = halves(means)
        spread = jnp.concatenate(
            [
                jnp.concatenate([mean_high, mean_high], 1),
                jnp.concatenate([mean_low, jnp.zeros_like(mean_low)], 1),
            ],
            0,
        )
        product = jnp.dot(spread, lag_ref[start + f], preferred_element_type=jnp.float32)
        product = product[: 4 * groups] + product[4 * groups :]
        by_cos, by_sin = product[:, :SLOWNESS], product[:, SLOWNESS:]
        real = by_cos[: 2 * groups] - by_sin[2 * groups :]
        imag = by_sin[: 2 * groups] + by_cos[2 * groups :]
        shift_cos, shift_sin = shift_ref[start + f, 0], shift_ref[start + f, 1]
        turned_re = real * shift_cos - imag * shift_sin
        turned_im = real * shift_sin + imag * shift_cos
        terms.append(turned_re[:groups] + turned_re[groups:])
        terms.append(turned_im[:groups] + turned_im[groups:])

    if parts is None:
        for entry, term in enumerate(terms):
            out_ref[entry] = term
        return
    for earlier_ref in reversed(earlier_refs):
        terms = [earlier_ref[entry] for entry in range(earlier_ref.shape[0])] + terms
    slow_dev = SLOWNESS // parts
    spans = BLOCK // slow_dev
    span_index = lax.broadcasted_iota(jnp.int32, (groups, BLOCK), 1) // slow_dev
    for part in range(parts):
        source = (part % spans) * slow_dev
        lanes = slice(part // spans * BLOCK, (part // spans + 1) * BLOCK)
        for row in range(out_ref.shape[2]):
            packed = jnp.zeros((groups, BLOCK), jnp.float32)
            for span, term in enumerate(terms[row * spans : (row + 1) * spans]):
                moved = pltpu.roll(term[:, lanes], (span * slow_dev - source) % BLOCK, 1)
                packed = jnp.where(span_index == span, moved, packed)
            for delta in range(groups):
                out_ref[groups - 1 - delta, parts - 1 - part, row] = packed[delta]


def image_kernel(slow_dev, spans, term_ref, table_ref, out_ref):
    arrived = term_ref[...]
    turned = arrived.reshape(-1, BLOCK).T
    sums = []
    for odd, chosen in enumerate(spans):
        terms = jnp.concatenate(
            [turned[span * slow_dev : (span + 1) * slow_dev] for span in chosen], 1
        )
        high, low = halves(terms)
        by_high = jnp.dot(
            jnp.concatenate([high, low], 0), table_ref[odd, 0], preferred_element_type=jnp.float32
        )
        by_low = jnp.dot(high, table_ref[odd, 1], preferred_element_type=jnp.float32)
        sums.append(by_high[:slow_dev] + by_high[slow_dev:] + by_low)
    even, odd = sums
    out_ref[0, :, : LAG_TIMES // 2] = even - odd
    out_ref[0, :, LAG_TIMES // 2 :] = even + odd


def time_table(groups, parts, bins, slow_dev, message_rows):
    count = min(BLOCK // slow_dev, 2 * bins)
    spans = [[span for span in range(count) if span // 2 % 2 == odd] for odd in range(2)]
    tables = []
    for chosen in spans:
        span, group, part, row = np.meshgrid(
            chosen,
            np.arange(groups)[::-1],
            np.arange(parts)[::-1],
            np.arange(message_rows),
            indexing="ij",
        )
        entry = row * count + span
        freq = (part * groups + group) * bins + entry // 2
        lag_time = np.arange(LAG_TIMES // 2)
        angle = 2.0 * math.pi / LAG_TIMES * ((freq[..., None] * lag_time) % LAG_TIMES)
        table = np.where((entry % 2 == 0)[..., None], np.cos(angle), -np.sin(angle))
        table = table.reshape(-1, LAG_TIMES // 2).astype(np.float32)
        high = table.astype(jnp.bfloat16)
        low = (table - high.astype(np.float32)).astype(jnp.bfloat16)
        tables.append(np.stack([high, low]))
    return spans, np.stack(tables)


def shards(spectra, block_position):
    groups = lax.axis_size("chan")
    parts = lax.axis_size("freq")
    rows = spectra.shape[0] * spectra.shape[1]
    freq_dev = spectra.shape[2]
    bins = freq_dev // groups
    slow_dev = SLOWNESS // parts
    message_rows = -(-2 * bins * slow_dev // BLOCK)
    vmem = pl.BlockSpec(memory_space=pltpu.VMEM)
    anywhere = pl.BlockSpec(memory_space=pl.ANY)
    params = pltpu.CompilerParams(vmem_limit_bytes=32 * 1024 * 1024)

    whole = spectra.reshape(rows, groups, bins, BLOCK)

    def cut(cuts, *earlier):
        distances = {distance for distance, _, _ in cuts}
        return pl.pallas_call(
            functools.partial(chunk_kernel, cuts),
            out_shape=tuple(
                jax.ShapeDtypeStruct((size, rows, BLOCK), jnp.bfloat16) for _, _, size in cuts
            ),
            in_specs=[vmem] + [anywhere] * len(earlier),
            out_specs=(vmem,) * len(cuts),
            scratch_shapes=[pltpu.VMEM((len(distances), rows * bins, BLOCK), jnp.float32)],
            compiler_params=params,
            cost_estimate=pl.CostEstimate(flops=10**7, bytes_accessed=10**6, transcendentals=0),
            name="chunks_of_bins",
        )(whole, *earlier)

    late = max(1, 3 * bins // 8) if bins > 1 else 0
    pieces = [(0, bins - late), (bins - late, late)] if late else [(0, bins)]
    order = sorted(range(1, groups), key=lambda steps: abs(2 * steps - groups)) + [0]
    cuts = [(distance, *piece) for piece in pieces for distance in order]
    (first_chunk,) = cut(cuts[:1])
    chunks = dict(zip(cuts, (first_chunk, *cut(cuts[1:], first_chunk))))
    for key in cuts:
        if key[0]:
            pairs = [(source, (source + key[0]) % groups) for source in range(groups)]
            chunks[key] = lax.ppermute(chunks[key], "chan", pairs)
    chunks[cuts[0]] = pl.pallas_call(
        copy_kernel,
        out_shape=jax.ShapeDtypeStruct(first_chunk.shape, jnp.bfloat16),
        in_specs=[vmem],
        out_specs=vmem,
        compiler_params=params,
        name="first_arrived",
    )(chunks[cuts[0]])
    places, lag_table, shift_table = pl.pallas_call(
        functools.partial(table_kernel, groups, bins, freq_dev),
        out_shape=(
            jax.ShapeDtypeStruct((groups, BLOCK), jnp.int32),
            jax.ShapeDtypeStruct((bins, 2 * BLOCK, 2 * SLOWNESS), jnp.bfloat16),
            jax.ShapeDtypeStruct((bins, 2, 2 * groups, SLOWNESS), jnp.float32),
        ),
        in_specs=[vmem],
        out_specs=(vmem, vmem, vmem),
        compiler_params=params,
        cost_estimate=pl.CostEstimate(flops=10**7, bytes_accessed=4 * 10**6, transcendentals=0),
        name="slant_tables",
    )(block_position.reshape(1, groups))
    earlier = []
    for start, size in pieces:
        last = start + size == bins
        shape = (groups, parts, message_rows, BLOCK) if last else (2 * size, groups, SLOWNESS)
        terms = pl.pallas_call(
            functools.partial(stack_kernel, order, start, size, parts if last else None),
            out_shape=jax.ShapeDtypeStruct(shape, jnp.float32),
            in_specs=[vmem] * (groups + 3 + len(earlier)),
            out_specs=vmem,
            scratch_shapes=[
                pltpu.VMEM((groups, size, rows, BLOCK), jnp.bfloat16),
                pltpu.VMEM((size, BLOCK, groups * rows), jnp.bfloat16),
                pltpu.VMEM((2, size * 2 * groups * 8, BLOCK), jnp.float32),
            ],
            compiler_params=params,
            cost_estimate=pl.CostEstimate(
                flops=2 * 10**8, bytes_accessed=4 * 10**6, transcendentals=0
            ),
            name="stack_and_slant",
        )(
            *[chunks[distance, start, size] for distance in order],
            places,
            lag_table,
            shift_table,
            *earlier,
        )
        earlier.append(terms)
    terms = terms.reshape(groups * parts, message_rows, BLOCK)
    arrived = lax.all_to_all(
        terms,
        ("chan", "freq"),
        split_axis=0,
        concat_axis=0,
        axis_index_groups=[list(range(groups * parts))[::-1]],
        tiled=True,
    )
    spans, table = time_table(groups, parts, bins, slow_dev, message_rows)
    return pl.pallas_call(
        functools.partial(image_kernel, slow_dev, spans),
        out_shape=jax.ShapeDtypeStruct((1, slow_dev, LAG_TIMES), jnp.float32),
        in_specs=[vmem, vmem],
        out_specs=vmem,
        compiler_params=params,
        name="sum_of_bins",
    )(arrived, jnp.asarray(table))


def solution(mesh):
    return jax.shard_map(
        shards,
        mesh=mesh,
        in_specs=(P(None, None, "freq", "chan"), P()),
        out_specs=P("chan", "freq", None),
        check_vma=False,
    )
```

```python
import functools
import math

import jax
import jax.numpy as jnp
import numpy as np
from jax import lax
from jax.experimental import pallas as pl
from jax.experimental.pallas import tpu as pltpu
from jax.sharding import PartitionSpec as P

SEGMENTS = 32
FREQS = 256
BLOCK = 128
SLOWNESS = 256
LAG_TIMES = 512
MODULUS = 8 * FREQS * BLOCK


def unit_phase(numerator):
    quarter = MODULUS // 4
    turn = numerator & (MODULUS - 1)
    quadrant = lax.shift_right_logical(turn + quarter // 2, quarter.bit_length() - 1)
    x = (turn - quadrant * quarter).astype(jnp.float32) * (2.0 * math.pi / MODULUS)
    y = x * x
    sine = x * (1.0 + y * (-1.0 / 6 + y * (1.0 / 120 + y * (-1.0 / 5040 + y * (1.0 / 362880)))))
    cosine = 1.0 + y * (-0.5 + y * (1.0 / 24 + y * (-1.0 / 720 + y * (1.0 / 40320))))
    odd = (quadrant & 1) == 1
    first = jnp.where(odd, sine, cosine)
    second = jnp.where(odd, cosine, sine)
    first = jnp.where(((quadrant + 1) & 2) == 2, -first, first)
    second = jnp.where((quadrant & 2) == 2, -second, second)
    return first, second


def halves(value):
    high = value.astype(jnp.bfloat16)
    return high, (value - high.astype(jnp.float32)).astype(jnp.bfloat16)


def copy_kernel(in_ref, out_ref):
    out_ref[...] = in_ref[...]


def table_kernel(groups, bins, freq_dev, position_ref, place_ref, lag_ref, shift_ref):
    low_rows = lax.broadcasted_iota(jnp.int32, (8, SLOWNESS), 0)
    high_rows = lax.broadcasted_iota(jnp.int32, (BLOCK // 8, SLOWNESS), 0) * 8
    shift_rows = lax.broadcasted_iota(jnp.int32, (2 * groups, SLOWNESS), 0)
    shift_rows = jnp.where(shift_rows < groups, shift_rows, shift_rows - groups - 1) * BLOCK
    own_group = lax.axis_index("chan")
    first_bin = lax.axis_index("freq") * freq_dev + own_group * bins
    sender = lax.broadcasted_iota(jnp.int32, (groups, groups), 1)
    distance = lax.broadcasted_iota(jnp.int32, (groups, groups), 0)
    sends = lax.rem(own_group + groups - distance, groups) == sender
    places = jnp.sum(jnp.where(sends, position_ref[...], 0), axis=1, keepdims=True)
    place_ref[...] = jnp.broadcast_to(places, place_ref.shape)

    def one_bin(f, carry):
        def phases(rows):
            slow = lax.broadcasted_iota(jnp.int32, rows.shape, 1) - SLOWNESS // 2
            return unit_phase((first_bin + f) * slow * rows)

        low_cos, low_sin = phases(low_rows)
        high_cos, high_sin = phases(high_rows)
        low_cos, low_sin = low_cos[None], low_sin[None]
        high_cos, high_sin = high_cos[:, None], high_sin[:, None]
        lag_cos = (high_cos * low_cos - high_sin * low_sin).reshape(BLOCK, SLOWNESS)
        lag_sin = (high_sin * low_cos + high_cos * low_sin).reshape(BLOCK, SLOWNESS)
        cos_high, cos_low = halves(lag_cos)
        sin_high, sin_low = halves(lag_sin)
        lag_ref[f, :BLOCK, :SLOWNESS] = cos_high
        lag_ref[f, BLOCK:, :SLOWNESS] = cos_low
        lag_ref[f, :BLOCK, SLOWNESS:] = sin_high
        lag_ref[f, BLOCK:, SLOWNESS:] = sin_low
        shift_cos, shift_sin = phases(shift_rows)
        shift_ref[f, 0] = shift_cos
        shift_ref[f, 1] = shift_sin
        return carry

    lax.fori_loop(0, bins, one_bin, 0)


def chunk_kernel(cuts, spec_ref, *refs):
    rows, groups, bins, _ = spec_ref.shape
    out_refs, wide_ref = refs[-1 - len(cuts) : -1], refs[-1]
    own_group = lax.axis_index("chan")
    widened = []
    for (distance, start, size), out_ref in zip(cuts, out_refs):
        if distance not in widened:
            group = lax.rem(own_group + distance, groups)
            index = len(widened)
            wide_ref[index] = spec_ref[:, group].astype(jnp.float32).reshape(rows * bins, BLOCK)
            widened.append(distance)
        for f in range(size):
            value = wide_ref[widened.index(distance), pl.ds(start + f, rows, stride=bins), :]
            out_ref[f] = value.astype(jnp.bfloat16)


def stack_weights(groups):
    row = lax.broadcasted_iota(jnp.int32, (2 * groups, BLOCK), 0)
    lag = lax.broadcasted_iota(jnp.int32, (2 * groups, BLOCK), 1)
    delta = jnp.where(row < groups, row, row - groups)
    lag = jnp.where(row < groups, lag, lag - BLOCK)
    usable = (lag > -BLOCK) & ((delta >= 1) | (lag >= 1))
    count = SEGMENTS * (groups - delta) * (BLOCK - jnp.abs(lag))
    scale = math.sqrt(SEGMENTS / FREQS)
    return jnp.where(usable, scale / jnp.maximum(count, 1).astype(jnp.float32), 0.0)


def stack_kernel(order, start, bins, parts, *refs):
    groups = len(order)
    chunk_refs = refs[:groups]
    place_ref, lag_ref, shift_ref = refs[groups : groups + 3]
    earlier_refs = refs[groups + 3 : -4]
    out_ref, placed_ref, left_ref, part_ref = refs[-4:]
    rows = placed_ref.shape[2]
    windows = rows // 2
    places = place_ref[...]
    for distance, chunk_ref in zip(order, chunk_refs):
        placed_ref[places[distance, 0]] = chunk_ref[...]

    row_index = lax.broadcasted_iota(jnp.int32, (BLOCK, BLOCK), 0)
    lag_index = lax.broadcasted_iota(jnp.int32, (BLOCK, BLOCK), 1)
    mirror = jnp.where(row_index + lag_index == BLOCK - 1, 1.0, 0.0).astype(jnp.bfloat16)
    ahead = lag_index <= row_index

    for f in range(bins):
        left_ref[f] = lax.dot_general(
            mirror,
            placed_ref[:, f].reshape(groups * rows, BLOCK),
            (((1,), (1,)), ((), ())),
            preferred_element_type=jnp.float32,
        ).astype(jnp.bfloat16)

    for f in range(bins):
        right = []
        for place in range(groups):
            value = placed_ref[place, f]
            real, imag = value[:windows], value[windows:]
            right.append(
                jnp.concatenate(
                    [jnp.concatenate([real, imag], 1), jnp.concatenate([imag, -real], 1)], 0
                )
            )
        right = jnp.concatenate(right, 0)
        for delta in range(groups):
            panel = jnp.dot(
                left_ref[f, :, : rows * (groups - delta)],
                right[rows * delta :],
                preferred_element_type=jnp.float32,
            )
            for half in range(2):
                lanes = slice(half * BLOCK, (half + 1) * BLOCK)
                skewed = pltpu.roll(panel[:, lanes], 1, 1, stride=1, stride_axis=0)
                forward = jnp.where(ahead, skewed, 0.0).reshape(-1, 8, BLOCK).sum(0)
                backward = jnp.where(ahead, 0.0, skewed).reshape(-1, 8, BLOCK).sum(0)
                first = (f * 2 * groups + delta) * 8
                part_ref[half, first : first + 8] = forward
                part_ref[half, first + groups * 8 : first + groups * 8 + 8] = backward

    lags = []
    for half in range(2):
        summed = part_ref[half, pl.ds(0, bins * 2 * groups, stride=8), :]
        for sublane in range(1, 8):
            summed = summed + part_ref[half, pl.ds(sublane, bins * 2 * groups, stride=8), :]
        lags.append(summed)
    weight = stack_weights(groups)

    terms = []
    for f in range(bins):
        lag_rows = slice(f * 2 * groups, (f + 1) * 2 * groups)
        means = jnp.concatenate([half[lag_rows] * weight for half in lags], 0)
        mean_high, mean_low = halves(means)
        spread = jnp.concatenate(
            [
                jnp.concatenate([mean_high, mean_high], 1),
                jnp.concatenate([mean_low, jnp.zeros_like(mean_low)], 1),
            ],
            0,
        )
        product = jnp.dot(spread, lag_ref[start + f], preferred_element_type=jnp.float32)
        product = product[: 4 * groups] + product[4 * groups :]
        by_cos, by_sin = product[:, :SLOWNESS], product[:, SLOWNESS:]
        real = by_cos[: 2 * groups] - by_sin[2 * groups :]
        imag = by_sin[: 2 * groups] + by_cos[2 * groups :]
        shift_cos, shift_sin = shift_ref[start + f, 0], shift_ref[start + f, 1]
        turned_re = real * shift_cos - imag * shift_sin
        turned_im = real * shift_sin + imag * shift_cos
        terms.append(turned_re[:groups] + turned_re[groups:])
        terms.append(turned_im[:groups] + turned_im[groups:])

    if parts is None:
        for entry, term in enumerate(terms):
            out_ref[entry] = term
        return
    for earlier_ref in reversed(earlier_refs):
        terms = [earlier_ref[entry] for entry in range(earlier_ref.shape[0])] + terms
    slow_dev = SLOWNESS // parts
    spans = BLOCK // slow_dev
    span_index = lax.broadcasted_iota(jnp.int32, (groups, BLOCK), 1) // slow_dev
    for part in range(parts):
        source = (part % spans) * slow_dev
        lanes = slice(part // spans * BLOCK, (part // spans + 1) * BLOCK)
        for row in range(out_ref.shape[2]):
            packed = jnp.zeros((groups, BLOCK), jnp.float32)
            for span, term in enumerate(terms[row * spans : (row + 1) * spans]):
                moved = pltpu.roll(term[:, lanes], (span * slow_dev - source) % BLOCK, 1)
                packed = jnp.where(span_index == span, moved, packed)
            for delta in range(groups):
                out_ref[groups - 1 - delta, parts - 1 - part, row] = packed[delta]


def image_kernel(slow_dev, spans, term_ref, table_ref, out_ref):
    arrived = term_ref[...]
    turned = arrived.reshape(-1, BLOCK).T
    sums = []
    for odd, chosen in enumerate(spans):
        terms = jnp.concatenate(
            [turned[span * slow_dev : (span + 1) * slow_dev] for span in chosen], 1
        )
        high, low = halves(terms)
        by_high = jnp.dot(
            jnp.concatenate([high, low], 0), table_ref[odd, 0], preferred_element_type=jnp.float32
        )
        by_low = jnp.dot(high, table_ref[odd, 1], preferred_element_type=jnp.float32)
        sums.append(by_high[:slow_dev] + by_high[slow_dev:] + by_low)
    even, odd = sums
    out_ref[0, :, : LAG_TIMES // 2] = even - odd
    out_ref[0, :, LAG_TIMES // 2 :] = even + odd


def time_table(groups, parts, bins, slow_dev, message_rows):
    count = min(BLOCK // slow_dev, 2 * bins)
    spans = [[span for span in range(count) if span // 2 % 2 == odd] for odd in range(2)]
    tables = []
    for chosen in spans:
        span, group, part, row = np.meshgrid(
            chosen,
            np.arange(groups)[::-1],
            np.arange(parts)[::-1],
            np.arange(message_rows),
            indexing="ij",
        )
        entry = row * count + span
        freq = (part * groups + group) * bins + entry // 2
        lag_time = np.arange(LAG_TIMES // 2)
        angle = 2.0 * math.pi / LAG_TIMES * ((freq[..., None] * lag_time) % LAG_TIMES)
        table = np.where((entry % 2 == 0)[..., None], np.cos(angle), -np.sin(angle))
        table = table.reshape(-1, LAG_TIMES // 2).astype(np.float32)
        high = table.astype(jnp.bfloat16)
        low = (table - high.astype(np.float32)).astype(jnp.bfloat16)
        tables.append(np.stack([high, low]))
    return spans, np.stack(tables)


def shards(spectra, block_position):
    groups = lax.axis_size("chan")
    parts = lax.axis_size("freq")
    rows = spectra.shape[0] * spectra.shape[1]
    freq_dev = spectra.shape[2]
    bins = freq_dev // groups
    slow_dev = SLOWNESS // parts
    message_rows = -(-2 * bins * slow_dev // BLOCK)
    vmem = pl.BlockSpec(memory_space=pltpu.VMEM)
    anywhere = pl.BlockSpec(memory_space=pl.ANY)
    params = pltpu.CompilerParams(vmem_limit_bytes=32 * 1024 * 1024)

    whole = spectra.reshape(rows, groups, bins, BLOCK)

    def cut(cuts, *earlier):
        distances = {distance for distance, _, _ in cuts}
        return pl.pallas_call(
            functools.partial(chunk_kernel, cuts),
            out_shape=tuple(
                jax.ShapeDtypeStruct((size, rows, BLOCK), jnp.bfloat16) for _, _, size in cuts
            ),
            in_specs=[vmem] + [anywhere] * len(earlier),
            out_specs=(vmem,) * len(cuts),
            scratch_shapes=[pltpu.VMEM((len(distances), rows * bins, BLOCK), jnp.float32)],
            compiler_params=params,
            cost_estimate=pl.CostEstimate(flops=10**7, bytes_accessed=10**6, transcendentals=0),
            name="chunks_of_bins",
        )(whole, *earlier)

    late = max(1, bins // 4) if bins > 1 else 0
    pieces = [(0, bins - late), (bins - late, late)] if late else [(0, bins)]
    far_first = sorted(range(1, groups), key=lambda steps: abs(2 * steps - groups)) + [0]
    near_first = list(range(1, groups)) + [0]
    orders = [far_first, near_first][: len(pieces)]
    cuts = [(distance, *piece) for piece, order in zip(pieces, orders) for distance in order]
    (first_chunk,) = cut(cuts[:1])
    chunks = dict(zip(cuts, (first_chunk, *cut(cuts[1:], first_chunk))))
    for key in cuts:
        if key[0]:
            pairs = [(source, (source + key[0]) % groups) for source in range(groups)]
            chunks[key] = lax.ppermute(chunks[key], "chan", pairs)
    chunks[cuts[0]] = pl.pallas_call(
        copy_kernel,
        out_shape=jax.ShapeDtypeStruct(first_chunk.shape, jnp.bfloat16),
        in_specs=[vmem],
        out_specs=vmem,
        compiler_params=params,
        name="first_arrived",
    )(chunks[cuts[0]])
    places, lag_table, shift_table = pl.pallas_call(
        functools.partial(table_kernel, groups, bins, freq_dev),
        out_shape=(
            jax.ShapeDtypeStruct((groups, BLOCK), jnp.int32),
            jax.ShapeDtypeStruct((bins, 2 * BLOCK, 2 * SLOWNESS), jnp.bfloat16),
            jax.ShapeDtypeStruct((bins, 2, 2 * groups, SLOWNESS), jnp.float32),
        ),
        in_specs=[vmem],
        out_specs=(vmem, vmem, vmem),
        compiler_params=params,
        cost_estimate=pl.CostEstimate(flops=10**7, bytes_accessed=4 * 10**6, transcendentals=0),
        name="slant_tables",
    )(block_position.reshape(1, groups))
    earlier = []
    for (start, size), order in zip(pieces, orders):
        last = start + size == bins
        shape = (groups, parts, message_rows, BLOCK) if last else (2 * size, groups, SLOWNESS)
        terms = pl.pallas_call(
            functools.partial(stack_kernel, order, start, size, parts if last else None),
            out_shape=jax.ShapeDtypeStruct(shape, jnp.float32),
            in_specs=[vmem] * (groups + 3 + len(earlier)),
            out_specs=vmem,
            scratch_shapes=[
                pltpu.VMEM((groups, size, rows, BLOCK), jnp.bfloat16),
                pltpu.VMEM((size, BLOCK, groups * rows), jnp.bfloat16),
                pltpu.VMEM((2, size * 2 * groups * 8, BLOCK), jnp.float32),
            ],
            compiler_params=params,
            cost_estimate=pl.CostEstimate(
                flops=2 * 10**8, bytes_accessed=4 * 10**6, transcendentals=0
            ),
            name="stack_and_slant",
        )(
            *[chunks[distance, start, size] for distance in order],
            places,
            lag_table,
            shift_table,
            *earlier,
        )
        earlier.append(terms)
    terms = terms.reshape(groups * parts, message_rows, BLOCK)
    arrived = lax.all_to_all(
        terms,
        ("chan", "freq"),
        split_axis=0,
        concat_axis=0,
        axis_index_groups=[list(range(groups * parts))[::-1]],
        tiled=True,
    )
    spans, table = time_table(groups, parts, bins, slow_dev, message_rows)
    return pl.pallas_call(
        functools.partial(image_kernel, slow_dev, spans),
        out_shape=jax.ShapeDtypeStruct((1, slow_dev, LAG_TIMES), jnp.float32),
        in_specs=[vmem, vmem],
        out_specs=vmem,
        compiler_params=params,
        name="sum_of_bins",
    )(arrived, jnp.asarray(table))


def solution(mesh):
    return jax.shard_map(
        shards,
        mesh=mesh,
        in_specs=(P(None, None, "freq", "chan"), P()),
        out_specs=P("chan", "freq", None),
        check_vma=False,
    )
```

```python
import functools
import math

import jax
import jax.numpy as jnp
import numpy as np
from jax import lax
from jax.experimental import pallas as pl
from jax.experimental.pallas import tpu as pltpu
from jax.sharding import PartitionSpec as P

SEGMENTS = 32
FREQS = 256
BLOCK = 128
SLOWNESS = 256
LAG_TIMES = 512
MODULUS = 8 * FREQS * BLOCK


def unit_phase(numerator):
    quarter = MODULUS // 4
    turn = numerator & (MODULUS - 1)
    quadrant = lax.shift_right_logical(turn + quarter // 2, quarter.bit_length() - 1)
    x = (turn - quadrant * quarter).astype(jnp.float32) * (2.0 * math.pi / MODULUS)
    y = x * x
    sine = x * (1.0 + y * (-1.0 / 6 + y * (1.0 / 120 + y * (-1.0 / 5040 + y * (1.0 / 362880)))))
    cosine = 1.0 + y * (-0.5 + y * (1.0 / 24 + y * (-1.0 / 720 + y * (1.0 / 40320))))
    odd = (quadrant & 1) == 1
    first = jnp.where(odd, sine, cosine)
    second = jnp.where(odd, cosine, sine)
    first = jnp.where(((quadrant + 1) & 2) == 2, -first, first)
    second = jnp.where((quadrant & 2) == 2, -second, second)
    return first, second


def halves(value):
    high = value.astype(jnp.bfloat16)
    return high, (value - high.astype(jnp.float32)).astype(jnp.bfloat16)


def copy_kernel(in_ref, out_ref):
    out_ref[...] = in_ref[...]


def table_kernel(groups, bins, freq_dev, position_ref, place_ref, lag_ref, shift_ref):
    low_rows = lax.broadcasted_iota(jnp.int32, (8, SLOWNESS), 0)
    high_rows = lax.broadcasted_iota(jnp.int32, (BLOCK // 8, SLOWNESS), 0) * 8
    shift_rows = lax.broadcasted_iota(jnp.int32, (2 * groups, SLOWNESS), 0)
    shift_rows = jnp.where(shift_rows < groups, shift_rows, shift_rows - groups - 1) * BLOCK
    own_group = lax.axis_index("chan")
    first_bin = lax.axis_index("freq") * freq_dev + own_group * bins
    sender = lax.broadcasted_iota(jnp.int32, (groups, groups), 1)
    distance = lax.broadcasted_iota(jnp.int32, (groups, groups), 0)
    sends = lax.rem(own_group + groups - distance, groups) == sender
    places = jnp.sum(jnp.where(sends, position_ref[...], 0), axis=1, keepdims=True)
    place_ref[...] = jnp.broadcast_to(places, place_ref.shape)

    def one_bin(f, carry):
        def phases(rows):
            slow = lax.broadcasted_iota(jnp.int32, rows.shape, 1) - SLOWNESS // 2
            return unit_phase((first_bin + f) * slow * rows)

        low_cos, low_sin = phases(low_rows)
        high_cos, high_sin = phases(high_rows)
        low_cos, low_sin = low_cos[None], low_sin[None]
        high_cos, high_sin = high_cos[:, None], high_sin[:, None]
        lag_cos = (high_cos * low_cos - high_sin * low_sin).reshape(BLOCK, SLOWNESS)
        lag_sin = (high_sin * low_cos + high_cos * low_sin).reshape(BLOCK, SLOWNESS)
        cos_high, cos_low = halves(lag_cos)
        sin_high, sin_low = halves(lag_sin)
        lag_ref[f, :BLOCK, :SLOWNESS] = cos_high
        lag_ref[f, BLOCK:, :SLOWNESS] = cos_low
        lag_ref[f, :BLOCK, SLOWNESS:] = sin_high
        lag_ref[f, BLOCK:, SLOWNESS:] = sin_low
        shift_cos, shift_sin = phases(shift_rows)
        shift_ref[f, 0] = shift_cos
        shift_ref[f, 1] = shift_sin
        return carry

    lax.fori_loop(0, bins, one_bin, 0)


def chunk_kernel(cuts, spec_ref, *refs):
    rows, groups, bins, _ = spec_ref.shape
    out_refs, wide_ref = refs[-1 - len(cuts) : -1], refs[-1]
    own_group = lax.axis_index("chan")
    widened = []
    for (distance, start, size), out_ref in zip(cuts, out_refs):
        if distance not in widened:
            group = lax.rem(own_group + distance, groups)
            index = len(widened)
            value = spec_ref[:, group].astype(jnp.float32).reshape(rows * bins, BLOCK)
            wide_ref[index, : rows * bins] = value
            widened.append(distance)
        for f in range(size):
            value = wide_ref[widened.index(distance), pl.ds(start + f, rows, stride=bins), :]
            out_ref[f] = value.astype(jnp.bfloat16)


def stack_weights(groups):
    row = lax.broadcasted_iota(jnp.int32, (2 * groups, BLOCK), 0)
    lag = lax.broadcasted_iota(jnp.int32, (2 * groups, BLOCK), 1)
    delta = jnp.where(row < groups, row, row - groups)
    lag = jnp.where(row < groups, lag, lag - BLOCK)
    usable = (lag > -BLOCK) & ((delta >= 1) | (lag >= 1))
    count = SEGMENTS * (groups - delta) * (BLOCK - jnp.abs(lag))
    scale = math.sqrt(SEGMENTS / FREQS)
    return jnp.where(usable, scale / jnp.maximum(count, 1).astype(jnp.float32), 0.0)


def stack_kernel(order, start, bins, parts, *refs):
    groups = len(order)
    chunk_refs = refs[:groups]
    place_ref, lag_ref, shift_ref = refs[groups : groups + 3]
    earlier_refs = refs[groups + 3 : -4]
    out_ref, placed_ref, left_ref, part_ref = refs[-4:]
    rows = placed_ref.shape[2]
    windows = rows // 2
    places = place_ref[...]
    for distance, chunk_ref in zip(order, chunk_refs):
        skip = start if chunk_ref.shape[0] > bins else 0
        placed_ref[places[distance, 0]] = chunk_ref[skip : skip + bins]

    row_index = lax.broadcasted_iota(jnp.int32, (BLOCK, BLOCK), 0)
    lag_index = lax.broadcasted_iota(jnp.int32, (BLOCK, BLOCK), 1)
    mirror = jnp.where(row_index + lag_index == BLOCK - 1, 1.0, 0.0).astype(jnp.bfloat16)
    ahead = lag_index <= row_index

    for f in range(bins):
        left_ref[f] = lax.dot_general(
            mirror,
            placed_ref[:, f].reshape(groups * rows, BLOCK),
            (((1,), (1,)), ((), ())),
            preferred_element_type=jnp.float32,
        ).astype(jnp.bfloat16)

    for f in range(bins):
        right = []
        for place in range(groups):
            value = placed_ref[place, f]
            real, imag = value[:windows], value[windows:]
            right.append(
                jnp.concatenate(
                    [jnp.concatenate([real, imag], 1), jnp.concatenate([imag, -real], 1)], 0
                )
            )
        right = jnp.concatenate(right, 0)
        for delta in range(groups):
            panel = jnp.dot(
                left_ref[f, :, : rows * (groups - delta)],
                right[rows * delta :],
                preferred_element_type=jnp.float32,
            )
            for half in range(2):
                lanes = slice(half * BLOCK, (half + 1) * BLOCK)
                skewed = pltpu.roll(panel[:, lanes], 1, 1, stride=1, stride_axis=0)
                forward = jnp.where(ahead, skewed, 0.0).reshape(-1, 8, BLOCK).sum(0)
                backward = jnp.where(ahead, 0.0, skewed).reshape(-1, 8, BLOCK).sum(0)
                first = (f * 2 * groups + delta) * 8
                part_ref[half, first : first + 8] = forward
                part_ref[half, first + groups * 8 : first + groups * 8 + 8] = backward

    lags = []
    for half in range(2):
        summed = part_ref[half, pl.ds(0, bins * 2 * groups, stride=8), :]
        for sublane in range(1, 8):
            summed = summed + part_ref[half, pl.ds(sublane, bins * 2 * groups, stride=8), :]
        lags.append(summed)
    weight = stack_weights(groups)

    terms = []
    for f in range(bins):
        lag_rows = slice(f * 2 * groups, (f + 1) * 2 * groups)
        means = jnp.concatenate([half[lag_rows] * weight for half in lags], 0)
        mean_high, mean_low = halves(means)
        spread = jnp.concatenate(
            [
                jnp.concatenate([mean_high, mean_high], 1),
                jnp.concatenate([mean_low, jnp.zeros_like(mean_low)], 1),
            ],
            0,
        )
        product = jnp.dot(spread, lag_ref[start + f], preferred_element_type=jnp.float32)
        product = product[: 4 * groups] + product[4 * groups :]
        by_cos, by_sin = product[:, :SLOWNESS], product[:, SLOWNESS:]
        real = by_cos[: 2 * groups] - by_sin[2 * groups :]
        imag = by_sin[: 2 * groups] + by_cos[2 * groups :]
        shift_cos, shift_sin = shift_ref[start + f, 0], shift_ref[start + f, 1]
        turned_re = real * shift_cos - imag * shift_sin
        turned_im = real * shift_sin + imag * shift_cos
        terms.append(turned_re[:groups] + turned_re[groups:])
        terms.append(turned_im[:groups] + turned_im[groups:])

    if parts is None:
        for entry, term in enumerate(terms):
            out_ref[entry] = term
        return
    for earlier_ref in reversed(earlier_refs):
        terms = [earlier_ref[entry] for entry in range(earlier_ref.shape[0])] + terms
    slow_dev = SLOWNESS // parts
    spans = BLOCK // slow_dev
    span_index = lax.broadcasted_iota(jnp.int32, (groups, BLOCK), 1) // slow_dev
    for part in range(parts):
        source = (part % spans) * slow_dev
        lanes = slice(part // spans * BLOCK, (part // spans + 1) * BLOCK)
        for row in range(out_ref.shape[2]):
            packed = jnp.zeros((groups, BLOCK), jnp.float32)
            for span, term in enumerate(terms[row * spans : (row + 1) * spans]):
                moved = pltpu.roll(term[:, lanes], (span * slow_dev - source) % BLOCK, 1)
                packed = jnp.where(span_index == span, moved, packed)
            for delta in range(groups):
                out_ref[groups - 1 - delta, parts - 1 - part, row] = packed[delta]


def image_kernel(slow_dev, spans, term_ref, table_ref, out_ref):
    arrived = term_ref[...]
    turned = arrived.reshape(-1, BLOCK).T
    sums = []
    for odd, chosen in enumerate(spans):
        terms = jnp.concatenate(
            [turned[span * slow_dev : (span + 1) * slow_dev] for span in chosen], 1
        )
        high, low = halves(terms)
        by_high = jnp.dot(
            jnp.concatenate([high, low], 0), table_ref[odd, 0], preferred_element_type=jnp.float32
        )
        by_low = jnp.dot(high, table_ref[odd, 1], preferred_element_type=jnp.float32)
        sums.append(by_high[:slow_dev] + by_high[slow_dev:] + by_low)
    even, odd = sums
    out_ref[0, :, : LAG_TIMES // 2] = even - odd
    out_ref[0, :, LAG_TIMES // 2 :] = even + odd


def time_table(groups, parts, bins, slow_dev, message_rows):
    count = min(BLOCK // slow_dev, 2 * bins)
    spans = [[span for span in range(count) if span // 2 % 2 == odd] for odd in range(2)]
    tables = []
    for chosen in spans:
        span, group, part, row = np.meshgrid(
            chosen,
            np.arange(groups)[::-1],
            np.arange(parts)[::-1],
            np.arange(message_rows),
            indexing="ij",
        )
        entry = row * count + span
        freq = (part * groups + group) * bins + entry // 2
        lag_time = np.arange(LAG_TIMES // 2)
        angle = 2.0 * math.pi / LAG_TIMES * ((freq[..., None] * lag_time) % LAG_TIMES)
        table = np.where((entry % 2 == 0)[..., None], np.cos(angle), -np.sin(angle))
        table = table.reshape(-1, LAG_TIMES // 2).astype(np.float32)
        high = table.astype(jnp.bfloat16)
        low = (table - high.astype(np.float32)).astype(jnp.bfloat16)
        tables.append(np.stack([high, low]))
    return spans, np.stack(tables)


def shards(spectra, block_position):
    groups = lax.axis_size("chan")
    parts = lax.axis_size("freq")
    rows = spectra.shape[0] * spectra.shape[1]
    freq_dev = spectra.shape[2]
    bins = freq_dev // groups
    slow_dev = SLOWNESS // parts
    message_rows = -(-2 * bins * slow_dev // BLOCK)
    vmem = pl.BlockSpec(memory_space=pltpu.VMEM)
    anywhere = pl.BlockSpec(memory_space=pl.ANY)
    params = pltpu.CompilerParams(vmem_limit_bytes=32 * 1024 * 1024)

    whole = spectra.reshape(rows, groups, bins, BLOCK)

    def cut(cuts, *earlier):
        distances = {distance for distance, _, _ in cuts}
        return pl.pallas_call(
            functools.partial(chunk_kernel, cuts),
            out_shape=tuple(
                jax.ShapeDtypeStruct((size, rows, BLOCK), jnp.bfloat16) for _, _, size in cuts
            ),
            in_specs=[vmem] + [anywhere] * len(earlier),
            out_specs=(vmem,) * len(cuts),
            scratch_shapes=[pltpu.VMEM((len(distances), (rows + 1) * bins, BLOCK), jnp.float32)],
            compiler_params=params,
            cost_estimate=pl.CostEstimate(flops=10**7, bytes_accessed=10**6, transcendentals=0),
            name="chunks_of_bins",
        )(whole, *earlier)

    late = max(1, 3 * bins // 8) if bins > 1 else 0
    pieces = [(0, bins - late), (bins - late, late)] if late else [(0, bins)]
    far_first = sorted(range(1, groups), key=lambda steps: abs(2 * steps - groups))
    kept, split = far_first[0], far_first[1:]
    orders = [[kept] + split + [0], [kept] + split[::-1] + [0]][: len(pieces)]
    parts_of = {
        (distance, piece): (distance, *(piece if distance in split else (0, bins)))
        for piece, order in zip(pieces, orders)
        for distance in order
    }
    cuts = list(dict.fromkeys(parts_of.values()))
    (first_chunk,) = cut(cuts[:1])
    chunks = dict(zip(cuts, (first_chunk, *cut(cuts[1:], first_chunk))))
    for key in cuts:
        if key[0]:
            pairs = [(source, (source + key[0]) % groups) for source in range(groups)]
            chunks[key] = lax.ppermute(chunks[key], "chan", pairs)
    chunks[cuts[0]] = pl.pallas_call(
        copy_kernel,
        out_shape=jax.ShapeDtypeStruct(first_chunk.shape, jnp.bfloat16),
        in_specs=[vmem],
        out_specs=vmem,
        compiler_params=params,
        name="first_arrived",
    )(chunks[cuts[0]])
    places, lag_table, shift_table = pl.pallas_call(
        functools.partial(table_kernel, groups, bins, freq_dev),
        out_shape=(
            jax.ShapeDtypeStruct((groups, BLOCK), jnp.int32),
            jax.ShapeDtypeStruct((bins, 2 * BLOCK, 2 * SLOWNESS), jnp.bfloat16),
            jax.ShapeDtypeStruct((bins, 2, 2 * groups, SLOWNESS), jnp.float32),
        ),
        in_specs=[vmem],
        out_specs=(vmem, vmem, vmem),
        compiler_params=params,
        cost_estimate=pl.CostEstimate(flops=10**7, bytes_accessed=4 * 10**6, transcendentals=0),
        name="slant_tables",
    )(block_position.reshape(1, groups))
    earlier = []
    for (start, size), order in zip(pieces, orders):
        last = start + size == bins
        shape = (groups, parts, message_rows, BLOCK) if last else (2 * size, groups, SLOWNESS)
        terms = pl.pallas_call(
            functools.partial(stack_kernel, order, start, size, parts if last else None),
            out_shape=jax.ShapeDtypeStruct(shape, jnp.float32),
            in_specs=[vmem] * (groups + 3 + len(earlier)),
            out_specs=vmem,
            scratch_shapes=[
                pltpu.VMEM((groups, size, rows, BLOCK), jnp.bfloat16),
                pltpu.VMEM((size, BLOCK, groups * rows), jnp.bfloat16),
                pltpu.VMEM((2, (size * 2 * groups + 1) * 8, BLOCK), jnp.float32),
            ],
            compiler_params=params,
            cost_estimate=pl.CostEstimate(
                flops=2 * 10**8, bytes_accessed=4 * 10**6, transcendentals=0
            ),
            name="stack_and_slant",
        )(
            *[chunks[parts_of[distance, (start, size)]] for distance in order],
            places,
            lag_table,
            shift_table,
            *earlier,
        )
        earlier.append(terms)
    terms = terms.reshape(groups * parts, message_rows, BLOCK)
    arrived = lax.all_to_all(
        terms,
        ("chan", "freq"),
        split_axis=0,
        concat_axis=0,
        axis_index_groups=[list(range(groups * parts))[::-1]],
        tiled=True,
    )
    spans, table = time_table(groups, parts, bins, slow_dev, message_rows)
    return pl.pallas_call(
        functools.partial(image_kernel, slow_dev, spans),
        out_shape=jax.ShapeDtypeStruct((1, slow_dev, LAG_TIMES), jnp.float32),
        in_specs=[vmem, vmem],
        out_specs=vmem,
        compiler_params=params,
        name="sum_of_bins",
    )(arrived, jnp.asarray(table))


def solution(mesh):
    return jax.shard_map(
        shards,
        mesh=mesh,
        in_specs=(P(None, None, "freq", "chan"), P()),
        out_specs=P("chan", "freq", None),
        check_vma=False,
    )
```

```python
import functools
import math

import jax
import jax.numpy as jnp
import numpy as np
from jax import lax
from jax.experimental import pallas as pl
from jax.experimental.pallas import tpu as pltpu
from jax.sharding import PartitionSpec as P

SEGMENTS = 32
FREQS = 256
BLOCK = 128
SLOWNESS = 256
LAG_TIMES = 512
MODULUS = 8 * FREQS * BLOCK


def unit_phase(numerator):
    quarter = MODULUS // 4
    turn = numerator & (MODULUS - 1)
    quadrant = lax.shift_right_logical(turn + quarter // 2, quarter.bit_length() - 1)
    x = (turn - quadrant * quarter).astype(jnp.float32) * (2.0 * math.pi / MODULUS)
    y = x * x
    sine = x * (1.0 + y * (-1.0 / 6 + y * (1.0 / 120 + y * (-1.0 / 5040 + y * (1.0 / 362880)))))
    cosine = 1.0 + y * (-0.5 + y * (1.0 / 24 + y * (-1.0 / 720 + y * (1.0 / 40320))))
    odd = (quadrant & 1) == 1
    first = jnp.where(odd, sine, cosine)
    second = jnp.where(odd, cosine, sine)
    first = jnp.where(((quadrant + 1) & 2) == 2, -first, first)
    second = jnp.where((quadrant & 2) == 2, -second, second)
    return first, second


def halves(value):
    high = value.astype(jnp.bfloat16)
    return high, (value - high.astype(jnp.float32)).astype(jnp.bfloat16)


def copy_kernel(in_ref, out_ref):
    out_ref[...] = in_ref[...]


def table_kernel(groups, bins, freq_dev, position_ref, place_ref, lag_ref, shift_ref):
    low_rows = lax.broadcasted_iota(jnp.int32, (8, SLOWNESS), 0)
    high_rows = lax.broadcasted_iota(jnp.int32, (BLOCK // 8, SLOWNESS), 0) * 8
    shift_rows = lax.broadcasted_iota(jnp.int32, (2 * groups, SLOWNESS), 0)
    shift_rows = jnp.where(shift_rows < groups, shift_rows, shift_rows - groups - 1) * BLOCK
    own_group = lax.axis_index("chan")
    first_bin = lax.axis_index("freq") * freq_dev + own_group * bins
    sender = lax.broadcasted_iota(jnp.int32, (groups, groups), 1)
    distance = lax.broadcasted_iota(jnp.int32, (groups, groups), 0)
    sends = lax.rem(own_group + groups - distance, groups) == sender
    places = jnp.sum(jnp.where(sends, position_ref[...], 0), axis=1, keepdims=True)
    place_ref[...] = jnp.broadcast_to(places, place_ref.shape)

    def one_bin(f, carry):
        def phases(rows):
            slow = lax.broadcasted_iota(jnp.int32, rows.shape, 1) - SLOWNESS // 2
            return unit_phase((first_bin + f) * slow * rows)

        low_cos, low_sin = phases(low_rows)
        high_cos, high_sin = phases(high_rows)
        low_cos, low_sin = low_cos[None], low_sin[None]
        high_cos, high_sin = high_cos[:, None], high_sin[:, None]
        lag_cos = (high_cos * low_cos - high_sin * low_sin).reshape(BLOCK, SLOWNESS)
        lag_sin = (high_sin * low_cos + high_cos * low_sin).reshape(BLOCK, SLOWNESS)
        cos_high, cos_low = halves(lag_cos)
        sin_high, sin_low = halves(lag_sin)
        lag_ref[f, :BLOCK, :SLOWNESS] = cos_high
        lag_ref[f, BLOCK:, :SLOWNESS] = cos_low
        lag_ref[f, :BLOCK, SLOWNESS:] = sin_high
        lag_ref[f, BLOCK:, SLOWNESS:] = sin_low
        shift_cos, shift_sin = phases(shift_rows)
        shift_ref[f, 0] = shift_cos
        shift_ref[f, 1] = shift_sin
        return carry

    lax.fori_loop(0, bins, one_bin, 0)


def chunk_kernel(cuts, spec_ref, *refs):
    rows, groups, bins, _ = spec_ref.shape
    out_refs, wide_ref = refs[-1 - len(cuts) : -1], refs[-1]
    own_group = lax.axis_index("chan")
    widened = []
    for (distance, start, size), out_ref in zip(cuts, out_refs):
        if distance not in widened:
            group = lax.rem(own_group + distance, groups)
            index = len(widened)
            value = spec_ref[:, group].astype(jnp.float32).reshape(rows * bins, BLOCK)
            wide_ref[index, : rows * bins] = value
            widened.append(distance)
        for f in range(size):
            value = wide_ref[widened.index(distance), pl.ds(start + f, rows, stride=bins), :]
            out_ref[f] = value.astype(jnp.bfloat16)


def stack_weights(groups):
    row = lax.broadcasted_iota(jnp.int32, (2 * groups, BLOCK), 0)
    lag = lax.broadcasted_iota(jnp.int32, (2 * groups, BLOCK), 1)
    delta = jnp.where(row < groups, row, row - groups)
    lag = jnp.where(row < groups, lag, lag - BLOCK)
    usable = (lag > -BLOCK) & ((delta >= 1) | (lag >= 1))
    count = SEGMENTS * (groups - delta) * (BLOCK - jnp.abs(lag))
    scale = math.sqrt(SEGMENTS / FREQS)
    return jnp.where(usable, scale / jnp.maximum(count, 1).astype(jnp.float32), 0.0)


def stack_kernel(order, start, bins, parts, *refs):
    groups = len(order)
    chunk_refs = refs[:groups]
    place_ref, lag_ref, shift_ref = refs[groups : groups + 3]
    placed_ref, left_ref, part_ref = refs[-3:]
    if parts is None:
        out_ref, rest_ref = refs[-5:-3]
        rest_ref[...] = chunk_refs[-2][bins:]
    else:
        earlier_refs, out_ref = refs[groups + 3 : -4], refs[-4]
    rows = placed_ref.shape[2]
    windows = rows // 2
    places = place_ref[...]
    for distance, chunk_ref in zip(order, chunk_refs):
        skip = start if chunk_ref.shape[0] > bins else 0
        placed_ref[places[distance, 0]] = chunk_ref[skip : skip + bins]

    row_index = lax.broadcasted_iota(jnp.int32, (BLOCK, BLOCK), 0)
    lag_index = lax.broadcasted_iota(jnp.int32, (BLOCK, BLOCK), 1)
    mirror = jnp.where(row_index + lag_index == BLOCK - 1, 1.0, 0.0).astype(jnp.bfloat16)
    ahead = lag_index <= row_index

    for f in range(bins):
        left_ref[f] = lax.dot_general(
            mirror,
            placed_ref[:, f].reshape(groups * rows, BLOCK),
            (((1,), (1,)), ((), ())),
            preferred_element_type=jnp.float32,
        ).astype(jnp.bfloat16)

    for f in range(bins):
        right = []
        for place in range(groups):
            value = placed_ref[place, f]
            real, imag = value[:windows], value[windows:]
            right.append(
                jnp.concatenate(
                    [jnp.concatenate([real, imag], 1), jnp.concatenate([imag, -real], 1)], 0
                )
            )
        right = jnp.concatenate(right, 0)
        for delta in range(groups):
            panel = jnp.dot(
                left_ref[f, :, : rows * (groups - delta)],
                right[rows * delta :],
                preferred_element_type=jnp.float32,
            )
            for half in range(2):
                lanes = slice(half * BLOCK, (half + 1) * BLOCK)
                skewed = pltpu.roll(panel[:, lanes], 1, 1, stride=1, stride_axis=0)
                forward = jnp.where(ahead, skewed, 0.0).reshape(-1, 8, BLOCK).sum(0)
                backward = jnp.where(ahead, 0.0, skewed).reshape(-1, 8, BLOCK).sum(0)
                first = (f * 2 * groups + delta) * 8
                part_ref[half, first : first + 8] = forward
                part_ref[half, first + groups * 8 : first + groups * 8 + 8] = backward

    lags = []
    for half in range(2):
        summed = part_ref[half, pl.ds(0, bins * 2 * groups, stride=8), :]
        for sublane in range(1, 8):
            summed = summed + part_ref[half, pl.ds(sublane, bins * 2 * groups, stride=8), :]
        lags.append(summed)
    weight = stack_weights(groups)

    terms = []
    for f in range(bins):
        lag_rows = slice(f * 2 * groups, (f + 1) * 2 * groups)
        means = jnp.concatenate([half[lag_rows] * weight for half in lags], 0)
        mean_high, mean_low = halves(means)
        spread = jnp.concatenate(
            [
                jnp.concatenate([mean_high, mean_high], 1),
                jnp.concatenate([mean_low, jnp.zeros_like(mean_low)], 1),
            ],
            0,
        )
        product = jnp.dot(spread, lag_ref[start + f], preferred_element_type=jnp.float32)
        product = product[: 4 * groups] + product[4 * groups :]
        by_cos, by_sin = product[:, :SLOWNESS], product[:, SLOWNESS:]
        real = by_cos[: 2 * groups] - by_sin[2 * groups :]
        imag = by_sin[: 2 * groups] + by_cos[2 * groups :]
        shift_cos, shift_sin = shift_ref[start + f, 0], shift_ref[start + f, 1]
        turned_re = real * shift_cos - imag * shift_sin
        turned_im = real * shift_sin + imag * shift_cos
        terms.append(turned_re[:groups] + turned_re[groups:])
        terms.append(turned_im[:groups] + turned_im[groups:])

    if parts is None:
        for entry, term in enumerate(terms):
            out_ref[entry] = term
        return
    for earlier_ref in reversed(earlier_refs):
        terms = [earlier_ref[entry] for entry in range(earlier_ref.shape[0])] + terms
    slow_dev = SLOWNESS // parts
    spans = BLOCK // slow_dev
    span_index = lax.broadcasted_iota(jnp.int32, (groups, BLOCK), 1) // slow_dev
    for part in range(parts):
        source = (part % spans) * slow_dev
        lanes = slice(part // spans * BLOCK, (part // spans + 1) * BLOCK)
        for row in range(out_ref.shape[2]):
            packed = jnp.zeros((groups, BLOCK), jnp.float32)
            for span, term in enumerate(terms[row * spans : (row + 1) * spans]):
                moved = pltpu.roll(term[:, lanes], (span * slow_dev - source) % BLOCK, 1)
                packed = jnp.where(span_index == span, moved, packed)
            for delta in range(groups):
                out_ref[groups - 1 - delta, parts - 1 - part, row] = packed[delta]


def image_kernel(slow_dev, spans, term_ref, table_ref, out_ref):
    arrived = term_ref[...]
    turned = arrived.reshape(-1, BLOCK).T
    sums = []
    for odd, chosen in enumerate(spans):
        terms = jnp.concatenate(
            [turned[span * slow_dev : (span + 1) * slow_dev] for span in chosen], 1
        )
        high, low = halves(terms)
        by_high = jnp.dot(
            jnp.concatenate([high, low], 0), table_ref[odd, 0], preferred_element_type=jnp.float32
        )
        by_low = jnp.dot(high, table_ref[odd, 1], preferred_element_type=jnp.float32)
        sums.append(by_high[:slow_dev] + by_high[slow_dev:] + by_low)
    even, odd = sums
    out_ref[0, :, : LAG_TIMES // 2] = even - odd
    out_ref[0, :, LAG_TIMES // 2 :] = even + odd


def time_table(groups, parts, bins, slow_dev, message_rows):
    count = min(BLOCK // slow_dev, 2 * bins)
    spans = [[span for span in range(count) if span // 2 % 2 == odd] for odd in range(2)]
    tables = []
    for chosen in spans:
        span, group, part, row = np.meshgrid(
            chosen,
            np.arange(groups)[::-1],
            np.arange(parts)[::-1],
            np.arange(message_rows),
            indexing="ij",
        )
        entry = row * count + span
        freq = (part * groups + group) * bins + entry // 2
        lag_time = np.arange(LAG_TIMES // 2)
        angle = 2.0 * math.pi / LAG_TIMES * ((freq[..., None] * lag_time) % LAG_TIMES)
        table = np.where((entry % 2 == 0)[..., None], np.cos(angle), -np.sin(angle))
        table = table.reshape(-1, LAG_TIMES // 2).astype(np.float32)
        high = table.astype(jnp.bfloat16)
        low = (table - high.astype(np.float32)).astype(jnp.bfloat16)
        tables.append(np.stack([high, low]))
    return spans, np.stack(tables)


def shards(spectra, block_position):
    groups = lax.axis_size("chan")
    parts = lax.axis_size("freq")
    rows = spectra.shape[0] * spectra.shape[1]
    freq_dev = spectra.shape[2]
    bins = freq_dev // groups
    slow_dev = SLOWNESS // parts
    message_rows = -(-2 * bins * slow_dev // BLOCK)
    vmem = pl.BlockSpec(memory_space=pltpu.VMEM)
    anywhere = pl.BlockSpec(memory_space=pl.ANY)
    params = pltpu.CompilerParams(vmem_limit_bytes=32 * 1024 * 1024)

    whole = spectra.reshape(rows, groups, bins, BLOCK)

    def cut(cuts, *earlier):
        distances = {distance for distance, _, _ in cuts}
        return pl.pallas_call(
            functools.partial(chunk_kernel, cuts),
            out_shape=tuple(
                jax.ShapeDtypeStruct((size, rows, BLOCK), jnp.bfloat16) for _, _, size in cuts
            ),
            in_specs=[vmem] + [anywhere] * len(earlier),
            out_specs=(vmem,) * len(cuts),
            scratch_shapes=[pltpu.VMEM((len(distances), (rows + 1) * bins, BLOCK), jnp.float32)],
            compiler_params=params,
            cost_estimate=pl.CostEstimate(flops=10**7, bytes_accessed=10**6, transcendentals=0),
            name="chunks_of_bins",
        )(whole, *earlier)

    late = max(1, 3 * bins // 8) if bins > 1 else 0
    pieces = [(0, bins - late), (bins - late, late)] if late else [(0, bins)]
    far_first = sorted(range(1, groups), key=lambda steps: abs(2 * steps - groups))
    order, kept = far_first + [0], far_first[-1]
    parts_of = {
        (distance, piece): (distance, *((0, bins) if distance in (kept, 0) else piece))
        for piece in pieces
        for distance in order
    }
    cuts = sorted(dict.fromkeys(parts_of.values()), key=lambda key: key[0] != kept)
    (first_chunk,) = cut(cuts[:1])
    chunks = dict(zip(cuts, (first_chunk, *cut(cuts[1:], first_chunk))))
    for key in cuts:
        if key[0]:
            pairs = [(source, (source + key[0]) % groups) for source in range(groups)]
            chunks[key] = lax.ppermute(chunks[key], "chan", pairs)
    chunks[cuts[0]] = pl.pallas_call(
        copy_kernel,
        out_shape=jax.ShapeDtypeStruct(first_chunk.shape, jnp.bfloat16),
        in_specs=[vmem],
        out_specs=vmem,
        compiler_params=params,
        name="first_arrived",
    )(chunks[cuts[0]])
    places, lag_table, shift_table = pl.pallas_call(
        functools.partial(table_kernel, groups, bins, freq_dev),
        out_shape=(
            jax.ShapeDtypeStruct((groups, BLOCK), jnp.int32),
            jax.ShapeDtypeStruct((bins, 2 * BLOCK, 2 * SLOWNESS), jnp.bfloat16),
            jax.ShapeDtypeStruct((bins, 2, 2 * groups, SLOWNESS), jnp.float32),
        ),
        in_specs=[vmem],
        out_specs=(vmem, vmem, vmem),
        compiler_params=params,
        cost_estimate=pl.CostEstimate(flops=10**7, bytes_accessed=4 * 10**6, transcendentals=0),
        name="slant_tables",
    )(block_position.reshape(1, groups))
    earlier = []
    for start, size in pieces:
        last = start + size == bins
        if last:
            shapes = (jax.ShapeDtypeStruct((groups, parts, message_rows, BLOCK), jnp.float32),)
        else:
            shapes = (
                jax.ShapeDtypeStruct((2 * size, groups, SLOWNESS), jnp.float32),
                jax.ShapeDtypeStruct((bins - size, rows, BLOCK), jnp.bfloat16),
            )
        terms, *rest = pl.pallas_call(
            functools.partial(stack_kernel, order, start, size, parts if last else None),
            out_shape=shapes,
            in_specs=[vmem] * (groups + 3 + len(earlier)),
            out_specs=(vmem,) * len(shapes),
            scratch_shapes=[
                pltpu.VMEM((groups, size, rows, BLOCK), jnp.bfloat16),
                pltpu.VMEM((size, BLOCK, groups * rows), jnp.bfloat16),
                pltpu.VMEM((2, (size * 2 * groups + 1) * 8, BLOCK), jnp.float32),
            ],
            compiler_params=params,
            cost_estimate=pl.CostEstimate(
                flops=2 * 10**8, bytes_accessed=4 * 10**6, transcendentals=0
            ),
            name="stack_and_slant",
        )(
            *[chunks[parts_of[distance, (start, size)]] for distance in order],
            places,
            lag_table,
            shift_table,
            *earlier,
        )
        earlier.append(terms)
        if not last:
            chunks[parts_of[kept, (start, size)]] = rest[0]
    terms = terms.reshape(groups * parts, message_rows, BLOCK)
    arrived = lax.all_to_all(
        terms,
        ("chan", "freq"),
        split_axis=0,
        concat_axis=0,
        axis_index_groups=[list(range(groups * parts))[::-1]],
        tiled=True,
    )
    spans, table = time_table(groups, parts, bins, slow_dev, message_rows)
    return pl.pallas_call(
        functools.partial(image_kernel, slow_dev, spans),
        out_shape=jax.ShapeDtypeStruct((1, slow_dev, LAG_TIMES), jnp.float32),
        in_specs=[vmem, vmem],
        out_specs=vmem,
        compiler_params=params,
        name="sum_of_bins",
    )(arrived, jnp.asarray(table))


def solution(mesh):
    return jax.shard_map(
        shards,
        mesh=mesh,
        in_specs=(P(None, None, "freq", "chan"), P()),
        out_specs=P("chan", "freq", None),
        check_vma=False,
    )
```

```python
import functools
import math

import jax
import jax.numpy as jnp
import numpy as np
from jax import lax
from jax.experimental import pallas as pl
from jax.experimental.pallas import tpu as pltpu
from jax.sharding import PartitionSpec as P

SEGMENTS = 32
FREQS = 256
BLOCK = 128
SLOWNESS = 256
LAG_TIMES = 512
MODULUS = 8 * FREQS * BLOCK


def unit_phase(numerator):
    quarter = MODULUS // 4
    turn = numerator & (MODULUS - 1)
    quadrant = lax.shift_right_logical(turn + quarter // 2, quarter.bit_length() - 1)
    x = (turn - quadrant * quarter).astype(jnp.float32) * (2.0 * math.pi / MODULUS)
    y = x * x
    sine = x * (1.0 + y * (-1.0 / 6 + y * (1.0 / 120 + y * (-1.0 / 5040 + y * (1.0 / 362880)))))
    cosine = 1.0 + y * (-0.5 + y * (1.0 / 24 + y * (-1.0 / 720 + y * (1.0 / 40320))))
    odd = (quadrant & 1) == 1
    first = jnp.where(odd, sine, cosine)
    second = jnp.where(odd, cosine, sine)
    first = jnp.where(((quadrant + 1) & 2) == 2, -first, first)
    second = jnp.where((quadrant & 2) == 2, -second, second)
    return first, second


def halves(value):
    high = value.astype(jnp.bfloat16)
    return high, (value - high.astype(jnp.float32)).astype(jnp.bfloat16)


def copy_kernel(in_ref, out_ref):
    out_ref[...] = in_ref[...]


def table_kernel(groups, bins, freq_dev, position_ref, place_ref, lag_ref, shift_ref):
    low_rows = lax.broadcasted_iota(jnp.int32, (8, SLOWNESS), 0)
    high_rows = lax.broadcasted_iota(jnp.int32, (BLOCK // 8, SLOWNESS), 0) * 8
    shift_rows = lax.broadcasted_iota(jnp.int32, (2 * groups, SLOWNESS), 0)
    shift_rows = jnp.where(shift_rows < groups, shift_rows, shift_rows - groups - 1) * BLOCK
    own_group = lax.axis_index("chan")
    first_bin = lax.axis_index("freq") * freq_dev + own_group * bins
    sender = lax.broadcasted_iota(jnp.int32, (groups, groups), 1)
    distance = lax.broadcasted_iota(jnp.int32, (groups, groups), 0)
    sends = lax.rem(own_group + groups - distance, groups) == sender
    places = jnp.sum(jnp.where(sends, position_ref[...], 0), axis=1, keepdims=True)
    place_ref[...] = jnp.broadcast_to(places, place_ref.shape)

    def one_bin(f, carry):
        def phases(rows):
            slow = lax.broadcasted_iota(jnp.int32, rows.shape, 1) - SLOWNESS // 2
            return unit_phase((first_bin + f) * slow * rows)

        low_cos, low_sin = phases(low_rows)
        high_cos, high_sin = phases(high_rows)
        low_cos, low_sin = low_cos[None], low_sin[None]
        high_cos, high_sin = high_cos[:, None], high_sin[:, None]
        lag_cos = (high_cos * low_cos - high_sin * low_sin).reshape(BLOCK, SLOWNESS)
        lag_sin = (high_sin * low_cos + high_cos * low_sin).reshape(BLOCK, SLOWNESS)
        cos_high, cos_low = halves(lag_cos)
        sin_high, sin_low = halves(lag_sin)
        lag_ref[f, :BLOCK, :SLOWNESS] = cos_high
        lag_ref[f, BLOCK:, :SLOWNESS] = cos_low
        lag_ref[f, :BLOCK, SLOWNESS:] = sin_high
        lag_ref[f, BLOCK:, SLOWNESS:] = sin_low
        shift_cos, shift_sin = phases(shift_rows)
        shift_ref[f, 0] = shift_cos
        shift_ref[f, 1] = shift_sin
        return carry

    lax.fori_loop(0, bins, one_bin, 0)


def chunk_kernel(cuts, spec_ref, *refs):
    rows, groups, bins, _ = spec_ref.shape
    out_refs, wide_ref = refs[-1 - len(cuts) : -1], refs[-1]
    own_group = lax.axis_index("chan")
    widened = []
    for (distance, start, size), out_ref in zip(cuts, out_refs):
        if distance not in widened:
            group = lax.rem(own_group + distance, groups)
            index = len(widened)
            value = spec_ref[:, group].astype(jnp.float32).reshape(rows * bins, BLOCK)
            wide_ref[index, : rows * bins] = value
            widened.append(distance)
        for f in range(size):
            value = wide_ref[widened.index(distance), pl.ds(start + f, rows, stride=bins), :]
            out_ref[f] = value.astype(jnp.bfloat16)


def stack_weights(groups):
    row = lax.broadcasted_iota(jnp.int32, (2 * groups, BLOCK), 0)
    lag = lax.broadcasted_iota(jnp.int32, (2 * groups, BLOCK), 1)
    delta = jnp.where(row < groups, row, row - groups)
    lag = jnp.where(row < groups, lag, lag - BLOCK)
    usable = (lag > -BLOCK) & ((delta >= 1) | (lag >= 1))
    count = SEGMENTS * (groups - delta) * (BLOCK - jnp.abs(lag))
    scale = math.sqrt(SEGMENTS / FREQS)
    return jnp.where(usable, scale / jnp.maximum(count, 1).astype(jnp.float32), 0.0)


def stack_kernel(order, start, bins, parts, *refs):
    groups = len(order)
    chunk_refs = refs[:groups]
    place_ref, lag_ref, shift_ref = refs[groups : groups + 3]
    earlier_refs = refs[groups + 3 : -4]
    out_ref, placed_ref, left_ref, part_ref = refs[-4:]
    rows = placed_ref.shape[2]
    windows = rows // 2
    places = place_ref[...]
    for distance, chunk_ref in zip(order, chunk_refs):
        placed_ref[places[distance, 0]] = chunk_ref[...]

    row_index = lax.broadcasted_iota(jnp.int32, (BLOCK, BLOCK), 0)
    lag_index = lax.broadcasted_iota(jnp.int32, (BLOCK, BLOCK), 1)
    mirror = jnp.where(row_index + lag_index == BLOCK - 1, 1.0, 0.0).astype(jnp.bfloat16)
    ahead = lag_index <= row_index

    for f in range(bins):
        left_ref[f] = lax.dot_general(
            mirror,
            placed_ref[:, f].reshape(groups * rows, BLOCK),
            (((1,), (1,)), ((), ())),
            preferred_element_type=jnp.float32,
        ).astype(jnp.bfloat16)

    for f in range(bins):
        right = []
        for place in range(groups):
            value = placed_ref[place, f]
            real, imag = value[:windows], value[windows:]
            right.append(
                jnp.concatenate(
                    [jnp.concatenate([real, imag], 1), jnp.concatenate([imag, -real], 1)], 0
                )
            )
        right = jnp.concatenate(right, 0)
        for delta in range(groups):
            panel = jnp.dot(
                left_ref[f, :, : rows * (groups - delta)],
                right[rows * delta :],
                preferred_element_type=jnp.float32,
            )
            for half in range(2):
                lanes = slice(half * BLOCK, (half + 1) * BLOCK)
                skewed = pltpu.roll(panel[:, lanes], 1, 1, stride=1, stride_axis=0)
                forward = jnp.where(ahead, skewed, 0.0).reshape(-1, 8, BLOCK).sum(0)
                backward = jnp.where(ahead, 0.0, skewed).reshape(-1, 8, BLOCK).sum(0)
                first = (f * 2 * groups + delta) * 8
                part_ref[half, first : first + 8] = forward
                part_ref[half, first + groups * 8 : first + groups * 8 + 8] = backward

    lags = []
    for half in range(2):
        summed = part_ref[half, pl.ds(0, bins * 2 * groups, stride=8), :]
        for sublane in range(1, 8):
            summed = summed + part_ref[half, pl.ds(sublane, bins * 2 * groups, stride=8), :]
        lags.append(summed)
    weight = stack_weights(groups)

    terms = []
    for f in range(bins):
        lag_rows = slice(f * 2 * groups, (f + 1) * 2 * groups)
        means = jnp.concatenate([half[lag_rows] * weight for half in lags], 0)
        mean_high, mean_low = halves(means)
        spread = jnp.concatenate(
            [
                jnp.concatenate([mean_high, mean_high], 1),
                jnp.concatenate([mean_low, jnp.zeros_like(mean_low)], 1),
            ],
            0,
        )
        product = jnp.dot(spread, lag_ref[start + f], preferred_element_type=jnp.float32)
        product = product[: 4 * groups] + product[4 * groups :]
        by_cos, by_sin = product[:, :SLOWNESS], product[:, SLOWNESS:]
        real = by_cos[: 2 * groups] - by_sin[2 * groups :]
        imag = by_sin[: 2 * groups] + by_cos[2 * groups :]
        shift_cos, shift_sin = shift_ref[start + f, 0], shift_ref[start + f, 1]
        turned_re = real * shift_cos - imag * shift_sin
        turned_im = real * shift_sin + imag * shift_cos
        terms.append(turned_re[:groups] + turned_re[groups:])
        terms.append(turned_im[:groups] + turned_im[groups:])

    if parts is None:
        for entry, term in enumerate(terms):
            out_ref[entry] = term
        return
    for earlier_ref in reversed(earlier_refs):
        terms = [earlier_ref[entry] for entry in range(earlier_ref.shape[0])] + terms
    slow_dev = SLOWNESS // parts
    spans = BLOCK // slow_dev
    span_index = lax.broadcasted_iota(jnp.int32, (groups, BLOCK), 1) // slow_dev
    for part in range(parts):
        source = (part % spans) * slow_dev
        lanes = slice(part // spans * BLOCK, (part // spans + 1) * BLOCK)
        for row in range(out_ref.shape[2]):
            packed = jnp.zeros((groups, BLOCK), jnp.float32)
            for span, term in enumerate(terms[row * spans : (row + 1) * spans]):
                moved = pltpu.roll(term[:, lanes], (span * slow_dev - source) % BLOCK, 1)
                packed = jnp.where(span_index == span, moved, packed)
            for delta in range(groups):
                out_ref[groups - 1 - delta, parts - 1 - part, row] = packed[delta]


def image_kernel(slow_dev, spans, term_ref, table_ref, out_ref):
    arrived = term_ref[...]
    turned = arrived.reshape(-1, BLOCK).T
    sums = []
    for odd, chosen in enumerate(spans):
        terms = jnp.concatenate(
            [turned[span * slow_dev : (span + 1) * slow_dev] for span in chosen], 1
        )
        high, low = halves(terms)
        by_high = jnp.dot(
            jnp.concatenate([high, low], 0), table_ref[odd, 0], preferred_element_type=jnp.float32
        )
        by_low = jnp.dot(high, table_ref[odd, 1], preferred_element_type=jnp.float32)
        sums.append(by_high[:slow_dev] + by_high[slow_dev:] + by_low)
    even, odd = sums
    out_ref[0, :, : LAG_TIMES // 2] = even - odd
    out_ref[0, :, LAG_TIMES // 2 :] = even + odd


def time_table(groups, parts, bins, slow_dev, message_rows):
    count = min(BLOCK // slow_dev, 2 * bins)
    spans = [[span for span in range(count) if span // 2 % 2 == odd] for odd in range(2)]
    tables = []
    for chosen in spans:
        span, group, part, row = np.meshgrid(
            chosen,
            np.arange(groups)[::-1],
            np.arange(parts)[::-1],
            np.arange(message_rows),
            indexing="ij",
        )
        entry = row * count + span
        freq = (part * groups + group) * bins + entry // 2
        lag_time = np.arange(LAG_TIMES // 2)
        angle = 2.0 * math.pi / LAG_TIMES * ((freq[..., None] * lag_time) % LAG_TIMES)
        table = np.where((entry % 2 == 0)[..., None], np.cos(angle), -np.sin(angle))
        table = table.reshape(-1, LAG_TIMES // 2).astype(np.float32)
        high = table.astype(jnp.bfloat16)
        low = (table - high.astype(np.float32)).astype(jnp.bfloat16)
        tables.append(np.stack([high, low]))
    return spans, np.stack(tables)


def shards(spectra, block_position):
    groups = lax.axis_size("chan")
    parts = lax.axis_size("freq")
    rows = spectra.shape[0] * spectra.shape[1]
    freq_dev = spectra.shape[2]
    bins = freq_dev // groups
    slow_dev = SLOWNESS // parts
    message_rows = -(-2 * bins * slow_dev // BLOCK)
    vmem = pl.BlockSpec(memory_space=pltpu.VMEM)
    anywhere = pl.BlockSpec(memory_space=pl.ANY)
    params = pltpu.CompilerParams(vmem_limit_bytes=32 * 1024 * 1024)

    whole = spectra.reshape(rows, groups, bins, BLOCK)

    def cut(cuts, *earlier):
        distances = {distance for distance, _, _ in cuts}
        return pl.pallas_call(
            functools.partial(chunk_kernel, cuts),
            out_shape=tuple(
                jax.ShapeDtypeStruct((size, rows, BLOCK), jnp.bfloat16) for _, _, size in cuts
            ),
            in_specs=[vmem] + [anywhere] * len(earlier),
            out_specs=(vmem,) * len(cuts),
            scratch_shapes=[pltpu.VMEM((len(distances), (rows + 1) * bins, BLOCK), jnp.float32)],
            compiler_params=params,
            cost_estimate=pl.CostEstimate(flops=10**7, bytes_accessed=10**6, transcendentals=0),
            name="chunks_of_bins",
        )(whole, *earlier)

    late = max(1, 3 * bins // 8) if bins > 1 else 0
    pieces = [(0, bins - late), (bins - late, late)] if late else [(0, bins)]
    order = sorted(range(1, groups), key=lambda steps: abs(2 * steps - groups)) + [0]
    cuts = [(distance, *piece) for piece in pieces for distance in order]
    (first_chunk,) = cut(cuts[:1])
    chunks = dict(zip(cuts, (first_chunk, *cut(cuts[1:], first_chunk))))
    for key in cuts:
        if key[0]:
            pairs = [(source, (source + key[0]) % groups) for source in range(groups)]
            chunks[key] = lax.ppermute(chunks[key], "chan", pairs)
    chunks[cuts[0]] = pl.pallas_call(
        copy_kernel,
        out_shape=jax.ShapeDtypeStruct(first_chunk.shape, jnp.bfloat16),
        in_specs=[vmem],
        out_specs=vmem,
        compiler_params=params,
        name="first_arrived",
    )(chunks[cuts[0]])
    places, lag_table, shift_table = pl.pallas_call(
        functools.partial(table_kernel, groups, bins, freq_dev),
        out_shape=(
            jax.ShapeDtypeStruct((groups, BLOCK), jnp.int32),
            jax.ShapeDtypeStruct((bins, 2 * BLOCK, 2 * SLOWNESS), jnp.bfloat16),
            jax.ShapeDtypeStruct((bins, 2, 2 * groups, SLOWNESS), jnp.float32),
        ),
        in_specs=[vmem],
        out_specs=(vmem, vmem, vmem),
        compiler_params=params,
        cost_estimate=pl.CostEstimate(flops=10**7, bytes_accessed=4 * 10**6, transcendentals=0),
        name="slant_tables",
    )(block_position.reshape(1, groups))
    earlier = []
    for start, size in pieces:
        last = start + size == bins
        shape = (groups, parts, message_rows, BLOCK) if last else (2 * size, groups, SLOWNESS)
        terms = pl.pallas_call(
            functools.partial(stack_kernel, order, start, size, parts if last else None),
            out_shape=jax.ShapeDtypeStruct(shape, jnp.float32),
            in_specs=[vmem] * (groups + 3 + len(earlier)),
            out_specs=vmem,
            scratch_shapes=[
                pltpu.VMEM((groups, size, rows, BLOCK), jnp.bfloat16),
                pltpu.VMEM((size, BLOCK, groups * rows), jnp.bfloat16),
                pltpu.VMEM((2, (size * 2 * groups + 1) * 8, BLOCK), jnp.float32),
            ],
            compiler_params=params,
            cost_estimate=pl.CostEstimate(
                flops=2 * 10**8, bytes_accessed=4 * 10**6, transcendentals=0
            ),
            name="stack_and_slant",
        )(
            *[chunks[distance, start, size] for distance in order],
            places,
            lag_table,
            shift_table,
            *earlier,
        )
        earlier.append(terms)
    terms = terms.reshape(groups * parts, message_rows, BLOCK)
    arrived = lax.all_to_all(
        terms,
        ("chan", "freq"),
        split_axis=0,
        concat_axis=0,
        axis_index_groups=[list(range(groups * parts))[::-1]],
        tiled=True,
    )
    spans, table = time_table(groups, parts, bins, slow_dev, message_rows)
    return pl.pallas_call(
        functools.partial(image_kernel, slow_dev, spans),
        out_shape=jax.ShapeDtypeStruct((1, slow_dev, LAG_TIMES), jnp.float32),
        in_specs=[vmem, vmem],
        out_specs=vmem,
        compiler_params=params,
        name="sum_of_bins",
    )(arrived, jnp.asarray(table))


def solution(mesh):
    return jax.shard_map(
        shards,
        mesh=mesh,
        in_specs=(P(None, None, "freq", "chan"), P()),
        out_specs=P("chan", "freq", None),
        check_vma=False,
    )
```

```python
import functools
import math

import jax
import jax.numpy as jnp
import numpy as np
from jax import lax
from jax.experimental import pallas as pl
from jax.experimental.pallas import tpu as pltpu
from jax.sharding import PartitionSpec as P

SEGMENTS = 32
FREQS = 256
BLOCK = 128
SLOWNESS = 256
LAG_TIMES = 512
MODULUS = 8 * FREQS * BLOCK


def unit_phase(numerator):
    quarter = MODULUS // 4
    turn = numerator & (MODULUS - 1)
    quadrant = lax.shift_right_logical(turn + quarter // 2, quarter.bit_length() - 1)
    x = (turn - quadrant * quarter).astype(jnp.float32) * (2.0 * math.pi / MODULUS)
    y = x * x
    sine = x * (1.0 + y * (-1.0 / 6 + y * (1.0 / 120 + y * (-1.0 / 5040 + y * (1.0 / 362880)))))
    cosine = 1.0 + y * (-0.5 + y * (1.0 / 24 + y * (-1.0 / 720 + y * (1.0 / 40320))))
    odd = (quadrant & 1) == 1
    first = jnp.where(odd, sine, cosine)
    second = jnp.where(odd, cosine, sine)
    first = jnp.where(((quadrant + 1) & 2) == 2, -first, first)
    second = jnp.where((quadrant & 2) == 2, -second, second)
    return first, second


def halves(value):
    high = value.astype(jnp.bfloat16)
    return high, (value - high.astype(jnp.float32)).astype(jnp.bfloat16)


def copy_kernel(in_ref, out_ref):
    out_ref[...] = in_ref[...]


def table_kernel(groups, bins, freq_dev, position_ref, place_ref, lag_ref, shift_ref):
    low_rows = lax.broadcasted_iota(jnp.int32, (8, SLOWNESS), 0)
    high_rows = lax.broadcasted_iota(jnp.int32, (BLOCK // 8, SLOWNESS), 0) * 8
    shift_rows = lax.broadcasted_iota(jnp.int32, (2 * groups, SLOWNESS), 0)
    shift_rows = jnp.where(shift_rows < groups, shift_rows, shift_rows - groups - 1) * BLOCK
    own_group = lax.axis_index("chan")
    first_bin = lax.axis_index("freq") * freq_dev + own_group * bins
    sender = lax.broadcasted_iota(jnp.int32, (groups, groups), 1)
    distance = lax.broadcasted_iota(jnp.int32, (groups, groups), 0)
    sends = lax.rem(own_group + groups - distance, groups) == sender
    places = jnp.sum(jnp.where(sends, position_ref[...], 0), axis=1, keepdims=True)
    place_ref[...] = jnp.broadcast_to(places, place_ref.shape)

    def one_bin(f, carry):
        def phases(rows):
            slow = lax.broadcasted_iota(jnp.int32, rows.shape, 1) - SLOWNESS // 2
            return unit_phase((first_bin + f) * slow * rows)

        low_cos, low_sin = phases(low_rows)
        high_cos, high_sin = phases(high_rows)
        low_cos, low_sin = low_cos[None], low_sin[None]
        high_cos, high_sin = high_cos[:, None], high_sin[:, None]
        lag_cos = (high_cos * low_cos - high_sin * low_sin).reshape(BLOCK, SLOWNESS)
        lag_sin = (high_sin * low_cos + high_cos * low_sin).reshape(BLOCK, SLOWNESS)
        cos_high, cos_low = halves(lag_cos)
        sin_high, sin_low = halves(lag_sin)
        lag_ref[f, :BLOCK, :SLOWNESS] = cos_high
        lag_ref[f, BLOCK:, :SLOWNESS] = cos_low
        lag_ref[f, :BLOCK, SLOWNESS:] = sin_high
        lag_ref[f, BLOCK:, SLOWNESS:] = sin_low
        shift_cos, shift_sin = phases(shift_rows)
        shift_ref[f, 0] = shift_cos
        shift_ref[f, 1] = shift_sin
        return carry

    lax.fori_loop(0, bins, one_bin, 0)


def chunk_kernel(cuts, spec_ref, *refs):
    rows, groups, bins, _ = spec_ref.shape
    out_refs, wide_ref = refs[-1 - len(cuts) : -1], refs[-1]
    own_group = lax.axis_index("chan")
    widened = []
    for (distance, start, size), out_ref in zip(cuts, out_refs):
        if distance not in widened:
            group = lax.rem(own_group + distance, groups)
            index = len(widened)
            value = spec_ref[:, group].astype(jnp.float32).reshape(rows * bins, BLOCK)
            wide_ref[index, : rows * bins] = value
            widened.append(distance)
        for f in range(size):
            value = wide_ref[widened.index(distance), pl.ds(start + f, rows, stride=bins), :]
            out_ref[f] = value.astype(jnp.bfloat16)


def stack_weights(groups):
    row = lax.broadcasted_iota(jnp.int32, (2 * groups, BLOCK), 0)
    lag = lax.broadcasted_iota(jnp.int32, (2 * groups, BLOCK), 1)
    delta = jnp.where(row < groups, row, row - groups)
    lag = jnp.where(row < groups, lag, lag - BLOCK)
    usable = (lag > -BLOCK) & ((delta >= 1) | (lag >= 1))
    count = SEGMENTS * (groups - delta) * (BLOCK - jnp.abs(lag))
    scale = math.sqrt(SEGMENTS / FREQS)
    return jnp.where(usable, scale / jnp.maximum(count, 1).astype(jnp.float32), 0.0)


def stack_kernel(order, start, bins, parts, *refs):
    groups = len(order)
    chunk_refs = refs[:groups]
    place_ref, lag_ref, shift_ref = refs[groups : groups + 3]
    earlier_refs = refs[groups + 3 : -4]
    out_ref, placed_ref, left_ref, part_ref = refs[-4:]
    rows = placed_ref.shape[2]
    windows = rows // 2
    places = place_ref[...]
    for distance, chunk_ref in zip(order, chunk_refs):
        placed_ref[places[distance, 0]] = chunk_ref[...]

    row_index = lax.broadcasted_iota(jnp.int32, (BLOCK, BLOCK), 0)
    lag_index = lax.broadcasted_iota(jnp.int32, (BLOCK, BLOCK), 1)
    mirror = jnp.where(row_index + lag_index == BLOCK - 1, 1.0, 0.0).astype(jnp.bfloat16)
    ahead = lag_index <= row_index

    for f in range(bins):
        left_ref[f] = lax.dot_general(
            mirror,
            placed_ref[:, f].reshape(groups * rows, BLOCK),
            (((1,), (1,)), ((), ())),
            preferred_element_type=jnp.float32,
        ).astype(jnp.bfloat16)

    for f in range(bins):
        right = []
        for place in range(groups):
            value = placed_ref[place, f]
            real, imag = value[:windows], value[windows:]
            right.append(
                jnp.concatenate(
                    [jnp.concatenate([real, imag], 1), jnp.concatenate([imag, -real], 1)], 0
                )
            )
        right = jnp.concatenate(right, 0)
        for delta in range(groups):
            panel = jnp.dot(
                left_ref[f, :, : rows * (groups - delta)],
                right[rows * delta :],
                preferred_element_type=jnp.float32,
            )
            for half in range(2):
                lanes = slice(half * BLOCK, (half + 1) * BLOCK)
                skewed = pltpu.roll(panel[:, lanes], 1, 1, stride=1, stride_axis=0)
                forward = jnp.where(ahead, skewed, 0.0).reshape(-1, 8, BLOCK).sum(0)
                backward = jnp.where(ahead, 0.0, skewed).reshape(-1, 8, BLOCK).sum(0)
                first = (f * 2 * groups + delta) * 8
                part_ref[half, first : first + 8] = forward
                part_ref[half, first + groups * 8 : first + groups * 8 + 8] = backward

    lags = []
    for half in range(2):
        summed = part_ref[half, pl.ds(0, bins * 2 * groups, stride=8), :]
        for sublane in range(1, 8):
            summed = summed + part_ref[half, pl.ds(sublane, bins * 2 * groups, stride=8), :]
        lags.append(summed)
    weight = stack_weights(groups)

    terms = []
    for f in range(bins):
        lag_rows = slice(f * 2 * groups, (f + 1) * 2 * groups)
        means = jnp.concatenate([half[lag_rows] * weight for half in lags], 0)
        mean_high, mean_low = halves(means)
        spread = jnp.concatenate(
            [
                jnp.concatenate([mean_high, mean_high], 1),
                jnp.concatenate([mean_low, jnp.zeros_like(mean_low)], 1),
            ],
            0,
        )
        product = jnp.dot(spread, lag_ref[start + f], preferred_element_type=jnp.float32)
        product = product[: 4 * groups] + product[4 * groups :]
        by_cos, by_sin = product[:, :SLOWNESS], product[:, SLOWNESS:]
        real = by_cos[: 2 * groups] - by_sin[2 * groups :]
        imag = by_sin[: 2 * groups] + by_cos[2 * groups :]
        shift_cos, shift_sin = shift_ref[start + f, 0], shift_ref[start + f, 1]
        turned_re = real * shift_cos - imag * shift_sin
        turned_im = real * shift_sin + imag * shift_cos
        terms.append(turned_re[:groups] + turned_re[groups:])
        terms.append(turned_im[:groups] + turned_im[groups:])

    if parts is None:
        for entry, term in enumerate(terms):
            out_ref[entry] = term
        return
    for earlier_ref in reversed(earlier_refs):
        terms = [earlier_ref[entry] for entry in range(earlier_ref.shape[0])] + terms
    slow_dev = SLOWNESS // parts
    spans = BLOCK // slow_dev
    span_index = lax.broadcasted_iota(jnp.int32, (groups, BLOCK), 1) // slow_dev
    for part in range(parts):
        source = (part % spans) * slow_dev
        lanes = slice(part // spans * BLOCK, (part // spans + 1) * BLOCK)
        for row in range(out_ref.shape[2]):
            packed = jnp.zeros((groups, BLOCK), jnp.float32)
            for span, term in enumerate(terms[row * spans : (row + 1) * spans]):
                moved = pltpu.roll(term[:, lanes], (span * slow_dev - source) % BLOCK, 1)
                packed = jnp.where(span_index == span, moved, packed)
            for delta in range(groups):
                out_ref[groups - 1 - delta, parts - 1 - part, row] = packed[delta]


def image_kernel(slow_dev, spans, term_ref, table_ref, out_ref):
    arrived = term_ref[...]
    turned = arrived.reshape(-1, BLOCK).T
    sums = []
    for odd, chosen in enumerate(spans):
        terms = jnp.concatenate(
            [turned[span * slow_dev : (span + 1) * slow_dev] for span in chosen], 1
        )
        high, low = halves(terms)
        by_high = jnp.dot(
            jnp.concatenate([high, low], 0), table_ref[odd, 0], preferred_element_type=jnp.float32
        )
        by_low = jnp.dot(high, table_ref[odd, 1], preferred_element_type=jnp.float32)
        sums.append(by_high[:slow_dev] + by_high[slow_dev:] + by_low)
    even, odd = sums
    out_ref[0, :, : LAG_TIMES // 2] = even - odd
    out_ref[0, :, LAG_TIMES // 2 :] = even + odd


def time_table(groups, parts, bins, slow_dev, message_rows):
    count = min(BLOCK // slow_dev, 2 * bins)
    spans = [[span for span in range(count) if span // 2 % 2 == odd] for odd in range(2)]
    tables = []
    for chosen in spans:
        span, group, part, row = np.meshgrid(
            chosen,
            np.arange(groups)[::-1],
            np.arange(parts)[::-1],
            np.arange(message_rows),
            indexing="ij",
        )
        entry = row * count + span
        freq = (part * groups + group) * bins + entry // 2
        lag_time = np.arange(LAG_TIMES // 2)
        angle = 2.0 * math.pi / LAG_TIMES * ((freq[..., None] * lag_time) % LAG_TIMES)
        table = np.where((entry % 2 == 0)[..., None], np.cos(angle), -np.sin(angle))
        table = table.reshape(-1, LAG_TIMES // 2).astype(np.float32)
        high = table.astype(jnp.bfloat16)
        low = (table - high.astype(np.float32)).astype(jnp.bfloat16)
        tables.append(np.stack([high, low]))
    return spans, np.stack(tables)


def shards(spectra, block_position):
    groups = lax.axis_size("chan")
    parts = lax.axis_size("freq")
    rows = spectra.shape[0] * spectra.shape[1]
    freq_dev = spectra.shape[2]
    bins = freq_dev // groups
    slow_dev = SLOWNESS // parts
    message_rows = -(-2 * bins * slow_dev // BLOCK)
    vmem = pl.BlockSpec(memory_space=pltpu.VMEM)
    anywhere = pl.BlockSpec(memory_space=pl.ANY)
    params = pltpu.CompilerParams(vmem_limit_bytes=32 * 1024 * 1024)

    whole = spectra.reshape(rows, groups, bins, BLOCK)

    def cut(cuts, *earlier):
        distances = {distance for distance, _, _ in cuts}
        return pl.pallas_call(
            functools.partial(chunk_kernel, cuts),
            out_shape=tuple(
                jax.ShapeDtypeStruct((size, rows, BLOCK), jnp.bfloat16) for _, _, size in cuts
            ),
            in_specs=[vmem] + [anywhere] * len(earlier),
            out_specs=(vmem,) * len(cuts),
            scratch_shapes=[pltpu.VMEM((len(distances), (rows + 1) * bins, BLOCK), jnp.float32)],
            compiler_params=params,
            cost_estimate=pl.CostEstimate(flops=10**7, bytes_accessed=10**6, transcendentals=0),
            name="chunks_of_bins",
        )(whole, *earlier)

    late = max(1, bins // 4) if bins > 1 else 0
    pieces = [(0, bins - late), (bins - late, late)] if late else [(0, bins)]
    order = sorted(range(1, groups), key=lambda steps: abs(2 * steps - groups)) + [0]
    cuts = [(distance, *piece) for piece in pieces for distance in order]
    (first_chunk,) = cut(cuts[:1])
    chunks = dict(zip(cuts, (first_chunk, *cut(cuts[1:], first_chunk))))
    for key in cuts:
        if key[0]:
            pairs = [(source, (source + key[0]) % groups) for source in range(groups)]
            chunks[key] = lax.ppermute(chunks[key], "chan", pairs)
    chunks[cuts[0]] = pl.pallas_call(
        copy_kernel,
        out_shape=jax.ShapeDtypeStruct(first_chunk.shape, jnp.bfloat16),
        in_specs=[vmem],
        out_specs=vmem,
        compiler_params=params,
        name="first_arrived",
    )(chunks[cuts[0]])
    places, lag_table, shift_table = pl.pallas_call(
        functools.partial(table_kernel, groups, bins, freq_dev),
        out_shape=(
            jax.ShapeDtypeStruct((groups, BLOCK), jnp.int32),
            jax.ShapeDtypeStruct((bins, 2 * BLOCK, 2 * SLOWNESS), jnp.bfloat16),
            jax.ShapeDtypeStruct((bins, 2, 2 * groups, SLOWNESS), jnp.float32),
        ),
        in_specs=[vmem],
        out_specs=(vmem, vmem, vmem),
        compiler_params=params,
        cost_estimate=pl.CostEstimate(flops=10**7, bytes_accessed=4 * 10**6, transcendentals=0),
        name="slant_tables",
    )(block_position.reshape(1, groups))
    earlier = []
    for start, size in pieces:
        last = start + size == bins
        shape = (groups, parts, message_rows, BLOCK) if last else (2 * size, groups, SLOWNESS)
        terms = pl.pallas_call(
            functools.partial(stack_kernel, order, start, size, parts if last else None),
            out_shape=jax.ShapeDtypeStruct(shape, jnp.float32),
            in_specs=[vmem] * (groups + 3 + len(earlier)),
            out_specs=vmem,
            scratch_shapes=[
                pltpu.VMEM((groups, size, rows, BLOCK), jnp.bfloat16),
                pltpu.VMEM((size, BLOCK, groups * rows), jnp.bfloat16),
                pltpu.VMEM((2, (size * 2 * groups + 1) * 8, BLOCK), jnp.float32),
            ],
            compiler_params=params,
            cost_estimate=pl.CostEstimate(
                flops=2 * 10**8, bytes_accessed=4 * 10**6, transcendentals=0
            ),
            name="stack_and_slant",
        )(
            *[chunks[distance, start, size] for distance in order],
            places,
            lag_table,
            shift_table,
            *earlier,
        )
        earlier.append(terms)
    terms = terms.reshape(groups * parts, message_rows, BLOCK)
    arrived = lax.all_to_all(
        terms,
        ("chan", "freq"),
        split_axis=0,
        concat_axis=0,
        axis_index_groups=[list(range(groups * parts))[::-1]],
        tiled=True,
    )
    spans, table = time_table(groups, parts, bins, slow_dev, message_rows)
    return pl.pallas_call(
        functools.partial(image_kernel, slow_dev, spans),
        out_shape=jax.ShapeDtypeStruct((1, slow_dev, LAG_TIMES), jnp.float32),
        in_specs=[vmem, vmem],
        out_specs=vmem,
        compiler_params=params,
        name="sum_of_bins",
    )(arrived, jnp.asarray(table))


def solution(mesh):
    return jax.shard_map(
        shards,
        mesh=mesh,
        in_specs=(P(None, None, "freq", "chan"), P()),
        out_specs=P("chan", "freq", None),
        check_vma=False,
    )
```

```python
import functools
import math

import jax
import jax.numpy as jnp
import numpy as np
from jax import lax
from jax.experimental import pallas as pl
from jax.experimental.pallas import tpu as pltpu
from jax.sharding import PartitionSpec as P

SEGMENTS = 32
FREQS = 256
BLOCK = 128
SLOWNESS = 256
LAG_TIMES = 512
MODULUS = 8 * FREQS * BLOCK


def unit_phase(numerator):
    quarter = MODULUS // 4
    turn = numerator & (MODULUS - 1)
    quadrant = lax.shift_right_logical(turn + quarter // 2, quarter.bit_length() - 1)
    x = (turn - quadrant * quarter).astype(jnp.float32) * (2.0 * math.pi / MODULUS)
    y = x * x
    sine = x * (1.0 + y * (-1.0 / 6 + y * (1.0 / 120 + y * (-1.0 / 5040 + y * (1.0 / 362880)))))
    cosine = 1.0 + y * (-0.5 + y * (1.0 / 24 + y * (-1.0 / 720 + y * (1.0 / 40320))))
    odd = (quadrant & 1) == 1
    first = jnp.where(odd, sine, cosine)
    second = jnp.where(odd, cosine, sine)
    first = jnp.where(((quadrant + 1) & 2) == 2, -first, first)
    second = jnp.where((quadrant & 2) == 2, -second, second)
    return first, second


def halves(value):
    high = value.astype(jnp.bfloat16)
    return high, (value - high.astype(jnp.float32)).astype(jnp.bfloat16)


def copy_kernel(in_ref, out_ref):
    out_ref[...] = in_ref[...]


def table_kernel(groups, bins, freq_dev, position_ref, place_ref, lag_ref, shift_ref):
    low_rows = lax.broadcasted_iota(jnp.int32, (8, SLOWNESS), 0)
    high_rows = lax.broadcasted_iota(jnp.int32, (BLOCK // 8, SLOWNESS), 0) * 8
    shift_rows = lax.broadcasted_iota(jnp.int32, (2 * groups, SLOWNESS), 0)
    shift_rows = jnp.where(shift_rows < groups, shift_rows, shift_rows - groups - 1) * BLOCK
    own_group = lax.axis_index("chan")
    first_bin = lax.axis_index("freq") * freq_dev + own_group * bins
    sender = lax.broadcasted_iota(jnp.int32, (groups, groups), 1)
    mask = lax.broadcasted_iota(jnp.int32, (groups, groups), 0)
    sends = lax.bitwise_xor(own_group, mask) == sender
    places = jnp.sum(jnp.where(sends, position_ref[...], 0), axis=1, keepdims=True)
    place_ref[...] = jnp.broadcast_to(places, place_ref.shape)

    def one_bin(f, carry):
        def phases(rows):
            slow = lax.broadcasted_iota(jnp.int32, rows.shape, 1) - SLOWNESS // 2
            return unit_phase((first_bin + f) * slow * rows)

        low_cos, low_sin = phases(low_rows)
        high_cos, high_sin = phases(high_rows)
        low_cos, low_sin = low_cos[None], low_sin[None]
        high_cos, high_sin = high_cos[:, None], high_sin[:, None]
        lag_cos = (high_cos * low_cos - high_sin * low_sin).reshape(BLOCK, SLOWNESS)
        lag_sin = (high_sin * low_cos + high_cos * low_sin).reshape(BLOCK, SLOWNESS)
        cos_high, cos_low = halves(lag_cos)
        sin_high, sin_low = halves(lag_sin)
        lag_ref[f, :BLOCK, :SLOWNESS] = cos_high
        lag_ref[f, BLOCK:, :SLOWNESS] = cos_low
        lag_ref[f, :BLOCK, SLOWNESS:] = sin_high
        lag_ref[f, BLOCK:, SLOWNESS:] = sin_low
        shift_cos, shift_sin = phases(shift_rows)
        shift_ref[f, 0] = shift_cos
        shift_ref[f, 1] = shift_sin
        return carry

    lax.fori_loop(0, bins, one_bin, 0)


def chunk_kernel(cuts, spec_ref, *refs):
    rows, groups, bins, _ = spec_ref.shape
    out_refs, wide_ref = refs[-1 - len(cuts) : -1], refs[-1]
    own_group = lax.axis_index("chan")
    widened = []
    for (mask, start, size), out_ref in zip(cuts, out_refs):
        if mask not in widened:
            group = lax.bitwise_xor(own_group, mask)
            index = len(widened)
            value = spec_ref[:, group].astype(jnp.float32).reshape(rows * bins, BLOCK)
            wide_ref[index, : rows * bins] = value
            widened.append(mask)
        for f in range(size):
            value = wide_ref[widened.index(mask), pl.ds(start + f, rows, stride=bins), :]
            out_ref[f] = value.astype(jnp.bfloat16)


def stack_weights(groups):
    row = lax.broadcasted_iota(jnp.int32, (2 * groups, BLOCK), 0)
    lag = lax.broadcasted_iota(jnp.int32, (2 * groups, BLOCK), 1)
    delta = jnp.where(row < groups, row, row - groups)
    lag = jnp.where(row < groups, lag, lag - BLOCK)
    usable = (lag > -BLOCK) & ((delta >= 1) | (lag >= 1))
    count = SEGMENTS * (groups - delta) * (BLOCK - jnp.abs(lag))
    scale = math.sqrt(SEGMENTS / FREQS)
    return jnp.where(usable, scale / jnp.maximum(count, 1).astype(jnp.float32), 0.0)


def stack_kernel(order, start, bins, parts, *refs):
    groups = len(order)
    chunk_refs = refs[:groups]
    place_ref, lag_ref, shift_ref = refs[groups : groups + 3]
    earlier_refs = refs[groups + 3 : -4]
    out_ref, placed_ref, left_ref, part_ref = refs[-4:]
    rows = placed_ref.shape[2]
    windows = rows // 2
    places = place_ref[...]
    for mask, chunk_ref in zip(order, chunk_refs):
        placed_ref[places[mask, 0]] = chunk_ref[...]

    row_index = lax.broadcasted_iota(jnp.int32, (BLOCK, BLOCK), 0)
    lag_index = lax.broadcasted_iota(jnp.int32, (BLOCK, BLOCK), 1)
    mirror = jnp.where(row_index + lag_index == BLOCK - 1, 1.0, 0.0).astype(jnp.bfloat16)
    ahead = lag_index <= row_index

    for f in range(bins):
        left_ref[f] = lax.dot_general(
            mirror,
            placed_ref[:, f].reshape(groups * rows, BLOCK),
            (((1,), (1,)), ((), ())),
            preferred_element_type=jnp.float32,
        ).astype(jnp.bfloat16)

    for f in range(bins):
        right = []
        for place in range(groups):
            value = placed_ref[place, f]
            real, imag = value[:windows], value[windows:]
            right.append(
                jnp.concatenate(
                    [jnp.concatenate([real, imag], 1), jnp.concatenate([imag, -real], 1)], 0
                )
            )
        right = jnp.concatenate(right, 0)
        for delta in range(groups):
            panel = jnp.dot(
                left_ref[f, :, : rows * (groups - delta)],
                right[rows * delta :],
                preferred_element_type=jnp.float32,
            )
            for half in range(2):
                lanes = slice(half * BLOCK, (half + 1) * BLOCK)
                skewed = pltpu.roll(panel[:, lanes], 1, 1, stride=1, stride_axis=0)
                forward = jnp.where(ahead, skewed, 0.0).reshape(-1, 8, BLOCK).sum(0)
                backward = jnp.where(ahead, 0.0, skewed).reshape(-1, 8, BLOCK).sum(0)
                first = (f * 2 * groups + delta) * 8
                part_ref[half, first : first + 8] = forward
                part_ref[half, first + groups * 8 : first + groups * 8 + 8] = backward

    lags = []
    for half in range(2):
        summed = part_ref[half, pl.ds(0, bins * 2 * groups, stride=8), :]
        for sublane in range(1, 8):
            summed = summed + part_ref[half, pl.ds(sublane, bins * 2 * groups, stride=8), :]
        lags.append(summed)
    weight = stack_weights(groups)

    terms = []
    for f in range(bins):
        lag_rows = slice(f * 2 * groups, (f + 1) * 2 * groups)
        means = jnp.concatenate([half[lag_rows] * weight for half in lags], 0)
        mean_high, mean_low = halves(means)
        spread = jnp.concatenate(
            [
                jnp.concatenate([mean_high, mean_high], 1),
                jnp.concatenate([mean_low, jnp.zeros_like(mean_low)], 1),
            ],
            0,
        )
        product = jnp.dot(spread, lag_ref[start + f], preferred_element_type=jnp.float32)
        product = product[: 4 * groups] + product[4 * groups :]
        by_cos, by_sin = product[:, :SLOWNESS], product[:, SLOWNESS:]
        real = by_cos[: 2 * groups] - by_sin[2 * groups :]
        imag = by_sin[: 2 * groups] + by_cos[2 * groups :]
        shift_cos, shift_sin = shift_ref[start + f, 0], shift_ref[start + f, 1]
        turned_re = real * shift_cos - imag * shift_sin
        turned_im = real * shift_sin + imag * shift_cos
        terms.append(turned_re[:groups] + turned_re[groups:])
        terms.append(turned_im[:groups] + turned_im[groups:])

    if parts is None:
        for entry, term in enumerate(terms):
            out_ref[entry] = term
        return
    for earlier_ref in reversed(earlier_refs):
        terms = [earlier_ref[entry] for entry in range(earlier_ref.shape[0])] + terms
    slow_dev = SLOWNESS // parts
    spans = BLOCK // slow_dev
    span_index = lax.broadcasted_iota(jnp.int32, (groups, BLOCK), 1) // slow_dev
    for part in range(parts):
        source = (part % spans) * slow_dev
        lanes = slice(part // spans * BLOCK, (part // spans + 1) * BLOCK)
        for row in range(out_ref.shape[2]):
            packed = jnp.zeros((groups, BLOCK), jnp.float32)
            for span, term in enumerate(terms[row * spans : (row + 1) * spans]):
                moved = pltpu.roll(term[:, lanes], (span * slow_dev - source) % BLOCK, 1)
                packed = jnp.where(span_index == span, moved, packed)
            for delta in range(groups):
                out_ref[groups - 1 - delta, parts - 1 - part, row] = packed[delta]


def image_kernel(slow_dev, spans, term_ref, table_ref, out_ref):
    arrived = term_ref[...]
    turned = arrived.reshape(-1, BLOCK).T
    sums = []
    for odd, chosen in enumerate(spans):
        terms = jnp.concatenate(
            [turned[span * slow_dev : (span + 1) * slow_dev] for span in chosen], 1
        )
        high, low = halves(terms)
        by_high = jnp.dot(
            jnp.concatenate([high, low], 0), table_ref[odd, 0], preferred_element_type=jnp.float32
        )
        by_low = jnp.dot(high, table_ref[odd, 1], preferred_element_type=jnp.float32)
        sums.append(by_high[:slow_dev] + by_high[slow_dev:] + by_low)
    even, odd = sums
    out_ref[0, :, : LAG_TIMES // 2] = even - odd
    out_ref[0, :, LAG_TIMES // 2 :] = even + odd


def time_table(groups, parts, bins, slow_dev, message_rows):
    count = min(BLOCK // slow_dev, 2 * bins)
    spans = [[span for span in range(count) if span // 2 % 2 == odd] for odd in range(2)]
    tables = []
    for chosen in spans:
        span, group, part, row = np.meshgrid(
            chosen,
            np.arange(groups)[::-1],
            np.arange(parts)[::-1],
            np.arange(message_rows),
            indexing="ij",
        )
        entry = row * count + span
        freq = (part * groups + group) * bins + entry // 2
        lag_time = np.arange(LAG_TIMES // 2)
        angle = 2.0 * math.pi / LAG_TIMES * ((freq[..., None] * lag_time) % LAG_TIMES)
        table = np.where((entry % 2 == 0)[..., None], np.cos(angle), -np.sin(angle))
        table = table.reshape(-1, LAG_TIMES // 2).astype(np.float32)
        high = table.astype(jnp.bfloat16)
        low = (table - high.astype(np.float32)).astype(jnp.bfloat16)
        tables.append(np.stack([high, low]))
    return spans, np.stack(tables)


def shards(spectra, block_position):
    groups = lax.axis_size("chan")
    parts = lax.axis_size("freq")
    rows = spectra.shape[0] * spectra.shape[1]
    freq_dev = spectra.shape[2]
    bins = freq_dev // groups
    slow_dev = SLOWNESS // parts
    message_rows = -(-2 * bins * slow_dev // BLOCK)
    vmem = pl.BlockSpec(memory_space=pltpu.VMEM)
    anywhere = pl.BlockSpec(memory_space=pl.ANY)
    params = pltpu.CompilerParams(vmem_limit_bytes=32 * 1024 * 1024)

    whole = spectra.reshape(rows, groups, bins, BLOCK)

    def cut(cuts, *earlier):
        masks = {mask for mask, _, _ in cuts}
        return pl.pallas_call(
            functools.partial(chunk_kernel, cuts),
            out_shape=tuple(
                jax.ShapeDtypeStruct((size, rows, BLOCK), jnp.bfloat16) for _, _, size in cuts
            ),
            in_specs=[vmem] + [anywhere] * len(earlier),
            out_specs=(vmem,) * len(cuts),
            scratch_shapes=[pltpu.VMEM((len(masks), (rows + 1) * bins, BLOCK), jnp.float32)],
            compiler_params=params,
            cost_estimate=pl.CostEstimate(flops=10**7, bytes_accessed=10**6, transcendentals=0),
            name="chunks_of_bins",
        )(whole, *earlier)

    late = max(1, 3 * bins // 8) if bins > 1 else 0
    pieces = [(0, bins - late), (bins - late, late)] if late else [(0, bins)]
    order = list(range(groups // 2, groups)) + list(range(groups // 2 - 1, -1, -1))
    cuts = [(mask, *piece) for piece in pieces for mask in order]
    (first_chunk,) = cut(cuts[:1])
    chunks = dict(zip(cuts, (first_chunk, *cut(cuts[1:], first_chunk))))
    for key in cuts:
        if key[0]:
            pairs = [(source, source ^ key[0]) for source in range(groups)]
            chunks[key] = lax.ppermute(chunks[key], "chan", pairs)
    chunks[cuts[0]] = pl.pallas_call(
        copy_kernel,
        out_shape=jax.ShapeDtypeStruct(first_chunk.shape, jnp.bfloat16),
        in_specs=[vmem],
        out_specs=vmem,
        compiler_params=params,
        name="first_arrived",
    )(chunks[cuts[0]])
    places, lag_table, shift_table = pl.pallas_call(
        functools.partial(table_kernel, groups, bins, freq_dev),
        out_shape=(
            jax.ShapeDtypeStruct((groups, BLOCK), jnp.int32),
            jax.ShapeDtypeStruct((bins, 2 * BLOCK, 2 * SLOWNESS), jnp.bfloat16),
            jax.ShapeDtypeStruct((bins, 2, 2 * groups, SLOWNESS), jnp.float32),
        ),
        in_specs=[vmem],
        out_specs=(vmem, vmem, vmem),
        compiler_params=params,
        cost_estimate=pl.CostEstimate(flops=10**7, bytes_accessed=4 * 10**6, transcendentals=0),
        name="slant_tables",
    )(block_position.reshape(1, groups))
    earlier = []
    for start, size in pieces:
        last = start + size == bins
        shape = (groups, parts, message_rows, BLOCK) if last else (2 * size, groups, SLOWNESS)
        terms = pl.pallas_call(
            functools.partial(stack_kernel, order, start, size, parts if last else None),
            out_shape=jax.ShapeDtypeStruct(shape, jnp.float32),
            in_specs=[vmem] * (groups + 3 + len(earlier)),
            out_specs=vmem,
            scratch_shapes=[
                pltpu.VMEM((groups, size, rows, BLOCK), jnp.bfloat16),
                pltpu.VMEM((size, BLOCK, groups * rows), jnp.bfloat16),
                pltpu.VMEM((2, (size * 2 * groups + 1) * 8, BLOCK), jnp.float32),
            ],
            compiler_params=params,
            cost_estimate=pl.CostEstimate(
                flops=2 * 10**8, bytes_accessed=4 * 10**6, transcendentals=0
            ),
            name="stack_and_slant",
        )(
            *[chunks[mask, start, size] for mask in order],
            places,
            lag_table,
            shift_table,
            *earlier,
        )
        earlier.append(terms)
    terms = terms.reshape(groups * parts, message_rows, BLOCK)
    arrived = lax.all_to_all(
        terms,
        ("chan", "freq"),
        split_axis=0,
        concat_axis=0,
        axis_index_groups=[list(range(groups * parts))[::-1]],
        tiled=True,
    )
    spans, table = time_table(groups, parts, bins, slow_dev, message_rows)
    return pl.pallas_call(
        functools.partial(image_kernel, slow_dev, spans),
        out_shape=jax.ShapeDtypeStruct((1, slow_dev, LAG_TIMES), jnp.float32),
        in_specs=[vmem, vmem],
        out_specs=vmem,
        compiler_params=params,
        name="sum_of_bins",
    )(arrived, jnp.asarray(table))


def solution(mesh):
    return jax.shard_map(
        shards,
        mesh=mesh,
        in_specs=(P(None, None, "freq", "chan"), P()),
        out_specs=P("chan", "freq", None),
        check_vma=False,
    )
```

```python
import functools
import math

import jax
import jax.numpy as jnp
import numpy as np
from jax import lax
from jax.experimental import pallas as pl
from jax.experimental.pallas import tpu as pltpu
from jax.sharding import PartitionSpec as P

SEGMENTS = 32
FREQS = 256
BLOCK = 128
SLOWNESS = 256
LAG_TIMES = 512
MODULUS = 8 * FREQS * BLOCK


def unit_phase(numerator):
    quarter = MODULUS // 4
    turn = numerator & (MODULUS - 1)
    quadrant = lax.shift_right_logical(turn + quarter // 2, quarter.bit_length() - 1)
    x = (turn - quadrant * quarter).astype(jnp.float32) * (2.0 * math.pi / MODULUS)
    y = x * x
    sine = x * (1.0 + y * (-1.0 / 6 + y * (1.0 / 120 + y * (-1.0 / 5040 + y * (1.0 / 362880)))))
    cosine = 1.0 + y * (-0.5 + y * (1.0 / 24 + y * (-1.0 / 720 + y * (1.0 / 40320))))
    odd = (quadrant & 1) == 1
    first = jnp.where(odd, sine, cosine)
    second = jnp.where(odd, cosine, sine)
    first = jnp.where(((quadrant + 1) & 2) == 2, -first, first)
    second = jnp.where((quadrant & 2) == 2, -second, second)
    return first, second


def halves(value):
    high = value.astype(jnp.bfloat16)
    return high, (value - high.astype(jnp.float32)).astype(jnp.bfloat16)


def copy_kernel(in_ref, out_ref):
    out_ref[...] = in_ref[...]


def table_kernel(groups, bins, freq_dev, position_ref, place_ref, lag_ref, shift_ref):
    low_rows = lax.broadcasted_iota(jnp.int32, (8, SLOWNESS), 0)
    high_rows = lax.broadcasted_iota(jnp.int32, (BLOCK // 8, SLOWNESS), 0) * 8
    shift_rows = lax.broadcasted_iota(jnp.int32, (2 * groups, SLOWNESS), 0)
    shift_rows = jnp.where(shift_rows < groups, shift_rows, shift_rows - groups - 1) * BLOCK
    own_group = lax.axis_index("chan")
    first_bin = lax.axis_index("freq") * freq_dev + own_group * bins
    sender = lax.broadcasted_iota(jnp.int32, (groups, groups), 1)
    distance = lax.broadcasted_iota(jnp.int32, (groups, groups), 0)
    sends = lax.rem(own_group + groups - distance, groups) == sender
    places = jnp.sum(jnp.where(sends, position_ref[...], 0), axis=1, keepdims=True)
    place_ref[...] = jnp.broadcast_to(places, place_ref.shape)

    def one_bin(f, carry):
        def phases(rows):
            slow = lax.broadcasted_iota(jnp.int32, rows.shape, 1) - SLOWNESS // 2
            return unit_phase((first_bin + f) * slow * rows)

        low_cos, low_sin = phases(low_rows)
        high_cos, high_sin = phases(high_rows)
        low_cos, low_sin = low_cos[None], low_sin[None]
        high_cos, high_sin = high_cos[:, None], high_sin[:, None]
        lag_cos = (high_cos * low_cos - high_sin * low_sin).reshape(BLOCK, SLOWNESS)
        lag_sin = (high_sin * low_cos + high_cos * low_sin).reshape(BLOCK, SLOWNESS)
        cos_high, cos_low = halves(lag_cos)
        sin_high, sin_low = halves(lag_sin)
        lag_ref[f, :BLOCK, :SLOWNESS] = cos_high
        lag_ref[f, BLOCK:, :SLOWNESS] = cos_low
        lag_ref[f, :BLOCK, SLOWNESS:] = sin_high
        lag_ref[f, BLOCK:, SLOWNESS:] = sin_low
        shift_cos, shift_sin = phases(shift_rows)
        shift_ref[f, 0] = shift_cos
        shift_ref[f, 1] = shift_sin
        return carry

    lax.fori_loop(0, bins, one_bin, 0)


def chunk_kernel(cuts, spec_ref, *refs):
    rows, groups, bins, _ = spec_ref.shape
    out_refs, wide_ref = refs[-1 - len(cuts) : -1], refs[-1]
    own_group = lax.axis_index("chan")
    widened = []
    for (distance, start, size), out_ref in zip(cuts, out_refs):
        if distance not in widened:
            group = lax.rem(own_group + distance, groups)
            index = len(widened)
            value = spec_ref[:, group].astype(jnp.float32).reshape(rows * bins, BLOCK)
            wide_ref[index, : rows * bins] = value
            widened.append(distance)
        for f in range(size):
            value = wide_ref[widened.index(distance), pl.ds(start + f, rows, stride=bins), :]
            out_ref[f] = value.astype(jnp.bfloat16)


def stack_weights(groups):
    row = lax.broadcasted_iota(jnp.int32, (2 * groups, BLOCK), 0)
    lag = lax.broadcasted_iota(jnp.int32, (2 * groups, BLOCK), 1)
    delta = jnp.where(row < groups, row, row - groups)
    lag = jnp.where(row < groups, lag, lag - BLOCK)
    usable = (lag > -BLOCK) & ((delta >= 1) | (lag >= 1))
    count = SEGMENTS * (groups - delta) * (BLOCK - jnp.abs(lag))
    scale = math.sqrt(SEGMENTS / FREQS)
    return jnp.where(usable, scale / jnp.maximum(count, 1).astype(jnp.float32), 0.0)


def stack_kernel(order, start, bins, parts, *refs):
    groups = len(order)
    chunk_refs = refs[:groups]
    place_ref, lag_ref, shift_ref = refs[groups : groups + 3]
    earlier_refs = refs[groups + 3 : -4]
    out_ref, placed_ref, left_ref, part_ref = refs[-4:]
    rows = placed_ref.shape[2]
    windows = rows // 2
    places = place_ref[...]
    for distance, chunk_ref in zip(order, chunk_refs):
        placed_ref[places[distance, 0]] = chunk_ref[...]

    row_index = lax.broadcasted_iota(jnp.int32, (BLOCK, BLOCK), 0)
    lag_index = lax.broadcasted_iota(jnp.int32, (BLOCK, BLOCK), 1)
    mirror = jnp.where(row_index + lag_index == BLOCK - 1, 1.0, 0.0).astype(jnp.bfloat16)
    ahead = lag_index <= row_index

    for f in range(bins):
        left_ref[f] = lax.dot_general(
            mirror,
            placed_ref[:, f].reshape(groups * rows, BLOCK),
            (((1,), (1,)), ((), ())),
            preferred_element_type=jnp.float32,
        ).astype(jnp.bfloat16)

    for f in range(bins):
        right = []
        for place in range(groups):
            value = placed_ref[place, f]
            real, imag = value[:windows], value[windows:]
            right.append(
                jnp.concatenate(
                    [jnp.concatenate([real, imag], 1), jnp.concatenate([imag, -real], 1)], 0
                )
            )
        right = jnp.concatenate(right, 0)
        for delta in range(groups):
            panel = jnp.dot(
                left_ref[f, :, : rows * (groups - delta)],
                right[rows * delta :],
                preferred_element_type=jnp.float32,
            )
            for half in range(2):
                lanes = slice(half * BLOCK, (half + 1) * BLOCK)
                skewed = pltpu.roll(panel[:, lanes], 1, 1, stride=1, stride_axis=0)
                forward = jnp.where(ahead, skewed, 0.0).reshape(-1, 8, BLOCK).sum(0)
                backward = jnp.where(ahead, 0.0, skewed).reshape(-1, 8, BLOCK).sum(0)
                first = (f * 2 * groups + delta) * 8
                part_ref[half, first : first + 8] = forward
                part_ref[half, first + groups * 8 : first + groups * 8 + 8] = backward

    lags = []
    for half in range(2):
        summed = part_ref[half, pl.ds(0, bins * 2 * groups, stride=8), :]
        for sublane in range(1, 8):
            summed = summed + part_ref[half, pl.ds(sublane, bins * 2 * groups, stride=8), :]
        lags.append(summed)
    weight = stack_weights(groups)

    terms = []
    for f in range(bins):
        lag_rows = slice(f * 2 * groups, (f + 1) * 2 * groups)
        means = jnp.concatenate([half[lag_rows] * weight for half in lags], 0)
        mean_high, mean_low = halves(means)
        spread = jnp.concatenate(
            [
                jnp.concatenate([mean_high, mean_high], 1),
                jnp.concatenate([mean_low, jnp.zeros_like(mean_low)], 1),
            ],
            0,
        )
        product = jnp.dot(spread, lag_ref[start + f], preferred_element_type=jnp.float32)
        product = product[: 4 * groups] + product[4 * groups :]
        by_cos, by_sin = product[:, :SLOWNESS], product[:, SLOWNESS:]
        real = by_cos[: 2 * groups] - by_sin[2 * groups :]
        imag = by_sin[: 2 * groups] + by_cos[2 * groups :]
        shift_cos, shift_sin = shift_ref[start + f, 0], shift_ref[start + f, 1]
        turned_re = real * shift_cos - imag * shift_sin
        turned_im = real * shift_sin + imag * shift_cos
        terms.append(turned_re[:groups] + turned_re[groups:])
        terms.append(turned_im[:groups] + turned_im[groups:])

    if parts is None:
        for entry, term in enumerate(terms):
            out_ref[entry] = term
        return
    for earlier_ref in reversed(earlier_refs):
        terms = [earlier_ref[entry] for entry in range(earlier_ref.shape[0])] + terms
    slow_dev = SLOWNESS // parts
    spans = BLOCK // slow_dev
    span_index = lax.broadcasted_iota(jnp.int32, (groups, BLOCK), 1) // slow_dev
    for part in range(parts):
        source = (part % spans) * slow_dev
        lanes = slice(part // spans * BLOCK, (part // spans + 1) * BLOCK)
        for row in range(out_ref.shape[2]):
            packed = jnp.zeros((groups, BLOCK), jnp.float32)
            for span, term in enumerate(terms[row * spans : (row + 1) * spans]):
                moved = pltpu.roll(term[:, lanes], (span * slow_dev - source) % BLOCK, 1)
                packed = jnp.where(span_index == span, moved, packed)
            for delta in range(groups):
                out_ref[groups - 1 - delta, parts - 1 - part, row] = packed[delta]


def image_kernel(slow_dev, spans, term_ref, table_ref, out_ref):
    arrived = term_ref[...]
    turned = arrived.reshape(-1, BLOCK).T
    sums = []
    for odd, chosen in enumerate(spans):
        terms = jnp.concatenate(
            [turned[span * slow_dev : (span + 1) * slow_dev] for span in chosen], 1
        )
        high, low = halves(terms)
        by_high = jnp.dot(
            jnp.concatenate([high, low], 0), table_ref[odd, 0], preferred_element_type=jnp.float32
        )
        by_low = jnp.dot(high, table_ref[odd, 1], preferred_element_type=jnp.float32)
        sums.append(by_high[:slow_dev] + by_high[slow_dev:] + by_low)
    even, odd = sums
    out_ref[0, :, : LAG_TIMES // 2] = even - odd
    out_ref[0, :, LAG_TIMES // 2 :] = even + odd


def time_table(groups, parts, bins, slow_dev, message_rows):
    count = min(BLOCK // slow_dev, 2 * bins)
    spans = [[span for span in range(count) if span // 2 % 2 == odd] for odd in range(2)]
    tables = []
    for chosen in spans:
        span, group, part, row = np.meshgrid(
            chosen,
            np.arange(groups)[::-1],
            np.arange(parts)[::-1],
            np.arange(message_rows),
            indexing="ij",
        )
        entry = row * count + span
        freq = (part * groups + group) * bins + entry // 2
        lag_time = np.arange(LAG_TIMES // 2)
        angle = 2.0 * math.pi / LAG_TIMES * ((freq[..., None] * lag_time) % LAG_TIMES)
        table = np.where((entry % 2 == 0)[..., None], np.cos(angle), -np.sin(angle))
        table = table.reshape(-1, LAG_TIMES // 2).astype(np.float32)
        high = table.astype(jnp.bfloat16)
        low = (table - high.astype(np.float32)).astype(jnp.bfloat16)
        tables.append(np.stack([high, low]))
    return spans, np.stack(tables)


def shards(spectra, block_position):
    groups = lax.axis_size("chan")
    parts = lax.axis_size("freq")
    rows = spectra.shape[0] * spectra.shape[1]
    freq_dev = spectra.shape[2]
    bins = freq_dev // groups
    slow_dev = SLOWNESS // parts
    message_rows = -(-2 * bins * slow_dev // BLOCK)
    vmem = pl.BlockSpec(memory_space=pltpu.VMEM)
    anywhere = pl.BlockSpec(memory_space=pl.ANY)
    params = pltpu.CompilerParams(vmem_limit_bytes=32 * 1024 * 1024)

    whole = spectra.reshape(rows, groups, bins, BLOCK)

    def cut(cuts, *earlier):
        distances = {distance for distance, _, _ in cuts}
        return pl.pallas_call(
            functools.partial(chunk_kernel, cuts),
            out_shape=tuple(
                jax.ShapeDtypeStruct((size, rows, BLOCK), jnp.bfloat16) for _, _, size in cuts
            ),
            in_specs=[vmem] + [anywhere] * len(earlier),
            out_specs=(vmem,) * len(cuts),
            scratch_shapes=[pltpu.VMEM((len(distances), (rows + 1) * bins, BLOCK), jnp.float32)],
            compiler_params=params,
            cost_estimate=pl.CostEstimate(flops=10**7, bytes_accessed=10**6, transcendentals=0),
            name="chunks_of_bins",
        )(whole, *earlier)

    late = bins // 2
    pieces = [(0, bins - late), (bins - late, late)] if late else [(0, bins)]
    order = sorted(range(1, groups), key=lambda steps: abs(2 * steps - groups)) + [0]
    cuts = [(distance, *piece) for piece in pieces for distance in order]
    (first_chunk,) = cut(cuts[:1])
    chunks = dict(zip(cuts, (first_chunk, *cut(cuts[1:], first_chunk))))
    for key in cuts:
        if key[0]:
            pairs = [(source, (source + key[0]) % groups) for source in range(groups)]
            chunks[key] = lax.ppermute(chunks[key], "chan", pairs)
    chunks[cuts[0]] = pl.pallas_call(
        copy_kernel,
        out_shape=jax.ShapeDtypeStruct(first_chunk.shape, jnp.bfloat16),
        in_specs=[vmem],
        out_specs=vmem,
        compiler_params=params,
        name="first_arrived",
    )(chunks[cuts[0]])
    places, lag_table, shift_table = pl.pallas_call(
        functools.partial(table_kernel, groups, bins, freq_dev),
        out_shape=(
            jax.ShapeDtypeStruct((groups, BLOCK), jnp.int32),
            jax.ShapeDtypeStruct((bins, 2 * BLOCK, 2 * SLOWNESS), jnp.bfloat16),
            jax.ShapeDtypeStruct((bins, 2, 2 * groups, SLOWNESS), jnp.float32),
        ),
        in_specs=[vmem],
        out_specs=(vmem, vmem, vmem),
        compiler_params=params,
        cost_estimate=pl.CostEstimate(flops=10**7, bytes_accessed=4 * 10**6, transcendentals=0),
        name="slant_tables",
    )(block_position.reshape(1, groups))
    earlier = []
    for start, size in pieces:
        last = start + size == bins
        shape = (groups, parts, message_rows, BLOCK) if last else (2 * size, groups, SLOWNESS)
        terms = pl.pallas_call(
            functools.partial(stack_kernel, order, start, size, parts if last else None),
            out_shape=jax.ShapeDtypeStruct(shape, jnp.float32),
            in_specs=[vmem] * (groups + 3 + len(earlier)),
            out_specs=vmem,
            scratch_shapes=[
                pltpu.VMEM((groups, size, rows, BLOCK), jnp.bfloat16),
                pltpu.VMEM((size, BLOCK, groups * rows), jnp.bfloat16),
                pltpu.VMEM((2, (size * 2 * groups + 1) * 8, BLOCK), jnp.float32),
            ],
            compiler_params=params,
            cost_estimate=pl.CostEstimate(
                flops=2 * 10**8, bytes_accessed=4 * 10**6, transcendentals=0
            ),
            name="stack_and_slant",
        )(
            *[chunks[distance, start, size] for distance in order],
            places,
            lag_table,
            shift_table,
            *earlier,
        )
        earlier.append(terms)
    terms = terms.reshape(groups * parts, message_rows, BLOCK)
    arrived = lax.all_to_all(
        terms,
        ("chan", "freq"),
        split_axis=0,
        concat_axis=0,
        axis_index_groups=[list(range(groups * parts))[::-1]],
        tiled=True,
    )
    spans, table = time_table(groups, parts, bins, slow_dev, message_rows)
    return pl.pallas_call(
        functools.partial(image_kernel, slow_dev, spans),
        out_shape=jax.ShapeDtypeStruct((1, slow_dev, LAG_TIMES), jnp.float32),
        in_specs=[vmem, vmem],
        out_specs=vmem,
        compiler_params=params,
        name="sum_of_bins",
    )(arrived, jnp.asarray(table))


def solution(mesh):
    return jax.shard_map(
        shards,
        mesh=mesh,
        in_specs=(P(None, None, "freq", "chan"), P()),
        out_specs=P("chan", "freq", None),
        check_vma=False,
    )
```

```python
import functools
import math

import jax
import jax.numpy as jnp
import numpy as np
from jax import lax
from jax.experimental import pallas as pl
from jax.experimental.pallas import tpu as pltpu
from jax.sharding import PartitionSpec as P

SEGMENTS = 32
FREQS = 256
BLOCK = 128
SLOWNESS = 256
LAG_TIMES = 512
MODULUS = 8 * FREQS * BLOCK


def unit_phase(numerator):
    quarter = MODULUS // 4
    turn = numerator & (MODULUS - 1)
    quadrant = lax.shift_right_logical(turn + quarter // 2, quarter.bit_length() - 1)
    x = (turn - quadrant * quarter).astype(jnp.float32) * (2.0 * math.pi / MODULUS)
    y = x * x
    sine = x * (1.0 + y * (-1.0 / 6 + y * (1.0 / 120 + y * (-1.0 / 5040 + y * (1.0 / 362880)))))
    cosine = 1.0 + y * (-0.5 + y * (1.0 / 24 + y * (-1.0 / 720 + y * (1.0 / 40320))))
    odd = (quadrant & 1) == 1
    first = jnp.where(odd, sine, cosine)
    second = jnp.where(odd, cosine, sine)
    first = jnp.where(((quadrant + 1) & 2) == 2, -first, first)
    second = jnp.where((quadrant & 2) == 2, -second, second)
    return first, second


def halves(value):
    high = value.astype(jnp.bfloat16)
    return high, (value - high.astype(jnp.float32)).astype(jnp.bfloat16)


def copy_kernel(in_ref, out_ref):
    out_ref[...] = in_ref[...]


def table_kernel(groups, bins, freq_dev, position_ref, place_ref, lag_ref, shift_ref):
    low_rows = lax.broadcasted_iota(jnp.int32, (8, SLOWNESS), 0)
    high_rows = lax.broadcasted_iota(jnp.int32, (BLOCK // 8, SLOWNESS), 0) * 8
    shift_rows = lax.broadcasted_iota(jnp.int32, (2 * groups, SLOWNESS), 0)
    shift_rows = jnp.where(shift_rows < groups, shift_rows, shift_rows - groups - 1) * BLOCK
    own_group = lax.axis_index("chan")
    first_bin = lax.axis_index("freq") * freq_dev + own_group * bins
    sender = lax.broadcasted_iota(jnp.int32, (groups, groups), 1)
    distance = lax.broadcasted_iota(jnp.int32, (groups, groups), 0)
    sends = lax.rem(own_group + groups - distance, groups) == sender
    places = jnp.sum(jnp.where(sends, position_ref[...], 0), axis=1, keepdims=True)
    place_ref[...] = jnp.broadcast_to(places, place_ref.shape)

    def one_bin(f, carry):
        def phases(rows):
            slow = lax.broadcasted_iota(jnp.int32, rows.shape, 1) - SLOWNESS // 2
            return unit_phase((first_bin + f) * slow * rows)

        low_cos, low_sin = phases(low_rows)
        high_cos, high_sin = phases(high_rows)
        low_cos, low_sin = low_cos[None], low_sin[None]
        high_cos, high_sin = high_cos[:, None], high_sin[:, None]
        lag_cos = (high_cos * low_cos - high_sin * low_sin).reshape(BLOCK, SLOWNESS)
        lag_sin = (high_sin * low_cos + high_cos * low_sin).reshape(BLOCK, SLOWNESS)
        cos_high, cos_low = halves(lag_cos)
        sin_high, sin_low = halves(lag_sin)
        lag_ref[f, :BLOCK, :SLOWNESS] = cos_high
        lag_ref[f, BLOCK:, :SLOWNESS] = cos_low
        lag_ref[f, :BLOCK, SLOWNESS:] = sin_high
        lag_ref[f, BLOCK:, SLOWNESS:] = sin_low
        shift_cos, shift_sin = phases(shift_rows)
        shift_ref[f, 0] = shift_cos
        shift_ref[f, 1] = shift_sin
        return carry

    lax.fori_loop(0, bins, one_bin, 0)


def chunk_kernel(cuts, spec_ref, *refs):
    rows, groups, bins, _ = spec_ref.shape
    out_refs, wide_ref = refs[-1 - len(cuts) : -1], refs[-1]
    own_group = lax.axis_index("chan")
    widened = []
    for (distance, start, size), out_ref in zip(cuts, out_refs):
        if distance not in widened:
            group = lax.rem(own_group + distance, groups)
            index = len(widened)
            value = spec_ref[:, group].astype(jnp.float32).reshape(rows * bins, BLOCK)
            wide_ref[index, : rows * bins] = value
            widened.append(distance)
        for f in range(size):
            value = wide_ref[widened.index(distance), pl.ds(start + f, rows, stride=bins), :]
            out_ref[f] = value.astype(jnp.bfloat16)


def stack_weights(groups):
    row = lax.broadcasted_iota(jnp.int32, (2 * groups, BLOCK), 0)
    lag = lax.broadcasted_iota(jnp.int32, (2 * groups, BLOCK), 1)
    delta = jnp.where(row < groups, row, row - groups)
    lag = jnp.where(row < groups, lag, lag - BLOCK)
    usable = (lag > -BLOCK) & ((delta >= 1) | (lag >= 1))
    count = SEGMENTS * (groups - delta) * (BLOCK - jnp.abs(lag))
    scale = math.sqrt(SEGMENTS / FREQS)
    return jnp.where(usable, scale / jnp.maximum(count, 1).astype(jnp.float32), 0.0)


def stack_kernel(order, start, bins, parts, last, *refs):
    groups = len(order)
    chunk_refs = refs[:groups]
    place_ref, lag_ref, shift_ref = refs[groups : groups + 3]
    earlier_refs = refs[groups + 3 : -4]
    out_ref, placed_ref, left_ref, part_ref = refs[-4:]
    rows = placed_ref.shape[2]
    windows = rows // 2
    places = place_ref[...]
    for distance, chunk_ref in zip(order, chunk_refs):
        placed_ref[places[distance, 0]] = chunk_ref[...]

    row_index = lax.broadcasted_iota(jnp.int32, (BLOCK, BLOCK), 0)
    lag_index = lax.broadcasted_iota(jnp.int32, (BLOCK, BLOCK), 1)
    mirror = jnp.where(row_index + lag_index == BLOCK - 1, 1.0, 0.0).astype(jnp.bfloat16)
    ahead = lag_index <= row_index

    for f in range(bins):
        left_ref[f] = lax.dot_general(
            mirror,
            placed_ref[:, f].reshape(groups * rows, BLOCK),
            (((1,), (1,)), ((), ())),
            preferred_element_type=jnp.float32,
        ).astype(jnp.bfloat16)

    for f in range(bins):
        right = []
        for place in range(groups):
            value = placed_ref[place, f]
            real, imag = value[:windows], value[windows:]
            right.append(
                jnp.concatenate(
                    [jnp.concatenate([real, imag], 1), jnp.concatenate([imag, -real], 1)], 0
                )
            )
        right = jnp.concatenate(right, 0)
        for delta in range(groups):
            panel = jnp.dot(
                left_ref[f, :, : rows * (groups - delta)],
                right[rows * delta :],
                preferred_element_type=jnp.float32,
            )
            for half in range(2):
                lanes = slice(half * BLOCK, (half + 1) * BLOCK)
                skewed = pltpu.roll(panel[:, lanes], 1, 1, stride=1, stride_axis=0)
                forward = jnp.where(ahead, skewed, 0.0).reshape(-1, 8, BLOCK).sum(0)
                backward = jnp.where(ahead, 0.0, skewed).reshape(-1, 8, BLOCK).sum(0)
                first = (f * 2 * groups + delta) * 8
                part_ref[half, first : first + 8] = forward
                part_ref[half, first + groups * 8 : first + groups * 8 + 8] = backward

    lags = []
    for half in range(2):
        summed = part_ref[half, pl.ds(0, bins * 2 * groups, stride=8), :]
        for sublane in range(1, 8):
            summed = summed + part_ref[half, pl.ds(sublane, bins * 2 * groups, stride=8), :]
        lags.append(summed)
    weight = stack_weights(groups)

    terms = []
    for f in range(bins):
        lag_rows = slice(f * 2 * groups, (f + 1) * 2 * groups)
        means = jnp.concatenate([half[lag_rows] * weight for half in lags], 0)
        mean_high, mean_low = halves(means)
        spread = jnp.concatenate(
            [
                jnp.concatenate([mean_high, mean_high], 1),
                jnp.concatenate([mean_low, jnp.zeros_like(mean_low)], 1),
            ],
            0,
        )
        product = jnp.dot(spread, lag_ref[start + f], preferred_element_type=jnp.float32)
        product = product[: 4 * groups] + product[4 * groups :]
        by_cos, by_sin = product[:, :SLOWNESS], product[:, SLOWNESS:]
        real = by_cos[: 2 * groups] - by_sin[2 * groups :]
        imag = by_sin[: 2 * groups] + by_cos[2 * groups :]
        shift_cos, shift_sin = shift_ref[start + f, 0], shift_ref[start + f, 1]
        turned_re = real * shift_cos - imag * shift_sin
        turned_im = real * shift_sin + imag * shift_cos
        terms.append(turned_re[:groups] + turned_re[groups:])
        terms.append(turned_im[:groups] + turned_im[groups:])

    slow_dev = SLOWNESS // parts
    spans = BLOCK // slow_dev
    packed_rows = 0
    if last:
        for earlier_ref in reversed(earlier_refs):
            if len(earlier_ref.shape) == 3:
                terms = [earlier_ref[entry] for entry in range(earlier_ref.shape[0])] + terms
            else:
                packed_rows = earlier_ref.shape[2]
                out_ref[:, :, :packed_rows] = earlier_ref[...]
    elif len(out_ref.shape) == 3:
        for entry, term in enumerate(terms):
            out_ref[entry] = term
        return
    span_index = lax.broadcasted_iota(jnp.int32, (groups, BLOCK), 1) // slow_dev
    for part in range(parts):
        source = (part % spans) * slow_dev
        lanes = slice(part // spans * BLOCK, (part // spans + 1) * BLOCK)
        for row in range(out_ref.shape[2] - packed_rows):
            packed = jnp.zeros((groups, BLOCK), jnp.float32)
            for span, term in enumerate(terms[row * spans : (row + 1) * spans]):
                moved = pltpu.roll(term[:, lanes], (span * slow_dev - source) % BLOCK, 1)
                packed = jnp.where(span_index == span, moved, packed)
            for delta in range(groups):
                out_ref[groups - 1 - delta, parts - 1 - part, packed_rows + row] = packed[delta]


def image_kernel(slow_dev, spans, term_ref, table_ref, out_ref):
    arrived = term_ref[...]
    turned = arrived.reshape(-1, BLOCK).T
    sums = []
    for odd, chosen in enumerate(spans):
        terms = jnp.concatenate(
            [turned[span * slow_dev : (span + 1) * slow_dev] for span in chosen], 1
        )
        high, low = halves(terms)
        by_high = jnp.dot(
            jnp.concatenate([high, low], 0), table_ref[odd, 0], preferred_element_type=jnp.float32
        )
        by_low = jnp.dot(high, table_ref[odd, 1], preferred_element_type=jnp.float32)
        sums.append(by_high[:slow_dev] + by_high[slow_dev:] + by_low)
    even, odd = sums
    out_ref[0, :, : LAG_TIMES // 2] = even - odd
    out_ref[0, :, LAG_TIMES // 2 :] = even + odd


def time_table(groups, parts, bins, slow_dev, message_rows):
    count = min(BLOCK // slow_dev, 2 * bins)
    spans = [[span for span in range(count) if span // 2 % 2 == odd] for odd in range(2)]
    tables = []
    for chosen in spans:
        span, group, part, row = np.meshgrid(
            chosen,
            np.arange(groups)[::-1],
            np.arange(parts)[::-1],
            np.arange(message_rows),
            indexing="ij",
        )
        entry = row * count + span
        freq = (part * groups + group) * bins + entry // 2
        lag_time = np.arange(LAG_TIMES // 2)
        angle = 2.0 * math.pi / LAG_TIMES * ((freq[..., None] * lag_time) % LAG_TIMES)
        table = np.where((entry % 2 == 0)[..., None], np.cos(angle), -np.sin(angle))
        table = table.reshape(-1, LAG_TIMES // 2).astype(np.float32)
        high = table.astype(jnp.bfloat16)
        low = (table - high.astype(np.float32)).astype(jnp.bfloat16)
        tables.append(np.stack([high, low]))
    return spans, np.stack(tables)


def shards(spectra, block_position):
    groups = lax.axis_size("chan")
    parts = lax.axis_size("freq")
    rows = spectra.shape[0] * spectra.shape[1]
    freq_dev = spectra.shape[2]
    bins = freq_dev // groups
    slow_dev = SLOWNESS // parts
    message_rows = -(-2 * bins * slow_dev // BLOCK)
    vmem = pl.BlockSpec(memory_space=pltpu.VMEM)
    anywhere = pl.BlockSpec(memory_space=pl.ANY)
    params = pltpu.CompilerParams(vmem_limit_bytes=32 * 1024 * 1024)

    whole = spectra.reshape(rows, groups, bins, BLOCK)

    def cut(cuts, *earlier):
        distances = {distance for distance, _, _ in cuts}
        return pl.pallas_call(
            functools.partial(chunk_kernel, cuts),
            out_shape=tuple(
                jax.ShapeDtypeStruct((size, rows, BLOCK), jnp.bfloat16) for _, _, size in cuts
            ),
            in_specs=[vmem] + [anywhere] * len(earlier),
            out_specs=(vmem,) * len(cuts),
            scratch_shapes=[pltpu.VMEM((len(distances), (rows + 1) * bins, BLOCK), jnp.float32)],
            compiler_params=params,
            cost_estimate=pl.CostEstimate(flops=10**7, bytes_accessed=10**6, transcendentals=0),
            name="chunks_of_bins",
        )(whole, *earlier)

    late = bins // 2
    pieces = [(0, bins - late), (bins - late, late)] if late else [(0, bins)]
    order = sorted(range(1, groups), key=lambda steps: abs(2 * steps - groups)) + [0]
    cuts = [(distance, *piece) for piece in pieces for distance in order]
    (first_chunk,) = cut(cuts[:1])
    chunks = dict(zip(cuts, (first_chunk, *cut(cuts[1:], first_chunk))))
    for key in cuts:
        if key[0]:
            pairs = [(source, (source + key[0]) % groups) for source in range(groups)]
            chunks[key] = lax.ppermute(chunks[key], "chan", pairs)
    chunks[cuts[0]] = pl.pallas_call(
        copy_kernel,
        out_shape=jax.ShapeDtypeStruct(first_chunk.shape, jnp.bfloat16),
        in_specs=[vmem],
        out_specs=vmem,
        compiler_params=params,
        name="first_arrived",
    )(chunks[cuts[0]])
    places, lag_table, shift_table = pl.pallas_call(
        functools.partial(table_kernel, groups, bins, freq_dev),
        out_shape=(
            jax.ShapeDtypeStruct((groups, BLOCK), jnp.int32),
            jax.ShapeDtypeStruct((bins, 2 * BLOCK, 2 * SLOWNESS), jnp.bfloat16),
            jax.ShapeDtypeStruct((bins, 2, 2 * groups, SLOWNESS), jnp.float32),
        ),
        in_specs=[vmem],
        out_specs=(vmem, vmem, vmem),
        compiler_params=params,
        cost_estimate=pl.CostEstimate(flops=10**7, bytes_accessed=4 * 10**6, transcendentals=0),
        name="slant_tables",
    )(block_position.reshape(1, groups))
    earlier = []
    for start, size in pieces:
        last = start + size == bins
        own_rows, loose = divmod(2 * size * slow_dev, BLOCK)
        if last:
            shape = (groups, parts, message_rows, BLOCK)
        elif loose:
            shape = (2 * size, groups, SLOWNESS)
        else:
            shape = (groups, parts, own_rows, BLOCK)
        terms = pl.pallas_call(
            functools.partial(stack_kernel, order, start, size, parts, last),
            out_shape=jax.ShapeDtypeStruct(shape, jnp.float32),
            in_specs=[vmem] * (groups + 3 + len(earlier)),
            out_specs=vmem,
            scratch_shapes=[
                pltpu.VMEM((groups, size, rows, BLOCK), jnp.bfloat16),
                pltpu.VMEM((size, BLOCK, groups * rows), jnp.bfloat16),
                pltpu.VMEM((2, (size * 2 * groups + 1) * 8, BLOCK), jnp.float32),
            ],
            compiler_params=params,
            cost_estimate=pl.CostEstimate(
                flops=2 * 10**8, bytes_accessed=4 * 10**6, transcendentals=0
            ),
            name="stack_and_slant",
        )(
            *[chunks[distance, start, size] for distance in order],
            places,
            lag_table,
            shift_table,
            *earlier,
        )
        earlier.append(terms)
    terms = terms.reshape(groups * parts, message_rows, BLOCK)
    arrived = lax.all_to_all(
        terms,
        ("chan", "freq"),
        split_axis=0,
        concat_axis=0,
        axis_index_groups=[list(range(groups * parts))[::-1]],
        tiled=True,
    )
    spans, table = time_table(groups, parts, bins, slow_dev, message_rows)
    return pl.pallas_call(
        functools.partial(image_kernel, slow_dev, spans),
        out_shape=jax.ShapeDtypeStruct((1, slow_dev, LAG_TIMES), jnp.float32),
        in_specs=[vmem, vmem],
        out_specs=vmem,
        compiler_params=params,
        name="sum_of_bins",
    )(arrived, jnp.asarray(table))


def solution(mesh):
    return jax.shard_map(
        shards,
        mesh=mesh,
        in_specs=(P(None, None, "freq", "chan"), P()),
        out_specs=P("chan", "freq", None),
        check_vma=False,
    )
```

```python
import functools
import math

import jax
import jax.numpy as jnp
import numpy as np
from jax import lax
from jax.experimental import pallas as pl
from jax.experimental.pallas import tpu as pltpu
from jax.sharding import PartitionSpec as P

SEGMENTS = 32
FREQS = 256
BLOCK = 128
SLOWNESS = 256
LAG_TIMES = 512
MODULUS = 8 * FREQS * BLOCK


def unit_phase(numerator):
    quarter = MODULUS // 4
    turn = numerator & (MODULUS - 1)
    quadrant = lax.shift_right_logical(turn + quarter // 2, quarter.bit_length() - 1)
    x = (turn - quadrant * quarter).astype(jnp.float32) * (2.0 * math.pi / MODULUS)
    y = x * x
    sine = x * (1.0 + y * (-1.0 / 6 + y * (1.0 / 120 + y * (-1.0 / 5040 + y * (1.0 / 362880)))))
    cosine = 1.0 + y * (-0.5 + y * (1.0 / 24 + y * (-1.0 / 720 + y * (1.0 / 40320))))
    odd = (quadrant & 1) == 1
    first = jnp.where(odd, sine, cosine)
    second = jnp.where(odd, cosine, sine)
    first = jnp.where(((quadrant + 1) & 2) == 2, -first, first)
    second = jnp.where((quadrant & 2) == 2, -second, second)
    return first, second


def halves(value):
    high = value.astype(jnp.bfloat16)
    return high, (value - high.astype(jnp.float32)).astype(jnp.bfloat16)


def copy_kernel(in_ref, out_ref):
    out_ref[...] = in_ref[...]


def table_kernel(groups, bins, freq_dev, position_ref, place_ref, lag_ref, shift_ref):
    low_rows = lax.broadcasted_iota(jnp.int32, (8, SLOWNESS), 0)
    high_rows = lax.broadcasted_iota(jnp.int32, (BLOCK // 8, SLOWNESS), 0) * 8
    shift_rows = lax.broadcasted_iota(jnp.int32, (2 * groups, SLOWNESS), 0)
    shift_rows = jnp.where(shift_rows < groups, shift_rows, shift_rows - groups - 1) * BLOCK
    own_group = lax.axis_index("chan")
    first_bin = lax.axis_index("freq") * freq_dev + own_group * bins
    sender = lax.broadcasted_iota(jnp.int32, (groups, groups), 1)
    distance = lax.broadcasted_iota(jnp.int32, (groups, groups), 0)
    sends = lax.rem(own_group + groups - distance, groups) == sender
    places = jnp.sum(jnp.where(sends, position_ref[...], 0), axis=1, keepdims=True)
    place_ref[...] = jnp.broadcast_to(places, place_ref.shape)

    def one_bin(f, carry):
        def phases(rows):
            slow = lax.broadcasted_iota(jnp.int32, rows.shape, 1) - SLOWNESS // 2
            return unit_phase((first_bin + f) * slow * rows)

        low_cos, low_sin = phases(low_rows)
        high_cos, high_sin = phases(high_rows)
        low_cos, low_sin = low_cos[None], low_sin[None]
        high_cos, high_sin = high_cos[:, None], high_sin[:, None]
        lag_cos = (high_cos * low_cos - high_sin * low_sin).reshape(BLOCK, SLOWNESS)
        lag_sin = (high_sin * low_cos + high_cos * low_sin).reshape(BLOCK, SLOWNESS)
        cos_high, cos_low = halves(lag_cos)
        sin_high, sin_low = halves(lag_sin)
        lag_ref[f, :BLOCK, :SLOWNESS] = cos_high
        lag_ref[f, BLOCK:, :SLOWNESS] = cos_low
        lag_ref[f, :BLOCK, SLOWNESS:] = sin_high
        lag_ref[f, BLOCK:, SLOWNESS:] = sin_low
        shift_cos, shift_sin = phases(shift_rows)
        shift_ref[f, 0] = shift_cos
        shift_ref[f, 1] = shift_sin
        return carry

    lax.fori_loop(0, bins, one_bin, 0)


def chunk_kernel(cuts, spec_ref, *refs):
    rows, groups, bins, _ = spec_ref.shape
    out_refs, wide_ref = refs[-1 - len(cuts) : -1], refs[-1]
    own_group = lax.axis_index("chan")
    widened = []
    for (distance, start, size), out_ref in zip(cuts, out_refs):
        if distance not in widened:
            group = lax.rem(own_group + distance, groups)
            index = len(widened)
            value = spec_ref[:, group].astype(jnp.float32).reshape(rows * bins, BLOCK)
            wide_ref[index, : rows * bins] = value
            widened.append(distance)
        for f in range(size):
            value = wide_ref[widened.index(distance), pl.ds(start + f, rows, stride=bins), :]
            out_ref[f] = value.astype(jnp.bfloat16)


def stack_weights(groups):
    row = lax.broadcasted_iota(jnp.int32, (2 * groups, BLOCK), 0)
    lag = lax.broadcasted_iota(jnp.int32, (2 * groups, BLOCK), 1)
    delta = jnp.where(row < groups, row, row - groups)
    lag = jnp.where(row < groups, lag, lag - BLOCK)
    usable = (lag > -BLOCK) & ((delta >= 1) | (lag >= 1))
    count = SEGMENTS * (groups - delta) * (BLOCK - jnp.abs(lag))
    scale = math.sqrt(SEGMENTS / FREQS)
    return jnp.where(usable, scale / jnp.maximum(count, 1).astype(jnp.float32), 0.0)


def stack_kernel(order, start, bins, parts, *refs):
    groups = len(order)
    chunk_refs = refs[:groups]
    place_ref, lag_ref, shift_ref = refs[groups : groups + 3]
    earlier_refs = refs[groups + 3 : -4]
    out_ref, placed_ref, left_ref, part_ref = refs[-4:]
    rows = placed_ref.shape[2]
    windows = rows // 2
    places = place_ref[...]
    for distance, chunk_ref in zip(order, chunk_refs):
        placed_ref[places[distance, 0]] = chunk_ref[...]

    row_index = lax.broadcasted_iota(jnp.int32, (BLOCK, BLOCK), 0)
    lag_index = lax.broadcasted_iota(jnp.int32, (BLOCK, BLOCK), 1)
    mirror = jnp.where(row_index + lag_index == BLOCK - 1, 1.0, 0.0).astype(jnp.bfloat16)
    ahead = lag_index <= row_index

    for f in range(bins):
        left_ref[f] = lax.dot_general(
            mirror,
            placed_ref[:, f].reshape(groups * rows, BLOCK),
            (((1,), (1,)), ((), ())),
            preferred_element_type=jnp.float32,
        ).astype(jnp.bfloat16)

    for f in range(bins):
        right = []
        for place in range(groups):
            value = placed_ref[place, f]
            real, imag = value[:windows], value[windows:]
            right.append(
                jnp.concatenate(
                    [jnp.concatenate([real, imag], 1), jnp.concatenate([imag, -real], 1)], 0
                )
            )
        right = jnp.concatenate(right, 0)
        for delta in range(groups):
            panel = jnp.dot(
                left_ref[f, :, : rows * (groups - delta)],
                right[rows * delta :],
                preferred_element_type=jnp.float32,
            )
            for half in range(2):
                lanes = slice(half * BLOCK, (half + 1) * BLOCK)
                skewed = pltpu.roll(panel[:, lanes], 1, 1, stride=1, stride_axis=0)
                forward = jnp.where(ahead, skewed, 0.0).reshape(-1, 8, BLOCK).sum(0)
                backward = jnp.where(ahead, 0.0, skewed).reshape(-1, 8, BLOCK).sum(0)
                first = (f * 2 * groups + delta) * 8
                part_ref[half, first : first + 8] = forward
                part_ref[half, first + groups * 8 : first + groups * 8 + 8] = backward

    lags = []
    for half in range(2):
        summed = part_ref[half, pl.ds(0, bins * 2 * groups, stride=8), :]
        for sublane in range(1, 8):
            summed = summed + part_ref[half, pl.ds(sublane, bins * 2 * groups, stride=8), :]
        lags.append(summed)
    weight = stack_weights(groups)

    terms = []
    for f in range(bins):
        lag_rows = slice(f * 2 * groups, (f + 1) * 2 * groups)
        means = jnp.concatenate([half[lag_rows] * weight for half in lags], 0)
        mean_high, mean_low = halves(means)
        spread = jnp.concatenate(
            [
                jnp.concatenate([mean_high, mean_high], 1),
                jnp.concatenate([mean_low, jnp.zeros_like(mean_low)], 1),
            ],
            0,
        )
        product = jnp.dot(spread, lag_ref[start + f], preferred_element_type=jnp.float32)
        product = product[: 4 * groups] + product[4 * groups :]
        by_cos, by_sin = product[:, :SLOWNESS], product[:, SLOWNESS:]
        real = by_cos[: 2 * groups] - by_sin[2 * groups :]
        imag = by_sin[: 2 * groups] + by_cos[2 * groups :]
        shift_cos, shift_sin = shift_ref[start + f, 0], shift_ref[start + f, 1]
        turned_re = real * shift_cos - imag * shift_sin
        turned_im = real * shift_sin + imag * shift_cos
        terms.append(turned_re[:groups] + turned_re[groups:])
        terms.append(turned_im[:groups] + turned_im[groups:])

    if parts is None:
        for entry, term in enumerate(terms):
            out_ref[entry] = term
        return
    for earlier_ref in reversed(earlier_refs):
        terms = [earlier_ref[entry] for entry in range(earlier_ref.shape[0])] + terms
    slow_dev = SLOWNESS // parts
    spans = BLOCK // slow_dev
    span_index = lax.broadcasted_iota(jnp.int32, (groups, BLOCK), 1) // slow_dev
    for part in range(parts):
        source = (part % spans) * slow_dev
        lanes = slice(part // spans * BLOCK, (part // spans + 1) * BLOCK)
        for row in range(out_ref.shape[2]):
            packed = jnp.zeros((groups, BLOCK), jnp.float32)
            for span, term in enumerate(terms[row * spans : (row + 1) * spans]):
                moved = pltpu.roll(term[:, lanes], (span * slow_dev - source) % BLOCK, 1)
                packed = jnp.where(span_index == span, moved, packed)
            for delta in range(groups):
                out_ref[groups - 1 - delta, parts - 1 - part, row] = packed[delta]


def image_kernel(slow_dev, spans, term_ref, table_ref, out_ref):
    arrived = term_ref[...]
    turned = arrived.reshape(-1, BLOCK).T
    sums = []
    for odd, chosen in enumerate(spans):
        terms = jnp.concatenate(
            [turned[span * slow_dev : (span + 1) * slow_dev] for span in chosen], 1
        )
        high, low = halves(terms)
        by_high = jnp.dot(
            jnp.concatenate([high, low], 0), table_ref[odd, 0], preferred_element_type=jnp.float32
        )
        by_low = jnp.dot(high, table_ref[odd, 1], preferred_element_type=jnp.float32)
        sums.append(by_high[:slow_dev] + by_high[slow_dev:] + by_low)
    even, odd = sums
    out_ref[0, :, : LAG_TIMES // 2] = even - odd
    out_ref[0, :, LAG_TIMES // 2 :] = even + odd


def time_table(groups, parts, bins, slow_dev, message_rows):
    count = min(BLOCK // slow_dev, 2 * bins)
    spans = [[span for span in range(count) if span // 2 % 2 == odd] for odd in range(2)]
    tables = []
    for chosen in spans:
        span, group, part, row = np.meshgrid(
            chosen,
            np.arange(groups)[::-1],
            np.arange(parts)[::-1],
            np.arange(message_rows),
            indexing="ij",
        )
        entry = row * count + span
        freq = (part * groups + group) * bins + entry // 2
        lag_time = np.arange(LAG_TIMES // 2)
        angle = 2.0 * math.pi / LAG_TIMES * ((freq[..., None] * lag_time) % LAG_TIMES)
        table = np.where((entry % 2 == 0)[..., None], np.cos(angle), -np.sin(angle))
        table = table.reshape(-1, LAG_TIMES // 2).astype(np.float32)
        high = table.astype(jnp.bfloat16)
        low = (table - high.astype(np.float32)).astype(jnp.bfloat16)
        tables.append(np.stack([high, low]))
    return spans, np.stack(tables)


def shards(spectra, block_position):
    groups = lax.axis_size("chan")
    parts = lax.axis_size("freq")
    rows = spectra.shape[0] * spectra.shape[1]
    freq_dev = spectra.shape[2]
    bins = freq_dev // groups
    slow_dev = SLOWNESS // parts
    message_rows = -(-2 * bins * slow_dev // BLOCK)
    vmem = pl.BlockSpec(memory_space=pltpu.VMEM)
    anywhere = pl.BlockSpec(memory_space=pl.ANY)
    params = pltpu.CompilerParams(vmem_limit_bytes=32 * 1024 * 1024)

    whole = spectra.reshape(rows, groups, bins, BLOCK)

    def cut(cuts, *earlier):
        distances = {distance for distance, _, _ in cuts}
        return pl.pallas_call(
            functools.partial(chunk_kernel, cuts),
            out_shape=tuple(
                jax.ShapeDtypeStruct((size, rows, BLOCK), jnp.bfloat16) for _, _, size in cuts
            ),
            in_specs=[vmem] + [anywhere] * len(earlier),
            out_specs=(vmem,) * len(cuts),
            scratch_shapes=[pltpu.VMEM((len(distances), (rows + 1) * bins, BLOCK), jnp.float32)],
            compiler_params=params,
            cost_estimate=pl.CostEstimate(flops=10**7, bytes_accessed=10**6, transcendentals=0),
            name="chunks_of_bins",
        )(whole, *earlier)

    late = max(1, 3 * bins // 8) if bins > 1 else 0
    pieces = [(0, bins - late), (bins - late, late)] if late else [(0, bins)]
    order = sorted(range(1, groups), key=lambda steps: abs(2 * steps - groups)) + [0]
    cuts = [(distance, *piece) for piece in pieces for distance in order]
    (first_chunk,) = cut(cuts[:1])
    near = cut(cuts[1 : groups - 1], first_chunk)
    chunks = dict(zip(cuts, (first_chunk, *near, *cut(cuts[groups - 1 :], near[0]))))
    for key in cuts:
        if key[0]:
            pairs = [(source, (source + key[0]) % groups) for source in range(groups)]
            chunks[key] = lax.ppermute(chunks[key], "chan", pairs)
    chunks[cuts[0]] = pl.pallas_call(
        copy_kernel,
        out_shape=jax.ShapeDtypeStruct(first_chunk.shape, jnp.bfloat16),
        in_specs=[vmem],
        out_specs=vmem,
        compiler_params=params,
        name="first_arrived",
    )(chunks[cuts[0]])
    places, lag_table, shift_table = pl.pallas_call(
        functools.partial(table_kernel, groups, bins, freq_dev),
        out_shape=(
            jax.ShapeDtypeStruct((groups, BLOCK), jnp.int32),
            jax.ShapeDtypeStruct((bins, 2 * BLOCK, 2 * SLOWNESS), jnp.bfloat16),
            jax.ShapeDtypeStruct((bins, 2, 2 * groups, SLOWNESS), jnp.float32),
        ),
        in_specs=[vmem],
        out_specs=(vmem, vmem, vmem),
        compiler_params=params,
        cost_estimate=pl.CostEstimate(flops=10**7, bytes_accessed=4 * 10**6, transcendentals=0),
        name="slant_tables",
    )(block_position.reshape(1, groups))
    earlier = []
    for start, size in pieces:
        last = start + size == bins
        shape = (groups, parts, message_rows, BLOCK) if last else (2 * size, groups, SLOWNESS)
        terms = pl.pallas_call(
            functools.partial(stack_kernel, order, start, size, parts if last else None),
            out_shape=jax.ShapeDtypeStruct(shape, jnp.float32),
            in_specs=[vmem] * (groups + 3 + len(earlier)),
            out_specs=vmem,
            scratch_shapes=[
                pltpu.VMEM((groups, size, rows, BLOCK), jnp.bfloat16),
                pltpu.VMEM((size, BLOCK, groups * rows), jnp.bfloat16),
                pltpu.VMEM((2, (size * 2 * groups + 1) * 8, BLOCK), jnp.float32),
            ],
            compiler_params=params,
            cost_estimate=pl.CostEstimate(
                flops=2 * 10**8, bytes_accessed=4 * 10**6, transcendentals=0
            ),
            name="stack_and_slant",
        )(
            *[chunks[distance, start, size] for distance in order],
            places,
            lag_table,
            shift_table,
            *earlier,
        )
        earlier.append(terms)
    terms = terms.reshape(groups * parts, message_rows, BLOCK)
    arrived = lax.all_to_all(
        terms,
        ("chan", "freq"),
        split_axis=0,
        concat_axis=0,
        axis_index_groups=[list(range(groups * parts))[::-1]],
        tiled=True,
    )
    spans, table = time_table(groups, parts, bins, slow_dev, message_rows)
    return pl.pallas_call(
        functools.partial(image_kernel, slow_dev, spans),
        out_shape=jax.ShapeDtypeStruct((1, slow_dev, LAG_TIMES), jnp.float32),
        in_specs=[vmem, vmem],
        out_specs=vmem,
        compiler_params=params,
        name="sum_of_bins",
    )(arrived, jnp.asarray(table))


def solution(mesh):
    return jax.shard_map(
        shards,
        mesh=mesh,
        in_specs=(P(None, None, "freq", "chan"), P()),
        out_specs=P("chan", "freq", None),
        check_vma=False,
    )
```

```python
import functools
import math

import jax
import jax.numpy as jnp
import numpy as np
from jax import lax
from jax.experimental import pallas as pl
from jax.experimental.pallas import tpu as pltpu
from jax.sharding import PartitionSpec as P

SEGMENTS = 32
FREQS = 256
BLOCK = 128
SLOWNESS = 256
LAG_TIMES = 512
MODULUS = 8 * FREQS * BLOCK


def unit_phase(numerator):
    quarter = MODULUS // 4
    turn = numerator & (MODULUS - 1)
    quadrant = lax.shift_right_logical(turn + quarter // 2, quarter.bit_length() - 1)
    x = (turn - quadrant * quarter).astype(jnp.float32) * (2.0 * math.pi / MODULUS)
    y = x * x
    sine = x * (1.0 + y * (-1.0 / 6 + y * (1.0 / 120 + y * (-1.0 / 5040 + y * (1.0 / 362880)))))
    cosine = 1.0 + y * (-0.5 + y * (1.0 / 24 + y * (-1.0 / 720 + y * (1.0 / 40320))))
    odd = (quadrant & 1) == 1
    first = jnp.where(odd, sine, cosine)
    second = jnp.where(odd, cosine, sine)
    first = jnp.where(((quadrant + 1) & 2) == 2, -first, first)
    second = jnp.where((quadrant & 2) == 2, -second, second)
    return first, second


def halves(value):
    high = value.astype(jnp.bfloat16)
    return high, (value - high.astype(jnp.float32)).astype(jnp.bfloat16)


def copy_kernel(in_ref, out_ref):
    out_ref[...] = in_ref[...]


def table_kernel(groups, bins, freq_dev, position_ref, place_ref, lag_ref, shift_ref):
    low_rows = lax.broadcasted_iota(jnp.int32, (8, SLOWNESS), 0)
    high_rows = lax.broadcasted_iota(jnp.int32, (BLOCK // 8, SLOWNESS), 0) * 8
    shift_rows = lax.broadcasted_iota(jnp.int32, (2 * groups, SLOWNESS), 0)
    shift_rows = jnp.where(shift_rows < groups, shift_rows, shift_rows - groups - 1) * BLOCK
    own_group = lax.axis_index("chan")
    first_bin = lax.axis_index("freq") * freq_dev + own_group * bins
    sender = lax.broadcasted_iota(jnp.int32, (groups, groups), 1)
    distance = lax.broadcasted_iota(jnp.int32, (groups, groups), 0)
    sends = lax.rem(own_group + groups - distance, groups) == sender
    places = jnp.sum(jnp.where(sends, position_ref[...], 0), axis=1, keepdims=True)
    place_ref[...] = jnp.broadcast_to(places, place_ref.shape)

    def one_bin(f, carry):
        def phases(rows):
            slow = lax.broadcasted_iota(jnp.int32, rows.shape, 1) - SLOWNESS // 2
            return unit_phase((first_bin + f) * slow * rows)

        low_cos, low_sin = phases(low_rows)
        high_cos, high_sin = phases(high_rows)
        low_cos, low_sin = low_cos[None], low_sin[None]
        high_cos, high_sin = high_cos[:, None], high_sin[:, None]
        lag_cos = (high_cos * low_cos - high_sin * low_sin).reshape(BLOCK, SLOWNESS)
        lag_sin = (high_sin * low_cos + high_cos * low_sin).reshape(BLOCK, SLOWNESS)
        cos_high, cos_low = halves(lag_cos)
        sin_high, sin_low = halves(lag_sin)
        lag_ref[f, :BLOCK, :SLOWNESS] = cos_high
        lag_ref[f, BLOCK:, :SLOWNESS] = cos_low
        lag_ref[f, :BLOCK, SLOWNESS:] = sin_high
        lag_ref[f, BLOCK:, SLOWNESS:] = sin_low
        shift_cos, shift_sin = phases(shift_rows)
        shift_ref[f, 0] = shift_cos
        shift_ref[f, 1] = shift_sin
        return carry

    lax.fori_loop(0, bins, one_bin, 0)


def chunk_kernel(cuts, spec_ref, *refs):
    rows, groups, bins, _ = spec_ref.shape
    out_refs, wide_ref = refs[-1 - len(cuts) : -1], refs[-1]
    own_group = lax.axis_index("chan")
    widened = []
    for (distance, start, size), out_ref in zip(cuts, out_refs):
        if distance not in widened:
            group = lax.rem(own_group + distance, groups)
            index = len(widened)
            value = spec_ref[:, group].astype(jnp.float32).reshape(rows * bins, BLOCK)
            wide_ref[index, : rows * bins] = value
            widened.append(distance)
        for f in range(size):
            value = wide_ref[widened.index(distance), pl.ds(start + f, rows, stride=bins), :]
            out_ref[f] = value.astype(jnp.bfloat16)


def stack_weights(groups):
    row = lax.broadcasted_iota(jnp.int32, (2 * groups, BLOCK), 0)
    lag = lax.broadcasted_iota(jnp.int32, (2 * groups, BLOCK), 1)
    delta = jnp.where(row < groups, row, row - groups)
    lag = jnp.where(row < groups, lag, lag - BLOCK)
    usable = (lag > -BLOCK) & ((delta >= 1) | (lag >= 1))
    count = SEGMENTS * (groups - delta) * (BLOCK - jnp.abs(lag))
    scale = math.sqrt(SEGMENTS / FREQS)
    return jnp.where(usable, scale / jnp.maximum(count, 1).astype(jnp.float32), 0.0)


def stack_kernel(order, start, bins, parts, *refs):
    groups = len(order)
    chunk_refs = refs[:groups]
    place_ref, lag_ref, shift_ref = refs[groups : groups + 3]
    earlier_refs = refs[groups + 3 : -4]
    out_ref, placed_ref, left_ref, part_ref = refs[-4:]
    rows = placed_ref.shape[2]
    windows = rows // 2
    places = place_ref[...]
    for distance, chunk_ref in zip(order, chunk_refs):
        placed_ref[places[distance, 0]] = chunk_ref[...]

    row_index = lax.broadcasted_iota(jnp.int32, (BLOCK, BLOCK), 0)
    lag_index = lax.broadcasted_iota(jnp.int32, (BLOCK, BLOCK), 1)
    mirror = jnp.where(row_index + lag_index == BLOCK - 1, 1.0, 0.0).astype(jnp.bfloat16)
    ahead = lag_index <= row_index

    for f in range(bins):
        left_ref[f] = lax.dot_general(
            mirror,
            placed_ref[:, f].reshape(groups * rows, BLOCK),
            (((1,), (1,)), ((), ())),
            preferred_element_type=jnp.float32,
        ).astype(jnp.bfloat16)

    for f in range(bins):
        right = []
        for place in range(groups):
            value = placed_ref[place, f]
            real, imag = value[:windows], value[windows:]
            right.append(
                jnp.concatenate(
                    [jnp.concatenate([real, imag], 1), jnp.concatenate([imag, -real], 1)], 0
                )
            )
        right = jnp.concatenate(right, 0)
        for delta in range(groups):
            panel = jnp.dot(
                left_ref[f, :, : rows * (groups - delta)],
                right[rows * delta :],
                preferred_element_type=jnp.float32,
            )
            for half in range(2):
                lanes = slice(half * BLOCK, (half + 1) * BLOCK)
                skewed = pltpu.roll(panel[:, lanes], 1, 1, stride=1, stride_axis=0)
                forward = jnp.where(ahead, skewed, 0.0).reshape(-1, 8, BLOCK).sum(0)
                backward = jnp.where(ahead, 0.0, skewed).reshape(-1, 8, BLOCK).sum(0)
                first = (f * 2 * groups + delta) * 8
                part_ref[half, first : first + 8] = forward
                part_ref[half, first + groups * 8 : first + groups * 8 + 8] = backward

    lags = []
    for half in range(2):
        summed = part_ref[half, pl.ds(0, bins * 2 * groups, stride=8), :]
        for sublane in range(1, 8):
            summed = summed + part_ref[half, pl.ds(sublane, bins * 2 * groups, stride=8), :]
        lags.append(summed)
    weight = stack_weights(groups)

    terms = []
    for f in range(bins):
        lag_rows = slice(f * 2 * groups, (f + 1) * 2 * groups)
        means = jnp.concatenate([half[lag_rows] * weight for half in lags], 0)
        mean_high, mean_low = halves(means)
        spread = jnp.concatenate(
            [
                jnp.concatenate([mean_high, mean_high], 1),
                jnp.concatenate([mean_low, jnp.zeros_like(mean_low)], 1),
            ],
            0,
        )
        product = jnp.dot(spread, lag_ref[start + f], preferred_element_type=jnp.float32)
        product = product[: 4 * groups] + product[4 * groups :]
        by_cos, by_sin = product[:, :SLOWNESS], product[:, SLOWNESS:]
        real = by_cos[: 2 * groups] - by_sin[2 * groups :]
        imag = by_sin[: 2 * groups] + by_cos[2 * groups :]
        shift_cos, shift_sin = shift_ref[start + f, 0], shift_ref[start + f, 1]
        turned_re = real * shift_cos - imag * shift_sin
        turned_im = real * shift_sin + imag * shift_cos
        terms.append(turned_re[:groups] + turned_re[groups:])
        terms.append(turned_im[:groups] + turned_im[groups:])

    if parts is None:
        for entry, term in enumerate(terms):
            out_ref[entry] = term
        return
    for earlier_ref in reversed(earlier_refs):
        terms = [earlier_ref[entry] for entry in range(earlier_ref.shape[0])] + terms
    slow_dev = SLOWNESS // parts
    spans = BLOCK // slow_dev
    span_index = lax.broadcasted_iota(jnp.int32, (groups, BLOCK), 1) // slow_dev
    for part in range(parts):
        source = (part % spans) * slow_dev
        lanes = slice(part // spans * BLOCK, (part // spans + 1) * BLOCK)
        for row in range(out_ref.shape[2]):
            packed = jnp.zeros((groups, BLOCK), jnp.float32)
            for span, term in enumerate(terms[row * spans : (row + 1) * spans]):
                moved = pltpu.roll(term[:, lanes], (span * slow_dev - source) % BLOCK, 1)
                packed = jnp.where(span_index == span, moved, packed)
            for delta in range(groups):
                out_ref[groups - 1 - delta, parts - 1 - part, row] = packed[delta]


def image_kernel(slow_dev, spans, term_ref, table_ref, out_ref):
    arrived = term_ref[...]
    turned = arrived.reshape(-1, BLOCK).T
    sums = []
    for odd, chosen in enumerate(spans):
        terms = jnp.concatenate(
            [turned[span * slow_dev : (span + 1) * slow_dev] for span in chosen], 1
        )
        high, low = halves(terms)
        by_high = jnp.dot(
            jnp.concatenate([high, low], 0), table_ref[odd, 0], preferred_element_type=jnp.float32
        )
        by_low = jnp.dot(high, table_ref[odd, 1], preferred_element_type=jnp.float32)
        sums.append(by_high[:slow_dev] + by_high[slow_dev:] + by_low)
    even, odd = sums
    out_ref[0, :, : LAG_TIMES // 2] = even - odd
    out_ref[0, :, LAG_TIMES // 2 :] = even + odd


def time_table(groups, parts, bins, slow_dev, message_rows):
    count = min(BLOCK // slow_dev, 2 * bins)
    spans = [[span for span in range(count) if span // 2 % 2 == odd] for odd in range(2)]
    tables = []
    for chosen in spans:
        span, group, part, row = np.meshgrid(
            chosen,
            np.arange(groups)[::-1],
            np.arange(parts)[::-1],
            np.arange(message_rows),
            indexing="ij",
        )
        entry = row * count + span
        freq = (part * groups + group) * bins + entry // 2
        lag_time = np.arange(LAG_TIMES // 2)
        angle = 2.0 * math.pi / LAG_TIMES * ((freq[..., None] * lag_time) % LAG_TIMES)
        table = np.where((entry % 2 == 0)[..., None], np.cos(angle), -np.sin(angle))
        table = table.reshape(-1, LAG_TIMES // 2).astype(np.float32)
        high = table.astype(jnp.bfloat16)
        low = (table - high.astype(np.float32)).astype(jnp.bfloat16)
        tables.append(np.stack([high, low]))
    return spans, np.stack(tables)


def shards(spectra, block_position):
    groups = lax.axis_size("chan")
    parts = lax.axis_size("freq")
    rows = spectra.shape[0] * spectra.shape[1]
    freq_dev = spectra.shape[2]
    bins = freq_dev // groups
    slow_dev = SLOWNESS // parts
    message_rows = -(-2 * bins * slow_dev // BLOCK)
    vmem = pl.BlockSpec(memory_space=pltpu.VMEM)
    anywhere = pl.BlockSpec(memory_space=pl.ANY)
    params = pltpu.CompilerParams(vmem_limit_bytes=32 * 1024 * 1024)

    whole = spectra.reshape(rows, groups, bins, BLOCK)

    def cut(cuts, *earlier):
        distances = {distance for distance, _, _ in cuts}
        return pl.pallas_call(
            functools.partial(chunk_kernel, cuts),
            out_shape=tuple(
                jax.ShapeDtypeStruct((size, rows, BLOCK), jnp.bfloat16) for _, _, size in cuts
            ),
            in_specs=[vmem] + [anywhere] * len(earlier),
            out_specs=(vmem,) * len(cuts),
            scratch_shapes=[pltpu.VMEM((len(distances), (rows + 1) * bins, BLOCK), jnp.float32)],
            compiler_params=params,
            cost_estimate=pl.CostEstimate(flops=10**7, bytes_accessed=10**6, transcendentals=0),
            name="chunks_of_bins",
        )(whole, *earlier)

    late = max(1, 3 * bins // 8) if bins > 1 else 0
    pieces = [(0, bins - late), (bins - late, late)] if late else [(0, bins)]
    order = sorted(range(1, groups), key=lambda steps: (abs(2 * steps - groups), -steps)) + [0]
    cuts = [(distance, *piece) for piece in pieces for distance in order]
    (first_chunk,) = cut(cuts[:1])
    chunks = dict(zip(cuts, (first_chunk, *cut(cuts[1:], first_chunk))))
    for key in cuts:
        if key[0]:
            pairs = [(source, (source + key[0]) % groups) for source in range(groups)]
            chunks[key] = lax.ppermute(chunks[key], "chan", pairs)
    chunks[cuts[0]] = pl.pallas_call(
        copy_kernel,
        out_shape=jax.ShapeDtypeStruct(first_chunk.shape, jnp.bfloat16),
        in_specs=[vmem],
        out_specs=vmem,
        compiler_params=params,
        name="first_arrived",
    )(chunks[cuts[0]])
    places, lag_table, shift_table = pl.pallas_call(
        functools.partial(table_kernel, groups, bins, freq_dev),
        out_shape=(
            jax.ShapeDtypeStruct((groups, BLOCK), jnp.int32),
            jax.ShapeDtypeStruct((bins, 2 * BLOCK, 2 * SLOWNESS), jnp.bfloat16),
            jax.ShapeDtypeStruct((bins, 2, 2 * groups, SLOWNESS), jnp.float32),
        ),
        in_specs=[vmem],
        out_specs=(vmem, vmem, vmem),
        compiler_params=params,
        cost_estimate=pl.CostEstimate(flops=10**7, bytes_accessed=4 * 10**6, transcendentals=0),
        name="slant_tables",
    )(block_position.reshape(1, groups))
    earlier = []
    for start, size in pieces:
        last = start + size == bins
        shape = (groups, parts, message_rows, BLOCK) if last else (2 * size, groups, SLOWNESS)
        terms = pl.pallas_call(
            functools.partial(stack_kernel, order, start, size, parts if last else None),
            out_shape=jax.ShapeDtypeStruct(shape, jnp.float32),
            in_specs=[vmem] * (groups + 3 + len(earlier)),
            out_specs=vmem,
            scratch_shapes=[
                pltpu.VMEM((groups, size, rows, BLOCK), jnp.bfloat16),
                pltpu.VMEM((size, BLOCK, groups * rows), jnp.bfloat16),
                pltpu.VMEM((2, (size * 2 * groups + 1) * 8, BLOCK), jnp.float32),
            ],
            compiler_params=params,
            cost_estimate=pl.CostEstimate(
                flops=2 * 10**8, bytes_accessed=4 * 10**6, transcendentals=0
            ),
            name="stack_and_slant",
        )(
            *[chunks[distance, start, size] for distance in order],
            places,
            lag_table,
            shift_table,
            *earlier,
        )
        earlier.append(terms)
    terms = terms.reshape(groups * parts, message_rows, BLOCK)
    arrived = lax.all_to_all(
        terms,
        ("chan", "freq"),
        split_axis=0,
        concat_axis=0,
        axis_index_groups=[list(range(groups * parts))[::-1]],
        tiled=True,
    )
    spans, table = time_table(groups, parts, bins, slow_dev, message_rows)
    return pl.pallas_call(
        functools.partial(image_kernel, slow_dev, spans),
        out_shape=jax.ShapeDtypeStruct((1, slow_dev, LAG_TIMES), jnp.float32),
        in_specs=[vmem, vmem],
        out_specs=vmem,
        compiler_params=params,
        name="sum_of_bins",
    )(arrived, jnp.asarray(table))


def solution(mesh):
    return jax.shard_map(
        shards,
        mesh=mesh,
        in_specs=(P(None, None, "freq", "chan"), P()),
        out_specs=P("chan", "freq", None),
        check_vma=False,
    )
```

```python
import functools
import math

import jax
import jax.numpy as jnp
import numpy as np
from jax import lax
from jax.experimental import pallas as pl
from jax.experimental.pallas import tpu as pltpu
from jax.sharding import PartitionSpec as P

SEGMENTS = 32
FREQS = 256
BLOCK = 128
SLOWNESS = 256
LAG_TIMES = 512
MODULUS = 8 * FREQS * BLOCK


def unit_phase(numerator):
    quarter = MODULUS // 4
    turn = numerator & (MODULUS - 1)
    quadrant = lax.shift_right_logical(turn + quarter // 2, quarter.bit_length() - 1)
    x = (turn - quadrant * quarter).astype(jnp.float32) * (2.0 * math.pi / MODULUS)
    y = x * x
    sine = x * (1.0 + y * (-1.0 / 6 + y * (1.0 / 120 + y * (-1.0 / 5040 + y * (1.0 / 362880)))))
    cosine = 1.0 + y * (-0.5 + y * (1.0 / 24 + y * (-1.0 / 720 + y * (1.0 / 40320))))
    odd = (quadrant & 1) == 1
    first = jnp.where(odd, sine, cosine)
    second = jnp.where(odd, cosine, sine)
    first = jnp.where(((quadrant + 1) & 2) == 2, -first, first)
    second = jnp.where((quadrant & 2) == 2, -second, second)
    return first, second


def halves(value):
    high = value.astype(jnp.bfloat16)
    return high, (value - high.astype(jnp.float32)).astype(jnp.bfloat16)


def copy_kernel(in_ref, out_ref):
    out_ref[...] = in_ref[...]


def table_kernel(groups, bins, freq_dev, position_ref, place_ref, lag_ref, shift_ref):
    low_rows = lax.broadcasted_iota(jnp.int32, (8, SLOWNESS), 0)
    high_rows = lax.broadcasted_iota(jnp.int32, (BLOCK // 8, SLOWNESS), 0) * 8
    shift_rows = lax.broadcasted_iota(jnp.int32, (2 * groups, SLOWNESS), 0)
    shift_rows = jnp.where(shift_rows < groups, shift_rows, shift_rows - groups - 1) * BLOCK
    own_group = lax.axis_index("chan")
    first_bin = lax.axis_index("freq") * freq_dev + own_group * bins
    sender = lax.broadcasted_iota(jnp.int32, (groups, groups), 1)
    distance = lax.broadcasted_iota(jnp.int32, (groups, groups), 0)
    sends = lax.rem(own_group + groups - distance, groups) == sender
    places = jnp.sum(jnp.where(sends, position_ref[...], 0), axis=1, keepdims=True)
    place_ref[...] = jnp.broadcast_to(places, place_ref.shape)

    def one_bin(f, carry):
        def phases(rows):
            slow = lax.broadcasted_iota(jnp.int32, rows.shape, 1) - SLOWNESS // 2
            return unit_phase((first_bin + f) * slow * rows)

        low_cos, low_sin = phases(low_rows)
        high_cos, high_sin = phases(high_rows)
        low_cos, low_sin = low_cos[None], low_sin[None]
        high_cos, high_sin = high_cos[:, None], high_sin[:, None]
        lag_cos = (high_cos * low_cos - high_sin * low_sin).reshape(BLOCK, SLOWNESS)
        lag_sin = (high_sin * low_cos + high_cos * low_sin).reshape(BLOCK, SLOWNESS)
        cos_high, cos_low = halves(lag_cos)
        sin_high, sin_low = halves(lag_sin)
        lag_ref[f, :BLOCK, :SLOWNESS] = cos_high
        lag_ref[f, BLOCK:, :SLOWNESS] = cos_low
        lag_ref[f, :BLOCK, SLOWNESS:] = sin_high
        lag_ref[f, BLOCK:, SLOWNESS:] = sin_low
        shift_cos, shift_sin = phases(shift_rows)
        shift_ref[f, 0] = shift_cos
        shift_ref[f, 1] = shift_sin
        return carry

    lax.fori_loop(0, bins, one_bin, 0)


def chunk_kernel(cuts, spec_ref, *refs):
    rows, groups, bins, _ = spec_ref.shape
    out_refs, wide_ref = refs[-1 - len(cuts) : -1], refs[-1]
    own_group = lax.axis_index("chan")
    widened = []
    for (distance, start, size), out_ref in zip(cuts, out_refs):
        if distance not in widened:
            group = lax.rem(own_group + distance, groups)
            index = len(widened)
            wide_ref[index] = spec_ref[:, group].astype(jnp.float32).reshape(rows * bins, BLOCK)
            widened.append(distance)
        for f in range(size):
            value = wide_ref[widened.index(distance), pl.ds(start + f, rows, stride=bins), :]
            out_ref[f] = value.astype(jnp.bfloat16)


def stack_weights(groups):
    row = lax.broadcasted_iota(jnp.int32, (2 * groups, BLOCK), 0)
    lag = lax.broadcasted_iota(jnp.int32, (2 * groups, BLOCK), 1)
    delta = jnp.where(row < groups, row, row - groups)
    lag = jnp.where(row < groups, lag, lag - BLOCK)
    usable = (lag > -BLOCK) & ((delta >= 1) | (lag >= 1))
    count = SEGMENTS * (groups - delta) * (BLOCK - jnp.abs(lag))
    scale = math.sqrt(SEGMENTS / FREQS)
    return jnp.where(usable, scale / jnp.maximum(count, 1).astype(jnp.float32), 0.0)


def stack_kernel(order, start, bins, parts, *refs):
    groups = len(order)
    chunk_refs = refs[:groups]
    place_ref, lag_ref, shift_ref = refs[groups : groups + 3]
    earlier_refs = refs[groups + 3 : -4]
    out_ref, placed_ref, left_ref, part_ref = refs[-4:]
    rows = placed_ref.shape[2]
    windows = rows // 2
    places = place_ref[...]
    for distance, chunk_ref in zip(order, chunk_refs):
        placed_ref[places[distance, 0]] = chunk_ref[...]

    row_index = lax.broadcasted_iota(jnp.int32, (BLOCK, BLOCK), 0)
    lag_index = lax.broadcasted_iota(jnp.int32, (BLOCK, BLOCK), 1)
    mirror = jnp.where(row_index + lag_index == BLOCK - 1, 1.0, 0.0).astype(jnp.bfloat16)
    ahead = lag_index <= row_index

    for f in range(bins):
        left_ref[f] = lax.dot_general(
            mirror,
            placed_ref[:, f].reshape(groups * rows, BLOCK),
            (((1,), (1,)), ((), ())),
            preferred_element_type=jnp.float32,
        ).astype(jnp.bfloat16)

    for f in range(bins):
        right = []
        for place in range(groups):
            value = placed_ref[place, f]
            real, imag = value[:windows], value[windows:]
            right.append(
                jnp.concatenate(
                    [jnp.concatenate([real, imag], 1), jnp.concatenate([imag, -real], 1)], 0
                )
            )
        right = jnp.concatenate(right, 0)
        for delta in range(groups):
            panel = jnp.dot(
                left_ref[f, :, : rows * (groups - delta)],
                right[rows * delta :],
                preferred_element_type=jnp.float32,
            )
            for half in range(2):
                lanes = slice(half * BLOCK, (half + 1) * BLOCK)
                skewed = pltpu.roll(panel[:, lanes], 1, 1, stride=1, stride_axis=0)
                forward = jnp.where(ahead, skewed, 0.0).reshape(-1, 8, BLOCK).sum(0)
                backward = jnp.where(ahead, 0.0, skewed).reshape(-1, 8, BLOCK).sum(0)
                first = (f * 2 * groups + delta) * 8
                part_ref[half, first : first + 8] = forward
                part_ref[half, first + groups * 8 : first + groups * 8 + 8] = backward

    lags = []
    for half in range(2):
        summed = part_ref[half, pl.ds(0, bins * 2 * groups, stride=8), :]
        for sublane in range(1, 8):
            summed = summed + part_ref[half, pl.ds(sublane, bins * 2 * groups, stride=8), :]
        lags.append(summed)
    weight = stack_weights(groups)

    terms = []
    for f in range(bins):
        lag_rows = slice(f * 2 * groups, (f + 1) * 2 * groups)
        means = jnp.concatenate([half[lag_rows] * weight for half in lags], 0)
        mean_high, mean_low = halves(means)
        spread = jnp.concatenate(
            [
                jnp.concatenate([mean_high, mean_high], 1),
                jnp.concatenate([mean_low, jnp.zeros_like(mean_low)], 1),
            ],
            0,
        )
        product = jnp.dot(spread, lag_ref[start + f], preferred_element_type=jnp.float32)
        product = product[: 4 * groups] + product[4 * groups :]
        by_cos, by_sin = product[:, :SLOWNESS], product[:, SLOWNESS:]
        real = by_cos[: 2 * groups] - by_sin[2 * groups :]
        imag = by_sin[: 2 * groups] + by_cos[2 * groups :]
        shift_cos, shift_sin = shift_ref[start + f, 0], shift_ref[start + f, 1]
        turned_re = real * shift_cos - imag * shift_sin
        turned_im = real * shift_sin + imag * shift_cos
        terms.append(turned_re[:groups] + turned_re[groups:])
        terms.append(turned_im[:groups] + turned_im[groups:])

    if parts is None:
        for entry, term in enumerate(terms):
            out_ref[entry] = term
        return
    for earlier_ref in reversed(earlier_refs):
        terms = [earlier_ref[entry] for entry in range(earlier_ref.shape[0])] + terms
    slow_dev = SLOWNESS // parts
    spans = BLOCK // slow_dev
    span_index = lax.broadcasted_iota(jnp.int32, (groups, BLOCK), 1) // slow_dev
    for part in range(parts):
        source = (part % spans) * slow_dev
        lanes = slice(part // spans * BLOCK, (part // spans + 1) * BLOCK)
        for row in range(out_ref.shape[2]):
            packed = jnp.zeros((groups, BLOCK), jnp.float32)
            for span, term in enumerate(terms[row * spans : (row + 1) * spans]):
                moved = pltpu.roll(term[:, lanes], (span * slow_dev - source) % BLOCK, 1)
                packed = jnp.where(span_index == span, moved, packed)
            for delta in range(groups):
                out_ref[groups - 1 - delta, parts - 1 - part, row] = packed[delta]


def image_kernel(slow_dev, spans, term_ref, table_ref, out_ref):
    arrived = term_ref[...]
    turned = arrived.reshape(-1, BLOCK).T
    sums = []
    for odd, chosen in enumerate(spans):
        terms = jnp.concatenate(
            [turned[span * slow_dev : (span + 1) * slow_dev] for span in chosen], 1
        )
        high, low = halves(terms)
        by_high = jnp.dot(
            jnp.concatenate([high, low], 0), table_ref[odd, 0], preferred_element_type=jnp.float32
        )
        by_low = jnp.dot(high, table_ref[odd, 1], preferred_element_type=jnp.float32)
        sums.append(by_high[:slow_dev] + by_high[slow_dev:] + by_low)
    even, odd = sums
    out_ref[0, :, : LAG_TIMES // 2] = even - odd
    out_ref[0, :, LAG_TIMES // 2 :] = even + odd


def time_table(groups, parts, bins, slow_dev, message_rows):
    count = min(BLOCK // slow_dev, 2 * bins)
    spans = [[span for span in range(count) if span // 2 % 2 == odd] for odd in range(2)]
    tables = []
    for chosen in spans:
        span, group, part, row = np.meshgrid(
            chosen,
            np.arange(groups)[::-1],
            np.arange(parts)[::-1],
            np.arange(message_rows),
            indexing="ij",
        )
        entry = row * count + span
        freq = (part * groups + group) * bins + entry // 2
        lag_time = np.arange(LAG_TIMES // 2)
        angle = 2.0 * math.pi / LAG_TIMES * ((freq[..., None] * lag_time) % LAG_TIMES)
        table = np.where((entry % 2 == 0)[..., None], np.cos(angle), -np.sin(angle))
        table = table.reshape(-1, LAG_TIMES // 2).astype(np.float32)
        high = table.astype(jnp.bfloat16)
        low = (table - high.astype(np.float32)).astype(jnp.bfloat16)
        tables.append(np.stack([high, low]))
    return spans, np.stack(tables)


def shards(spectra, block_position):
    groups = lax.axis_size("chan")
    parts = lax.axis_size("freq")
    rows = spectra.shape[0] * spectra.shape[1]
    freq_dev = spectra.shape[2]
    bins = freq_dev // groups
    slow_dev = SLOWNESS // parts
    message_rows = -(-2 * bins * slow_dev // BLOCK)
    vmem = pl.BlockSpec(memory_space=pltpu.VMEM)
    anywhere = pl.BlockSpec(memory_space=pl.ANY)
    params = pltpu.CompilerParams(vmem_limit_bytes=32 * 1024 * 1024)

    whole = spectra.reshape(rows, groups, bins, BLOCK)

    def cut(cuts, *earlier):
        distances = {distance for distance, _, _ in cuts}
        return pl.pallas_call(
            functools.partial(chunk_kernel, cuts),
            out_shape=tuple(
                jax.ShapeDtypeStruct((size, rows, BLOCK), jnp.bfloat16) for _, _, size in cuts
            ),
            in_specs=[vmem] + [anywhere] * len(earlier),
            out_specs=(vmem,) * len(cuts),
            scratch_shapes=[pltpu.VMEM((len(distances), rows * bins, BLOCK), jnp.float32)],
            compiler_params=params,
            cost_estimate=pl.CostEstimate(flops=10**7, bytes_accessed=10**6, transcendentals=0),
            name="chunks_of_bins",
        )(whole, *earlier)

    late = max(1, 3 * bins // 8) if bins > 1 else 0
    pieces = [(0, bins - late), (bins - late, late)] if late else [(0, bins)]
    far_first = sorted(range(1, groups), key=lambda steps: abs(2 * steps - groups)) + [0]
    near_first = list(range(1, groups)) + [0]
    orders = [far_first, near_first][: len(pieces)]
    cuts = [(distance, *piece) for piece, order in zip(pieces, orders) for distance in order]
    (first_chunk,) = cut(cuts[:1])
    chunks = dict(zip(cuts, (first_chunk, *cut(cuts[1:], first_chunk))))
    for key in cuts:
        if key[0]:
            pairs = [(source, (source + key[0]) % groups) for source in range(groups)]
            chunks[key] = lax.ppermute(chunks[key], "chan", pairs)
    chunks[cuts[0]] = pl.pallas_call(
        copy_kernel,
        out_shape=jax.ShapeDtypeStruct(first_chunk.shape, jnp.bfloat16),
        in_specs=[vmem],
        out_specs=vmem,
        compiler_params=params,
        name="first_arrived",
    )(chunks[cuts[0]])
    places, lag_table, shift_table = pl.pallas_call(
        functools.partial(table_kernel, groups, bins, freq_dev),
        out_shape=(
            jax.ShapeDtypeStruct((groups, BLOCK), jnp.int32),
            jax.ShapeDtypeStruct((bins, 2 * BLOCK, 2 * SLOWNESS), jnp.bfloat16),
            jax.ShapeDtypeStruct((bins, 2, 2 * groups, SLOWNESS), jnp.float32),
        ),
        in_specs=[vmem],
        out_specs=(vmem, vmem, vmem),
        compiler_params=params,
        cost_estimate=pl.CostEstimate(flops=10**7, bytes_accessed=4 * 10**6, transcendentals=0),
        name="slant_tables",
    )(block_position.reshape(1, groups))
    earlier = []
    for (start, size), order in zip(pieces, orders):
        last = start + size == bins
        shape = (groups, parts, message_rows, BLOCK) if last else (2 * size, groups, SLOWNESS)
        terms = pl.pallas_call(
            functools.partial(stack_kernel, order, start, size, parts if last else None),
            out_shape=jax.ShapeDtypeStruct(shape, jnp.float32),
            in_specs=[vmem] * (groups + 3 + len(earlier)),
            out_specs=vmem,
            scratch_shapes=[
                pltpu.VMEM((groups, size, rows, BLOCK), jnp.bfloat16),
                pltpu.VMEM((size, BLOCK, groups * rows), jnp.bfloat16),
                pltpu.VMEM((2, size * 2 * groups * 8, BLOCK), jnp.float32),
            ],
            compiler_params=params,
            cost_estimate=pl.CostEstimate(
                flops=2 * 10**8, bytes_accessed=4 * 10**6, transcendentals=0
            ),
            name="stack_and_slant",
        )(
            *[chunks[distance, start, size] for distance in order],
            places,
            lag_table,
            shift_table,
            *earlier,
        )
        earlier.append(terms)
    terms = terms.reshape(groups * parts, message_rows, BLOCK)
    arrived = lax.all_to_all(
        terms,
        ("chan", "freq"),
        split_axis=0,
        concat_axis=0,
        axis_index_groups=[list(range(groups * parts))[::-1]],
        tiled=True,
    )
    spans, table = time_table(groups, parts, bins, slow_dev, message_rows)
    return pl.pallas_call(
        functools.partial(image_kernel, slow_dev, spans),
        out_shape=jax.ShapeDtypeStruct((1, slow_dev, LAG_TIMES), jnp.float32),
        in_specs=[vmem, vmem],
        out_specs=vmem,
        compiler_params=params,
        name="sum_of_bins",
    )(arrived, jnp.asarray(table))


def solution(mesh):
    return jax.shard_map(
        shards,
        mesh=mesh,
        in_specs=(P(None, None, "freq", "chan"), P()),
        out_specs=P("chan", "freq", None),
        check_vma=False,
    )
```
